32 devices in a mesh: groups: 2 (over y), expert: 8 (over z, x), dp: 2 (over core).
Axes of the slice: x: 2, y: 2, z: 4, core: 2. Of those that a mesh axis runs over, the one named last changes fastest.
Arguments:
- cotangent: bfloat16 [4096, 3584], P(('groups', 'expert', 'dp')), parts along dimension 0, may hold values from -6 to 6
- hidden: bfloat16 [4096, 8, 128], P(('groups', 'expert', 'dp')), parts along dimension 0, may hold values from -1.5 to 1.5
- probs: bfloat16 [4096, 8], P(('groups', 'expert', 'dp')), parts along dimension 0, may hold values from 0.049804688 to 0.5
- expert_ids: int32 [4096, 8], P(('groups', 'expert', 'dp')), parts along dimension 0, may hold values from 0 to 15, as said below
- send_counts: int32 [32, 8], P(('groups', 'expert', 'dp')), parts along dimension 0, may hold values from 0 to 3
- replica_of: int32 [16], P('groups'), parts along dimension 0, may hold values from 0 to 15, as said below
- weights: bfloat16 [16, 128, 3584], P('expert'), may hold values from -0.09375 to 0.09375
Outputs:
- hidden_gradient: bfloat16 [4096, 8, 128], P(('groups', 'expert', 'dp')), parts along dimension 0
- grad_probs: bfloat16 [4096, 8], P(('groups', 'expert', 'dp')), parts along dimension 0
- grad_weights: bfloat16 [32, 128, 3584], P(('groups', 'expert'), None, 'dp'), parts along dimension 0
The draws below stay inside these ranges and needn't reach their ends.
There are 2 independent parts, one for each index of `groups`. The reference program is written for one: setup_inputs(seed, part) draws one part's arguments, and reference() takes and returns one part's arrays. A program takes and returns all parts, laid end to end along the dimension named above; an argument that names none is the same for every part. Nothing has to cross between parts.
Inputs may be any that keep to these rules, and one draw needn't show every extreme that they name: `expert_ids`: each row names 8 different experts. `replica_of`: entry d is never one of the experts homed on device d, d * 2 to d * 2 + 1.
All inputs are finite; a program needn't handle non-finite values.
Results may differ from the reference program's by a relative error of at most 0.0058.
Values may be sent and summed in bfloat16 or wider, within the bound.
No kernel may reach another device: no remote copies, remote signals or barrier semaphores. Data moves between devices by JAX's collectives and lax.ppermute only.
A program may use at most 128 MiB of HBM per device.

```python
import jax
import jax.numpy as jnp
from jax import lax

D = 3584
HIDDEN_PER_UNIT = 128
EXP_DEV = 2
TOP = 8
CAPH = 3
CAPR = 3
TOK_DEV = 128
EXPERT_COUNT = 16
HOT = 2
TOKENS = 2048
N_EXPERT = 8
N_DP = 2


def hot_experts(key):
    middle_devices = 1 + jax.random.permutation(key, N_EXPERT - 2)[:HOT - 2]
    within_dev = jax.random.randint(jax.random.fold_in(key, 7), (HOT - 2,), 0, EXP_DEV)
    middle = (middle_devices * EXP_DEV + within_dev).astype(jnp.int32)
    ends = jnp.array([EXPERT_COUNT - 1, 0], jnp.int32)
    return jnp.concatenate([ends, middle]).astype(jnp.int32)


def draw_expert_ids(key, part):
    popular_experts = hot_experts(key)
    key = jax.random.fold_in(key, 11)
    expert_scores = jax.random.randint(key, (TOKENS, EXPERT_COUNT), 0, 1 << 20)
    extra_credit = jnp.zeros((EXPERT_COUNT,), jnp.int32).at[popular_experts].set(63000)
    running_totals = (expert_scores + extra_credit[None, :]) * EXPERT_COUNT + jnp.arange(EXPERT_COUNT, dtype=jnp.int32)[None, :]
    return lax.top_k(running_totals, TOP)[1].astype(jnp.int32)


def draw_replica_of(key, part):
    popular_experts = hot_experts(key)
    key = jax.random.fold_in(key, 23)
    chosen = jax.random.randint(key, (N_EXPERT,), 0, HOT)
    home_dev = popular_experts // EXP_DEV
    clashes = home_dev[chosen] == jnp.arange(N_EXPERT, dtype=jnp.int32)
    chosen = jnp.where(clashes, (chosen + 1) % HOT, chosen)
    chosen = chosen.at[0].set(0).at[N_EXPERT - 1].set(1)
    return popular_experts[chosen].astype(jnp.int32)


def with_ends(values, own_key, least, top_value):
    index_at = [jax.random.randint(jax.random.fold_in(own_key, axis), (), 0, length) for axis, length in enumerate(values.shape)]
    main_axis = values.shape.index(max(values.shape))
    next_to = index_at[:main_axis] + [(index_at[main_axis] + 1) % values.shape[main_axis]] + index_at[main_axis + 1:]
    return values.at[tuple(index_at)].set(least).at[tuple(next_to)].set(top_value)


def level_of(stream_key, dims, shards, smallest, top_value):
    loudness, own = 1.0, jax.random.fold_in(stream_key, 6)
    for axis_at, blocks in shards:
        heights = jnp.exp(jax.random.uniform(jax.random.fold_in(own, axis_at), (blocks,), jnp.float32, smallest / len(shards), top_value / len(shards)))
        loudness = loudness * jnp.repeat(heights, dims[axis_at] // blocks).reshape([-1 if axis == axis_at else 1 for axis in range(len(dims))])
    return loudness


def centred(rng, extent, deviation, bound, split=(), kind=jnp.bfloat16):
    gain = level_of(rng, extent, split, -0.22, 0.18) if split else 1.0
    drawn = jax.random.normal(rng, extent, jnp.float32) * deviation * gain
    return jnp.minimum(jnp.maximum(drawn, -bound), bound).astype(kind)


def setup_inputs(seed: int = 0, part: int = 0) -> dict:
    key_list = jax.random.split(jax.random.key(seed), 8)
    own_keys = jax.random.split(jax.random.fold_in(key_list[7], part), 8)
    cotangent = centred(own_keys[0], (TOKENS, D), 1.0, 6.0, ((0, 16),))
    hidden = centred(own_keys[1], (TOKENS, TOP, HIDDEN_PER_UNIT), 0.25, 1.5, ((0, 16),))
    probs = jnp.clip(0.049804688 + 0.4501953 * jax.random.uniform(own_keys[2], (TOKENS, TOP), jnp.float32) ** level_of(own_keys[2], (TOKENS, TOP), ((0, 16),), -0.2, 0.2), 0.049804688, 0.5).astype(jnp.bfloat16)
    expert_ids = draw_expert_ids(jax.random.fold_in(jax.random.fold_in(key_list[7], part), 71), part)
    send_counts = with_ends(jax.random.randint(own_keys[4], (N_EXPERT * N_DP, N_EXPERT), 0, CAPR + 1), jax.random.fold_in(own_keys[4], 1), 0, CAPR).astype(jnp.int32)
    replica_of = draw_replica_of(jax.random.fold_in(jax.random.fold_in(key_list[7], part), 71), part)
    weights = centred(key_list[6], (EXPERT_COUNT, HIDDEN_PER_UNIT, D), D ** -0.5, 0.09375, ((0, 8),))
    return dict(cotangent=cotangent, hidden=hidden, probs=probs, expert_ids=expert_ids, send_counts=send_counts, replica_of=replica_of, weights=weights)


def ranks_within(keys):
    total_rows = keys.shape[0]
    sort_order = jnp.argsort(keys * total_rows + jnp.arange(total_rows, dtype=jnp.int32))
    sorted_keys = keys[sort_order]
    first_seen = jnp.searchsorted(sorted_keys, sorted_keys, side="left").astype(jnp.int32)
    ranked = jnp.arange(total_rows, dtype=jnp.int32) - first_seen
    return jnp.zeros((total_rows,), jnp.int32).at[sort_order].set(ranked)


def route_rows(ids_block, counts_row, replica_of, local_count, cap_home, cap_copy):
    dev_count = replica_of.shape[0]
    experts = ids_block.reshape(-1).astype(jnp.int32)
    rank_expert = ranks_within(experts)
    devices = jnp.arange(dev_count, dtype=jnp.int32)
    same_copy = (replica_of[:, None] == replica_of[None, :]) & (devices[None, :] < devices[:, None])
    lower_rank = jnp.sum(jnp.where(same_copy, counts_row[None, :], 0), axis=1).astype(jnp.int32)
    upper_rank = lower_rank + counts_row
    hit_table = (replica_of[None, :] == experts[:, None]) & (lower_rank[None, :] <= rank_expert[:, None]) & (rank_expert[:, None] < upper_rank[None, :])
    copied = jnp.any(hit_table, axis=1)
    copy_dev = jnp.sum(jnp.where(hit_table, devices[None, :], 0), axis=1).astype(jnp.int32)
    dest_dev = jnp.where(copied, copy_dev, experts // local_count)
    index_of_slot = jnp.where(copied, local_count, experts % local_count)
    rank_bucket = ranks_within(dest_dev * (local_count + 1) + index_of_slot)
    keep_row = rank_bucket < jnp.where(copied, cap_copy, cap_home)
    per_dev = local_count * cap_home + cap_copy
    target = dest_dev * per_dev + index_of_slot * cap_home + rank_bucket
    return jnp.where(keep_row, target, dev_count * per_dev).astype(jnp.int32)


def slot_products(dy_rows, h_rows, p_rows, matrix):
    grad_in = jnp.dot(dy_rows, matrix.T, preferred_element_type=jnp.float32)
    p_wide = p_rows.astype(jnp.float32)[:, None]
    grad_h = (p_wide * grad_in).astype(jnp.bfloat16)
    grad_p = jnp.sum(h_rows.astype(jnp.float32) * grad_in, axis=1).astype(jnp.bfloat16)
    scaled = (p_wide * h_rows.astype(jnp.float32)).astype(jnp.bfloat16)
    partial_value = jnp.dot(scaled.T, dy_rows, preferred_element_type=jnp.float32).astype(jnp.bfloat16)
    return grad_h, grad_p, partial_value


def reference(cotangent, hidden, probs, expert_ids, send_counts, replica_of, weights):
    dev_count = N_EXPERT
    src_count = N_EXPERT * N_DP
    per_dev = EXP_DEV * CAPH + CAPR
    row_count = TOK_DEV * TOP

    def route_block(ids_block, counts_row):
        return route_rows(ids_block, counts_row, replica_of, EXP_DEV, CAPH, CAPR)

    targets = jax.vmap(route_block)(expert_ids.reshape(src_count, TOK_DEV, TOP), send_counts)

    def invert(target):
        return jnp.full((dev_count * per_dev,), row_count, jnp.int32).at[target].set(jnp.arange(row_count, dtype=jnp.int32), mode="drop")

    inverse = jax.vmap(invert)(targets).reshape(dev_count, N_DP, dev_count, per_dev)
    dy_blocks = jnp.concatenate([cotangent.reshape(src_count, TOK_DEV, D), jnp.zeros((src_count, 1, D), cotangent.dtype)], axis=1)
    h_blocks = jnp.concatenate([hidden.reshape(src_count, row_count, HIDDEN_PER_UNIT), jnp.zeros((src_count, 1, HIDDEN_PER_UNIT), hidden.dtype)], axis=1)
    p_blocks = jnp.concatenate([probs.reshape(src_count, row_count), jnp.zeros((src_count, 1), probs.dtype)], axis=1)
    sources = jnp.arange(dev_count, dtype=jnp.int32)

    def one_host(grad_total, host_index):
        dest_dev = host_index // N_DP
        data_idx = host_index % N_DP
        slot_rows = inverse[:, data_idx, dest_dev, :]
        src_rows = (sources * N_DP + data_idx)[:, None]
        dy_rows = dy_blocks[src_rows, slot_rows // TOP]
        h_rows = h_blocks[src_rows, slot_rows]
        p_rows = p_blocks[src_rows, slot_rows]
        grads_h = []
        grads_p = []
        for slot_num in range(EXP_DEV + 1):
            row_start = slot_num * CAPH
            slot_size = CAPR if slot_num == EXP_DEV else CAPH
            expert = replica_of[dest_dev] if slot_num == EXP_DEV else dest_dev * EXP_DEV + slot_num
            grad_h, grad_p, partial_value = slot_products(
                dy_rows[:, row_start:row_start + slot_size].reshape(-1, D),
                h_rows[:, row_start:row_start + slot_size].reshape(-1, HIDDEN_PER_UNIT),
                p_rows[:, row_start:row_start + slot_size].reshape(-1),
                weights[expert])
            grads_h.append(grad_h.reshape(dev_count, slot_size, HIDDEN_PER_UNIT))
            grads_p.append(grad_p.reshape(dev_count, slot_size))
            grad_total = grad_total.at[expert].add(partial_value.astype(jnp.float32))
        return grad_total, (jnp.concatenate(grads_h, axis=1), jnp.concatenate(grads_p, axis=1))

    grad_init = jnp.zeros((EXPERT_COUNT, HIDDEN_PER_UNIT, D), jnp.float32)
    grad_total, (back_h, back_p) = lax.scan(one_host, grad_init, jnp.arange(dev_count * N_DP, dtype=jnp.int32))
    back_h = back_h.reshape(dev_count, N_DP, dev_count, per_dev, HIDDEN_PER_UNIT).transpose(2, 1, 0, 3, 4).reshape(src_count, dev_count * per_dev, HIDDEN_PER_UNIT)
    back_p = back_p.reshape(dev_count, N_DP, dev_count, per_dev).transpose(2, 1, 0, 3).reshape(src_count, dev_count * per_dev)
    back_h = jnp.concatenate([back_h, jnp.zeros((src_count, 1, HIDDEN_PER_UNIT), back_h.dtype)], axis=1)
    back_p = jnp.concatenate([back_p, jnp.zeros((src_count, 1), back_p.dtype)], axis=1)
    hidden_gradient = jnp.take_along_axis(back_h, targets[:, :, None], axis=1).reshape(TOKENS, TOP, HIDDEN_PER_UNIT)
    grad_probs = jnp.take_along_axis(back_p, targets, axis=1).reshape(TOKENS, TOP)
    return hidden_gradient, grad_probs, grad_total.astype(jnp.bfloat16)
```

```python
import functools

import jax
import jax.numpy as jnp
from jax import lax
from jax.experimental import pallas as pl
from jax.experimental.pallas import tpu as pltpu
from jax.sharding import PartitionSpec as P

CAPH = 3
CAPR = 3


def ranks_within(keys):
    total_rows = keys.shape[0]
    sort_order = jnp.argsort(keys * total_rows + jnp.arange(total_rows, dtype=jnp.int32))
    sorted_keys = keys[sort_order]
    first_seen = jnp.searchsorted(sorted_keys, sorted_keys, side="left")
    ranked = jnp.arange(total_rows, dtype=jnp.int32) - first_seen
    return jnp.zeros((total_rows,), jnp.int32).at[sort_order].set(ranked)


def route_rows(ids_block, counts_row, replica_of, local_count, cap_home, cap_copy):
    dev_count = replica_of.shape[0]
    experts = ids_block.reshape(-1)
    rank_expert = ranks_within(experts)
    devices = jnp.arange(dev_count, dtype=jnp.int32)
    same_copy = (replica_of[:, None] == replica_of[None, :]) & (devices[None, :] < devices[:, None])
    lower_rank = jnp.sum(jnp.where(same_copy, counts_row[None, :], 0), axis=1)
    upper_rank = lower_rank + counts_row
    hit_table = (
        (replica_of[None, :] == experts[:, None])
        & (lower_rank[None, :] <= rank_expert[:, None])
        & (rank_expert[:, None] < upper_rank[None, :])
    )
    copied = jnp.any(hit_table, axis=1)
    copy_dev = jnp.sum(jnp.where(hit_table, devices[None, :], 0), axis=1)
    dest_dev = jnp.where(copied, copy_dev, experts // local_count)
    index_of_slot = jnp.where(copied, local_count, experts % local_count)
    rank_bucket = ranks_within(dest_dev * (local_count + 1) + index_of_slot)
    keep_row = rank_bucket < jnp.where(copied, cap_copy, cap_home)
    per_dev = local_count * cap_home + cap_copy
    target = dest_dev * per_dev + index_of_slot * cap_home + rank_bucket
    return jnp.where(keep_row, target, dev_count * per_dev)


def replica_body(cotangent, hidden, probs, expert_ids, send_counts, replica_of, weights):
    tok_rows, d_model = cotangent.shape
    top_count = expert_ids.shape[1]
    hidden_width = hidden.shape[2]
    local_count = weights.shape[0]
    dev_count = lax.axis_size("expert")
    data_count = lax.axis_size("dp")
    per_dev = local_count * CAPH + CAPR
    row_count = tok_rows * top_count
    recv_count = dev_count * per_dev
    target = route_rows(expert_ids, send_counts[0], replica_of, local_count, CAPH, CAPR)
    inverse = (
        jnp.full((recv_count,), row_count, jnp.int32)
        .at[target]
        .set(jnp.arange(row_count, dtype=jnp.int32), mode="drop")
    )
    dy_pad = jnp.concatenate([cotangent, jnp.zeros((1, d_model), cotangent.dtype)], axis=0)
    h_pad = jnp.concatenate(
        [hidden.reshape(row_count, hidden_width), jnp.zeros((1, hidden_width), hidden.dtype)],
        axis=0,
    )
    p_pad = jnp.concatenate([probs.reshape(row_count), jnp.zeros((1,), probs.dtype)], axis=0)
    send_dy = dy_pad[inverse // top_count]
    send_h = h_pad[inverse]
    send_p = p_pad[inverse]
    recv_dy, recv_h, recv_p = (
        lax.all_to_all(send_dy, "expert", split_axis=0, concat_axis=0, tiled=True),
        lax.all_to_all(send_h, "expert", split_axis=0, concat_axis=0, tiled=True),
        lax.all_to_all(send_p, "expert", split_axis=0, concat_axis=0, tiled=True),
    )
    flat_size = hidden_width * d_model
    flat_w = weights.reshape(local_count, flat_size)
    pieces = lax.all_to_all(flat_w, "expert", split_axis=1, concat_axis=0, tiled=True)
    chosen = pieces[replica_of]
    copy_weight = lax.all_to_all(chosen, "expert", split_axis=0, concat_axis=0, tiled=True).reshape(
        hidden_width, d_model
    )
    slot_total = local_count + 1
    home_rows = local_count * CAPH
    row_pos = jnp.arange(recv_count, dtype=jnp.int32) % per_dev
    row_slot = jnp.where(row_pos < home_rows, row_pos // CAPH, local_count)
    all_weights = jnp.concatenate(
        [weights.reshape(local_count * hidden_width, d_model), copy_weight], axis=0
    )
    all_in = lax.dot_general(
        recv_dy, all_weights, (((1,), (1,)), ((), ())), preferred_element_type=jnp.float32
    )
    grad_in = jnp.zeros((recv_count, hidden_width), jnp.float32)
    for slot_num in range(slot_total):
        grad_in = grad_in + jnp.where(
            (row_slot == slot_num)[:, None],
            all_in[:, slot_num * hidden_width : (slot_num + 1) * hidden_width],
            0.0,
        )
    p_wide = recv_p.astype(jnp.float32)[:, None]
    h_wide = recv_h.astype(jnp.float32)
    grad_h_buf = (p_wide * grad_in).astype(jnp.bfloat16)
    grad_p_buf = jnp.sum(h_wide * grad_in, axis=1).astype(jnp.bfloat16)
    scaled = (p_wide * h_wide).astype(jnp.bfloat16)
    zero_rows = jnp.zeros_like(scaled)
    scaled_wide = jnp.concatenate(
        [
            jnp.where((row_slot == slot_num)[:, None], scaled, zero_rows)
            for slot_num in range(slot_total)
        ],
        axis=1,
    )
    parts = lax.dot_general(
        scaled_wide, recv_dy, (((0,), (0,)), ((), ())), preferred_element_type=jnp.float32
    ).astype(jnp.bfloat16)
    home_part = parts[: local_count * hidden_width].reshape(local_count, hidden_width, d_model)
    copy_part = parts[local_count * hidden_width :]
    back_h, back_p = (
        lax.all_to_all(grad_h_buf, "expert", split_axis=0, concat_axis=0, tiled=True),
        lax.all_to_all(grad_p_buf, "expert", split_axis=0, concat_axis=0, tiled=True),
    )
    flat_h = jnp.concatenate([back_h, jnp.zeros((1, hidden_width), back_h.dtype)], axis=0)
    flat_p = jnp.concatenate([back_p, jnp.zeros((1,), back_p.dtype)], axis=0)
    hidden_gradient = flat_h[target].reshape(tok_rows, top_count, hidden_width)
    grad_probs = flat_p[target].reshape(tok_rows, top_count)
    expert_total = dev_count * local_count
    cover = replica_of[None, :] == jnp.arange(expert_total, dtype=jnp.int32)[:, None]
    half_width = d_model // data_count
    halves = lax.all_to_all(copy_part, "dp", split_axis=1, concat_axis=0, tiled=True)
    copy_half = jnp.sum(
        halves.reshape(data_count, hidden_width, half_width).astype(jnp.float32), axis=0
    )
    piece_len = hidden_width * half_width // dev_count
    slabs = copy_half.reshape(dev_count, piece_len)
    arrived = lax.all_to_all(slabs, "expert", split_axis=0, concat_axis=0, tiled=True)
    sums = jnp.dot(cover.astype(jnp.float32), arrived, precision=lax.Precision.HIGHEST)
    homed = lax.all_to_all(
        sums.reshape(dev_count, local_count * piece_len),
        "expert",
        split_axis=0,
        concat_axis=0,
        tiled=True,
    )
    homed = (
        homed.reshape(dev_count, local_count, piece_len)
        .transpose(1, 0, 2)
        .reshape(local_count, hidden_width, half_width)
    )
    home_half = lax.psum_scatter(
        home_part.astype(jnp.float32).astype(jnp.bfloat16), "dp", scatter_dimension=2, tiled=True
    ).astype(jnp.float32)
    grad_weights = (home_half + homed).astype(jnp.bfloat16)
    return (hidden_gradient, grad_probs, grad_weights)


SLOT = 4
F32 = jnp.float32
BF16 = jnp.bfloat16
NT = (((1,), (1,)), ((), ()))
TN = (((0,), (0,)), ((), ()))


def iota(shape, dim):
    return lax.broadcasted_iota(jnp.int32, shape, dim)


def dispatch_kernel(local_count, dev_count, replica_ref, counts_ref, ids_ref, probs_ref, cot_ref, hid_ref,
                    home_ref, copy_ref, pick_ref, expert_ref, hs_ref, ps_ref, wide):
    top, toks = ids_ref.shape
    d_model = cot_ref.shape[1]
    homes = dev_count * local_count * SLOT
    slots = homes + dev_count * CAPR
    row = iota((slots, toks), 0)
    expert = row // SLOT
    within = row % SLOT
    allowed = jnp.where(within < CAPH, 1, 0)
    for d in range(dev_count):
        first = homes + d * CAPR
        mine = (row >= first) & (row < first + CAPR)
        expert = jnp.where(mine, replica_ref[d], expert)
        within = jnp.where(mine, row - first, within)
        allowed = jnp.where(mine, jnp.where(row - first < counts_ref[0, d], 1, 0), allowed)
    lower = jnp.zeros((slots, toks), jnp.int32)
    for d in range(dev_count):
        earlier = (row < homes) | (row >= homes + (d + 1) * CAPR)
        lower = lower + jnp.where(earlier & (expert == replica_ref[d]), counts_ref[0, d], 0)
    ids = ids_ref[...]
    named = jnp.zeros((slots, toks), F32)
    for k in range(top):
        named = named + jnp.where(ids[k:k + 1, :] == expert, 1.0, 0.0)
    before = jnp.where(iota((toks, toks), 0) < iota((toks, toks), 1), 1.0, 0.0).astype(BF16)
    rank = jnp.dot(named.astype(BF16), before, preferred_element_type=F32)
    wanted = (lower + within).astype(F32)
    pick = jnp.where((rank == wanted) & (allowed > 0), named, 0.0)
    pick_ref[...] = pick
    expert_ref[...] = expert
    wide[...] = hid_ref[...].astype(F32)
    h_slot = jnp.zeros((slots, hid_ref.shape[1]), F32)
    p_slot = jnp.zeros((slots, toks), F32)
    probs = probs_ref[...].astype(F32)
    for k in range(top):
        sel = jnp.where(ids[k:k + 1, :] == expert, pick, 0.0)
        h_k = wide[pl.ds(k, toks, stride=top), :].astype(BF16)
        h_slot = h_slot + jnp.dot(sel.astype(BF16), h_k, preferred_element_type=F32)
        p_slot = p_slot + sel * probs[k:k + 1, :]
    p_slot = jnp.sum(p_slot, axis=1, keepdims=True)
    hs_ref[...] = h_slot
    ps_ref[...] = jnp.broadcast_to(p_slot, ps_ref.shape)
    scaled = p_slot * h_slot
    rows = jnp.dot(pick.astype(BF16), cot_ref[...], preferred_element_type=F32)
    home_ref[:, :d_model] = rows[:homes].astype(BF16)
    home_ref[:, d_model:] = scaled[:homes].astype(BF16)
    copy_ref[:, :d_model] = rows[homes:].astype(BF16)
    copy_ref[:, d_model:] = scaled[homes:].astype(BF16)


def local_slots(local_count, dev_count, width, replica_ref):
    first = lax.axis_index("expert") * local_count
    home = (iota((dev_count * local_count * SLOT, width), 0) // SLOT) % local_count
    row = iota((dev_count * CAPR, width), 0)
    copy = jnp.full((dev_count * CAPR, width), -1, jnp.int32)
    for d in range(dev_count):
        mine = (row >= d * CAPR) & (row < (d + 1) * CAPR)
        copy = jnp.where(mine, replica_ref[d] - first, copy)
    copy = jnp.broadcast_to(copy[None], (dev_count, dev_count * CAPR, width))
    return home, copy.reshape(dev_count * dev_count * CAPR, width)


def grad_in_kernel(local_count, dev_count, replica_ref, home_ref, copy_ref, w_ref, out_ref):
    d_model = w_ref.shape[1]
    width = w_ref.shape[0] // local_count
    per_home, per_copy = local_count * SLOT, dev_count * CAPR
    results = []
    for ref, slot in zip((home_ref, copy_ref), local_slots(local_count, dev_count, width, replica_ref)):
        every = lax.dot_general(ref[:, :d_model], w_ref[...], NT, preferred_element_type=F32)
        own = jnp.zeros((ref.shape[0], width), F32)
        for e in range(local_count):
            own = jnp.where(slot == e, every[:, e * width:(e + 1) * width], own)
        results.append(own)
    home, copy = results
    both = jnp.concatenate(
        [home.reshape(dev_count, per_home, width), copy.reshape(dev_count, per_copy, width)], axis=1)
    out_ref[...] = both.reshape(dev_count * (per_home + per_copy), width).astype(out_ref.dtype)


def grad_weights_half(local_count, dev_count, half, replica_ref, home_ref, copy_ref, columns):
    width = home_ref.shape[1] - 2 * columns
    start = pl.multiple_of(half * columns, 128)
    total = None
    for ref, slot in zip((home_ref, copy_ref), local_slots(local_count, dev_count, width, replica_ref)):
        scaled = ref[:, 2 * columns:].astype(F32)
        spread = jnp.concatenate([jnp.where(slot == e, scaled, 0.0) for e in range(local_count)], axis=1)
        part = lax.dot_general(spread.astype(BF16), ref[:, pl.ds(start, columns)], TN, preferred_element_type=F32)
        total = part if total is None else total + part
    return total


def other_half_kernel(local_count, dev_count, replica_ref, home_ref, copy_ref, out_ref):
    half = 1 - lax.axis_index("dp")
    out_ref[...] = grad_weights_half(
        local_count, dev_count, half, replica_ref, home_ref, copy_ref, out_ref.shape[1]).astype(out_ref.dtype)


def own_half_kernel(local_count, dev_count, replica_ref, home_ref, copy_ref, arrived_ref, out_ref):
    half = lax.axis_index("dp")
    total = grad_weights_half(
        local_count, dev_count, half, replica_ref, home_ref, copy_ref, out_ref.shape[1])
    out_ref[...] = (total + arrived_ref[...].astype(F32)).astype(out_ref.dtype)


def combine_kernel(local_count, dev_count, back_ref, pick_ref, expert_ref, hs_ref, ps_ref, ids_ref,
                   grad_h_ref, grad_p_ref, wide):
    top, toks = ids_ref.shape
    width = back_ref.shape[1]
    per_home, per_copy = local_count * SLOT, dev_count * CAPR
    back = back_ref[...].astype(F32).reshape(dev_count, per_home + per_copy, width)
    home = back[:, :per_home].reshape(dev_count * per_home, width)
    copy = jnp.sum(back[:, per_home:], axis=0)
    grad_in = jnp.concatenate([home, copy], axis=0)
    h_rows = (ps_ref[...] * grad_in).astype(BF16)
    p_rows = jnp.sum(hs_ref[...] * grad_in, axis=1, keepdims=True)
    ids = ids_ref[...]
    pick = pick_ref[...]
    expert = expert_ref[...]
    for k in range(top):
        sel = jnp.where(ids[k:k + 1, :] == expert, pick, 0.0)
        wide[pl.ds(k, toks, stride=top), :] = lax.dot_general(
            sel.astype(BF16), h_rows, TN, preferred_element_type=F32)
        grad_p_ref[k:k + 1, :] = jnp.sum(sel * p_rows, axis=0, keepdims=True)
    grad_h_ref[...] = wide[...].astype(grad_h_ref.dtype)


def call(kernel, out_shape, smem, operands, scratch=(), flops=0):
    vmem = pl.BlockSpec(memory_space=pltpu.VMEM)
    shapes = jax.tree.leaves(out_shape)
    moved = sum(a.size * a.dtype.itemsize for a in (*operands, *shapes))
    return pl.pallas_call(
        kernel,
        out_shape=out_shape,
        in_specs=[pl.BlockSpec(memory_space=pltpu.SMEM)] * len(smem) + [vmem] * len(operands),
        out_specs=jax.tree.map(lambda _: vmem, out_shape),
        scratch_shapes=list(scratch),
        compiler_params=pltpu.CompilerParams(vmem_limit_bytes=24 << 20),
        cost_estimate=pl.CostEstimate(flops=flops, bytes_accessed=moved, transcendentals=0),
    )(*smem, *operands)


def gather_body(cotangent, hidden, probs, expert_ids, send_counts, replica_of, weights):
    toks, d_model = cotangent.shape
    top = expert_ids.shape[1]
    width = hidden.shape[2]
    local_count = weights.shape[0]
    dev_count = lax.axis_size("expert")
    homes = dev_count * local_count * SLOT
    copies = dev_count * CAPR
    slots = homes + copies
    sizes = (local_count, dev_count)
    ids = expert_ids.T
    shape = jax.ShapeDtypeStruct
    home_rows, copy_rows, pick, expert, h_slot, p_slot = call(
        functools.partial(dispatch_kernel, *sizes),
        (shape((homes, d_model + width), BF16), shape((copies, d_model + width), BF16), shape((slots, toks), F32),
         shape((slots, toks), jnp.int32), shape((slots, width), F32), shape((slots, width), F32)),
        (replica_of, send_counts),
        (ids, probs.T, cotangent, hidden.reshape(toks * top, width)),
        [pltpu.VMEM((toks * top, width), F32)],
        flops=2 * slots * toks * d_model,
    )
    home_in = lax.all_to_all(home_rows, "expert", split_axis=0, concat_axis=0, tiled=True)
    copy_in = lax.all_gather(copy_rows, "expert", axis=0, tiled=True)
    rows = homes + dev_count * copies
    w_flat = weights.reshape(local_count * width, d_model)
    back = call(
        functools.partial(grad_in_kernel, *sizes),
        shape((rows, width), BF16),
        (replica_of,),
        (home_in, copy_in, w_flat),
        flops=2 * rows * d_model * local_count * width,
    )
    back = lax.all_to_all(back, "expert", split_axis=0, concat_axis=0, tiled=True)
    columns = d_model // 2
    half_flops = 2 * rows * columns * local_count * width
    other = call(
        functools.partial(other_half_kernel, *sizes),
        shape((local_count * width, columns), BF16),
        (replica_of,),
        (home_in, copy_in),
        flops=half_flops,
    )
    arrived = lax.ppermute(other, "dp", [(0, 1), (1, 0)])
    grad_h, grad_p = call(
        functools.partial(combine_kernel, *sizes),
        (shape((toks * top, width), BF16), shape((top, toks), F32)),
        (),
        (back, pick, expert, h_slot, p_slot, ids),
        [pltpu.VMEM((toks * top, width), F32)],
        flops=2 * slots * toks * width * top,
    )
    grad_w = call(
        functools.partial(own_half_kernel, *sizes),
        shape((local_count * width, columns), BF16),
        (replica_of,),
        (home_in, copy_in, arrived),
        flops=half_flops,
    )
    return (
        grad_h.reshape(toks, top, width),
        grad_p.T.astype(BF16),
        grad_w.reshape(local_count, width, columns),
    )


def body(cotangent, hidden, probs, expert_ids, send_counts, replica_of, weights):
    dev_count = lax.axis_size("expert")
    local_count, width, _ = weights.shape
    gathered = dev_count * dev_count * CAPR
    if gathered <= (local_count + 3) * width and lax.axis_size("dp") == 2:
        run = gather_body
    else:
        run = replica_body
    return run(cotangent, hidden, probs, expert_ids, send_counts, replica_of, weights)


def solution(mesh):
    in_specs = (
        P(("groups", "expert", "dp"), None),
        P(("groups", "expert", "dp"), None, None),
        P(("groups", "expert", "dp"), None),
        P(("groups", "expert", "dp"), None),
        P(("groups", "expert", "dp"), None),
        P("groups"),
        P("expert", None, None),
    )
    out_specs = (
        P(("groups", "expert", "dp"), None, None),
        P(("groups", "expert", "dp"), None),
        P(("groups", "expert"), None, "dp"),
    )
    return jax.shard_map(body, mesh=mesh, in_specs=in_specs, out_specs=out_specs, check_vma=False)
```

```python
import functools

import jax
import jax.numpy as jnp
from jax import lax
from jax.experimental import pallas as pl
from jax.experimental.pallas import tpu as pltpu
from jax.sharding import PartitionSpec as P

CAPH = 3
CAPR = 3


def ranks_within(keys):
    total_rows = keys.shape[0]
    sort_order = jnp.argsort(keys * total_rows + jnp.arange(total_rows, dtype=jnp.int32))
    sorted_keys = keys[sort_order]
    first_seen = jnp.searchsorted(sorted_keys, sorted_keys, side="left")
    ranked = jnp.arange(total_rows, dtype=jnp.int32) - first_seen
    return jnp.zeros((total_rows,), jnp.int32).at[sort_order].set(ranked)


def route_rows(ids_block, counts_row, replica_of, local_count, cap_home, cap_copy):
    dev_count = replica_of.shape[0]
    experts = ids_block.reshape(-1)
    rank_expert = ranks_within(experts)
    devices = jnp.arange(dev_count, dtype=jnp.int32)
    same_copy = (replica_of[:, None] == replica_of[None, :]) & (devices[None, :] < devices[:, None])
    lower_rank = jnp.sum(jnp.where(same_copy, counts_row[None, :], 0), axis=1)
    upper_rank = lower_rank + counts_row
    hit_table = (
        (replica_of[None, :] == experts[:, None])
        & (lower_rank[None, :] <= rank_expert[:, None])
        & (rank_expert[:, None] < upper_rank[None, :])
    )
    copied = jnp.any(hit_table, axis=1)
    copy_dev = jnp.sum(jnp.where(hit_table, devices[None, :], 0), axis=1)
    dest_dev = jnp.where(copied, copy_dev, experts // local_count)
    index_of_slot = jnp.where(copied, local_count, experts % local_count)
    rank_bucket = ranks_within(dest_dev * (local_count + 1) + index_of_slot)
    keep_row = rank_bucket < jnp.where(copied, cap_copy, cap_home)
    per_dev = local_count * cap_home + cap_copy
    target = dest_dev * per_dev + index_of_slot * cap_home + rank_bucket
    return jnp.where(keep_row, target, dev_count * per_dev)


def replica_body(cotangent, hidden, probs, expert_ids, send_counts, replica_of, weights):
    tok_rows, d_model = cotangent.shape
    top_count = expert_ids.shape[1]
    hidden_width = hidden.shape[2]
    local_count = weights.shape[0]
    dev_count = lax.axis_size("expert")
    data_count = lax.axis_size("dp")
    per_dev = local_count * CAPH + CAPR
    row_count = tok_rows * top_count
    recv_count = dev_count * per_dev
    target = route_rows(expert_ids, send_counts[0], replica_of, local_count, CAPH, CAPR)
    inverse = (
        jnp.full((recv_count,), row_count, jnp.int32)
        .at[target]
        .set(jnp.arange(row_count, dtype=jnp.int32), mode="drop")
    )
    dy_pad = jnp.concatenate([cotangent, jnp.zeros((1, d_model), cotangent.dtype)], axis=0)
    h_pad = jnp.concatenate(
        [hidden.reshape(row_count, hidden_width), jnp.zeros((1, hidden_width), hidden.dtype)],
        axis=0,
    )
    p_pad = jnp.concatenate([probs.reshape(row_count), jnp.zeros((1,), probs.dtype)], axis=0)
    send_dy = dy_pad[inverse // top_count]
    send_h = h_pad[inverse]
    send_p = p_pad[inverse]
    recv_dy, recv_h, recv_p = (
        lax.all_to_all(send_dy, "expert", split_axis=0, concat_axis=0, tiled=True),
        lax.all_to_all(send_h, "expert", split_axis=0, concat_axis=0, tiled=True),
        lax.all_to_all(send_p, "expert", split_axis=0, concat_axis=0, tiled=True),
    )
    flat_size = hidden_width * d_model
    flat_w = weights.reshape(local_count, flat_size)
    pieces = lax.all_to_all(flat_w, "expert", split_axis=1, concat_axis=0, tiled=True)
    chosen = pieces[replica_of]
    copy_weight = lax.all_to_all(chosen, "expert", split_axis=0, concat_axis=0, tiled=True).reshape(
        hidden_width, d_model
    )
    slot_total = local_count + 1
    home_rows = local_count * CAPH
    row_pos = jnp.arange(recv_count, dtype=jnp.int32) % per_dev
    row_slot = jnp.where(row_pos < home_rows, row_pos // CAPH, local_count)
    all_weights = jnp.concatenate(
        [weights.reshape(local_count * hidden_width, d_model), copy_weight], axis=0
    )
    all_in = lax.dot_general(
        recv_dy, all_weights, (((1,), (1,)), ((), ())), preferred_element_type=jnp.float32
    )
    grad_in = jnp.zeros((recv_count, hidden_width), jnp.float32)
    for slot_num in range(slot_total):
        grad_in = grad_in + jnp.where(
            (row_slot == slot_num)[:, None],
            all_in[:, slot_num * hidden_width : (slot_num + 1) * hidden_width],
            0.0,
        )
    p_wide = recv_p.astype(jnp.float32)[:, None]
    h_wide = recv_h.astype(jnp.float32)
    grad_h_buf = (p_wide * grad_in).astype(jnp.bfloat16)
    grad_p_buf = jnp.sum(h_wide * grad_in, axis=1).astype(jnp.bfloat16)
    scaled = (p_wide * h_wide).astype(jnp.bfloat16)
    zero_rows = jnp.zeros_like(scaled)
    scaled_wide = jnp.concatenate(
        [
            jnp.where((row_slot == slot_num)[:, None], scaled, zero_rows)
            for slot_num in range(slot_total)
        ],
        axis=1,
    )
    parts = lax.dot_general(
        scaled_wide, recv_dy, (((0,), (0,)), ((), ())), preferred_element_type=jnp.float32
    ).astype(jnp.bfloat16)
    home_part = parts[: local_count * hidden_width].reshape(local_count, hidden_width, d_model)
    copy_part = parts[local_count * hidden_width :]
    back_h, back_p = (
        lax.all_to_all(grad_h_buf, "expert", split_axis=0, concat_axis=0, tiled=True),
        lax.all_to_all(grad_p_buf, "expert", split_axis=0, concat_axis=0, tiled=True),
    )
    flat_h = jnp.concatenate([back_h, jnp.zeros((1, hidden_width), back_h.dtype)], axis=0)
    flat_p = jnp.concatenate([back_p, jnp.zeros((1,), back_p.dtype)], axis=0)
    hidden_gradient = flat_h[target].reshape(tok_rows, top_count, hidden_width)
    grad_probs = flat_p[target].reshape(tok_rows, top_count)
    expert_total = dev_count * local_count
    cover = replica_of[None, :] == jnp.arange(expert_total, dtype=jnp.int32)[:, None]
    half_width = d_model // data_count
    halves = lax.all_to_all(copy_part, "dp", split_axis=1, concat_axis=0, tiled=True)
    copy_half = jnp.sum(
        halves.reshape(data_count, hidden_width, half_width).astype(jnp.float32), axis=0
    )
    piece_len = hidden_width * half_width // dev_count
    slabs = copy_half.reshape(dev_count, piece_len)
    arrived = lax.all_to_all(slabs, "expert", split_axis=0, concat_axis=0, tiled=True)
    sums = jnp.dot(cover.astype(jnp.float32), arrived, precision=lax.Precision.HIGHEST)
    homed = lax.all_to_all(
        sums.reshape(dev_count, local_count * piece_len),
        "expert",
        split_axis=0,
        concat_axis=0,
        tiled=True,
    )
    homed = (
        homed.reshape(dev_count, local_count, piece_len)
        .transpose(1, 0, 2)
        .reshape(local_count, hidden_width, half_width)
    )
    home_half = lax.psum_scatter(
        home_part.astype(jnp.float32).astype(jnp.bfloat16), "dp", scatter_dimension=2, tiled=True
    ).astype(jnp.float32)
    grad_weights = (home_half + homed).astype(jnp.bfloat16)
    return (hidden_gradient, grad_probs, grad_weights)


SLOT = 4
F32 = jnp.float32
BF16 = jnp.bfloat16
NT = (((1,), (1,)), ((), ()))
TN = (((0,), (0,)), ((), ()))


def iota(shape, dim):
    return lax.broadcasted_iota(jnp.int32, shape, dim)


def dispatch_kernel(local_count, dev_count, *refs):
    sources, refs = refs[:6], refs[6:]
    copy_ref, home_refs, refs = refs[0], refs[1:1 + dev_count], refs[1 + dev_count:]
    pick_ref, expert_ref, hs_ref, ps_ref = refs[:4]
    held, wide, sems = refs[4:10], refs[10], refs[11]
    moves = [pltpu.make_async_copy(s, h, sems.at[n]) for n, (s, h) in enumerate(zip(sources, held))]
    for move in moves:
        move.start()
    replica_ref, counts_ref, ids_ref, probs_ref, hid_ref, cot_ref = held
    top, toks = ids_ref.shape
    d_model = cot_ref.shape[1]
    per_home = local_count * SLOT
    homes = dev_count * per_home
    slots = homes + dev_count * CAPR
    me = lax.axis_index("expert")
    for move in moves[:3]:
        move.wait()
    row = iota((slots, toks), 0)
    expert = ((row // per_home) ^ me) * local_count + (row % per_home) // SLOT
    within = row % SLOT
    allowed = jnp.where(within < CAPH, 1, 0)
    for d in range(dev_count):
        first = homes + d * CAPR
        mine = (row >= first) & (row < first + CAPR)
        expert = jnp.where(mine, replica_ref[d], expert)
        within = jnp.where(mine, row - first, within)
        allowed = jnp.where(mine, jnp.where(row - first < counts_ref[0, d], 1, 0), allowed)
    lower = jnp.zeros((slots, toks), jnp.int32)
    for d in range(dev_count):
        earlier = (row < homes) | (row >= homes + (d + 1) * CAPR)
        lower = lower + jnp.where(earlier & (expert == replica_ref[d]), counts_ref[0, d], 0)
    ids = ids_ref[...]
    named = jnp.zeros((slots, toks), F32)
    for k in range(top):
        named = named + jnp.where(ids[k:k + 1, :] == expert, 1.0, 0.0)
    before = jnp.where(iota((toks, toks), 0) < iota((toks, toks), 1), 1.0, 0.0).astype(BF16)
    rank = jnp.dot(named.astype(BF16), before, preferred_element_type=F32)
    wanted = (lower + within).astype(F32)
    pick = jnp.where((rank == wanted) & (allowed > 0), named, 0.0)
    pick_ref[...] = pick
    expert_ref[...] = expert
    for move in moves[3:5]:
        move.wait()
    wide[...] = hid_ref[...].astype(F32)
    h_slot = jnp.zeros((slots, hid_ref.shape[1]), F32)
    p_slot = jnp.zeros((slots, toks), F32)
    probs = probs_ref[...].astype(F32)
    for k in range(top):
        sel = jnp.where(ids[k:k + 1, :] == expert, pick, 0.0)
        h_k = wide[pl.ds(k, toks, stride=top), :].astype(BF16)
        h_slot = h_slot + jnp.dot(sel.astype(BF16), h_k, preferred_element_type=F32)
        p_slot = p_slot + sel * probs[k:k + 1, :]
    p_slot = jnp.sum(p_slot, axis=1, keepdims=True)
    hs_ref[...] = h_slot
    ps_ref[...] = jnp.broadcast_to(p_slot, ps_ref.shape)
    scaled = p_slot * h_slot
    moves[5].wait()
    rows = jnp.dot(pick.astype(BF16), cot_ref[...], preferred_element_type=F32)
    copy_ref[:, :d_model] = rows[homes:].astype(BF16)
    copy_ref[:, d_model:] = scaled[homes:].astype(BF16)
    for m, home_ref in enumerate(home_refs):
        home_ref[:, :d_model] = rows[m * per_home:(m + 1) * per_home].astype(BF16)
        home_ref[:, d_model:] = scaled[m * per_home:(m + 1) * per_home].astype(BF16)


def local_slots(local_count, dev_count, width, replica_ref):
    first = lax.axis_index("expert") * local_count
    home = (iota((dev_count * local_count * SLOT, width), 0) // SLOT) % local_count
    row = iota((dev_count * CAPR, width), 0)
    copy = jnp.full((dev_count * CAPR, width), -1, jnp.int32)
    for d in range(dev_count):
        mine = (row >= d * CAPR) & (row < (d + 1) * CAPR)
        copy = jnp.where(mine, replica_ref[d] - first, copy)
    return jnp.concatenate([home] + [copy] * dev_count, axis=0)


def grad_in_kernel(local_count, dev_count, replica_ref, w_ref, *refs):
    home_refs, copy_refs, refs = refs[:dev_count], refs[dev_count:2 * dev_count], refs[2 * dev_count:]
    rows_ref, back_refs = refs[0], refs[1:]
    d_model = w_ref.shape[1]
    width = w_ref.shape[0] // local_count
    per_home, per_copy = local_count * SLOT, dev_count * CAPR
    homes = dev_count * per_home
    rows_ref[:homes] = jnp.concatenate([r[...].astype(F32) for r in home_refs], axis=0).astype(BF16)
    rows_ref[homes:] = jnp.concatenate([r[...].astype(F32) for r in copy_refs], axis=0).astype(BF16)
    every = lax.dot_general(rows_ref[:, :d_model], w_ref[...], NT, preferred_element_type=F32)
    slot = local_slots(local_count, dev_count, width, replica_ref)
    own = jnp.zeros((rows_ref.shape[0], width), F32)
    for e in range(local_count):
        own = jnp.where(slot == e, every[:, e * width:(e + 1) * width], own)
    for m, back_ref in enumerate(back_refs):
        home = own[m * per_home:(m + 1) * per_home]
        copy = own[homes + m * per_copy:homes + (m + 1) * per_copy]
        back_ref[...] = jnp.concatenate([home, copy], axis=0).astype(back_ref.dtype)


def grad_weights_half(local_count, dev_count, half, replica_ref, rows_ref, columns):
    width = rows_ref.shape[1] - 2 * columns
    start = pl.multiple_of(half * columns, 128)
    slot = local_slots(local_count, dev_count, width, replica_ref)
    scaled = rows_ref[:, 2 * columns:].astype(F32)
    spread = jnp.concatenate([jnp.where(slot == e, scaled, 0.0) for e in range(local_count)], axis=1)
    return lax.dot_general(spread.astype(BF16), rows_ref[:, pl.ds(start, columns)], TN, preferred_element_type=F32)


def other_half_kernel(local_count, dev_count, replica_ref, rows_ref, out_ref):
    half = 1 - lax.axis_index("dp")
    out_ref[...] = grad_weights_half(
        local_count, dev_count, half, replica_ref, rows_ref, out_ref.shape[1]).astype(out_ref.dtype)


def own_half_kernel(local_count, dev_count, replica_ref, rows_ref, arrived_ref, out_ref):
    half = lax.axis_index("dp")
    total = grad_weights_half(local_count, dev_count, half, replica_ref, rows_ref, out_ref.shape[1])
    out_ref[...] = (total + arrived_ref[...].astype(F32)).astype(out_ref.dtype)


def combine_kernel(local_count, dev_count, *refs):
    back_refs, refs = refs[:dev_count], refs[dev_count:]
    pick_ref, expert_ref, hs_ref, ps_ref, ids_ref, grad_h_ref, grad_p_ref, wide, narrow = refs
    top, toks = ids_ref.shape
    per_home = local_count * SLOT
    back = [r[...].astype(F32) for r in back_refs]
    copy = back[0][per_home:]
    for b in back[1:]:
        copy = copy + b[per_home:]
    grad_in = jnp.concatenate([b[:per_home] for b in back] + [copy], axis=0)
    h_rows = (ps_ref[...] * grad_in).astype(BF16)
    p_rows = jnp.sum(hs_ref[...] * grad_in, axis=1, keepdims=True)
    ids = ids_ref[...]
    pick = pick_ref[...]
    expert = expert_ref[...]
    for k in range(top):
        sel = jnp.where(ids[k:k + 1, :] == expert, pick, 0.0)
        wide[pl.ds(k, toks, stride=top), :] = lax.dot_general(
            sel.astype(BF16), h_rows, TN, preferred_element_type=F32)
        narrow[k:k + 1, :] = jnp.sum(sel * p_rows, axis=0, keepdims=True)
    grad_h_ref[...] = wide[...].astype(grad_h_ref.dtype)
    grad_p_ref[...] = narrow[...].astype(grad_p_ref.dtype)


def call(kernel, out_shape, smem, operands, scratch=(), flops=0, limit=24, space=pltpu.VMEM):
    shapes = jax.tree.leaves(out_shape)
    moved = sum(a.size * a.dtype.itemsize for a in (*operands, *shapes))
    return pl.pallas_call(
        kernel,
        out_shape=out_shape,
        in_specs=[pl.BlockSpec(memory_space=pltpu.SMEM)] * len(smem)
        + [pl.BlockSpec(memory_space=space)] * len(operands),
        out_specs=jax.tree.map(lambda _: pl.BlockSpec(memory_space=pltpu.VMEM), out_shape),
        scratch_shapes=list(scratch),
        compiler_params=pltpu.CompilerParams(vmem_limit_bytes=limit << 20),
        cost_estimate=pl.CostEstimate(flops=flops, bytes_accessed=moved, transcendentals=0),
    )(*smem, *operands)


def swap(x, bits, count):
    return lax.ppermute(x, "expert", [(i, i ^ bits) for i in range(count)])


def gather_body(cotangent, hidden, probs, expert_ids, send_counts, replica_of, weights):
    toks, d_model = cotangent.shape
    top = expert_ids.shape[1]
    width = hidden.shape[2]
    local_count = weights.shape[0]
    dev_count = lax.axis_size("expert")
    per_home = local_count * SLOT
    homes = dev_count * per_home
    copies = dev_count * CAPR
    slots = homes + copies
    sizes = (local_count, dev_count)
    ids = expert_ids.T
    shape = jax.ShapeDtypeStruct
    sources = (replica_of, send_counts, ids, probs.T, hidden.reshape(toks * top, width), cotangent)
    copy_rows, *rest = call(
        functools.partial(dispatch_kernel, *sizes),
        [shape((copies, d_model + width), BF16)]
        + [shape((per_home, d_model + width), BF16)] * dev_count
        + [shape((slots, toks), F32), shape((slots, toks), jnp.int32),
           shape((slots, width), F32), shape((slots, width), F32)],
        (),
        sources,
        [(pltpu.SMEM if n < 2 else pltpu.VMEM)(a.shape, a.dtype) for n, a in enumerate(sources)]
        + [pltpu.VMEM((toks * top, width), F32), pltpu.SemaphoreType.DMA((len(sources),))],
        flops=2 * slots * toks * d_model,
        limit=48,
        space=pl.ANY,
    )
    home_rows, (pick, expert, h_slot, p_slot) = rest[:dev_count], rest[dev_count:]
    copy_in = [copy_rows] + [None] * (dev_count - 1)
    for m in sorted(range(1, dev_count), key=lambda m: (m.bit_count(), -m)):
        low = m & -m
        copy_in[m] = swap(copy_in[m ^ low], low, dev_count)
    home_in = [home_rows[0]] + [swap(home_rows[m], m, dev_count) for m in range(1, dev_count)]
    rows = homes + dev_count * copies
    w_flat = weights.reshape(local_count * width, d_model)
    all_rows, *back = call(
        functools.partial(grad_in_kernel, *sizes),
        [shape((rows, d_model + width), BF16)] + [shape((per_home + copies, width), BF16)] * dev_count,
        (replica_of,),
        (w_flat, *home_in, *copy_in),
        flops=2 * rows * d_model * local_count * width,
    )
    back = [back[0]] + [swap(back[m], m, dev_count) for m in range(1, dev_count)]
    columns = d_model // 2
    half_flops = 2 * rows * columns * local_count * width
    other = call(
        functools.partial(other_half_kernel, *sizes),
        shape((local_count * width, columns), BF16),
        (replica_of,),
        (all_rows,),
        flops=half_flops,
    )
    arrived = lax.ppermute(other, "dp", [(0, 1), (1, 0)])
    grad_h, grad_p = call(
        functools.partial(combine_kernel, *sizes),
        (shape((toks * top, width), BF16), shape((top, toks), BF16)),
        (),
        (*back, pick, expert, h_slot, p_slot, ids),
        [pltpu.VMEM((toks * top, width), F32), pltpu.VMEM((top, toks), F32)],
        flops=2 * slots * toks * width * top,
    )
    grad_w = call(
        functools.partial(own_half_kernel, *sizes),
        shape((local_count * width, columns), BF16),
        (replica_of,),
        (all_rows, arrived),
        flops=half_flops,
    )
    return (
        grad_h.reshape(toks, top, width),
        grad_p.T,
        grad_w.reshape(local_count, width, columns),
    )


def body(cotangent, hidden, probs, expert_ids, send_counts, replica_of, weights):
    dev_count = lax.axis_size("expert")
    local_count, width, _ = weights.shape
    gathered = dev_count * dev_count * CAPR
    if gathered <= (local_count + 3) * width and dev_count.bit_count() == 1 and lax.axis_size("dp") == 2:
        run = gather_body
    else:
        run = replica_body
    return run(cotangent, hidden, probs, expert_ids, send_counts, replica_of, weights)


def solution(mesh):
    in_specs = (
        P(("groups", "expert", "dp"), None),
        P(("groups", "expert", "dp"), None, None),
        P(("groups", "expert", "dp"), None),
        P(("groups", "expert", "dp"), None),
        P(("groups", "expert", "dp"), None),
        P("groups"),
        P("expert", None, None),
    )
    out_specs = (
        P(("groups", "expert", "dp"), None, None),
        P(("groups", "expert", "dp"), None),
        P(("groups", "expert"), None, "dp"),
    )
    return jax.shard_map(body, mesh=mesh, in_specs=in_specs, out_specs=out_specs, check_vma=False)
```

```python
import functools

import jax
import jax.numpy as jnp
from jax import lax
from jax.experimental import pallas as pl
from jax.experimental.pallas import tpu as pltpu
from jax.sharding import PartitionSpec as P

CAPH = 3
CAPR = 3


def ranks_within(keys):
    total_rows = keys.shape[0]
    sort_order = jnp.argsort(keys * total_rows + jnp.arange(total_rows, dtype=jnp.int32))
    sorted_keys = keys[sort_order]
    first_seen = jnp.searchsorted(sorted_keys, sorted_keys, side="left")
    ranked = jnp.arange(total_rows, dtype=jnp.int32) - first_seen
    return jnp.zeros((total_rows,), jnp.int32).at[sort_order].set(ranked)


def route_rows(ids_block, counts_row, replica_of, local_count, cap_home, cap_copy):
    dev_count = replica_of.shape[0]
    experts = ids_block.reshape(-1)
    rank_expert = ranks_within(experts)
    devices = jnp.arange(dev_count, dtype=jnp.int32)
    same_copy = (replica_of[:, None] == replica_of[None, :]) & (devices[None, :] < devices[:, None])
    lower_rank = jnp.sum(jnp.where(same_copy, counts_row[None, :], 0), axis=1)
    upper_rank = lower_rank + counts_row
    hit_table = (
        (replica_of[None, :] == experts[:, None])
        & (lower_rank[None, :] <= rank_expert[:, None])
        & (rank_expert[:, None] < upper_rank[None, :])
    )
    copied = jnp.any(hit_table, axis=1)
    copy_dev = jnp.sum(jnp.where(hit_table, devices[None, :], 0), axis=1)
    dest_dev = jnp.where(copied, copy_dev, experts // local_count)
    index_of_slot = jnp.where(copied, local_count, experts % local_count)
    rank_bucket = ranks_within(dest_dev * (local_count + 1) + index_of_slot)
    keep_row = rank_bucket < jnp.where(copied, cap_copy, cap_home)
    per_dev = local_count * cap_home + cap_copy
    target = dest_dev * per_dev + index_of_slot * cap_home + rank_bucket
    return jnp.where(keep_row, target, dev_count * per_dev)


def replica_body(cotangent, hidden, probs, expert_ids, send_counts, replica_of, weights):
    tok_rows, d_model = cotangent.shape
    top_count = expert_ids.shape[1]
    hidden_width = hidden.shape[2]
    local_count = weights.shape[0]
    dev_count = lax.axis_size("expert")
    data_count = lax.axis_size("dp")
    per_dev = local_count * CAPH + CAPR
    row_count = tok_rows * top_count
    recv_count = dev_count * per_dev
    target = route_rows(expert_ids, send_counts[0], replica_of, local_count, CAPH, CAPR)
    inverse = (
        jnp.full((recv_count,), row_count, jnp.int32)
        .at[target]
        .set(jnp.arange(row_count, dtype=jnp.int32), mode="drop")
    )
    dy_pad = jnp.concatenate([cotangent, jnp.zeros((1, d_model), cotangent.dtype)], axis=0)
    h_pad = jnp.concatenate(
        [hidden.reshape(row_count, hidden_width), jnp.zeros((1, hidden_width), hidden.dtype)],
        axis=0,
    )
    p_pad = jnp.concatenate([probs.reshape(row_count), jnp.zeros((1,), probs.dtype)], axis=0)
    send_dy = dy_pad[inverse // top_count]
    send_h = h_pad[inverse]
    send_p = p_pad[inverse]
    recv_dy, recv_h, recv_p = (
        lax.all_to_all(send_dy, "expert", split_axis=0, concat_axis=0, tiled=True),
        lax.all_to_all(send_h, "expert", split_axis=0, concat_axis=0, tiled=True),
        lax.all_to_all(send_p, "expert", split_axis=0, concat_axis=0, tiled=True),
    )
    flat_size = hidden_width * d_model
    flat_w = weights.reshape(local_count, flat_size)
    pieces = lax.all_to_all(flat_w, "expert", split_axis=1, concat_axis=0, tiled=True)
    chosen = pieces[replica_of]
    copy_weight = lax.all_to_all(chosen, "expert", split_axis=0, concat_axis=0, tiled=True).reshape(
        hidden_width, d_model
    )
    slot_total = local_count + 1
    home_rows = local_count * CAPH
    row_pos = jnp.arange(recv_count, dtype=jnp.int32) % per_dev
    row_slot = jnp.where(row_pos < home_rows, row_pos // CAPH, local_count)
    all_weights = jnp.concatenate(
        [weights.reshape(local_count * hidden_width, d_model), copy_weight], axis=0
    )
    all_in = lax.dot_general(
        recv_dy, all_weights, (((1,), (1,)), ((), ())), preferred_element_type=jnp.float32
    )
    grad_in = jnp.zeros((recv_count, hidden_width), jnp.float32)
    for slot_num in range(slot_total):
        grad_in = grad_in + jnp.where(
            (row_slot == slot_num)[:, None],
            all_in[:, slot_num * hidden_width : (slot_num + 1) * hidden_width],
            0.0,
        )
    p_wide = recv_p.astype(jnp.float32)[:, None]
    h_wide = recv_h.astype(jnp.float32)
    grad_h_buf = (p_wide * grad_in).astype(jnp.bfloat16)
    grad_p_buf = jnp.sum(h_wide * grad_in, axis=1).astype(jnp.bfloat16)
    scaled = (p_wide * h_wide).astype(jnp.bfloat16)
    zero_rows = jnp.zeros_like(scaled)
    scaled_wide = jnp.concatenate(
        [
            jnp.where((row_slot == slot_num)[:, None], scaled, zero_rows)
            for slot_num in range(slot_total)
        ],
        axis=1,
    )
    parts = lax.dot_general(
        scaled_wide, recv_dy, (((0,), (0,)), ((), ())), preferred_element_type=jnp.float32
    ).astype(jnp.bfloat16)
    home_part = parts[: local_count * hidden_width].reshape(local_count, hidden_width, d_model)
    copy_part = parts[local_count * hidden_width :]
    back_h, back_p = (
        lax.all_to_all(grad_h_buf, "expert", split_axis=0, concat_axis=0, tiled=True),
        lax.all_to_all(grad_p_buf, "expert", split_axis=0, concat_axis=0, tiled=True),
    )
    flat_h = jnp.concatenate([back_h, jnp.zeros((1, hidden_width), back_h.dtype)], axis=0)
    flat_p = jnp.concatenate([back_p, jnp.zeros((1,), back_p.dtype)], axis=0)
    hidden_gradient = flat_h[target].reshape(tok_rows, top_count, hidden_width)
    grad_probs = flat_p[target].reshape(tok_rows, top_count)
    expert_total = dev_count * local_count
    cover = replica_of[None, :] == jnp.arange(expert_total, dtype=jnp.int32)[:, None]
    half_width = d_model // data_count
    halves = lax.all_to_all(copy_part, "dp", split_axis=1, concat_axis=0, tiled=True)
    copy_half = jnp.sum(
        halves.reshape(data_count, hidden_width, half_width).astype(jnp.float32), axis=0
    )
    piece_len = hidden_width * half_width // dev_count
    slabs = copy_half.reshape(dev_count, piece_len)
    arrived = lax.all_to_all(slabs, "expert", split_axis=0, concat_axis=0, tiled=True)
    sums = jnp.dot(cover.astype(jnp.float32), arrived, precision=lax.Precision.HIGHEST)
    homed = lax.all_to_all(
        sums.reshape(dev_count, local_count * piece_len),
        "expert",
        split_axis=0,
        concat_axis=0,
        tiled=True,
    )
    homed = (
        homed.reshape(dev_count, local_count, piece_len)
        .transpose(1, 0, 2)
        .reshape(local_count, hidden_width, half_width)
    )
    home_half = lax.psum_scatter(
        home_part.astype(jnp.float32).astype(jnp.bfloat16), "dp", scatter_dimension=2, tiled=True
    ).astype(jnp.float32)
    grad_weights = (home_half + homed).astype(jnp.bfloat16)
    return (hidden_gradient, grad_probs, grad_weights)


SLOT = 4
F32 = jnp.float32
BF16 = jnp.bfloat16
NT = (((1,), (1,)), ((), ()))
TN = (((0,), (0,)), ((), ()))


def iota(shape, dim):
    return lax.broadcasted_iota(jnp.int32, shape, dim)


def dispatch_kernel(local_count, dev_count, *refs):
    sources, refs = refs[:6], refs[6:]
    copy_ref, home_ref, pick_ref, expert_ref, hs_ref, ps_ref = refs[:6]
    held, wide, sems = refs[6:12], refs[12], refs[13]
    moves = [pltpu.make_async_copy(s, h, sems.at[n]) for n, (s, h) in enumerate(zip(sources, held))]
    for move in moves:
        move.start()
    replica_ref, counts_ref, ids_ref, probs_ref, hid_ref, cot_ref = held
    top, toks = ids_ref.shape
    d_model = cot_ref.shape[1]
    homes = dev_count * local_count * SLOT
    slots = homes + dev_count * CAPR
    for move in moves[:3]:
        move.wait()
    row = iota((slots, toks), 0)
    expert = row // SLOT
    within = row % SLOT
    allowed = jnp.where(within < CAPH, 1, 0)
    for d in range(dev_count):
        first = homes + d * CAPR
        mine = (row >= first) & (row < first + CAPR)
        expert = jnp.where(mine, replica_ref[d], expert)
        within = jnp.where(mine, row - first, within)
        allowed = jnp.where(mine, jnp.where(row - first < counts_ref[0, d], 1, 0), allowed)
    lower = jnp.zeros((slots, toks), jnp.int32)
    for d in range(dev_count):
        earlier = (row < homes) | (row >= homes + (d + 1) * CAPR)
        lower = lower + jnp.where(earlier & (expert == replica_ref[d]), counts_ref[0, d], 0)
    ids = ids_ref[...]
    named = jnp.zeros((slots, toks), F32)
    for k in range(top):
        named = named + jnp.where(ids[k:k + 1, :] == expert, 1.0, 0.0)
    before = jnp.where(iota((toks, toks), 0) < iota((toks, toks), 1), 1.0, 0.0).astype(BF16)
    rank = jnp.dot(named.astype(BF16), before, preferred_element_type=F32)
    wanted = (lower + within).astype(F32)
    pick = jnp.where((rank == wanted) & (allowed > 0), named, 0.0)
    pick_ref[...] = pick
    expert_ref[...] = expert
    for move in moves[3:5]:
        move.wait()
    wide[...] = hid_ref[...].astype(F32)
    h_slot = jnp.zeros((slots, hid_ref.shape[1]), F32)
    p_slot = jnp.zeros((slots, toks), F32)
    probs = probs_ref[...].astype(F32)
    for k in range(top):
        sel = jnp.where(ids[k:k + 1, :] == expert, pick, 0.0)
        h_k = wide[pl.ds(k, toks, stride=top), :].astype(BF16)
        h_slot = h_slot + jnp.dot(sel.astype(BF16), h_k, preferred_element_type=F32)
        p_slot = p_slot + sel * probs[k:k + 1, :]
    p_slot = jnp.sum(p_slot, axis=1, keepdims=True)
    hs_ref[...] = h_slot
    ps_ref[...] = jnp.broadcast_to(p_slot, ps_ref.shape)
    scaled = p_slot * h_slot
    moves[5].wait()
    rows = jnp.dot(pick.astype(BF16), cot_ref[...], preferred_element_type=F32)
    copy_ref[:, :d_model] = rows[homes:].astype(BF16)
    copy_ref[:, d_model:] = scaled[homes:].astype(BF16)
    home_ref[:, :d_model] = rows[:homes].astype(BF16)
    home_ref[:, d_model:] = scaled[:homes].astype(BF16)


def local_slots(local_count, dev_count, width, replica_ref):
    first = lax.axis_index("expert") * local_count
    home = (iota((dev_count * local_count * SLOT, width), 0) // SLOT) % local_count
    row = iota((dev_count * CAPR, width), 0)
    copy = jnp.full((dev_count * CAPR, width), -1, jnp.int32)
    for d in range(dev_count):
        mine = (row >= d * CAPR) & (row < (d + 1) * CAPR)
        copy = jnp.where(mine, replica_ref[d] - first, copy)
    return jnp.concatenate([home] + [copy] * dev_count, axis=0)


def grad_in_kernel(local_count, dev_count, replica_ref, w_hbm, home_ref, *refs):
    copy_refs, (rows_ref, back_ref, w_ref, passed, sem) = refs[:dev_count], refs[dev_count:]
    fetch = pltpu.make_async_copy(w_hbm, w_ref, sem)
    fetch.start()
    d_model = w_ref.shape[1]
    width = w_ref.shape[0] // local_count
    per_home, per_copy = local_count * SLOT, dev_count * CAPR
    homes = dev_count * per_home
    rows_ref[:homes] = home_ref[...]
    rows_ref[homes:] = jnp.concatenate([r[...].astype(F32) for r in copy_refs], axis=0).astype(BF16)
    slot = local_slots(local_count, dev_count, width, replica_ref)
    fetch.wait()
    every = lax.dot_general(rows_ref[:, :d_model], w_ref[...], NT, preferred_element_type=F32)
    own = jnp.zeros((rows_ref.shape[0], width), F32)
    for e in range(local_count):
        own = jnp.where(slot == e, every[:, e * width:(e + 1) * width], own)
    passed[...] = own[homes:].reshape(passed.shape)
    me = lax.axis_index("expert")
    blocks = []
    for source in range(dev_count):
        blocks += [own[source * per_home:(source + 1) * per_home], passed[me ^ source]]
    back_ref[...] = jnp.concatenate(blocks, axis=0).astype(back_ref.dtype)


def grad_weights_half(local_count, dev_count, half, replica_ref, rows_ref, columns):
    width = rows_ref.shape[1] - 2 * columns
    start = pl.multiple_of(half * columns, 128)
    slot = local_slots(local_count, dev_count, width, replica_ref)
    scaled = rows_ref[:, 2 * columns:].astype(F32)
    spread = jnp.concatenate([jnp.where(slot == e, scaled, 0.0) for e in range(local_count)], axis=1)
    return lax.dot_general(spread.astype(BF16), rows_ref[:, pl.ds(start, columns)], TN, preferred_element_type=F32)


def other_half_kernel(local_count, dev_count, replica_ref, rows_ref, out_ref):
    half = 1 - lax.axis_index("dp")
    out_ref[...] = grad_weights_half(
        local_count, dev_count, half, replica_ref, rows_ref, out_ref.shape[1]).astype(out_ref.dtype)


def own_half_kernel(local_count, dev_count, replica_ref, rows_ref, arrived_ref, out_ref):
    half = lax.axis_index("dp")
    total = grad_weights_half(local_count, dev_count, half, replica_ref, rows_ref, out_ref.shape[1])
    out_ref[...] = (total + arrived_ref[...].astype(F32)).astype(out_ref.dtype)


def combine_kernel(local_count, dev_count, back_ref, pick_ref, expert_ref, hs_ref, ps_ref, ids_ref,
                   grad_h_ref, grad_p_ref, wide, narrow):
    top, toks = ids_ref.shape
    width = back_ref.shape[1]
    per_home, per_copy = local_count * SLOT, dev_count * CAPR
    back = back_ref[...].astype(F32).reshape(dev_count, per_home + per_copy, width)
    home = back[:, :per_home].reshape(dev_count * per_home, width)
    grad_in = jnp.concatenate([home, jnp.sum(back[:, per_home:], axis=0)], axis=0)
    h_rows = (ps_ref[...] * grad_in).astype(BF16)
    p_rows = jnp.sum(hs_ref[...] * grad_in, axis=1, keepdims=True)
    ids = ids_ref[...]
    pick = pick_ref[...]
    expert = expert_ref[...]
    for k in range(top):
        sel = jnp.where(ids[k:k + 1, :] == expert, pick, 0.0)
        wide[pl.ds(k, toks, stride=top), :] = lax.dot_general(
            sel.astype(BF16), h_rows, TN, preferred_element_type=F32)
        narrow[k:k + 1, :] = jnp.sum(sel * p_rows, axis=0, keepdims=True)
    grad_h_ref[...] = wide[...].astype(grad_h_ref.dtype)
    grad_p_ref[...] = narrow[...].astype(grad_p_ref.dtype)


def call(kernel, out_shape, operands, scratch=(), flops=0, limit=24):
    shapes = jax.tree.leaves(out_shape)
    moved = sum(a.size * a.dtype.itemsize for a in (*(a for _, a in operands), *shapes))
    return pl.pallas_call(
        kernel,
        out_shape=out_shape,
        in_specs=[pl.BlockSpec(memory_space=space) for space, _ in operands],
        out_specs=jax.tree.map(lambda _: pl.BlockSpec(memory_space=pltpu.VMEM), out_shape),
        scratch_shapes=list(scratch),
        compiler_params=pltpu.CompilerParams(vmem_limit_bytes=limit << 20),
        cost_estimate=pl.CostEstimate(flops=flops, bytes_accessed=moved, transcendentals=0),
    )(*(a for _, a in operands))


def swap(x, bits, count):
    return lax.ppermute(x, "expert", [(i, i ^ bits) for i in range(count)])


def gather_body(cotangent, hidden, probs, expert_ids, send_counts, replica_of, weights):
    toks, d_model = cotangent.shape
    top = expert_ids.shape[1]
    width = hidden.shape[2]
    local_count = weights.shape[0]
    dev_count = lax.axis_size("expert")
    homes = dev_count * local_count * SLOT
    copies = dev_count * CAPR
    slots = homes + copies
    rows = homes + dev_count * copies
    columns = d_model // 2
    sizes = (local_count, dev_count)
    ids = expert_ids.T
    shape = jax.ShapeDtypeStruct
    hbm, vmem, smem = pltpu.HBM, pltpu.VMEM, pltpu.SMEM
    sources = (replica_of, send_counts, ids, probs.T, hidden.reshape(toks * top, width), cotangent)
    copy_rows, home_rows, pick, expert, h_slot, p_slot = call(
        functools.partial(dispatch_kernel, *sizes),
        (shape((copies, d_model + width), BF16), shape((homes, d_model + width), BF16), shape((slots, toks), F32),
         shape((slots, toks), jnp.int32), shape((slots, width), F32), shape((slots, width), F32)),
        [(hbm, a) for a in sources],
        [(smem if n < 2 else vmem)(a.shape, a.dtype) for n, a in enumerate(sources)]
        + [vmem((toks * top, width), F32), pltpu.SemaphoreType.DMA((len(sources),))],
        flops=2 * slots * toks * d_model,
        limit=60,
    )
    copy_in = [copy_rows] + [None] * (dev_count - 1)
    for m in sorted(range(1, dev_count), key=lambda m: (m.bit_count(), -m)):
        low = m & -m
        copy_in[m] = swap(copy_in[m ^ low], low, dev_count)
    home_in = lax.all_to_all(home_rows, "expert", split_axis=0, concat_axis=0, tiled=True)
    all_rows, back = call(
        functools.partial(grad_in_kernel, *sizes),
        (shape((rows, d_model + width), BF16), shape((rows, width), BF16)),
        [(smem, replica_of), (hbm, weights.reshape(local_count * width, d_model)), (vmem, home_in)]
        + [(vmem, a) for a in copy_in],
        [vmem((local_count * width, d_model), BF16), vmem((dev_count, copies, width), F32),
         pltpu.SemaphoreType.DMA(())],
        flops=2 * rows * d_model * local_count * width,
    )
    back = lax.all_to_all(back, "expert", split_axis=0, concat_axis=0, tiled=True)
    half_flops = 2 * rows * columns * local_count * width
    other = call(
        functools.partial(other_half_kernel, *sizes),
        shape((local_count * width, columns), BF16),
        [(smem, replica_of), (vmem, all_rows)],
        flops=half_flops,
    )
    arrived = lax.ppermute(other, "dp", [(0, 1), (1, 0)])
    grad_h, grad_p = call(
        functools.partial(combine_kernel, *sizes),
        (shape((toks * top, width), BF16), shape((top, toks), BF16)),
        [(vmem, a) for a in (back, pick, expert, h_slot, p_slot, ids)],
        [vmem((toks * top, width), F32), vmem((top, toks), F32)],
        flops=2 * slots * toks * width * top,
    )
    grad_w = call(
        functools.partial(own_half_kernel, *sizes),
        shape((local_count * width, columns), BF16),
        [(smem, replica_of), (vmem, all_rows), (vmem, arrived)],
        flops=half_flops,
    )
    return (
        grad_h.reshape(toks, top, width),
        grad_p.T,
        grad_w.reshape(local_count, width, columns),
    )


def body(cotangent, hidden, probs, expert_ids, send_counts, replica_of, weights):
    dev_count = lax.axis_size("expert")
    local_count, width, _ = weights.shape
    gathered = dev_count * dev_count * CAPR
    if gathered <= (local_count + 3) * width and dev_count.bit_count() == 1 and lax.axis_size("dp") == 2:
        run = gather_body
    else:
        run = replica_body
    return run(cotangent, hidden, probs, expert_ids, send_counts, replica_of, weights)


def solution(mesh):
    in_specs = (
        P(("groups", "expert", "dp"), None),
        P(("groups", "expert", "dp"), None, None),
        P(("groups", "expert", "dp"), None),
        P(("groups", "expert", "dp"), None),
        P(("groups", "expert", "dp"), None),
        P("groups"),
        P("expert", None, None),
    )
    out_specs = (
        P(("groups", "expert", "dp"), None, None),
        P(("groups", "expert", "dp"), None),
        P(("groups", "expert"), None, "dp"),
    )
    return jax.shard_map(body, mesh=mesh, in_specs=in_specs, out_specs=out_specs, check_vma=False)
```

```python
import functools

import jax
import jax.numpy as jnp
from jax import lax
from jax.experimental import pallas as pl
from jax.experimental.pallas import tpu as pltpu
from jax.sharding import PartitionSpec as P

CAPH = 3
CAPR = 3


def ranks_within(keys):
    total_rows = keys.shape[0]
    sort_order = jnp.argsort(keys * total_rows + jnp.arange(total_rows, dtype=jnp.int32))
    sorted_keys = keys[sort_order]
    first_seen = jnp.searchsorted(sorted_keys, sorted_keys, side="left")
    ranked = jnp.arange(total_rows, dtype=jnp.int32) - first_seen
    return jnp.zeros((total_rows,), jnp.int32).at[sort_order].set(ranked)


def route_rows(ids_block, counts_row, replica_of, local_count, cap_home, cap_copy):
    dev_count = replica_of.shape[0]
    experts = ids_block.reshape(-1)
    rank_expert = ranks_within(experts)
    devices = jnp.arange(dev_count, dtype=jnp.int32)
    same_copy = (replica_of[:, None] == replica_of[None, :]) & (devices[None, :] < devices[:, None])
    lower_rank = jnp.sum(jnp.where(same_copy, counts_row[None, :], 0), axis=1)
    upper_rank = lower_rank + counts_row
    hit_table = (
        (replica_of[None, :] == experts[:, None])
        & (lower_rank[None, :] <= rank_expert[:, None])
        & (rank_expert[:, None] < upper_rank[None, :])
    )
    copied = jnp.any(hit_table, axis=1)
    copy_dev = jnp.sum(jnp.where(hit_table, devices[None, :], 0), axis=1)
    dest_dev = jnp.where(copied, copy_dev, experts // local_count)
    index_of_slot = jnp.where(copied, local_count, experts % local_count)
    rank_bucket = ranks_within(dest_dev * (local_count + 1) + index_of_slot)
    keep_row = rank_bucket < jnp.where(copied, cap_copy, cap_home)
    per_dev = local_count * cap_home + cap_copy
    target = dest_dev * per_dev + index_of_slot * cap_home + rank_bucket
    return jnp.where(keep_row, target, dev_count * per_dev)


def replica_body(cotangent, hidden, probs, expert_ids, send_counts, replica_of, weights):
    tok_rows, d_model = cotangent.shape
    top_count = expert_ids.shape[1]
    hidden_width = hidden.shape[2]
    local_count = weights.shape[0]
    dev_count = lax.axis_size("expert")
    data_count = lax.axis_size("dp")
    per_dev = local_count * CAPH + CAPR
    row_count = tok_rows * top_count
    recv_count = dev_count * per_dev
    target = route_rows(expert_ids, send_counts[0], replica_of, local_count, CAPH, CAPR)
    inverse = (
        jnp.full((recv_count,), row_count, jnp.int32)
        .at[target]
        .set(jnp.arange(row_count, dtype=jnp.int32), mode="drop")
    )
    dy_pad = jnp.concatenate([cotangent, jnp.zeros((1, d_model), cotangent.dtype)], axis=0)
    h_pad = jnp.concatenate(
        [hidden.reshape(row_count, hidden_width), jnp.zeros((1, hidden_width), hidden.dtype)],
        axis=0,
    )
    p_pad = jnp.concatenate([probs.reshape(row_count), jnp.zeros((1,), probs.dtype)], axis=0)
    send_dy = dy_pad[inverse // top_count]
    send_h = h_pad[inverse]
    send_p = p_pad[inverse]
    recv_dy, recv_h, recv_p = (
        lax.all_to_all(send_dy, "expert", split_axis=0, concat_axis=0, tiled=True),
        lax.all_to_all(send_h, "expert", split_axis=0, concat_axis=0, tiled=True),
        lax.all_to_all(send_p, "expert", split_axis=0, concat_axis=0, tiled=True),
    )
    flat_size = hidden_width * d_model
    flat_w = weights.reshape(local_count, flat_size)
    pieces = lax.all_to_all(flat_w, "expert", split_axis=1, concat_axis=0, tiled=True)
    chosen = pieces[replica_of]
    copy_weight = lax.all_to_all(chosen, "expert", split_axis=0, concat_axis=0, tiled=True).reshape(
        hidden_width, d_model
    )
    slot_total = local_count + 1
    home_rows = local_count * CAPH
    row_pos = jnp.arange(recv_count, dtype=jnp.int32) % per_dev
    row_slot = jnp.where(row_pos < home_rows, row_pos // CAPH, local_count)
    all_weights = jnp.concatenate(
        [weights.reshape(local_count * hidden_width, d_model), copy_weight], axis=0
    )
    all_in = lax.dot_general(
        recv_dy, all_weights, (((1,), (1,)), ((), ())), preferred_element_type=jnp.float32
    )
    grad_in = jnp.zeros((recv_count, hidden_width), jnp.float32)
    for slot_num in range(slot_total):
        grad_in = grad_in + jnp.where(
            (row_slot == slot_num)[:, None],
            all_in[:, slot_num * hidden_width : (slot_num + 1) * hidden_width],
            0.0,
        )
    p_wide = recv_p.astype(jnp.float32)[:, None]
    h_wide = recv_h.astype(jnp.float32)
    grad_h_buf = (p_wide * grad_in).astype(jnp.bfloat16)
    grad_p_buf = jnp.sum(h_wide * grad_in, axis=1).astype(jnp.bfloat16)
    scaled = (p_wide * h_wide).astype(jnp.bfloat16)
    zero_rows = jnp.zeros_like(scaled)
    scaled_wide = jnp.concatenate(
        [
            jnp.where((row_slot == slot_num)[:, None], scaled, zero_rows)
            for slot_num in range(slot_total)
        ],
        axis=1,
    )
    parts = lax.dot_general(
        scaled_wide, recv_dy, (((0,), (0,)), ((), ())), preferred_element_type=jnp.float32
    ).astype(jnp.bfloat16)
    home_part = parts[: local_count * hidden_width].reshape(local_count, hidden_width, d_model)
    copy_part = parts[local_count * hidden_width :]
    back_h, back_p = (
        lax.all_to_all(grad_h_buf, "expert", split_axis=0, concat_axis=0, tiled=True),
        lax.all_to_all(grad_p_buf, "expert", split_axis=0, concat_axis=0, tiled=True),
    )
    flat_h = jnp.concatenate([back_h, jnp.zeros((1, hidden_width), back_h.dtype)], axis=0)
    flat_p = jnp.concatenate([back_p, jnp.zeros((1,), back_p.dtype)], axis=0)
    hidden_gradient = flat_h[target].reshape(tok_rows, top_count, hidden_width)
    grad_probs = flat_p[target].reshape(tok_rows, top_count)
    expert_total = dev_count * local_count
    cover = replica_of[None, :] == jnp.arange(expert_total, dtype=jnp.int32)[:, None]
    half_width = d_model // data_count
    halves = lax.all_to_all(copy_part, "dp", split_axis=1, concat_axis=0, tiled=True)
    copy_half = jnp.sum(
        halves.reshape(data_count, hidden_width, half_width).astype(jnp.float32), axis=0
    )
    piece_len = hidden_width * half_width // dev_count
    slabs = copy_half.reshape(dev_count, piece_len)
    arrived = lax.all_to_all(slabs, "expert", split_axis=0, concat_axis=0, tiled=True)
    sums = jnp.dot(cover.astype(jnp.float32), arrived, precision=lax.Precision.HIGHEST)
    homed = lax.all_to_all(
        sums.reshape(dev_count, local_count * piece_len),
        "expert",
        split_axis=0,
        concat_axis=0,
        tiled=True,
    )
    homed = (
        homed.reshape(dev_count, local_count, piece_len)
        .transpose(1, 0, 2)
        .reshape(local_count, hidden_width, half_width)
    )
    home_half = lax.psum_scatter(
        home_part.astype(jnp.float32).astype(jnp.bfloat16), "dp", scatter_dimension=2, tiled=True
    ).astype(jnp.float32)
    grad_weights = (home_half + homed).astype(jnp.bfloat16)
    return (hidden_gradient, grad_probs, grad_weights)


SLOT = 4
F32 = jnp.float32
BF16 = jnp.bfloat16
NT = (((1,), (1,)), ((), ()))
TN = (((0,), (0,)), ((), ()))


def iota(shape, dim):
    return lax.broadcasted_iota(jnp.int32, shape, dim)


def dispatch_kernel(local_count, dev_count, *refs):
    sources, refs = refs[:6], refs[6:]
    copy_ref, home_ref, pick_ref, expert_ref, hs_ref, ps_ref = refs[:6]
    held, wide, sems = refs[6:12], refs[12], refs[13]
    moves = [pltpu.make_async_copy(s, h, sems.at[n]) for n, (s, h) in enumerate(zip(sources, held))]
    for move in moves:
        move.start()
    replica_ref, counts_ref, ids_ref, probs_ref, hid_ref, cot_ref = held
    top, toks = ids_ref.shape
    d_model = cot_ref.shape[1]
    homes = dev_count * local_count * SLOT
    slots = homes + dev_count * CAPR
    for move in moves[:3]:
        move.wait()
    row = iota((slots, toks), 0)
    expert = row // SLOT
    within = row % SLOT
    allowed = jnp.where(within < CAPH, 1, 0)
    for d in range(dev_count):
        first = homes + d * CAPR
        mine = (row >= first) & (row < first + CAPR)
        expert = jnp.where(mine, replica_ref[d], expert)
        within = jnp.where(mine, row - first, within)
        allowed = jnp.where(mine, jnp.where(row - first < counts_ref[0, d], 1, 0), allowed)
    lower = jnp.zeros((slots, toks), jnp.int32)
    for d in range(dev_count):
        earlier = (row < homes) | (row >= homes + (d + 1) * CAPR)
        lower = lower + jnp.where(earlier & (expert == replica_ref[d]), counts_ref[0, d], 0)
    ids = ids_ref[...]
    named = jnp.zeros((slots, toks), F32)
    for k in range(top):
        named = named + jnp.where(ids[k:k + 1, :] == expert, 1.0, 0.0)
    before = jnp.where(iota((toks, toks), 0) < iota((toks, toks), 1), 1.0, 0.0).astype(BF16)
    rank = jnp.dot(named.astype(BF16), before, preferred_element_type=F32)
    wanted = (lower + within).astype(F32)
    pick = jnp.where((rank == wanted) & (allowed > 0), named, 0.0)
    pick_ref[...] = pick
    expert_ref[...] = expert
    for move in moves[3:5]:
        move.wait()
    wide[...] = hid_ref[...].astype(F32)
    h_slot = jnp.zeros((slots, hid_ref.shape[1]), F32)
    p_slot = jnp.zeros((slots, toks), F32)
    probs = probs_ref[...].astype(F32)
    for k in range(top):
        sel = jnp.where(ids[k:k + 1, :] == expert, pick, 0.0)
        h_k = wide[pl.ds(k, toks, stride=top), :].astype(BF16)
        h_slot = h_slot + jnp.dot(sel.astype(BF16), h_k, preferred_element_type=F32)
        p_slot = p_slot + sel * probs[k:k + 1, :]
    p_slot = jnp.sum(p_slot, axis=1, keepdims=True)
    hs_ref[...] = h_slot
    ps_ref[...] = jnp.broadcast_to(p_slot, ps_ref.shape)
    scaled = p_slot * h_slot
    moves[5].wait()
    rows = jnp.dot(pick.astype(BF16), cot_ref[...], preferred_element_type=F32)
    copy_ref[:, :d_model] = rows[homes:].astype(BF16)
    copy_ref[:, d_model:] = scaled[homes:].astype(BF16)
    home_ref[:, :d_model] = rows[:homes].astype(BF16)
    home_ref[:, d_model:] = scaled[:homes].astype(BF16)


def local_slots(local_count, dev_count, width, replica_ref):
    first = lax.axis_index("expert") * local_count
    home = (iota((dev_count * local_count * SLOT, width), 0) // SLOT) % local_count
    row = iota((dev_count * CAPR, width), 0)
    copy = jnp.full((dev_count * CAPR, width), -1, jnp.int32)
    for d in range(dev_count):
        mine = (row >= d * CAPR) & (row < (d + 1) * CAPR)
        copy = jnp.where(mine, replica_ref[d] - first, copy)
    return jnp.concatenate([home] + [copy] * dev_count, axis=0)


def grad_in_kernel(local_count, dev_count, replica_ref, w_hbm, home_ref, *refs):
    copy_refs, (rows_ref, back_ref, w_ref, passed, sem) = refs[:dev_count], refs[dev_count:]
    fetch = pltpu.make_async_copy(w_hbm, w_ref, sem)
    fetch.start()
    d_model = w_ref.shape[1]
    width = w_ref.shape[0] // local_count
    per_home, per_copy = local_count * SLOT, dev_count * CAPR
    homes = dev_count * per_home
    rows_ref[:homes] = home_ref[...]
    rows_ref[homes:] = jnp.concatenate([r[...].astype(F32) for r in copy_refs], axis=0).astype(BF16)
    slot = local_slots(local_count, dev_count, width, replica_ref)
    fetch.wait()
    every = lax.dot_general(rows_ref[:, :d_model], w_ref[...], NT, preferred_element_type=F32)
    own = jnp.zeros((rows_ref.shape[0], width), F32)
    for e in range(local_count):
        own = jnp.where(slot == e, every[:, e * width:(e + 1) * width], own)
    passed[...] = own[homes:].reshape(passed.shape)
    me = lax.axis_index("expert")
    blocks = []
    for source in range(dev_count):
        blocks += [own[source * per_home:(source + 1) * per_home], passed[me ^ source]]
    back_ref[...] = jnp.concatenate(blocks, axis=0).astype(back_ref.dtype)


def grad_weights_half(local_count, dev_count, half, replica_ref, rows_ref, columns):
    width = rows_ref.shape[1] - 2 * columns
    start = pl.multiple_of(half * columns, 128)
    slot = local_slots(local_count, dev_count, width, replica_ref)
    scaled = rows_ref[:, 2 * columns:].astype(F32)
    spread = jnp.concatenate([jnp.where(slot == e, scaled, 0.0) for e in range(local_count)], axis=1)
    return lax.dot_general(spread.astype(BF16), rows_ref[:, pl.ds(start, columns)], TN, preferred_element_type=F32)


def other_half_kernel(local_count, dev_count, replica_ref, rows_ref, out_ref):
    half = 1 - lax.axis_index("dp")
    out_ref[...] = grad_weights_half(
        local_count, dev_count, half, replica_ref, rows_ref, out_ref.shape[1]).astype(out_ref.dtype)


def own_half_kernel(local_count, dev_count, replica_ref, rows_ref, arrived_ref, out_ref):
    half = lax.axis_index("dp")
    total = grad_weights_half(local_count, dev_count, half, replica_ref, rows_ref, out_ref.shape[1])
    out_ref[...] = (total + arrived_ref[...].astype(F32)).astype(out_ref.dtype)


def combine_kernel(local_count, dev_count, back_ref, pick_ref, expert_ref, hs_ref, ps_ref, ids_ref,
                   grad_h_ref, grad_p_ref, wide, narrow):
    top, toks = ids_ref.shape
    width = back_ref.shape[1]
    per_home, per_copy = local_count * SLOT, dev_count * CAPR
    back = back_ref[...].astype(F32).reshape(dev_count, per_home + per_copy, width)
    home = back[:, :per_home].reshape(dev_count * per_home, width)
    grad_in = jnp.concatenate([home, jnp.sum(back[:, per_home:], axis=0)], axis=0)
    h_rows = (ps_ref[...] * grad_in).astype(BF16)
    p_rows = jnp.sum(hs_ref[...] * grad_in, axis=1, keepdims=True)
    ids = ids_ref[...]
    pick = pick_ref[...]
    expert = expert_ref[...]
    for k in range(top):
        sel = jnp.where(ids[k:k + 1, :] == expert, pick, 0.0)
        wide[pl.ds(k, toks, stride=top), :] = lax.dot_general(
            sel.astype(BF16), h_rows, TN, preferred_element_type=F32)
        narrow[k:k + 1, :] = jnp.sum(sel * p_rows, axis=0, keepdims=True)
    grad_h_ref[...] = wide[...].astype(grad_h_ref.dtype)
    grad_p_ref[...] = narrow[...].astype(grad_p_ref.dtype)


def call(kernel, out_shape, operands, scratch=(), flops=0, limit=24):
    shapes = jax.tree.leaves(out_shape)
    moved = sum(a.size * a.dtype.itemsize for a in (*(a for _, a in operands), *shapes))
    return pl.pallas_call(
        kernel,
        out_shape=out_shape,
        in_specs=[pl.BlockSpec(memory_space=space) for space, _ in operands],
        out_specs=jax.tree.map(lambda _: pl.BlockSpec(memory_space=pltpu.VMEM), out_shape),
        scratch_shapes=list(scratch),
        compiler_params=pltpu.CompilerParams(vmem_limit_bytes=limit << 20),
        cost_estimate=pl.CostEstimate(flops=flops, bytes_accessed=moved, transcendentals=0),
    )(*(a for _, a in operands))


def swap(x, bits, count):
    return lax.ppermute(x, "expert", [(i, i ^ bits) for i in range(count)])


def gather_body(cotangent, hidden, probs, expert_ids, send_counts, replica_of, weights):
    toks, d_model = cotangent.shape
    top = expert_ids.shape[1]
    width = hidden.shape[2]
    local_count = weights.shape[0]
    dev_count = lax.axis_size("expert")
    homes = dev_count * local_count * SLOT
    copies = dev_count * CAPR
    slots = homes + copies
    rows = homes + dev_count * copies
    columns = d_model // 2
    sizes = (local_count, dev_count)
    ids = expert_ids.T
    shape = jax.ShapeDtypeStruct
    hbm, vmem, smem = pltpu.HBM, pltpu.VMEM, pltpu.SMEM
    sources = (replica_of, send_counts, ids, probs.T, hidden.reshape(toks * top, width), cotangent)
    copy_rows, home_rows, pick, expert, h_slot, p_slot = call(
        functools.partial(dispatch_kernel, *sizes),
        (shape((copies, d_model + width), BF16), shape((homes, d_model + width), BF16), shape((slots, toks), F32),
         shape((slots, toks), jnp.int32), shape((slots, width), F32), shape((slots, width), F32)),
        [(hbm, a) for a in sources],
        [(smem if n < 2 else vmem)(a.shape, a.dtype) for n, a in enumerate(sources)]
        + [vmem((toks * top, width), F32), pltpu.SemaphoreType.DMA((len(sources),))],
        flops=2 * slots * toks * d_model,
        limit=60,
    )
    copy_in = {0: copy_rows}
    for bits in reversed(range(dev_count.bit_length() - 1)):
        copy_in[1 << bits] = swap(copy_rows, 1 << bits, dev_count)
    copy_in, home_rows = lax.optimization_barrier((copy_in, home_rows))
    for m in sorted(range(1, dev_count), key=lambda m: (m.bit_count(), -m)):
        low = m & -m
        if m != low:
            copy_in[m] = swap(copy_in[m ^ low], low, dev_count)
    home_in = lax.all_to_all(home_rows, "expert", split_axis=0, concat_axis=0, tiled=True)
    all_rows, back = call(
        functools.partial(grad_in_kernel, *sizes),
        (shape((rows, d_model + width), BF16), shape((rows, width), BF16)),
        [(smem, replica_of), (hbm, weights.reshape(local_count * width, d_model)), (vmem, home_in)]
        + [(vmem, copy_in[m]) for m in range(dev_count)],
        [vmem((local_count * width, d_model), BF16), vmem((dev_count, copies, width), F32),
         pltpu.SemaphoreType.DMA(())],
        flops=2 * rows * d_model * local_count * width,
    )
    back = lax.all_to_all(back, "expert", split_axis=0, concat_axis=0, tiled=True)
    half_flops = 2 * rows * columns * local_count * width
    other = call(
        functools.partial(other_half_kernel, *sizes),
        shape((local_count * width, columns), BF16),
        [(smem, replica_of), (vmem, all_rows)],
        flops=half_flops,
    )
    arrived = lax.ppermute(other, "dp", [(0, 1), (1, 0)])
    grad_h, grad_p = call(
        functools.partial(combine_kernel, *sizes),
        (shape((toks * top, width), BF16), shape((top, toks), BF16)),
        [(vmem, a) for a in (back, pick, expert, h_slot, p_slot, ids)],
        [vmem((toks * top, width), F32), vmem((top, toks), F32)],
        flops=2 * slots * toks * width * top,
    )
    grad_w = call(
        functools.partial(own_half_kernel, *sizes),
        shape((local_count * width, columns), BF16),
        [(smem, replica_of), (vmem, all_rows), (vmem, arrived)],
        flops=half_flops,
    )
    return (
        grad_h.reshape(toks, top, width),
        grad_p.T,
        grad_w.reshape(local_count, width, columns),
    )


def body(cotangent, hidden, probs, expert_ids, send_counts, replica_of, weights):
    dev_count = lax.axis_size("expert")
    local_count, width, _ = weights.shape
    gathered = dev_count * dev_count * CAPR
    if gathered <= (local_count + 3) * width and dev_count.bit_count() == 1 and lax.axis_size("dp") == 2:
        run = gather_body
    else:
        run = replica_body
    return run(cotangent, hidden, probs, expert_ids, send_counts, replica_of, weights)


def solution(mesh):
    in_specs = (
        P(("groups", "expert", "dp"), None),
        P(("groups", "expert", "dp"), None, None),
        P(("groups", "expert", "dp"), None),
        P(("groups", "expert", "dp"), None),
        P(("groups", "expert", "dp"), None),
        P("groups"),
        P("expert", None, None),
    )
    out_specs = (
        P(("groups", "expert", "dp"), None, None),
        P(("groups", "expert", "dp"), None),
        P(("groups", "expert"), None, "dp"),
    )
    return jax.shard_map(body, mesh=mesh, in_specs=in_specs, out_specs=out_specs, check_vma=False)
```

```python
import functools

import jax
import jax.numpy as jnp
from jax import lax
from jax.experimental import pallas as pl
from jax.experimental.pallas import tpu as pltpu
from jax.sharding import PartitionSpec as P

CAPH = 3
CAPR = 3


def ranks_within(keys):
    total_rows = keys.shape[0]
    sort_order = jnp.argsort(keys * total_rows + jnp.arange(total_rows, dtype=jnp.int32))
    sorted_keys = keys[sort_order]
    first_seen = jnp.searchsorted(sorted_keys, sorted_keys, side="left")
    ranked = jnp.arange(total_rows, dtype=jnp.int32) - first_seen
    return jnp.zeros((total_rows,), jnp.int32).at[sort_order].set(ranked)


def route_rows(ids_block, counts_row, replica_of, local_count, cap_home, cap_copy):
    dev_count = replica_of.shape[0]
    experts = ids_block.reshape(-1)
    rank_expert = ranks_within(experts)
    devices = jnp.arange(dev_count, dtype=jnp.int32)
    same_copy = (replica_of[:, None] == replica_of[None, :]) & (devices[None, :] < devices[:, None])
    lower_rank = jnp.sum(jnp.where(same_copy, counts_row[None, :], 0), axis=1)
    upper_rank = lower_rank + counts_row
    hit_table = (
        (replica_of[None, :] == experts[:, None])
        & (lower_rank[None, :] <= rank_expert[:, None])
        & (rank_expert[:, None] < upper_rank[None, :])
    )
    copied = jnp.any(hit_table, axis=1)
    copy_dev = jnp.sum(jnp.where(hit_table, devices[None, :], 0), axis=1)
    dest_dev = jnp.where(copied, copy_dev, experts // local_count)
    index_of_slot = jnp.where(copied, local_count, experts % local_count)
    rank_bucket = ranks_within(dest_dev * (local_count + 1) + index_of_slot)
    keep_row = rank_bucket < jnp.where(copied, cap_copy, cap_home)
    per_dev = local_count * cap_home + cap_copy
    target = dest_dev * per_dev + index_of_slot * cap_home + rank_bucket
    return jnp.where(keep_row, target, dev_count * per_dev)


def replica_body(cotangent, hidden, probs, expert_ids, send_counts, replica_of, weights):
    tok_rows, d_model = cotangent.shape
    top_count = expert_ids.shape[1]
    hidden_width = hidden.shape[2]
    local_count = weights.shape[0]
    dev_count = lax.axis_size("expert")
    data_count = lax.axis_size("dp")
    per_dev = local_count * CAPH + CAPR
    row_count = tok_rows * top_count
    recv_count = dev_count * per_dev
    target = route_rows(expert_ids, send_counts[0], replica_of, local_count, CAPH, CAPR)
    inverse = (
        jnp.full((recv_count,), row_count, jnp.int32)
        .at[target]
        .set(jnp.arange(row_count, dtype=jnp.int32), mode="drop")
    )
    dy_pad = jnp.concatenate([cotangent, jnp.zeros((1, d_model), cotangent.dtype)], axis=0)
    h_pad = jnp.concatenate(
        [hidden.reshape(row_count, hidden_width), jnp.zeros((1, hidden_width), hidden.dtype)],
        axis=0,
    )
    p_pad = jnp.concatenate([probs.reshape(row_count), jnp.zeros((1,), probs.dtype)], axis=0)
    send_dy = dy_pad[inverse // top_count]
    send_h = h_pad[inverse]
    send_p = p_pad[inverse]
    recv_dy, recv_h, recv_p = (
        lax.all_to_all(send_dy, "expert", split_axis=0, concat_axis=0, tiled=True),
        lax.all_to_all(send_h, "expert", split_axis=0, concat_axis=0, tiled=True),
        lax.all_to_all(send_p, "expert", split_axis=0, concat_axis=0, tiled=True),
    )
    flat_size = hidden_width * d_model
    flat_w = weights.reshape(local_count, flat_size)
    pieces = lax.all_to_all(flat_w, "expert", split_axis=1, concat_axis=0, tiled=True)
    chosen = pieces[replica_of]
    copy_weight = lax.all_to_all(chosen, "expert", split_axis=0, concat_axis=0, tiled=True).reshape(
        hidden_width, d_model
    )
    slot_total = local_count + 1
    home_rows = local_count * CAPH
    row_pos = jnp.arange(recv_count, dtype=jnp.int32) % per_dev
    row_slot = jnp.where(row_pos < home_rows, row_pos // CAPH, local_count)
    all_weights = jnp.concatenate(
        [weights.reshape(local_count * hidden_width, d_model), copy_weight], axis=0
    )
    all_in = lax.dot_general(
        recv_dy, all_weights, (((1,), (1,)), ((), ())), preferred_element_type=jnp.float32
    )
    grad_in = jnp.zeros((recv_count, hidden_width), jnp.float32)
    for slot_num in range(slot_total):
        grad_in = grad_in + jnp.where(
            (row_slot == slot_num)[:, None],
            all_in[:, slot_num * hidden_width : (slot_num + 1) * hidden_width],
            0.0,
        )
    p_wide = recv_p.astype(jnp.float32)[:, None]
    h_wide = recv_h.astype(jnp.float32)
    grad_h_buf = (p_wide * grad_in).astype(jnp.bfloat16)
    grad_p_buf = jnp.sum(h_wide * grad_in, axis=1).astype(jnp.bfloat16)
    scaled = (p_wide * h_wide).astype(jnp.bfloat16)
    zero_rows = jnp.zeros_like(scaled)
    scaled_wide = jnp.concatenate(
        [
            jnp.where((row_slot == slot_num)[:, None], scaled, zero_rows)
            for slot_num in range(slot_total)
        ],
        axis=1,
    )
    parts = lax.dot_general(
        scaled_wide, recv_dy, (((0,), (0,)), ((), ())), preferred_element_type=jnp.float32
    ).astype(jnp.bfloat16)
    home_part = parts[: local_count * hidden_width].reshape(local_count, hidden_width, d_model)
    copy_part = parts[local_count * hidden_width :]
    back_h, back_p = (
        lax.all_to_all(grad_h_buf, "expert", split_axis=0, concat_axis=0, tiled=True),
        lax.all_to_all(grad_p_buf, "expert", split_axis=0, concat_axis=0, tiled=True),
    )
    flat_h = jnp.concatenate([back_h, jnp.zeros((1, hidden_width), back_h.dtype)], axis=0)
    flat_p = jnp.concatenate([back_p, jnp.zeros((1,), back_p.dtype)], axis=0)
    hidden_gradient = flat_h[target].reshape(tok_rows, top_count, hidden_width)
    grad_probs = flat_p[target].reshape(tok_rows, top_count)
    expert_total = dev_count * local_count
    cover = replica_of[None, :] == jnp.arange(expert_total, dtype=jnp.int32)[:, None]
    half_width = d_model // data_count
    halves = lax.all_to_all(copy_part, "dp", split_axis=1, concat_axis=0, tiled=True)
    copy_half = jnp.sum(
        halves.reshape(data_count, hidden_width, half_width).astype(jnp.float32), axis=0
    )
    piece_len = hidden_width * half_width // dev_count
    slabs = copy_half.reshape(dev_count, piece_len)
    arrived = lax.all_to_all(slabs, "expert", split_axis=0, concat_axis=0, tiled=True)
    sums = jnp.dot(cover.astype(jnp.float32), arrived, precision=lax.Precision.HIGHEST)
    homed = lax.all_to_all(
        sums.reshape(dev_count, local_count * piece_len),
        "expert",
        split_axis=0,
        concat_axis=0,
        tiled=True,
    )
    homed = (
        homed.reshape(dev_count, local_count, piece_len)
        .transpose(1, 0, 2)
        .reshape(local_count, hidden_width, half_width)
    )
    home_half = lax.psum_scatter(
        home_part.astype(jnp.float32).astype(jnp.bfloat16), "dp", scatter_dimension=2, tiled=True
    ).astype(jnp.float32)
    grad_weights = (home_half + homed).astype(jnp.bfloat16)
    return (hidden_gradient, grad_probs, grad_weights)


SLOT = 4
HOME, COPIES = "home", "copies"
F32 = jnp.float32
BF16 = jnp.bfloat16
NT = (((1,), (1,)), ((), ()))
TN = (((0,), (0,)), ((), ()))


def iota(shape, dim):
    return lax.broadcasted_iota(jnp.int32, shape, dim)


def dispatch_kernel(local_count, dev_count, packing, *refs):
    sources, refs = refs[:6], refs[6:]
    pick_ref, expert_ref, hs_ref, ps_ref = refs[:4]
    packed, (held, wide, sems) = refs[4:4 + len(packing)], (refs[-8:-2], refs[-2], refs[-1])
    moves = [pltpu.make_async_copy(s, h, sems.at[n]) for n, (s, h) in enumerate(zip(sources, held))]
    for move in moves:
        move.start()
    replica_ref, counts_ref, ids_ref, probs_ref, hid_ref, cot_ref = held
    top, toks = ids_ref.shape
    d_model = cot_ref.shape[1]
    per_home = local_count * SLOT
    homes = dev_count * per_home
    slots = homes + dev_count * CAPR
    me = lax.axis_index("expert")
    for move in moves[:3]:
        move.wait()
    row = iota((slots, toks), 0)
    expert = ((row // per_home) ^ me) * local_count + (row % per_home) // SLOT
    within = row % SLOT
    allowed = jnp.where(within < CAPH, 1, 0)
    for d in range(dev_count):
        first = homes + d * CAPR
        mine = (row >= first) & (row < first + CAPR)
        expert = jnp.where(mine, replica_ref[d], expert)
        within = jnp.where(mine, row - first, within)
        allowed = jnp.where(mine, jnp.where(row - first < counts_ref[0, d], 1, 0), allowed)
    lower = jnp.zeros((slots, toks), jnp.int32)
    for d in range(dev_count):
        earlier = (row < homes) | (row >= homes + (d + 1) * CAPR)
        lower = lower + jnp.where(earlier & (expert == replica_ref[d]), counts_ref[0, d], 0)
    ids = ids_ref[...]
    named = jnp.zeros((slots, toks), F32)
    for k in range(top):
        named = named + jnp.where(ids[k:k + 1, :] == expert, 1.0, 0.0)
    before = jnp.where(iota((toks, toks), 0) < iota((toks, toks), 1), 1.0, 0.0).astype(BF16)
    rank = jnp.dot(named.astype(BF16), before, preferred_element_type=F32)
    wanted = (lower + within).astype(F32)
    pick = jnp.where((rank == wanted) & (allowed > 0), named, 0.0)
    pick_ref[...] = pick
    expert_ref[...] = expert
    for move in moves[3:5]:
        move.wait()
    wide[...] = hid_ref[...].astype(F32)
    h_slot = jnp.zeros((slots, hid_ref.shape[1]), F32)
    p_slot = jnp.zeros((slots, toks), F32)
    probs = probs_ref[...].astype(F32)
    for k in range(top):
        sel = jnp.where(ids[k:k + 1, :] == expert, pick, 0.0)
        h_k = wide[pl.ds(k, toks, stride=top), :].astype(BF16)
        h_slot = h_slot + jnp.dot(sel.astype(BF16), h_k, preferred_element_type=F32)
        p_slot = p_slot + sel * probs[k:k + 1, :]
    p_slot = jnp.sum(p_slot, axis=1, keepdims=True)
    hs_ref[...] = h_slot
    ps_ref[...] = jnp.broadcast_to(p_slot, ps_ref.shape)
    scaled = p_slot * h_slot
    moves[5].wait()
    rows = jnp.dot(pick.astype(BF16), cot_ref[...], preferred_element_type=F32)
    for out_ref, blocks in zip(packed, packing):
        spans = [(homes, slots) if b == COPIES else (b * per_home, (b + 1) * per_home) for b in blocks]
        out_ref[:, :d_model] = jnp.concatenate([rows[i:j] for i, j in spans], axis=0).astype(BF16)
        out_ref[:, d_model:] = jnp.concatenate([scaled[i:j] for i, j in spans], axis=0).astype(BF16)


def padded(rows):
    return -(-rows // 16) * 16


def stack(order, blocks, height):
    values = [blocks[key] for key in order]
    missing = height - sum(v.shape[0] for v in values)
    if missing:
        values.append(jnp.zeros((missing, values[0].shape[1]), values[0].dtype))
    return jnp.concatenate(values, axis=0)


def slots_of(order, slot_ref, per_home, height):
    kinds = {HOME: slot_ref[:per_home], COPIES: slot_ref[per_home:]}
    return stack(order, {key: kinds[key[1]] for key in order}, height)


def fill_rows(order, pieces, per_home, per_copy, piece_refs, rows_ref):
    values = [r[...].astype(F32) for r in piece_refs]
    blocks = {}
    for key in order:
        n, start = pieces[key]
        blocks[key] = values[n][start:start + (per_home if key[1] == HOME else per_copy)]
    rows_ref[...] = stack(order, blocks, rows_ref.shape[0]).astype(BF16)


def own_columns(rows_ref, w_ref, slot, local_count):
    d_model = w_ref.shape[1]
    width = w_ref.shape[0] // local_count
    every = lax.dot_general(rows_ref[:, :d_model], w_ref[...], NT, preferred_element_type=F32)
    own = jnp.zeros((rows_ref.shape[0], width), F32)
    for e in range(local_count):
        own = jnp.where(slot == e, every[:, e * width:(e + 1) * width], own)
    return own


def early_kernel(local_count, dev_count, order, pieces, replica_ref, w_hbm, *refs):
    piece_refs, (rows_ref, w_ref, slot_ref, own_ref, sem) = refs[:-5], refs[-5:]
    fetch = pltpu.make_async_copy(w_hbm, w_ref, sem)
    fetch.start()
    per_home, per_copy = local_count * SLOT, dev_count * CAPR
    first = lax.axis_index("expert") * local_count
    width = slot_ref.shape[1]
    slot_ref[:per_home] = iota((per_home, width), 0) // SLOT
    row = iota((per_copy, width), 0)
    copy = jnp.full((per_copy, width), -1, jnp.int32)
    for d in range(dev_count):
        mine = (row >= d * CAPR) & (row < (d + 1) * CAPR)
        copy = jnp.where(mine, replica_ref[d] - first, copy)
    slot_ref[per_home:] = copy
    fill_rows(order, pieces, per_home, per_copy, piece_refs, rows_ref)
    fetch.wait()
    slot = slots_of(order, slot_ref, per_home, rows_ref.shape[0])
    own_ref[...] = own_columns(rows_ref, w_ref, slot, local_count)


def late_kernel(local_count, dev_count, early, order, pieces, own_ref, w_ref, slot_ref, *refs):
    piece_refs, (rows_ref, back_ref, passed) = refs[:-3], refs[-3:]
    per_home, per_copy = local_count * SLOT, dev_count * CAPR
    fill_rows(order, pieces, per_home, per_copy, piece_refs, rows_ref)
    own = own_columns(rows_ref, w_ref, slots_of(order, slot_ref, per_home, rows_ref.shape[0]), local_count)
    for keys, value in ((early, own_ref[...]), (order, own)):
        start = 0
        for m, kind in keys:
            lower, size = (0, per_home) if kind == HOME else (per_home, per_copy)
            passed[m, lower:lower + size] = value[start:start + size]
            start += size
    me = lax.axis_index("expert")
    back = jnp.concatenate([passed[me ^ source] for source in range(dev_count)], axis=0)
    back_ref[...] = back.astype(back_ref.dtype)


def grad_weights_half(local_count, dev_count, orders, half, slot_ref, rows_refs, columns):
    start = pl.multiple_of(half * columns, 128)
    total = None
    for order, ref in zip(orders, rows_refs):
        slot = slots_of(order, slot_ref, local_count * SLOT, ref.shape[0])
        scaled = ref[:, 2 * columns:].astype(F32)
        spread = jnp.concatenate([jnp.where(slot == e, scaled, 0.0) for e in range(local_count)], axis=1)
        part = lax.dot_general(spread.astype(BF16), ref[:, pl.ds(start, columns)], TN, preferred_element_type=F32)
        total = part if total is None else total + part
    return total


def other_half_kernel(local_count, dev_count, orders, slot_ref, early_ref, late_ref, out_ref):
    half = 1 - lax.axis_index("dp")
    out_ref[...] = grad_weights_half(
        local_count, dev_count, orders, half, slot_ref, (early_ref, late_ref), out_ref.shape[1]).astype(out_ref.dtype)


def own_half_kernel(local_count, dev_count, orders, slot_ref, early_ref, late_ref, arrived_ref, out_ref):
    half = lax.axis_index("dp")
    total = grad_weights_half(
        local_count, dev_count, orders, half, slot_ref, (early_ref, late_ref), out_ref.shape[1])
    out_ref[...] = (total + arrived_ref[...].astype(F32)).astype(out_ref.dtype)


def combine_kernel(local_count, dev_count, back_ref, pick_ref, expert_ref, hs_ref, ps_ref, ids_ref,
                   grad_h_ref, grad_p_ref, wide, narrow):
    top, toks = ids_ref.shape
    per_home = local_count * SLOT
    me = lax.axis_index("expert")
    back = [back_ref[me ^ m].astype(F32) for m in range(dev_count)]
    copy = functools.reduce(jnp.add, [b[per_home:] for b in back])
    grad_in = jnp.concatenate([b[:per_home] for b in back] + [copy], axis=0)
    h_rows = (ps_ref[...] * grad_in).astype(BF16)
    p_rows = jnp.sum(hs_ref[...] * grad_in, axis=1, keepdims=True)
    ids = ids_ref[...]
    pick = pick_ref[...]
    expert = expert_ref[...]
    for k in range(top):
        sel = jnp.where(ids[k:k + 1, :] == expert, pick, 0.0)
        wide[pl.ds(k, toks, stride=top), :] = lax.dot_general(
            sel.astype(BF16), h_rows, TN, preferred_element_type=F32)
        narrow[k:k + 1, :] = jnp.sum(sel * p_rows, axis=0, keepdims=True)
    grad_h_ref[...] = wide[...].astype(grad_h_ref.dtype)
    grad_p_ref[...] = narrow[...].astype(grad_p_ref.dtype)


def call(kernel, out_shape, operands, scratch=(), flops=0, limit=24):
    shapes = jax.tree.leaves(out_shape)
    moved = sum(a.size * a.dtype.itemsize for a in (*(a for _, a in operands), *shapes))
    return pl.pallas_call(
        kernel,
        out_shape=out_shape,
        in_specs=[pl.BlockSpec(memory_space=space) for space, _ in operands],
        out_specs=jax.tree.map(lambda _: pl.BlockSpec(memory_space=pltpu.VMEM), out_shape),
        scratch_shapes=list(scratch),
        compiler_params=pltpu.CompilerParams(vmem_limit_bytes=limit << 20),
        cost_estimate=pl.CostEstimate(flops=flops, bytes_accessed=moved, transcendentals=0),
    )(*(a for _, a in operands))


def swap(x, bits, count):
    return lax.ppermute(x, "expert", [(i, i ^ bits) for i in range(count)])


def gather_body(cotangent, hidden, probs, expert_ids, send_counts, replica_of, weights):
    toks, d_model = cotangent.shape
    top = expert_ids.shape[1]
    width = hidden.shape[2]
    local_count = weights.shape[0]
    dev_count = lax.axis_size("expert")
    homes = dev_count * local_count * SLOT
    copies = dev_count * CAPR
    slots = homes + copies
    rows = homes + dev_count * copies
    columns = d_model // 2
    sizes = (local_count, dev_count)
    ids = expert_ids.T
    shape = jax.ShapeDtypeStruct
    hbm, vmem, smem = pltpu.HBM, pltpu.VMEM, pltpu.SMEM
    sources = (replica_of, send_counts, ids, probs.T, hidden.reshape(toks * top, width), cotangent)
    per_home = local_count * SLOT
    firsts = [1 << n for n in reversed(range(dev_count.bit_length() - 1))]
    riders = {low: [low] + [low + 1] * (low == 2) for low in firsts if low < firsts[0]}
    packing = [[COPIES] + riders.get(low, [])[::-1] for low in firsts]
    direct = [m for m in range(1, dev_count) if not any(m in ride for ride in riders.values())]
    packing += [[0], [COPIES]] + [[m] for m in direct]
    sized = [sum(copies if b == COPIES else per_home for b in blocks) for blocks in packing]
    pick, expert, h_slot, p_slot, *packed = call(
        functools.partial(dispatch_kernel, *sizes, packing),
        [shape((slots, toks), F32), shape((slots, toks), jnp.int32), shape((slots, width), F32),
         shape((slots, width), F32)] + [shape((n, d_model + width), BF16) for n in sized],
        [(hbm, a) for a in sources],
        [(smem if n < 2 else vmem)(a.shape, a.dtype) for n, a in enumerate(sources)]
        + [vmem((toks * top, width), F32), pltpu.SemaphoreType.DMA((len(sources),))],
        flops=2 * slots * toks * d_model,
        limit=60,
    )
    pieces, arrays = {(0, HOME): (0, 0), (0, COPIES): (1, 0)}, packed[len(firsts):len(firsts) + 2]
    arrived = [swap(a, low, dev_count) for a, low in zip(packed, firsts)]
    arrived, packed, arrays = lax.optimization_barrier((arrived, packed, arrays))
    passing = {}
    for low, a in zip(firsts, arrived):
        pieces[low, COPIES] = (len(arrays), 0)
        if low in riders:
            pieces[low, HOME] = (len(arrays), a.shape[0] - per_home)
        passing[low] = a[:a.shape[0] - per_home] if low in riders else a
        arrays.append(a)
    flat_w = weights.reshape(local_count * width, d_model)
    orders = [list(pieces)]
    height = padded(sum(per_home if kind == HOME else copies for _, kind in pieces))
    early_rows, w_held, slot, own = call(
        functools.partial(early_kernel, *sizes, orders[0], pieces),
        (shape((height, d_model + width), BF16), shape(flat_w.shape, BF16),
         shape((per_home + copies, width), jnp.int32), shape((height, width), F32)),
        [(smem, replica_of), (hbm, flat_w)] + [(vmem, a) for a in arrays],
        [pltpu.SemaphoreType.DMA(())],
        flops=2 * height * d_model * local_count * width,
    )
    pieces, arrays = {}, []
    for m in sorted(range(1, dev_count), key=lambda m: (m.bit_count(), -m)):
        low = m & -m
        if m != low:
            passing[m] = swap(passing[m ^ low], low, dev_count)
            pieces[m, COPIES] = (len(arrays), 0)
            if passing[m].shape[0] > copies:
                pieces[m, HOME] = (len(arrays), copies)
            arrays.append(passing[m])
    for m, a in zip(direct, packed[len(firsts) + 2:]):
        pieces[m, HOME] = (len(arrays), 0)
        arrays.append(swap(a, m, dev_count))
    orders.append(list(pieces))
    height = padded(sum(per_home if kind == HOME else copies for _, kind in pieces))
    late_rows, back = call(
        functools.partial(late_kernel, *sizes, *orders, pieces),
        (shape((height, d_model + width), BF16), shape((dev_count * (per_home + copies), width), BF16)),
        [(vmem, a) for a in (own, w_held, slot, *arrays)],
        [vmem((dev_count, per_home + copies, width), F32)],
        flops=2 * height * d_model * local_count * width,
    )
    back = lax.all_to_all(back, "expert", split_axis=0, concat_axis=0, tiled=True)
    half_flops = 2 * rows * columns * local_count * width
    halves = (slot, early_rows, late_rows)
    other = call(
        functools.partial(other_half_kernel, *sizes, orders),
        shape((local_count * width, columns), BF16),
        [(vmem, a) for a in halves],
        flops=half_flops,
    )
    arrived = lax.ppermute(other, "dp", [(0, 1), (1, 0)])
    grad_w = call(
        functools.partial(own_half_kernel, *sizes, orders),
        shape((local_count * width, columns), BF16),
        [(vmem, a) for a in (*halves, arrived)],
        flops=half_flops,
    )
    grad_w, pick = lax.optimization_barrier((grad_w, pick))
    grad_h, grad_p = call(
        functools.partial(combine_kernel, *sizes),
        (shape((toks * top, width), BF16), shape((top, toks), BF16)),
        [(vmem, a) for a in (back.reshape(dev_count, per_home + copies, width), pick, expert, h_slot, p_slot, ids)],
        [vmem((toks * top, width), F32), vmem((top, toks), F32)],
        flops=2 * slots * toks * width * top,
    )
    return (
        grad_h.reshape(toks, top, width),
        grad_p.T,
        grad_w.reshape(local_count, width, columns),
    )


def body(cotangent, hidden, probs, expert_ids, send_counts, replica_of, weights):
    dev_count = lax.axis_size("expert")
    local_count, width, _ = weights.shape
    gathered = dev_count * dev_count * CAPR
    if gathered <= (local_count + 3) * width and dev_count.bit_count() == 1 and lax.axis_size("dp") == 2:
        run = gather_body
    else:
        run = replica_body
    return run(cotangent, hidden, probs, expert_ids, send_counts, replica_of, weights)


def solution(mesh):
    in_specs = (
        P(("groups", "expert", "dp"), None),
        P(("groups", "expert", "dp"), None, None),
        P(("groups", "expert", "dp"), None),
        P(("groups", "expert", "dp"), None),
        P(("groups", "expert", "dp"), None),
        P("groups"),
        P("expert", None, None),
    )
    out_specs = (
        P(("groups", "expert", "dp"), None, None),
        P(("groups", "expert", "dp"), None),
        P(("groups", "expert"), None, "dp"),
    )
    return jax.shard_map(body, mesh=mesh, in_specs=in_specs, out_specs=out_specs, check_vma=False)
```

```python
import functools

import jax
import jax.numpy as jnp
from jax import lax
from jax.experimental import pallas as pl
from jax.experimental.pallas import tpu as pltpu
from jax.sharding import PartitionSpec as P

CAPH = 3
CAPR = 3


def ranks_within(keys):
    total_rows = keys.shape[0]
    sort_order = jnp.argsort(keys * total_rows + jnp.arange(total_rows, dtype=jnp.int32))
    sorted_keys = keys[sort_order]
    first_seen = jnp.searchsorted(sorted_keys, sorted_keys, side="left")
    ranked = jnp.arange(total_rows, dtype=jnp.int32) - first_seen
    return jnp.zeros((total_rows,), jnp.int32).at[sort_order].set(ranked)


def route_rows(ids_block, counts_row, replica_of, local_count, cap_home, cap_copy):
    dev_count = replica_of.shape[0]
    experts = ids_block.reshape(-1)
    rank_expert = ranks_within(experts)
    devices = jnp.arange(dev_count, dtype=jnp.int32)
    same_copy = (replica_of[:, None] == replica_of[None, :]) & (devices[None, :] < devices[:, None])
    lower_rank = jnp.sum(jnp.where(same_copy, counts_row[None, :], 0), axis=1)
    upper_rank = lower_rank + counts_row
    hit_table = (
        (replica_of[None, :] == experts[:, None])
        & (lower_rank[None, :] <= rank_expert[:, None])
        & (rank_expert[:, None] < upper_rank[None, :])
    )
    copied = jnp.any(hit_table, axis=1)
    copy_dev = jnp.sum(jnp.where(hit_table, devices[None, :], 0), axis=1)
    dest_dev = jnp.where(copied, copy_dev, experts // local_count)
    index_of_slot = jnp.where(copied, local_count, experts % local_count)
    rank_bucket = ranks_within(dest_dev * (local_count + 1) + index_of_slot)
    keep_row = rank_bucket < jnp.where(copied, cap_copy, cap_home)
    per_dev = local_count * cap_home + cap_copy
    target = dest_dev * per_dev + index_of_slot * cap_home + rank_bucket
    return jnp.where(keep_row, target, dev_count * per_dev)


def replica_body(cotangent, hidden, probs, expert_ids, send_counts, replica_of, weights):
    tok_rows, d_model = cotangent.shape
    top_count = expert_ids.shape[1]
    hidden_width = hidden.shape[2]
    local_count = weights.shape[0]
    dev_count = lax.axis_size("expert")
    data_count = lax.axis_size("dp")
    per_dev = local_count * CAPH + CAPR
    row_count = tok_rows * top_count
    recv_count = dev_count * per_dev
    target = route_rows(expert_ids, send_counts[0], replica_of, local_count, CAPH, CAPR)
    inverse = (
        jnp.full((recv_count,), row_count, jnp.int32)
        .at[target]
        .set(jnp.arange(row_count, dtype=jnp.int32), mode="drop")
    )
    dy_pad = jnp.concatenate([cotangent, jnp.zeros((1, d_model), cotangent.dtype)], axis=0)
    h_pad = jnp.concatenate(
        [hidden.reshape(row_count, hidden_width), jnp.zeros((1, hidden_width), hidden.dtype)],
        axis=0,
    )
    p_pad = jnp.concatenate([probs.reshape(row_count), jnp.zeros((1,), probs.dtype)], axis=0)
    send_dy = dy_pad[inverse // top_count]
    send_h = h_pad[inverse]
    send_p = p_pad[inverse]
    recv_dy, recv_h, recv_p = (
        lax.all_to_all(send_dy, "expert", split_axis=0, concat_axis=0, tiled=True),
        lax.all_to_all(send_h, "expert", split_axis=0, concat_axis=0, tiled=True),
        lax.all_to_all(send_p, "expert", split_axis=0, concat_axis=0, tiled=True),
    )
    flat_size = hidden_width * d_model
    flat_w = weights.reshape(local_count, flat_size)
    pieces = lax.all_to_all(flat_w, "expert", split_axis=1, concat_axis=0, tiled=True)
    chosen = pieces[replica_of]
    copy_weight = lax.all_to_all(chosen, "expert", split_axis=0, concat_axis=0, tiled=True).reshape(
        hidden_width, d_model
    )
    slot_total = local_count + 1
    home_rows = local_count * CAPH
    row_pos = jnp.arange(recv_count, dtype=jnp.int32) % per_dev
    row_slot = jnp.where(row_pos < home_rows, row_pos // CAPH, local_count)
    all_weights = jnp.concatenate(
        [weights.reshape(local_count * hidden_width, d_model), copy_weight], axis=0
    )
    all_in = lax.dot_general(
        recv_dy, all_weights, (((1,), (1,)), ((), ())), preferred_element_type=jnp.float32
    )
    grad_in = jnp.zeros((recv_count, hidden_width), jnp.float32)
    for slot_num in range(slot_total):
        grad_in = grad_in + jnp.where(
            (row_slot == slot_num)[:, None],
            all_in[:, slot_num * hidden_width : (slot_num + 1) * hidden_width],
            0.0,
        )
    p_wide = recv_p.astype(jnp.float32)[:, None]
    h_wide = recv_h.astype(jnp.float32)
    grad_h_buf = (p_wide * grad_in).astype(jnp.bfloat16)
    grad_p_buf = jnp.sum(h_wide * grad_in, axis=1).astype(jnp.bfloat16)
    scaled = (p_wide * h_wide).astype(jnp.bfloat16)
    zero_rows = jnp.zeros_like(scaled)
    scaled_wide = jnp.concatenate(
        [
            jnp.where((row_slot == slot_num)[:, None], scaled, zero_rows)
            for slot_num in range(slot_total)
        ],
        axis=1,
    )
    parts = lax.dot_general(
        scaled_wide, recv_dy, (((0,), (0,)), ((), ())), preferred_element_type=jnp.float32
    ).astype(jnp.bfloat16)
    home_part = parts[: local_count * hidden_width].reshape(local_count, hidden_width, d_model)
    copy_part = parts[local_count * hidden_width :]
    back_h, back_p = (
        lax.all_to_all(grad_h_buf, "expert", split_axis=0, concat_axis=0, tiled=True),
        lax.all_to_all(grad_p_buf, "expert", split_axis=0, concat_axis=0, tiled=True),
    )
    flat_h = jnp.concatenate([back_h, jnp.zeros((1, hidden_width), back_h.dtype)], axis=0)
    flat_p = jnp.concatenate([back_p, jnp.zeros((1,), back_p.dtype)], axis=0)
    hidden_gradient = flat_h[target].reshape(tok_rows, top_count, hidden_width)
    grad_probs = flat_p[target].reshape(tok_rows, top_count)
    expert_total = dev_count * local_count
    cover = replica_of[None, :] == jnp.arange(expert_total, dtype=jnp.int32)[:, None]
    half_width = d_model // data_count
    halves = lax.all_to_all(copy_part, "dp", split_axis=1, concat_axis=0, tiled=True)
    copy_half = jnp.sum(
        halves.reshape(data_count, hidden_width, half_width).astype(jnp.float32), axis=0
    )
    piece_len = hidden_width * half_width // dev_count
    slabs = copy_half.reshape(dev_count, piece_len)
    arrived = lax.all_to_all(slabs, "expert", split_axis=0, concat_axis=0, tiled=True)
    sums = jnp.dot(cover.astype(jnp.float32), arrived, precision=lax.Precision.HIGHEST)
    homed = lax.all_to_all(
        sums.reshape(dev_count, local_count * piece_len),
        "expert",
        split_axis=0,
        concat_axis=0,
        tiled=True,
    )
    homed = (
        homed.reshape(dev_count, local_count, piece_len)
        .transpose(1, 0, 2)
        .reshape(local_count, hidden_width, half_width)
    )
    home_half = lax.psum_scatter(
        home_part.astype(jnp.float32).astype(jnp.bfloat16), "dp", scatter_dimension=2, tiled=True
    ).astype(jnp.float32)
    grad_weights = (home_half + homed).astype(jnp.bfloat16)
    return (hidden_gradient, grad_probs, grad_weights)


SLOT = 4
HOME, COPIES = "home", "copies"
F32 = jnp.float32
BF16 = jnp.bfloat16
NT = (((1,), (1,)), ((), ()))
TN = (((0,), (0,)), ((), ()))


def iota(shape, dim):
    return lax.broadcasted_iota(jnp.int32, shape, dim)


def dispatch_kernel(local_count, dev_count, packing, *refs):
    sources, refs = refs[:6], refs[6:]
    pick_ref, expert_ref, hs_ref, ps_ref = refs[:4]
    packed, (held, wide, sems) = refs[4:4 + len(packing)], (refs[-8:-2], refs[-2], refs[-1])
    moves = [pltpu.make_async_copy(s, h, sems.at[n]) for n, (s, h) in enumerate(zip(sources, held))]
    for move in moves:
        move.start()
    replica_ref, counts_ref, ids_ref, probs_ref, hid_ref, cot_ref = held
    top, toks = ids_ref.shape
    per_home = local_count * SLOT
    homes = dev_count * per_home
    slots = homes + dev_count * CAPR
    me = lax.axis_index("expert")
    for move in moves[:3]:
        move.wait()
    row = iota((slots, toks), 0)
    expert = ((row // per_home) ^ me) * local_count + (row % per_home) // SLOT
    within = row % SLOT
    allowed = jnp.where(within < CAPH, 1, 0)
    for d in range(dev_count):
        first = homes + d * CAPR
        mine = (row >= first) & (row < first + CAPR)
        expert = jnp.where(mine, replica_ref[d], expert)
        within = jnp.where(mine, row - first, within)
        allowed = jnp.where(mine, jnp.where(row - first < counts_ref[0, d], 1, 0), allowed)
    lower = jnp.zeros((slots, toks), jnp.int32)
    for d in range(dev_count):
        earlier = (row < homes) | (row >= homes + (d + 1) * CAPR)
        lower = lower + jnp.where(earlier & (expert == replica_ref[d]), counts_ref[0, d], 0)
    ids = ids_ref[...]
    named = jnp.zeros((slots, toks), F32)
    for k in range(top):
        named = named + jnp.where(ids[k:k + 1, :] == expert, 1.0, 0.0)
    before = jnp.where(iota((toks, toks), 0) < iota((toks, toks), 1), 1.0, 0.0).astype(BF16)
    rank = jnp.dot(named.astype(BF16), before, preferred_element_type=F32)
    wanted = (lower + within).astype(F32)
    pick = jnp.where((rank == wanted) & (allowed > 0), named, 0.0)
    pick_ref[...] = pick
    expert_ref[...] = expert
    for move in moves[3:5]:
        move.wait()
    wide[...] = hid_ref[...].astype(F32)
    h_slot = jnp.zeros((slots, hid_ref.shape[1]), F32)
    p_slot = jnp.zeros((slots, toks), F32)
    probs = probs_ref[...].astype(F32)
    for k in range(top):
        sel = jnp.where(ids[k:k + 1, :] == expert, pick, 0.0)
        h_k = wide[pl.ds(k, toks, stride=top), :].astype(BF16)
        h_slot = h_slot + jnp.dot(sel.astype(BF16), h_k, preferred_element_type=F32)
        p_slot = p_slot + sel * probs[k:k + 1, :]
    p_slot = jnp.sum(p_slot, axis=1, keepdims=True)
    hs_ref[...] = h_slot
    ps_ref[...] = jnp.broadcast_to(p_slot, ps_ref.shape)
    scaled = p_slot * h_slot
    moves[5].wait()
    pack_rows(homes, per_home, packing, pick, scaled, cot_ref, packed)


def pack_rows(homes, per_home, packing, pick, scaled, cot_ref, packed):
    d_model = cot_ref.shape[1]
    for out_ref, blocks in zip(packed, packing):
        spans = [(homes, pick.shape[0]) if b == COPIES else (b * per_home, (b + 1) * per_home) for b in blocks]
        chosen, extra = (jnp.concatenate([v[i:j] for i, j in spans], axis=0) for v in (pick, scaled))
        rows = jnp.dot(chosen.astype(BF16), cot_ref[...], preferred_element_type=F32)
        out_ref[:, :d_model] = rows.astype(BF16)
        out_ref[:, d_model:] = extra.astype(BF16)


def pack_kernel(local_count, dev_count, packing, pick_ref, hs_ref, ps_ref, cot_ref, *packed):
    d_model = cot_ref.shape[1]
    per_home = local_count * SLOT
    homes = dev_count * per_home
    pick, scaled = pick_ref[...], ps_ref[...] * hs_ref[...]
    rows = jnp.dot(pick.astype(BF16), cot_ref[...], preferred_element_type=F32)
    for out_ref, blocks in zip(packed, packing):
        spans = [(homes, pick.shape[0]) if b == COPIES else (b * per_home, (b + 1) * per_home) for b in blocks]
        out_ref[:, :d_model] = jnp.concatenate([rows[i:j] for i, j in spans], axis=0).astype(BF16)
        out_ref[:, d_model:] = jnp.concatenate([scaled[i:j] for i, j in spans], axis=0).astype(BF16)


def padded(rows):
    return -(-rows // 16) * 16


def stack(order, blocks, height):
    values = [blocks[key] for key in order]
    missing = height - sum(v.shape[0] for v in values)
    if missing:
        values.append(jnp.zeros((missing, values[0].shape[1]), values[0].dtype))
    return jnp.concatenate(values, axis=0)


def slots_of(order, slot_ref, per_home, height):
    kinds = {HOME: slot_ref[:per_home], COPIES: slot_ref[per_home:]}
    return stack(order, {key: kinds[key[1]] for key in order}, height)


def fill_rows(order, pieces, per_home, per_copy, piece_refs, rows_ref):
    values = [r[...].astype(F32) for r in piece_refs]
    blocks = {}
    for key in order:
        n, start = pieces[key]
        blocks[key] = values[n][start:start + (per_home if key[1] == HOME else per_copy)]
    rows_ref[...] = stack(order, blocks, rows_ref.shape[0]).astype(BF16)


def own_columns(rows_ref, w_ref, slot, local_count):
    d_model = w_ref.shape[1]
    width = w_ref.shape[0] // local_count
    every = lax.dot_general(rows_ref[:, :d_model], w_ref[...], NT, preferred_element_type=F32)
    own = jnp.zeros((rows_ref.shape[0], width), F32)
    for e in range(local_count):
        own = jnp.where(slot == e, every[:, e * width:(e + 1) * width], own)
    return own


def hold_kernel(local_count, dev_count, replica_ref, w_hbm, home_ref, copy_ref, rows_ref, w_ref, slot_ref, sem):
    fetch = pltpu.make_async_copy(w_hbm, w_ref, sem)
    fetch.start()
    per_home, per_copy = local_count * SLOT, dev_count * CAPR
    rows_ref[...] = jnp.concatenate([home_ref[...].astype(F32), copy_ref[...].astype(F32)], axis=0).astype(BF16)
    first = lax.axis_index("expert") * local_count
    width = slot_ref.shape[1]
    slot_ref[:per_home] = iota((per_home, width), 0) // SLOT
    row = iota((per_copy, width), 0)
    copy = jnp.full((per_copy, width), -1, jnp.int32)
    for d in range(dev_count):
        mine = (row >= d * CAPR) & (row < (d + 1) * CAPR)
        copy = jnp.where(mine, replica_ref[d] - first, copy)
    slot_ref[per_home:] = copy
    fetch.wait()


def early_kernel(local_count, dev_count, order, pieces, w_ref, slot_ref, *refs):
    piece_refs, (rows_ref, own_ref) = refs[:-2], refs[-2:]
    per_home, per_copy = local_count * SLOT, dev_count * CAPR
    fill_rows(order, pieces, per_home, per_copy, piece_refs, rows_ref)
    slot = slots_of(order, slot_ref, per_home, rows_ref.shape[0])
    own_ref[...] = own_columns(rows_ref, w_ref, slot, local_count)


def late_kernel(local_count, dev_count, early, order, pieces, own_ref, w_ref, slot_ref, *refs):
    piece_refs, (rows_ref, back_ref, passed) = refs[:-3], refs[-3:]
    per_home, per_copy = local_count * SLOT, dev_count * CAPR
    fill_rows(order, pieces, per_home, per_copy, piece_refs, rows_ref)
    own = own_columns(rows_ref, w_ref, slots_of(order, slot_ref, per_home, rows_ref.shape[0]), local_count)
    for keys, value in ((early, own_ref[...]), (order, own)):
        start = 0
        for m, kind in keys:
            lower, size = (0, per_home) if kind == HOME else (per_home, per_copy)
            passed[m, lower:lower + size] = value[start:start + size]
            start += size
    me = lax.axis_index("expert")
    back = jnp.concatenate([passed[me ^ source] for source in range(dev_count)], axis=0)
    back_ref[...] = back.astype(back_ref.dtype)


def grad_weights_half(local_count, dev_count, orders, half, slot_ref, rows_refs, columns):
    start = pl.multiple_of(half * columns, 128)
    total = None
    for order, ref in zip(orders, rows_refs):
        slot = slots_of(order, slot_ref, local_count * SLOT, ref.shape[0])
        scaled = ref[:, 2 * columns:].astype(F32)
        spread = jnp.concatenate([jnp.where(slot == e, scaled, 0.0) for e in range(local_count)], axis=1)
        part = lax.dot_general(spread.astype(BF16), ref[:, pl.ds(start, columns)], TN, preferred_element_type=F32)
        total = part if total is None else total + part
    return total


def other_half_kernel(local_count, dev_count, orders, slot_ref, early_ref, late_ref, out_ref):
    half = 1 - lax.axis_index("dp")
    out_ref[...] = grad_weights_half(
        local_count, dev_count, orders, half, slot_ref, (early_ref, late_ref), out_ref.shape[1]).astype(out_ref.dtype)


def own_half_kernel(local_count, dev_count, orders, slot_ref, early_ref, late_ref, arrived_ref, out_ref):
    half = lax.axis_index("dp")
    total = grad_weights_half(
        local_count, dev_count, orders, half, slot_ref, (early_ref, late_ref), out_ref.shape[1])
    out_ref[...] = (total + arrived_ref[...].astype(F32)).astype(out_ref.dtype)


def combine_kernel(local_count, dev_count, back_ref, pick_ref, expert_ref, hs_ref, ps_ref, ids_ref,
                   grad_h_ref, grad_p_ref, wide, narrow):
    top, toks = ids_ref.shape
    per_home = local_count * SLOT
    me = lax.axis_index("expert")
    back = [back_ref[me ^ m].astype(F32) for m in range(dev_count)]
    copy = functools.reduce(jnp.add, [b[per_home:] for b in back])
    grad_in = jnp.concatenate([b[:per_home] for b in back] + [copy], axis=0)
    h_rows = (ps_ref[...] * grad_in).astype(BF16)
    p_rows = jnp.sum(hs_ref[...] * grad_in, axis=1, keepdims=True)
    ids = ids_ref[...]
    pick = pick_ref[...]
    expert = expert_ref[...]
    for k in range(top):
        sel = jnp.where(ids[k:k + 1, :] == expert, pick, 0.0)
        wide[pl.ds(k, toks, stride=top), :] = lax.dot_general(
            sel.astype(BF16), h_rows, TN, preferred_element_type=F32)
        narrow[k:k + 1, :] = jnp.sum(sel * p_rows, axis=0, keepdims=True)
    grad_h_ref[...] = wide[...].astype(grad_h_ref.dtype)
    grad_p_ref[...] = narrow[...].astype(grad_p_ref.dtype)


def call(kernel, out_shape, operands, scratch=(), flops=0, limit=24):
    shapes = jax.tree.leaves(out_shape)
    moved = sum(a.size * a.dtype.itemsize for a in (*(a for _, a in operands), *shapes))
    return pl.pallas_call(
        kernel,
        out_shape=out_shape,
        in_specs=[pl.BlockSpec(memory_space=space) for space, _ in operands],
        out_specs=jax.tree.map(lambda _: pl.BlockSpec(memory_space=pltpu.VMEM), out_shape),
        scratch_shapes=list(scratch),
        compiler_params=pltpu.CompilerParams(vmem_limit_bytes=limit << 20),
        cost_estimate=pl.CostEstimate(flops=flops, bytes_accessed=moved, transcendentals=0),
    )(*(a for _, a in operands))


def swap(x, bits, count):
    return lax.ppermute(x, "expert", [(i, i ^ bits) for i in range(count)])


def gather_body(cotangent, hidden, probs, expert_ids, send_counts, replica_of, weights):
    toks, d_model = cotangent.shape
    top = expert_ids.shape[1]
    width = hidden.shape[2]
    local_count = weights.shape[0]
    dev_count = lax.axis_size("expert")
    homes = dev_count * local_count * SLOT
    copies = dev_count * CAPR
    slots = homes + copies
    rows = homes + dev_count * copies
    columns = d_model // 2
    sizes = (local_count, dev_count)
    ids = expert_ids.T
    shape = jax.ShapeDtypeStruct
    hbm, vmem, smem = pltpu.HBM, pltpu.VMEM, pltpu.SMEM
    sources = (replica_of, send_counts, ids, probs.T, hidden.reshape(toks * top, width), cotangent)
    per_home = local_count * SLOT
    firsts = [1 << n for n in reversed(range(dev_count.bit_length() - 1))]
    packing = [[COPIES, low | 1] for low in firsts]
    direct = [m for m in reversed(range(1, dev_count)) if m not in [low | 1 for low in firsts]]
    packing += [[0], [COPIES]] + [[m] for m in direct]
    sized = [sum(copies if b == COPIES else per_home for b in blocks) for blocks in packing]
    pick, expert, h_slot, p_slot, *packed = call(
        functools.partial(dispatch_kernel, *sizes, packing[:1]),
        [shape((slots, toks), F32), shape((slots, toks), jnp.int32), shape((slots, width), F32),
         shape((slots, width), F32)] + [shape((n, d_model + width), BF16) for n in sized[:1]],
        [(hbm, a) for a in sources],
        [(smem if n < 2 else vmem)(a.shape, a.dtype) for n, a in enumerate(sources)]
        + [vmem((toks * top, width), F32), pltpu.SemaphoreType.DMA((len(sources),))],
        flops=2 * slots * toks * d_model,
        limit=60,
    )
    packed += call(
        functools.partial(pack_kernel, *sizes, packing[1:]),
        [shape((n, d_model + width), BF16) for n in sized[1:]],
        [(vmem, a) for a in (pick, h_slot, p_slot, cotangent)],
        flops=2 * slots * toks * d_model,
        limit=60,
    )
    flat_w = weights.reshape(local_count * width, d_model)
    own_rows, w_held, slot = call(
        functools.partial(hold_kernel, *sizes),
        (shape((per_home + copies, d_model + width), BF16), shape(flat_w.shape, BF16),
         shape((per_home + copies, width), jnp.int32)),
        [(smem, replica_of), (hbm, flat_w)] + [(vmem, a) for a in packed[len(firsts):len(firsts) + 2]],
        [pltpu.SemaphoreType.DMA(())],
    )
    direct = dict(zip(direct, packed[len(firsts) + 2:]))
    first_in = {low: swap(a, low, dev_count) for a, low in zip(packed, firsts)}
    passing = {low: swap(a, 1, dev_count) for low, a in first_in.items() if 1 < low < firsts[0]}
    first_in, direct, own_rows, w_held, slot = lax.optimization_barrier((first_in, direct, own_rows, w_held, slot))
    far = first_in[firsts[0]]
    low_three = [low for low in firsts[1:] if low > 1]
    onward = {firsts[0] | low: swap(far[:copies], low, dev_count) for low in low_three}
    if firsts[0] > 1:
        passing[firsts[0]] = swap(far, 1, dev_count)
    direct_in = {m: swap(direct[m], m, dev_count) for m in direct if m > firsts[0]}
    pieces = {(0, HOME): (0, 0), (0, COPIES): (0, per_home), (1, COPIES): (len(firsts), 0), (1, HOME): (len(firsts), copies)}
    pieces.update({(low, COPIES): (1 + n, 0) for n, low in enumerate(firsts)})
    orders = [list(pieces)]
    height = padded(sum(per_home if kind == HOME else copies for _, kind in pieces))
    early_rows, own = call(
        functools.partial(early_kernel, *sizes, orders[0], pieces),
        (shape((height, d_model + width), BF16), shape((height, width), F32)),
        [(vmem, a) for a in (w_held, slot, own_rows, *(first_in[low] for low in firsts))],
        flops=2 * height * d_model * local_count * width,
    )
    passing[firsts[0]], direct_in, direct, early_rows, own = lax.optimization_barrier(
        (passing[firsts[0]], direct_in, direct, early_rows, own))
    last = {m | 1: swap(passing[firsts[0]][:copies], m ^ firsts[0], dev_count) for m in onward}
    direct_in.update({m: swap(direct[m], m, dev_count) for m in direct if m < firsts[0] or m == firsts[0]})
    pieces, arrays = {}, []
    for blocks in (passing, onward, last, direct_in):
        for m, a in blocks.items():
            if blocks is direct_in:
                pieces[m, HOME] = (len(arrays), 0)
            elif blocks is passing:
                pieces[m | 1, COPIES], pieces[m | 1, HOME] = (len(arrays), 0), (len(arrays), copies)
            else:
                pieces[m, COPIES] = (len(arrays), 0)
            arrays.append(a)
    orders.append(list(pieces))
    height = padded(sum(per_home if kind == HOME else copies for _, kind in pieces))
    late_rows, back = call(
        functools.partial(late_kernel, *sizes, *orders, pieces),
        (shape((height, d_model + width), BF16), shape((dev_count * (per_home + copies), width), BF16)),
        [(vmem, a) for a in (own, w_held, slot, *arrays)],
        [vmem((dev_count, per_home + copies, width), F32)],
        flops=2 * height * d_model * local_count * width,
    )
    back = lax.all_to_all(back, "expert", split_axis=0, concat_axis=0, tiled=True)
    half_flops = 2 * rows * columns * local_count * width
    halves = (slot, early_rows, late_rows)
    other = call(
        functools.partial(other_half_kernel, *sizes, orders),
        shape((local_count * width, columns), BF16),
        [(vmem, a) for a in halves],
        flops=half_flops,
    )
    arrived = lax.ppermute(other, "dp", [(0, 1), (1, 0)])
    grad_w = call(
        functools.partial(own_half_kernel, *sizes, orders),
        shape((local_count * width, columns), BF16),
        [(vmem, a) for a in (*halves, arrived)],
        flops=half_flops,
    )
    grad_w, pick = lax.optimization_barrier((grad_w, pick))
    grad_h, grad_p = call(
        functools.partial(combine_kernel, *sizes),
        (shape((toks * top, width), BF16), shape((top, toks), BF16)),
        [(vmem, a) for a in (back.reshape(dev_count, per_home + copies, width), pick, expert, h_slot, p_slot, ids)],
        [vmem((toks * top, width), F32), vmem((top, toks), F32)],
        flops=2 * slots * toks * width * top,
    )
    return (
        grad_h.reshape(toks, top, width),
        grad_p.T,
        grad_w.reshape(local_count, width, columns),
    )


def body(cotangent, hidden, probs, expert_ids, send_counts, replica_of, weights):
    dev_count = lax.axis_size("expert")
    local_count, width, _ = weights.shape
    gathered = dev_count * dev_count * CAPR
    if gathered <= (local_count + 3) * width and dev_count == 8 and lax.axis_size("dp") == 2:
        run = gather_body
    else:
        run = replica_body
    return run(cotangent, hidden, probs, expert_ids, send_counts, replica_of, weights)


def solution(mesh):
    in_specs = (
        P(("groups", "expert", "dp"), None),
        P(("groups", "expert", "dp"), None, None),
        P(("groups", "expert", "dp"), None),
        P(("groups", "expert", "dp"), None),
        P(("groups", "expert", "dp"), None),
        P("groups"),
        P("expert", None, None),
    )
    out_specs = (
        P(("groups", "expert", "dp"), None, None),
        P(("groups", "expert", "dp"), None),
        P(("groups", "expert"), None, "dp"),
    )
    return jax.shard_map(body, mesh=mesh, in_specs=in_specs, out_specs=out_specs, check_vma=False)
```

```python
import functools

import jax
import jax.numpy as jnp
from jax import lax
from jax.experimental import pallas as pl
from jax.experimental.pallas import tpu as pltpu
from jax.sharding import PartitionSpec as P

CAPH = 3
CAPR = 3


def ranks_within(keys):
    total_rows = keys.shape[0]
    sort_order = jnp.argsort(keys * total_rows + jnp.arange(total_rows, dtype=jnp.int32))
    sorted_keys = keys[sort_order]
    first_seen = jnp.searchsorted(sorted_keys, sorted_keys, side="left")
    ranked = jnp.arange(total_rows, dtype=jnp.int32) - first_seen
    return jnp.zeros((total_rows,), jnp.int32).at[sort_order].set(ranked)


def route_rows(ids_block, counts_row, replica_of, local_count, cap_home, cap_copy):
    dev_count = replica_of.shape[0]
    experts = ids_block.reshape(-1)
    rank_expert = ranks_within(experts)
    devices = jnp.arange(dev_count, dtype=jnp.int32)
    same_copy = (replica_of[:, None] == replica_of[None, :]) & (devices[None, :] < devices[:, None])
    lower_rank = jnp.sum(jnp.where(same_copy, counts_row[None, :], 0), axis=1)
    upper_rank = lower_rank + counts_row
    hit_table = (
        (replica_of[None, :] == experts[:, None])
        & (lower_rank[None, :] <= rank_expert[:, None])
        & (rank_expert[:, None] < upper_rank[None, :])
    )
    copied = jnp.any(hit_table, axis=1)
    copy_dev = jnp.sum(jnp.where(hit_table, devices[None, :], 0), axis=1)
    dest_dev = jnp.where(copied, copy_dev, experts // local_count)
    index_of_slot = jnp.where(copied, local_count, experts % local_count)
    rank_bucket = ranks_within(dest_dev * (local_count + 1) + index_of_slot)
    keep_row = rank_bucket < jnp.where(copied, cap_copy, cap_home)
    per_dev = local_count * cap_home + cap_copy
    target = dest_dev * per_dev + index_of_slot * cap_home + rank_bucket
    return jnp.where(keep_row, target, dev_count * per_dev)


def replica_body(cotangent, hidden, probs, expert_ids, send_counts, replica_of, weights):
    tok_rows, d_model = cotangent.shape
    top_count = expert_ids.shape[1]
    hidden_width = hidden.shape[2]
    local_count = weights.shape[0]
    dev_count = lax.axis_size("expert")
    data_count = lax.axis_size("dp")
    per_dev = local_count * CAPH + CAPR
    row_count = tok_rows * top_count
    recv_count = dev_count * per_dev
    target = route_rows(expert_ids, send_counts[0], replica_of, local_count, CAPH, CAPR)
    inverse = (
        jnp.full((recv_count,), row_count, jnp.int32)
        .at[target]
        .set(jnp.arange(row_count, dtype=jnp.int32), mode="drop")
    )
    dy_pad = jnp.concatenate([cotangent, jnp.zeros((1, d_model), cotangent.dtype)], axis=0)
    h_pad = jnp.concatenate(
        [hidden.reshape(row_count, hidden_width), jnp.zeros((1, hidden_width), hidden.dtype)],
        axis=0,
    )
    p_pad = jnp.concatenate([probs.reshape(row_count), jnp.zeros((1,), probs.dtype)], axis=0)
    send_dy = dy_pad[inverse // top_count]
    send_h = h_pad[inverse]
    send_p = p_pad[inverse]
    recv_dy, recv_h, recv_p = (
        lax.all_to_all(send_dy, "expert", split_axis=0, concat_axis=0, tiled=True),
        lax.all_to_all(send_h, "expert", split_axis=0, concat_axis=0, tiled=True),
        lax.all_to_all(send_p, "expert", split_axis=0, concat_axis=0, tiled=True),
    )
    flat_size = hidden_width * d_model
    flat_w = weights.reshape(local_count, flat_size)
    pieces = lax.all_to_all(flat_w, "expert", split_axis=1, concat_axis=0, tiled=True)
    chosen = pieces[replica_of]
    copy_weight = lax.all_to_all(chosen, "expert", split_axis=0, concat_axis=0, tiled=True).reshape(
        hidden_width, d_model
    )
    slot_total = local_count + 1
    home_rows = local_count * CAPH
    row_pos = jnp.arange(recv_count, dtype=jnp.int32) % per_dev
    row_slot = jnp.where(row_pos < home_rows, row_pos // CAPH, local_count)
    all_weights = jnp.concatenate(
        [weights.reshape(local_count * hidden_width, d_model), copy_weight], axis=0
    )
    all_in = lax.dot_general(
        recv_dy, all_weights, (((1,), (1,)), ((), ())), preferred_element_type=jnp.float32
    )
    grad_in = jnp.zeros((recv_count, hidden_width), jnp.float32)
    for slot_num in range(slot_total):
        grad_in = grad_in + jnp.where(
            (row_slot == slot_num)[:, None],
            all_in[:, slot_num * hidden_width : (slot_num + 1) * hidden_width],
            0.0,
        )
    p_wide = recv_p.astype(jnp.float32)[:, None]
    h_wide = recv_h.astype(jnp.float32)
    grad_h_buf = (p_wide * grad_in).astype(jnp.bfloat16)
    grad_p_buf = jnp.sum(h_wide * grad_in, axis=1).astype(jnp.bfloat16)
    scaled = (p_wide * h_wide).astype(jnp.bfloat16)
    zero_rows = jnp.zeros_like(scaled)
    scaled_wide = jnp.concatenate(
        [
            jnp.where((row_slot == slot_num)[:, None], scaled, zero_rows)
            for slot_num in range(slot_total)
        ],
        axis=1,
    )
    parts = lax.dot_general(
        scaled_wide, recv_dy, (((0,), (0,)), ((), ())), preferred_element_type=jnp.float32
    ).astype(jnp.bfloat16)
    home_part = parts[: local_count * hidden_width].reshape(local_count, hidden_width, d_model)
    copy_part = parts[local_count * hidden_width :]
    back_h, back_p = (
        lax.all_to_all(grad_h_buf, "expert", split_axis=0, concat_axis=0, tiled=True),
        lax.all_to_all(grad_p_buf, "expert", split_axis=0, concat_axis=0, tiled=True),
    )
    flat_h = jnp.concatenate([back_h, jnp.zeros((1, hidden_width), back_h.dtype)], axis=0)
    flat_p = jnp.concatenate([back_p, jnp.zeros((1,), back_p.dtype)], axis=0)
    hidden_gradient = flat_h[target].reshape(tok_rows, top_count, hidden_width)
    grad_probs = flat_p[target].reshape(tok_rows, top_count)
    expert_total = dev_count * local_count
    cover = replica_of[None, :] == jnp.arange(expert_total, dtype=jnp.int32)[:, None]
    half_width = d_model // data_count
    halves = lax.all_to_all(copy_part, "dp", split_axis=1, concat_axis=0, tiled=True)
    copy_half = jnp.sum(
        halves.reshape(data_count, hidden_width, half_width).astype(jnp.float32), axis=0
    )
    piece_len = hidden_width * half_width // dev_count
    slabs = copy_half.reshape(dev_count, piece_len)
    arrived = lax.all_to_all(slabs, "expert", split_axis=0, concat_axis=0, tiled=True)
    sums = jnp.dot(cover.astype(jnp.float32), arrived, precision=lax.Precision.HIGHEST)
    homed = lax.all_to_all(
        sums.reshape(dev_count, local_count * piece_len),
        "expert",
        split_axis=0,
        concat_axis=0,
        tiled=True,
    )
    homed = (
        homed.reshape(dev_count, local_count, piece_len)
        .transpose(1, 0, 2)
        .reshape(local_count, hidden_width, half_width)
    )
    home_half = lax.psum_scatter(
        home_part.astype(jnp.float32).astype(jnp.bfloat16), "dp", scatter_dimension=2, tiled=True
    ).astype(jnp.float32)
    grad_weights = (home_half + homed).astype(jnp.bfloat16)
    return (hidden_gradient, grad_probs, grad_weights)


SLOT = 4
HOME, COPIES = "home", "copies"
F32 = jnp.float32
BF16 = jnp.bfloat16
NT = (((1,), (1,)), ((), ()))
TN = (((0,), (0,)), ((), ()))


def iota(shape, dim):
    return lax.broadcasted_iota(jnp.int32, shape, dim)


def dispatch_kernel(local_count, dev_count, packing, *refs):
    sources, refs = refs[:6], refs[6:]
    pick_ref, expert_ref, hs_ref, ps_ref = refs[:4]
    packed, (held, wide, sems) = refs[4:4 + len(packing)], (refs[-8:-2], refs[-2], refs[-1])
    moves = [pltpu.make_async_copy(s, h, sems.at[n]) for n, (s, h) in enumerate(zip(sources, held))]
    for move in moves:
        move.start()
    replica_ref, counts_ref, ids_ref, probs_ref, hid_ref, cot_ref = held
    top, toks = ids_ref.shape
    per_home = local_count * SLOT
    homes = dev_count * per_home
    slots = homes + dev_count * CAPR
    me = lax.axis_index("expert")
    for move in moves[:3]:
        move.wait()
    row = iota((slots, toks), 0)
    expert = ((row // per_home) ^ me) * local_count + (row % per_home) // SLOT
    within = row % SLOT
    allowed = jnp.where(within < CAPH, 1, 0)
    for d in range(dev_count):
        first = homes + d * CAPR
        mine = (row >= first) & (row < first + CAPR)
        expert = jnp.where(mine, replica_ref[d], expert)
        within = jnp.where(mine, row - first, within)
        allowed = jnp.where(mine, jnp.where(row - first < counts_ref[0, d], 1, 0), allowed)
    lower = jnp.zeros((slots, toks), jnp.int32)
    for d in range(dev_count):
        earlier = (row < homes) | (row >= homes + (d + 1) * CAPR)
        lower = lower + jnp.where(earlier & (expert == replica_ref[d]), counts_ref[0, d], 0)
    ids = ids_ref[...]
    named = jnp.zeros((slots, toks), F32)
    for k in range(top):
        named = named + jnp.where(ids[k:k + 1, :] == expert, 1.0, 0.0)
    before = jnp.where(iota((toks, toks), 0) < iota((toks, toks), 1), 1.0, 0.0).astype(BF16)
    rank = jnp.dot(named.astype(BF16), before, preferred_element_type=F32)
    wanted = (lower + within).astype(F32)
    pick = jnp.where((rank == wanted) & (allowed > 0), named, 0.0)
    pick_ref[...] = pick
    expert_ref[...] = expert
    for move in moves[3:5]:
        move.wait()
    wide[...] = hid_ref[...].astype(F32)
    h_slot = jnp.zeros((slots, hid_ref.shape[1]), F32)
    p_slot = jnp.zeros((slots, toks), F32)
    probs = probs_ref[...].astype(F32)
    for k in range(top):
        sel = jnp.where(ids[k:k + 1, :] == expert, pick, 0.0)
        h_k = wide[pl.ds(k, toks, stride=top), :].astype(BF16)
        h_slot = h_slot + jnp.dot(sel.astype(BF16), h_k, preferred_element_type=F32)
        p_slot = p_slot + sel * probs[k:k + 1, :]
    p_slot = jnp.sum(p_slot, axis=1, keepdims=True)
    hs_ref[...] = h_slot
    ps_ref[...] = jnp.broadcast_to(p_slot, ps_ref.shape)
    scaled = p_slot * h_slot
    moves[5].wait()
    rows = jnp.dot(pick.astype(BF16), cot_ref[...], preferred_element_type=F32)
    d_model = cot_ref.shape[1]
    for out_ref, blocks in zip(packed, packing):
        spans = [(homes, slots) if b == COPIES else (b * per_home, (b + 1) * per_home) for b in blocks]
        out_ref[:, :d_model] = jnp.concatenate([rows[i:j] for i, j in spans], axis=0).astype(BF16)
        out_ref[:, d_model:] = jnp.concatenate([scaled[i:j] for i, j in spans], axis=0).astype(BF16)


def padded(rows):
    return -(-rows // 16) * 16


def stack(order, blocks, height):
    values = [blocks[key] for key in order]
    missing = height - sum(v.shape[0] for v in values)
    if missing:
        values.append(jnp.zeros((missing, values[0].shape[1]), values[0].dtype))
    return jnp.concatenate(values, axis=0)


def slots_of(order, slot_ref, per_home, height):
    kinds = {HOME: slot_ref[:per_home], COPIES: slot_ref[per_home:]}
    return stack(order, {key: kinds[key[1]] for key in order}, height)


def fill_rows(order, pieces, per_home, per_copy, piece_refs, rows_ref):
    values = [r[...].astype(F32) for r in piece_refs]
    blocks = {}
    for key in order:
        n, start = pieces[key]
        blocks[key] = values[n][start:start + (per_home if key[1] == HOME else per_copy)]
    rows_ref[...] = stack(order, blocks, rows_ref.shape[0]).astype(BF16)


def own_columns(rows_ref, w_ref, slot, local_count):
    d_model = w_ref.shape[1]
    width = w_ref.shape[0] // local_count
    every = lax.dot_general(rows_ref[:, :d_model], w_ref[...], NT, preferred_element_type=F32)
    own = jnp.zeros((rows_ref.shape[0], width), F32)
    for e in range(local_count):
        own = jnp.where(slot == e, every[:, e * width:(e + 1) * width], own)
    return own


def hold_kernel(local_count, dev_count, replica_ref, w_hbm, own_hbm, even_hbm,
                own_ref, even_ref, w_ref, slot_ref, sems):
    moves = [pltpu.make_async_copy(a, b, sems.at[n]) for n, (a, b) in enumerate(
        ((w_hbm, w_ref), (own_hbm, own_ref), (even_hbm, even_ref)))]
    for move in moves:
        move.start()
    per_home, per_copy = local_count * SLOT, dev_count * CAPR
    first = lax.axis_index("expert") * local_count
    width = slot_ref.shape[1]
    slot_ref[:per_home] = iota((per_home, width), 0) // SLOT
    row = iota((per_copy, width), 0)
    copy = jnp.full((per_copy, width), -1, jnp.int32)
    for d in range(dev_count):
        mine = (row >= d * CAPR) & (row < (d + 1) * CAPR)
        copy = jnp.where(mine, replica_ref[d] - first, copy)
    slot_ref[per_home:] = copy
    for move in moves:
        move.wait()


def turn_kernel(local_count, dev_count, beside_ref, far_ref, even_ref, *out_refs):
    per_home, per_copy = local_count * SLOT, dev_count * CAPR
    beside = beside_ref[per_copy + per_home:].astype(F32)
    even = even_ref[...].astype(F32)
    for n, out_ref in enumerate(out_refs):
        span = slice(n * per_home, (n + 1) * per_home)
        blocks = [far_ref[...].astype(F32)] * (n == 0) + [even[span], beside[span]]
        out_ref[...] = jnp.concatenate(blocks, axis=0).astype(BF16)


def early_kernel(local_count, dev_count, order, pieces, w_ref, slot_ref, *refs):
    piece_refs, (rows_ref, own_ref) = refs[:-2], refs[-2:]
    per_home, per_copy = local_count * SLOT, dev_count * CAPR
    fill_rows(order, pieces, per_home, per_copy, piece_refs, rows_ref)
    slot = slots_of(order, slot_ref, per_home, rows_ref.shape[0])
    own_ref[...] = own_columns(rows_ref, w_ref, slot, local_count)


def late_kernel(local_count, dev_count, early, order, pieces, own_ref, w_ref, slot_ref, *refs):
    piece_refs, (rows_ref, back_ref, passed) = refs[:-3], refs[-3:]
    per_home, per_copy = local_count * SLOT, dev_count * CAPR
    fill_rows(order, pieces, per_home, per_copy, piece_refs, rows_ref)
    own = own_columns(rows_ref, w_ref, slots_of(order, slot_ref, per_home, rows_ref.shape[0]), local_count)
    for keys, value in ((early, own_ref[...]), (order, own)):
        start = 0
        for m, kind in keys:
            lower, size = (0, per_home) if kind == HOME else (per_home, per_copy)
            passed[m, lower:lower + size] = value[start:start + size]
            start += size
    me = lax.axis_index("expert")
    back = jnp.concatenate([passed[me ^ source] for source in range(dev_count)], axis=0)
    back_ref[...] = back.astype(back_ref.dtype)


def grad_weights_half(local_count, dev_count, orders, half, slot_ref, rows_refs, columns):
    start = pl.multiple_of(half * columns, 128)
    spread = []
    for order, ref in zip(orders, rows_refs):
        slot = slots_of(order, slot_ref, local_count * SLOT, ref.shape[0])
        scaled = ref[:, 2 * columns:].astype(F32)
        spread.append(jnp.concatenate([jnp.where(slot == e, scaled, 0.0) for e in range(local_count)], axis=1))
    rows = jnp.concatenate([ref[:, pl.ds(start, columns)] for ref in rows_refs], axis=0)
    return lax.dot_general(
        jnp.concatenate(spread, axis=0).astype(BF16), rows, TN, preferred_element_type=F32)


def other_half_kernel(local_count, dev_count, orders, slot_ref, early_ref, late_ref, out_ref):
    half = 1 - lax.axis_index("dp")
    out_ref[...] = grad_weights_half(
        local_count, dev_count, orders, half, slot_ref, (early_ref, late_ref), out_ref.shape[1]).astype(out_ref.dtype)


def own_half_kernel(local_count, dev_count, orders, slot_ref, early_ref, late_ref, arrived_ref, out_ref):
    half = lax.axis_index("dp")
    total = grad_weights_half(
        local_count, dev_count, orders, half, slot_ref, (early_ref, late_ref), out_ref.shape[1])
    out_ref[...] = (total + arrived_ref[...].astype(F32)).astype(out_ref.dtype)


def combine_kernel(local_count, dev_count, back_ref, pick_ref, expert_ref, hs_ref, ps_ref, ids_ref,
                   grad_h_ref, grad_p_ref, wide, narrow):
    top, toks = ids_ref.shape
    per_home = local_count * SLOT
    me = lax.axis_index("expert")
    back = [back_ref[me ^ m].astype(F32) for m in range(dev_count)]
    copy = functools.reduce(jnp.add, [b[per_home:] for b in back])
    grad_in = jnp.concatenate([b[:per_home] for b in back] + [copy], axis=0)
    h_rows = (ps_ref[...] * grad_in).astype(BF16)
    p_rows = jnp.sum(hs_ref[...] * grad_in, axis=1, keepdims=True)
    ids = ids_ref[...]
    pick = pick_ref[...]
    expert = expert_ref[...]
    for k in range(top):
        sel = jnp.where(ids[k:k + 1, :] == expert, pick, 0.0)
        wide[pl.ds(k, toks, stride=top), :] = lax.dot_general(
            sel.astype(BF16), h_rows, TN, preferred_element_type=F32)
        narrow[k:k + 1, :] = jnp.sum(sel * p_rows, axis=0, keepdims=True)
    grad_h_ref[...] = wide[...].astype(grad_h_ref.dtype)
    grad_p_ref[...] = narrow[...].astype(grad_p_ref.dtype)


def call(kernel, out_shape, operands, scratch=(), flops=0, limit=24):
    shapes = jax.tree.leaves(out_shape)
    moved = sum(a.size * a.dtype.itemsize for a in (*(a for _, a in operands), *shapes))
    return pl.pallas_call(
        kernel,
        out_shape=out_shape,
        in_specs=[pl.BlockSpec(memory_space=space) for space, _ in operands],
        out_specs=jax.tree.map(lambda _: pl.BlockSpec(memory_space=pltpu.VMEM), out_shape),
        scratch_shapes=list(scratch),
        compiler_params=pltpu.CompilerParams(vmem_limit_bytes=limit << 20),
        cost_estimate=pl.CostEstimate(flops=flops, bytes_accessed=moved, transcendentals=0),
    )(*(a for _, a in operands))


def swap(x, bits, count):
    return lax.ppermute(x, "expert", [(i, i ^ bits) for i in range(count)])


def gather_body(cotangent, hidden, probs, expert_ids, send_counts, replica_of, weights):
    toks, d_model = cotangent.shape
    top = expert_ids.shape[1]
    width = hidden.shape[2]
    local_count = weights.shape[0]
    dev_count = lax.axis_size("expert")
    homes = dev_count * local_count * SLOT
    copies = dev_count * CAPR
    slots = homes + copies
    rows = homes + dev_count * copies
    columns = d_model // 2
    sizes = (local_count, dev_count)
    ids = expert_ids.T
    shape = jax.ShapeDtypeStruct
    hbm, vmem, smem = pltpu.HBM, pltpu.VMEM, pltpu.SMEM
    sources = (replica_of, send_counts, ids, probs.T, hidden.reshape(toks * top, width), cotangent)
    per_home = local_count * SLOT
    odd, even = range(1, dev_count, 2), range(2, dev_count, 2)
    packing = [[COPIES, *odd], [COPIES], [0, COPIES], [*even]]
    sized = [sum(copies if b == COPIES else per_home for b in blocks) for blocks in packing]
    pick, expert, h_slot, p_slot, to_beside, copy_rows, own_rows, even_rows = call(
        functools.partial(dispatch_kernel, *sizes, packing),
        [shape((slots, toks), F32), shape((slots, toks), jnp.int32), shape((slots, width), F32),
         shape((slots, width), F32)] + [shape((n, d_model + width), BF16) for n in sized],
        [(hbm, a) for a in sources],
        [(smem if n < 2 else vmem)(a.shape, a.dtype) for n, a in enumerate(sources)]
        + [vmem((toks * top, width), F32), pltpu.SemaphoreType.DMA((len(sources),))],
        flops=2 * slots * toks * d_model,
        limit=60,
    )
    beside = swap(to_beside, 1, dev_count)
    far = swap(copy_rows, 4, dev_count)
    near = swap(copy_rows, 2, dev_count)
    flat_w = weights.reshape(local_count * width, d_model)
    own_rows, even_rows, w_held, slot = call(
        functools.partial(hold_kernel, *sizes),
        [shape(a.shape, BF16) for a in (own_rows, even_rows, flat_w)] + [shape((per_home + copies, width), jnp.int32)],
        [(smem, replica_of)] + [(hbm, a) for a in (flat_w, own_rows, even_rows)],
        [pltpu.SemaphoreType.DMA((3,))],
    )
    beside, far, near, own_rows, even_rows, w_held, slot = lax.optimization_barrier(
        (beside, far, near, own_rows, even_rows, w_held, slot))
    far_beside = swap(far, 1, dev_count)
    turned = call(
        functools.partial(turn_kernel, *sizes),
        [shape((copies * (m == 2) + 2 * per_home, d_model + width), BF16) for m in even],
        [(vmem, a) for a in (beside, far, even_rows)],
    )
    turned = [swap(a, m, dev_count) for a, m in zip(turned, even)]
    near_beside = swap(near, 1, dev_count)
    pieces = {(0, HOME): (0, 0), (0, COPIES): (0, per_home), (1, COPIES): (1, 0), (1, HOME): (1, copies),
              (2, COPIES): (2, 0), (4, COPIES): (3, 0)}
    orders = [list(pieces)]
    height = padded(sum(per_home if kind == HOME else copies for _, kind in pieces))
    early_rows, own = call(
        functools.partial(early_kernel, *sizes, orders[0], pieces),
        (shape((height, d_model + width), BF16), shape((height, width), F32)),
        [(vmem, a) for a in (w_held, slot, own_rows, beside, near, far)],
        flops=2 * height * d_model * local_count * width,
    )
    far_beside, early_rows, own, turned[2] = lax.optimization_barrier((far_beside, early_rows, own, turned[2]))
    far_across = swap(far_beside, 2, dev_count)
    arrays = [far_beside, near_beside, far_across, *turned]
    pieces = {(5, COPIES): (0, 0), (3, COPIES): (1, 0), (7, COPIES): (2, 0), (6, COPIES): (3, 0)}
    for n, m in enumerate(even):
        pieces[m, HOME], pieces[m + 1, HOME] = ((3 + n, copies * (m == 2) + k * per_home) for k in range(2))
    orders.append(list(pieces))
    height = padded(sum(per_home if kind == HOME else copies for _, kind in pieces))
    late_rows, back = call(
        functools.partial(late_kernel, *sizes, *orders, pieces),
        (shape((height, d_model + width), BF16), shape((dev_count * (per_home + copies), width), BF16)),
        [(vmem, a) for a in (own, w_held, slot, *arrays)],
        [vmem((dev_count, per_home + copies, width), F32)],
        flops=2 * height * d_model * local_count * width,
    )
    back = lax.all_to_all(back, "expert", split_axis=0, concat_axis=0, tiled=True)
    half_flops = 2 * rows * columns * local_count * width
    halves = (slot, early_rows, late_rows)
    other = call(
        functools.partial(other_half_kernel, *sizes, orders),
        shape((local_count * width, columns), BF16),
        [(vmem, a) for a in halves],
        flops=half_flops,
    )
    arrived = lax.ppermute(other, "dp", [(0, 1), (1, 0)])
    grad_w = call(
        functools.partial(own_half_kernel, *sizes, orders),
        shape((local_count * width, columns), BF16),
        [(vmem, a) for a in (*halves, arrived)],
        flops=half_flops,
    )
    grad_w, pick = lax.optimization_barrier((grad_w, pick))
    grad_h, grad_p = call(
        functools.partial(combine_kernel, *sizes),
        (shape((toks * top, width), BF16), shape((top, toks), BF16)),
        [(vmem, a) for a in (back.reshape(dev_count, per_home + copies, width), pick, expert, h_slot, p_slot, ids)],
        [vmem((toks * top, width), F32), vmem((top, toks), F32)],
        flops=2 * slots * toks * width * top,
    )
    return (
        grad_h.reshape(toks, top, width),
        grad_p.T,
        grad_w.reshape(local_count, width, columns),
    )


def body(cotangent, hidden, probs, expert_ids, send_counts, replica_of, weights):
    dev_count = lax.axis_size("expert")
    local_count, width, _ = weights.shape
    gathered = dev_count * dev_count * CAPR
    if gathered <= (local_count + 3) * width and dev_count == 8 and lax.axis_size("dp") == 2:
        run = gather_body
    else:
        run = replica_body
    return run(cotangent, hidden, probs, expert_ids, send_counts, replica_of, weights)


def solution(mesh):
    in_specs = (
        P(("groups", "expert", "dp"), None),
        P(("groups", "expert", "dp"), None, None),
        P(("groups", "expert", "dp"), None),
        P(("groups", "expert", "dp"), None),
        P(("groups", "expert", "dp"), None),
        P("groups"),
        P("expert", None, None),
    )
    out_specs = (
        P(("groups", "expert", "dp"), None, None),
        P(("groups", "expert", "dp"), None),
        P(("groups", "expert"), None, "dp"),
    )
    return jax.shard_map(body, mesh=mesh, in_specs=in_specs, out_specs=out_specs, check_vma=False)
```

```python
import functools

import jax
import jax.numpy as jnp
from jax import lax
from jax.experimental import pallas as pl
from jax.experimental.pallas import tpu as pltpu
from jax.sharding import PartitionSpec as P

CAPH = 3
CAPR = 3


def ranks_within(keys):
    total_rows = keys.shape[0]
    sort_order = jnp.argsort(keys * total_rows + jnp.arange(total_rows, dtype=jnp.int32))
    sorted_keys = keys[sort_order]
    first_seen = jnp.searchsorted(sorted_keys, sorted_keys, side="left")
    ranked = jnp.arange(total_rows, dtype=jnp.int32) - first_seen
    return jnp.zeros((total_rows,), jnp.int32).at[sort_order].set(ranked)


def route_rows(ids_block, counts_row, replica_of, local_count, cap_home, cap_copy):
    dev_count = replica_of.shape[0]
    experts = ids_block.reshape(-1)
    rank_expert = ranks_within(experts)
    devices = jnp.arange(dev_count, dtype=jnp.int32)
    same_copy = (replica_of[:, None] == replica_of[None, :]) & (devices[None, :] < devices[:, None])
    lower_rank = jnp.sum(jnp.where(same_copy, counts_row[None, :], 0), axis=1)
    upper_rank = lower_rank + counts_row
    hit_table = (
        (replica_of[None, :] == experts[:, None])
        & (lower_rank[None, :] <= rank_expert[:, None])
        & (rank_expert[:, None] < upper_rank[None, :])
    )
    copied = jnp.any(hit_table, axis=1)
    copy_dev = jnp.sum(jnp.where(hit_table, devices[None, :], 0), axis=1)
    dest_dev = jnp.where(copied, copy_dev, experts // local_count)
    index_of_slot = jnp.where(copied, local_count, experts % local_count)
    rank_bucket = ranks_within(dest_dev * (local_count + 1) + index_of_slot)
    keep_row = rank_bucket < jnp.where(copied, cap_copy, cap_home)
    per_dev = local_count * cap_home + cap_copy
    target = dest_dev * per_dev + index_of_slot * cap_home + rank_bucket
    return jnp.where(keep_row, target, dev_count * per_dev)


def replica_body(cotangent, hidden, probs, expert_ids, send_counts, replica_of, weights):
    tok_rows, d_model = cotangent.shape
    top_count = expert_ids.shape[1]
    hidden_width = hidden.shape[2]
    local_count = weights.shape[0]
    dev_count = lax.axis_size("expert")
    data_count = lax.axis_size("dp")
    per_dev = local_count * CAPH + CAPR
    row_count = tok_rows * top_count
    recv_count = dev_count * per_dev
    target = route_rows(expert_ids, send_counts[0], replica_of, local_count, CAPH, CAPR)
    inverse = (
        jnp.full((recv_count,), row_count, jnp.int32)
        .at[target]
        .set(jnp.arange(row_count, dtype=jnp.int32), mode="drop")
    )
    dy_pad = jnp.concatenate([cotangent, jnp.zeros((1, d_model), cotangent.dtype)], axis=0)
    h_pad = jnp.concatenate(
        [hidden.reshape(row_count, hidden_width), jnp.zeros((1, hidden_width), hidden.dtype)],
        axis=0,
    )
    p_pad = jnp.concatenate([probs.reshape(row_count), jnp.zeros((1,), probs.dtype)], axis=0)
    send_dy = dy_pad[inverse // top_count]
    send_h = h_pad[inverse]
    send_p = p_pad[inverse]
    recv_dy, recv_h, recv_p = (
        lax.all_to_all(send_dy, "expert", split_axis=0, concat_axis=0, tiled=True),
        lax.all_to_all(send_h, "expert", split_axis=0, concat_axis=0, tiled=True),
        lax.all_to_all(send_p, "expert", split_axis=0, concat_axis=0, tiled=True),
    )
    flat_size = hidden_width * d_model
    flat_w = weights.reshape(local_count, flat_size)
    pieces = lax.all_to_all(flat_w, "expert", split_axis=1, concat_axis=0, tiled=True)
    chosen = pieces[replica_of]
    copy_weight = lax.all_to_all(chosen, "expert", split_axis=0, concat_axis=0, tiled=True).reshape(
        hidden_width, d_model
    )
    slot_total = local_count + 1
    home_rows = local_count * CAPH
    row_pos = jnp.arange(recv_count, dtype=jnp.int32) % per_dev
    row_slot = jnp.where(row_pos < home_rows, row_pos // CAPH, local_count)
    all_weights = jnp.concatenate(
        [weights.reshape(local_count * hidden_width, d_model), copy_weight], axis=0
    )
    all_in = lax.dot_general(
        recv_dy, all_weights, (((1,), (1,)), ((), ())), preferred_element_type=jnp.float32
    )
    grad_in = jnp.zeros((recv_count, hidden_width), jnp.float32)
    for slot_num in range(slot_total):
        grad_in = grad_in + jnp.where(
            (row_slot == slot_num)[:, None],
            all_in[:, slot_num * hidden_width : (slot_num + 1) * hidden_width],
            0.0,
        )
    p_wide = recv_p.astype(jnp.float32)[:, None]
    h_wide = recv_h.astype(jnp.float32)
    grad_h_buf = (p_wide * grad_in).astype(jnp.bfloat16)
    grad_p_buf = jnp.sum(h_wide * grad_in, axis=1).astype(jnp.bfloat16)
    scaled = (p_wide * h_wide).astype(jnp.bfloat16)
    zero_rows = jnp.zeros_like(scaled)
    scaled_wide = jnp.concatenate(
        [
            jnp.where((row_slot == slot_num)[:, None], scaled, zero_rows)
            for slot_num in range(slot_total)
        ],
        axis=1,
    )
    parts = lax.dot_general(
        scaled_wide, recv_dy, (((0,), (0,)), ((), ())), preferred_element_type=jnp.float32
    ).astype(jnp.bfloat16)
    home_part = parts[: local_count * hidden_width].reshape(local_count, hidden_width, d_model)
    copy_part = parts[local_count * hidden_width :]
    back_h, back_p = (
        lax.all_to_all(grad_h_buf, "expert", split_axis=0, concat_axis=0, tiled=True),
        lax.all_to_all(grad_p_buf, "expert", split_axis=0, concat_axis=0, tiled=True),
    )
    flat_h = jnp.concatenate([back_h, jnp.zeros((1, hidden_width), back_h.dtype)], axis=0)
    flat_p = jnp.concatenate([back_p, jnp.zeros((1,), back_p.dtype)], axis=0)
    hidden_gradient = flat_h[target].reshape(tok_rows, top_count, hidden_width)
    grad_probs = flat_p[target].reshape(tok_rows, top_count)
    expert_total = dev_count * local_count
    cover = replica_of[None, :] == jnp.arange(expert_total, dtype=jnp.int32)[:, None]
    half_width = d_model // data_count
    halves = lax.all_to_all(copy_part, "dp", split_axis=1, concat_axis=0, tiled=True)
    copy_half = jnp.sum(
        halves.reshape(data_count, hidden_width, half_width).astype(jnp.float32), axis=0
    )
    piece_len = hidden_width * half_width // dev_count
    slabs = copy_half.reshape(dev_count, piece_len)
    arrived = lax.all_to_all(slabs, "expert", split_axis=0, concat_axis=0, tiled=True)
    sums = jnp.dot(cover.astype(jnp.float32), arrived, precision=lax.Precision.HIGHEST)
    homed = lax.all_to_all(
        sums.reshape(dev_count, local_count * piece_len),
        "expert",
        split_axis=0,
        concat_axis=0,
        tiled=True,
    )
    homed = (
        homed.reshape(dev_count, local_count, piece_len)
        .transpose(1, 0, 2)
        .reshape(local_count, hidden_width, half_width)
    )
    home_half = lax.psum_scatter(
        home_part.astype(jnp.float32).astype(jnp.bfloat16), "dp", scatter_dimension=2, tiled=True
    ).astype(jnp.float32)
    grad_weights = (home_half + homed).astype(jnp.bfloat16)
    return (hidden_gradient, grad_probs, grad_weights)


SLOT = 4
HOME, COPIES = "home", "copies"
F32 = jnp.float32
BF16 = jnp.bfloat16
NT = (((1,), (1,)), ((), ()))
TN = (((0,), (0,)), ((), ()))


def iota(shape, dim):
    return lax.broadcasted_iota(jnp.int32, shape, dim)


def dispatch_kernel(local_count, dev_count, packing, *refs):
    sources, refs = refs[:6], refs[6:]
    pick_ref, expert_ref, hs_ref, ps_ref = refs[:4]
    packed, (held, wide, sems) = refs[4:4 + len(packing)], (refs[-8:-2], refs[-2], refs[-1])
    moves = [pltpu.make_async_copy(s, h, sems.at[n]) for n, (s, h) in enumerate(zip(sources, held))]
    for move in moves:
        move.start()
    replica_ref, counts_ref, ids_ref, probs_ref, hid_ref, cot_ref = held
    top, toks = ids_ref.shape
    per_home = local_count * SLOT
    homes = dev_count * per_home
    slots = homes + dev_count * CAPR
    me = lax.axis_index("expert")
    for move in moves[:3]:
        move.wait()
    row = iota((slots, toks), 0)
    expert = ((row // per_home) ^ me) * local_count + (row % per_home) // SLOT
    within = row % SLOT
    allowed = jnp.where(within < CAPH, 1, 0)
    for d in range(dev_count):
        first = homes + d * CAPR
        mine = (row >= first) & (row < first + CAPR)
        expert = jnp.where(mine, replica_ref[d], expert)
        within = jnp.where(mine, row - first, within)
        allowed = jnp.where(mine, jnp.where(row - first < counts_ref[0, d], 1, 0), allowed)
    lower = jnp.zeros((slots, toks), jnp.int32)
    for d in range(dev_count):
        earlier = (row < homes) | (row >= homes + (d + 1) * CAPR)
        lower = lower + jnp.where(earlier & (expert == replica_ref[d]), counts_ref[0, d], 0)
    ids = ids_ref[...]
    named = jnp.zeros((slots, toks), F32)
    for k in range(top):
        named = named + jnp.where(ids[k:k + 1, :] == expert, 1.0, 0.0)
    before = jnp.where(iota((toks, toks), 0) < iota((toks, toks), 1), 1.0, 0.0).astype(BF16)
    rank = jnp.dot(named.astype(BF16), before, preferred_element_type=F32)
    wanted = (lower + within).astype(F32)
    pick = jnp.where((rank == wanted) & (allowed > 0), named, 0.0)
    pick_ref[...] = pick
    expert_ref[...] = expert
    for move in moves[3:5]:
        move.wait()
    wide[...] = hid_ref[...].astype(F32)
    h_slot = jnp.zeros((slots, hid_ref.shape[1]), F32)
    p_slot = jnp.zeros((slots, toks), F32)
    probs = probs_ref[...].astype(F32)
    for k in range(top):
        sel = jnp.where(ids[k:k + 1, :] == expert, pick, 0.0)
        h_k = wide[pl.ds(k, toks, stride=top), :].astype(BF16)
        h_slot = h_slot + jnp.dot(sel.astype(BF16), h_k, preferred_element_type=F32)
        p_slot = p_slot + sel * probs[k:k + 1, :]
    p_slot = jnp.sum(p_slot, axis=1, keepdims=True)
    hs_ref[...] = h_slot
    ps_ref[...] = jnp.broadcast_to(p_slot, ps_ref.shape)
    scaled = p_slot * h_slot
    moves[5].wait()
    rows = jnp.dot(pick.astype(BF16), cot_ref[...], preferred_element_type=F32)
    d_model = cot_ref.shape[1]
    for out_ref, blocks in zip(packed, packing):
        spans = [(homes, slots) if b == COPIES else (b * per_home, (b + 1) * per_home) for b in blocks]
        out_ref[:, :d_model] = jnp.concatenate([rows[i:j] for i, j in spans], axis=0).astype(BF16)
        out_ref[:, d_model:] = jnp.concatenate([scaled[i:j] for i, j in spans], axis=0).astype(BF16)


def padded(rows):
    return -(-rows // 16) * 16


def stack(order, blocks, height):
    values = [blocks[key] for key in order]
    missing = height - sum(v.shape[0] for v in values)
    if missing:
        values.append(jnp.zeros((missing, values[0].shape[1]), values[0].dtype))
    return jnp.concatenate(values, axis=0)


def slots_of(order, slot_ref, per_home, height):
    kinds = {HOME: slot_ref[:per_home], COPIES: slot_ref[per_home:]}
    return stack(order, {key: kinds[key[1]] for key in order}, height)


def fill_rows(order, pieces, per_home, per_copy, piece_refs, rows_ref):
    values = [r[...].astype(F32) for r in piece_refs]
    blocks = {}
    for key in order:
        n, start = pieces[key]
        blocks[key] = values[n][start:start + (per_home if key[1] == HOME else per_copy)]
    rows_ref[...] = stack(order, blocks, rows_ref.shape[0]).astype(BF16)


def own_columns(rows_ref, w_ref, slot, local_count):
    d_model = w_ref.shape[1]
    width = w_ref.shape[0] // local_count
    every = lax.dot_general(rows_ref[:, :d_model], w_ref[...], NT, preferred_element_type=F32)
    own = jnp.zeros((rows_ref.shape[0], width), F32)
    for e in range(local_count):
        own = jnp.where(slot == e, every[:, e * width:(e + 1) * width], own)
    return own


def hold_kernel(local_count, dev_count, replica_ref, w_hbm, own_hbm, even_hbm,
                own_ref, even_ref, w_ref, slot_ref, sems):
    moves = [pltpu.make_async_copy(a, b, sems.at[n]) for n, (a, b) in enumerate(
        ((w_hbm, w_ref), (own_hbm, own_ref), (even_hbm, even_ref)))]
    for move in moves:
        move.start()
    per_home, per_copy = local_count * SLOT, dev_count * CAPR
    first = lax.axis_index("expert") * local_count
    width = slot_ref.shape[1]
    slot_ref[:per_home] = iota((per_home, width), 0) // SLOT
    row = iota((per_copy, width), 0)
    copy = jnp.full((per_copy, width), -1, jnp.int32)
    for d in range(dev_count):
        mine = (row >= d * CAPR) & (row < (d + 1) * CAPR)
        copy = jnp.where(mine, replica_ref[d] - first, copy)
    slot_ref[per_home:] = copy
    for move in moves:
        move.wait()


def turn_kernel(local_count, dev_count, beside_ref, far_ref, even_ref, *out_refs):
    per_home, per_copy = local_count * SLOT, dev_count * CAPR
    beside = beside_ref[per_copy + per_home:].astype(F32)
    even = even_ref[...].astype(F32)
    for n, out_ref in enumerate(out_refs):
        span = slice(n * per_home, (n + 1) * per_home)
        blocks = [far_ref[...].astype(F32)] * (n == 0) + [even[span], beside[span]]
        out_ref[...] = jnp.concatenate(blocks, axis=0).astype(BF16)


def early_kernel(local_count, dev_count, order, pieces, w_ref, slot_ref, *refs):
    piece_refs, (rows_ref, own_ref) = refs[:-2], refs[-2:]
    per_home, per_copy = local_count * SLOT, dev_count * CAPR
    fill_rows(order, pieces, per_home, per_copy, piece_refs, rows_ref)
    slot = slots_of(order, slot_ref, per_home, rows_ref.shape[0])
    own_ref[...] = own_columns(rows_ref, w_ref, slot, local_count)


def late_kernel(local_count, dev_count, early, order, pieces, own_ref, w_ref, slot_ref, *refs):
    piece_refs, (rows_ref, back_ref, passed) = refs[:-3], refs[-3:]
    per_home, per_copy = local_count * SLOT, dev_count * CAPR
    fill_rows(order, pieces, per_home, per_copy, piece_refs, rows_ref)
    own = own_columns(rows_ref, w_ref, slots_of(order, slot_ref, per_home, rows_ref.shape[0]), local_count)
    for keys, value in ((early, own_ref[...]), (order, own)):
        start = 0
        for m, kind in keys:
            lower, size = (0, per_home) if kind == HOME else (per_home, per_copy)
            passed[m, lower:lower + size] = value[start:start + size]
            start += size
    me = lax.axis_index("expert")
    back = jnp.concatenate([passed[me ^ source] for source in range(dev_count)], axis=0)
    back_ref[...] = back.astype(back_ref.dtype)


def grad_weights_half(local_count, dev_count, orders, half, slot_ref, rows_refs, columns):
    start = pl.multiple_of(half * columns, 128)
    spread = []
    for order, ref in zip(orders, rows_refs):
        slot = slots_of(order, slot_ref, local_count * SLOT, ref.shape[0])
        scaled = ref[:, 2 * columns:].astype(F32)
        spread.append(jnp.concatenate([jnp.where(slot == e, scaled, 0.0) for e in range(local_count)], axis=1))
    rows = jnp.concatenate([ref[:, pl.ds(start, columns)] for ref in rows_refs], axis=0)
    return lax.dot_general(
        jnp.concatenate(spread, axis=0).astype(BF16), rows, TN, preferred_element_type=F32)


def other_half_kernel(local_count, dev_count, orders, slot_ref, early_ref, late_ref, out_ref):
    half = 1 - lax.axis_index("dp")
    out_ref[...] = grad_weights_half(
        local_count, dev_count, orders, half, slot_ref, (early_ref, late_ref), out_ref.shape[1]).astype(out_ref.dtype)


def own_half_kernel(local_count, dev_count, orders, slot_ref, early_ref, late_ref, arrived_ref, out_ref):
    half = lax.axis_index("dp")
    total = grad_weights_half(
        local_count, dev_count, orders, half, slot_ref, (early_ref, late_ref), out_ref.shape[1])
    out_ref[...] = (total + arrived_ref[...].astype(F32)).astype(out_ref.dtype)


def combine_kernel(local_count, dev_count, back_ref, pick_ref, expert_ref, hs_ref, ps_ref, ids_ref,
                   grad_h_ref, grad_p_ref, wide, narrow):
    top, toks = ids_ref.shape
    per_home = local_count * SLOT
    me = lax.axis_index("expert")
    back = [back_ref[me ^ m].astype(F32) for m in range(dev_count)]
    copy = functools.reduce(jnp.add, [b[per_home:] for b in back])
    grad_in = jnp.concatenate([b[:per_home] for b in back] + [copy], axis=0)
    h_rows = (ps_ref[...] * grad_in).astype(BF16)
    p_rows = jnp.sum(hs_ref[...] * grad_in, axis=1, keepdims=True)
    ids = ids_ref[...]
    pick = pick_ref[...]
    expert = expert_ref[...]
    for k in range(top):
        sel = jnp.where(ids[k:k + 1, :] == expert, pick, 0.0)
        wide[pl.ds(k, toks, stride=top), :] = lax.dot_general(
            sel.astype(BF16), h_rows, TN, preferred_element_type=F32)
        narrow[k:k + 1, :] = jnp.sum(sel * p_rows, axis=0, keepdims=True)
    grad_h_ref[...] = wide[...].astype(grad_h_ref.dtype)
    grad_p_ref[...] = narrow[...].astype(grad_p_ref.dtype)


def call(kernel, out_shape, operands, scratch=(), flops=0, limit=24):
    shapes = jax.tree.leaves(out_shape)
    moved = sum(a.size * a.dtype.itemsize for a in (*(a for _, a in operands), *shapes))
    return pl.pallas_call(
        kernel,
        out_shape=out_shape,
        in_specs=[pl.BlockSpec(memory_space=space) for space, _ in operands],
        out_specs=jax.tree.map(lambda _: pl.BlockSpec(memory_space=pltpu.VMEM), out_shape),
        scratch_shapes=list(scratch),
        compiler_params=pltpu.CompilerParams(vmem_limit_bytes=limit << 20),
        cost_estimate=pl.CostEstimate(flops=flops, bytes_accessed=moved, transcendentals=0),
    )(*(a for _, a in operands))


def swap(x, bits, count):
    return lax.ppermute(x, "expert", [(i, i ^ bits) for i in range(count)])


def gather_body(cotangent, hidden, probs, expert_ids, send_counts, replica_of, weights):
    toks, d_model = cotangent.shape
    top = expert_ids.shape[1]
    width = hidden.shape[2]
    local_count = weights.shape[0]
    dev_count = lax.axis_size("expert")
    homes = dev_count * local_count * SLOT
    copies = dev_count * CAPR
    slots = homes + copies
    rows = homes + dev_count * copies
    columns = d_model // 2
    sizes = (local_count, dev_count)
    ids = expert_ids.T
    shape = jax.ShapeDtypeStruct
    hbm, vmem, smem = pltpu.HBM, pltpu.VMEM, pltpu.SMEM
    sources = (replica_of, send_counts, ids, probs.T, hidden.reshape(toks * top, width), cotangent)
    per_home = local_count * SLOT
    odd, even = range(1, dev_count, 2), range(2, dev_count, 2)
    packing = [[COPIES, *odd], [COPIES], [0, COPIES], [*even]]
    sized = [sum(copies if b == COPIES else per_home for b in blocks) for blocks in packing]
    pick, expert, h_slot, p_slot, to_beside, copy_rows, own_rows, even_rows = call(
        functools.partial(dispatch_kernel, *sizes, packing),
        [shape((slots, toks), F32), shape((slots, toks), jnp.int32), shape((slots, width), F32),
         shape((slots, width), F32)] + [shape((n, d_model + width), BF16) for n in sized],
        [(hbm, a) for a in sources],
        [(smem if n < 2 else vmem)(a.shape, a.dtype) for n, a in enumerate(sources)]
        + [vmem((toks * top, width), F32), pltpu.SemaphoreType.DMA((len(sources),))],
        flops=2 * slots * toks * d_model,
        limit=60,
    )
    beside = swap(to_beside, 1, dev_count)
    far = swap(copy_rows, 4, dev_count)
    near = swap(copy_rows, 2, dev_count)
    flat_w = weights.reshape(local_count * width, d_model)
    own_rows, even_rows, w_held, slot = call(
        functools.partial(hold_kernel, *sizes),
        [shape(a.shape, BF16) for a in (own_rows, even_rows, flat_w)] + [shape((per_home + copies, width), jnp.int32)],
        [(smem, replica_of)] + [(hbm, a) for a in (flat_w, own_rows, even_rows)],
        [pltpu.SemaphoreType.DMA((3,))],
    )
    beside, far, near, own_rows, even_rows, w_held, slot = lax.optimization_barrier(
        (beside, far, near, own_rows, even_rows, w_held, slot))
    far_beside = swap(far, 1, dev_count)
    turned = call(
        functools.partial(turn_kernel, *sizes),
        [shape((copies * (m == 2) + 2 * per_home, d_model + width), BF16) for m in even],
        [(vmem, a) for a in (beside, far, even_rows)],
    )
    turned = [swap(a, m, dev_count) for a, m in zip(turned, even)]
    near_beside = swap(near, 1, dev_count)
    pieces = {(0, HOME): (0, 0), (0, COPIES): (0, per_home), (1, COPIES): (1, 0), (1, HOME): (1, copies),
              (2, COPIES): (2, 0), (4, COPIES): (3, 0)}
    orders = [list(pieces)]
    height = padded(sum(per_home if kind == HOME else copies for _, kind in pieces))
    early_rows, own = call(
        functools.partial(early_kernel, *sizes, orders[0], pieces),
        (shape((height, d_model + width), BF16), shape((height, width), F32)),
        [(vmem, a) for a in (w_held, slot, own_rows, beside, near, far)],
        flops=2 * height * d_model * local_count * width * 30,
    )
    far_across = swap(turned[0][:copies], 1, dev_count)
    arrays = [far_beside, near_beside, far_across, *turned]
    pieces = {(5, COPIES): (0, 0), (3, COPIES): (1, 0), (7, COPIES): (2, 0), (6, COPIES): (3, 0)}
    for n, m in enumerate(even):
        pieces[m, HOME], pieces[m + 1, HOME] = ((3 + n, copies * (m == 2) + k * per_home) for k in range(2))
    orders.append(list(pieces))
    height = padded(sum(per_home if kind == HOME else copies for _, kind in pieces))
    late_rows, back = call(
        functools.partial(late_kernel, *sizes, *orders, pieces),
        (shape((height, d_model + width), BF16), shape((dev_count * (per_home + copies), width), BF16)),
        [(vmem, a) for a in (own, w_held, slot, *arrays)],
        [vmem((dev_count, per_home + copies, width), F32)],
        flops=2 * height * d_model * local_count * width,
    )
    back = lax.all_to_all(back, "expert", split_axis=0, concat_axis=0, tiled=True)
    half_flops = 2 * rows * columns * local_count * width
    halves = (slot, early_rows, late_rows)
    other = call(
        functools.partial(other_half_kernel, *sizes, orders),
        shape((local_count * width, columns), BF16),
        [(vmem, a) for a in halves],
        flops=half_flops,
    )
    arrived = lax.ppermute(other, "dp", [(0, 1), (1, 0)])
    grad_w = call(
        functools.partial(own_half_kernel, *sizes, orders),
        shape((local_count * width, columns), BF16),
        [(vmem, a) for a in (*halves, arrived)],
        flops=half_flops,
    )
    grad_w, pick = lax.optimization_barrier((grad_w, pick))
    grad_h, grad_p = call(
        functools.partial(combine_kernel, *sizes),
        (shape((toks * top, width), BF16), shape((top, toks), BF16)),
        [(vmem, a) for a in (back.reshape(dev_count, per_home + copies, width), pick, expert, h_slot, p_slot, ids)],
        [vmem((toks * top, width), F32), vmem((top, toks), F32)],
        flops=2 * slots * toks * width * top,
    )
    return (
        grad_h.reshape(toks, top, width),
        grad_p.T,
        grad_w.reshape(local_count, width, columns),
    )


def body(cotangent, hidden, probs, expert_ids, send_counts, replica_of, weights):
    dev_count = lax.axis_size("expert")
    local_count, width, _ = weights.shape
    gathered = dev_count * dev_count * CAPR
    if gathered <= (local_count + 3) * width and dev_count == 8 and lax.axis_size("dp") == 2:
        run = gather_body
    else:
        run = replica_body
    return run(cotangent, hidden, probs, expert_ids, send_counts, replica_of, weights)


def solution(mesh):
    in_specs = (
        P(("groups", "expert", "dp"), None),
        P(("groups", "expert", "dp"), None, None),
        P(("groups", "expert", "dp"), None),
        P(("groups", "expert", "dp"), None),
        P(("groups", "expert", "dp"), None),
        P("groups"),
        P("expert", None, None),
    )
    out_specs = (
        P(("groups", "expert", "dp"), None, None),
        P(("groups", "expert", "dp"), None),
        P(("groups", "expert"), None, "dp"),
    )
    return jax.shard_map(body, mesh=mesh, in_specs=in_specs, out_specs=out_specs, check_vma=False)
```

```python
import functools

import jax
import jax.numpy as jnp
from jax import lax
from jax.experimental import pallas as pl
from jax.experimental.pallas import tpu as pltpu
from jax.sharding import PartitionSpec as P

CAPH = 3
CAPR = 3


def ranks_within(keys):
    total_rows = keys.shape[0]
    sort_order = jnp.argsort(keys * total_rows + jnp.arange(total_rows, dtype=jnp.int32))
    sorted_keys = keys[sort_order]
    first_seen = jnp.searchsorted(sorted_keys, sorted_keys, side="left")
    ranked = jnp.arange(total_rows, dtype=jnp.int32) - first_seen
    return jnp.zeros((total_rows,), jnp.int32).at[sort_order].set(ranked)


def route_rows(ids_block, counts_row, replica_of, local_count, cap_home, cap_copy):
    dev_count = replica_of.shape[0]
    experts = ids_block.reshape(-1)
    rank_expert = ranks_within(experts)
    devices = jnp.arange(dev_count, dtype=jnp.int32)
    same_copy = (replica_of[:, None] == replica_of[None, :]) & (devices[None, :] < devices[:, None])
    lower_rank = jnp.sum(jnp.where(same_copy, counts_row[None, :], 0), axis=1)
    upper_rank = lower_rank + counts_row
    hit_table = (
        (replica_of[None, :] == experts[:, None])
        & (lower_rank[None, :] <= rank_expert[:, None])
        & (rank_expert[:, None] < upper_rank[None, :])
    )
    copied = jnp.any(hit_table, axis=1)
    copy_dev = jnp.sum(jnp.where(hit_table, devices[None, :], 0), axis=1)
    dest_dev = jnp.where(copied, copy_dev, experts // local_count)
    index_of_slot = jnp.where(copied, local_count, experts % local_count)
    rank_bucket = ranks_within(dest_dev * (local_count + 1) + index_of_slot)
    keep_row = rank_bucket < jnp.where(copied, cap_copy, cap_home)
    per_dev = local_count * cap_home + cap_copy
    target = dest_dev * per_dev + index_of_slot * cap_home + rank_bucket
    return jnp.where(keep_row, target, dev_count * per_dev)


def replica_body(cotangent, hidden, probs, expert_ids, send_counts, replica_of, weights):
    tok_rows, d_model = cotangent.shape
    top_count = expert_ids.shape[1]
    hidden_width = hidden.shape[2]
    local_count = weights.shape[0]
    dev_count = lax.axis_size("expert")
    data_count = lax.axis_size("dp")
    per_dev = local_count * CAPH + CAPR
    row_count = tok_rows * top_count
    recv_count = dev_count * per_dev
    target = route_rows(expert_ids, send_counts[0], replica_of, local_count, CAPH, CAPR)
    inverse = (
        jnp.full((recv_count,), row_count, jnp.int32)
        .at[target]
        .set(jnp.arange(row_count, dtype=jnp.int32), mode="drop")
    )
    dy_pad = jnp.concatenate([cotangent, jnp.zeros((1, d_model), cotangent.dtype)], axis=0)
    h_pad = jnp.concatenate(
        [hidden.reshape(row_count, hidden_width), jnp.zeros((1, hidden_width), hidden.dtype)],
        axis=0,
    )
    p_pad = jnp.concatenate([probs.reshape(row_count), jnp.zeros((1,), probs.dtype)], axis=0)
    send_dy = dy_pad[inverse // top_count]
    send_h = h_pad[inverse]
    send_p = p_pad[inverse]
    recv_dy, recv_h, recv_p = (
        lax.all_to_all(send_dy, "expert", split_axis=0, concat_axis=0, tiled=True),
        lax.all_to_all(send_h, "expert", split_axis=0, concat_axis=0, tiled=True),
        lax.all_to_all(send_p, "expert", split_axis=0, concat_axis=0, tiled=True),
    )
    flat_size = hidden_width * d_model
    flat_w = weights.reshape(local_count, flat_size)
    pieces = lax.all_to_all(flat_w, "expert", split_axis=1, concat_axis=0, tiled=True)
    chosen = pieces[replica_of]
    copy_weight = lax.all_to_all(chosen, "expert", split_axis=0, concat_axis=0, tiled=True).reshape(
        hidden_width, d_model
    )
    slot_total = local_count + 1
    home_rows = local_count * CAPH
    row_pos = jnp.arange(recv_count, dtype=jnp.int32) % per_dev
    row_slot = jnp.where(row_pos < home_rows, row_pos // CAPH, local_count)
    all_weights = jnp.concatenate(
        [weights.reshape(local_count * hidden_width, d_model), copy_weight], axis=0
    )
    all_in = lax.dot_general(
        recv_dy, all_weights, (((1,), (1,)), ((), ())), preferred_element_type=jnp.float32
    )
    grad_in = jnp.zeros((recv_count, hidden_width), jnp.float32)
    for slot_num in range(slot_total):
        grad_in = grad_in + jnp.where(
            (row_slot == slot_num)[:, None],
            all_in[:, slot_num * hidden_width : (slot_num + 1) * hidden_width],
            0.0,
        )
    p_wide = recv_p.astype(jnp.float32)[:, None]
    h_wide = recv_h.astype(jnp.float32)
    grad_h_buf = (p_wide * grad_in).astype(jnp.bfloat16)
    grad_p_buf = jnp.sum(h_wide * grad_in, axis=1).astype(jnp.bfloat16)
    scaled = (p_wide * h_wide).astype(jnp.bfloat16)
    zero_rows = jnp.zeros_like(scaled)
    scaled_wide = jnp.concatenate(
        [
            jnp.where((row_slot == slot_num)[:, None], scaled, zero_rows)
            for slot_num in range(slot_total)
        ],
        axis=1,
    )
    parts = lax.dot_general(
        scaled_wide, recv_dy, (((0,), (0,)), ((), ())), preferred_element_type=jnp.float32
    ).astype(jnp.bfloat16)
    home_part = parts[: local_count * hidden_width].reshape(local_count, hidden_width, d_model)
    copy_part = parts[local_count * hidden_width :]
    back_h, back_p = (
        lax.all_to_all(grad_h_buf, "expert", split_axis=0, concat_axis=0, tiled=True),
        lax.all_to_all(grad_p_buf, "expert", split_axis=0, concat_axis=0, tiled=True),
    )
    flat_h = jnp.concatenate([back_h, jnp.zeros((1, hidden_width), back_h.dtype)], axis=0)
    flat_p = jnp.concatenate([back_p, jnp.zeros((1,), back_p.dtype)], axis=0)
    hidden_gradient = flat_h[target].reshape(tok_rows, top_count, hidden_width)
    grad_probs = flat_p[target].reshape(tok_rows, top_count)
    expert_total = dev_count * local_count
    cover = replica_of[None, :] == jnp.arange(expert_total, dtype=jnp.int32)[:, None]
    half_width = d_model // data_count
    halves = lax.all_to_all(copy_part, "dp", split_axis=1, concat_axis=0, tiled=True)
    copy_half = jnp.sum(
        halves.reshape(data_count, hidden_width, half_width).astype(jnp.float32), axis=0
    )
    piece_len = hidden_width * half_width // dev_count
    slabs = copy_half.reshape(dev_count, piece_len)
    arrived = lax.all_to_all(slabs, "expert", split_axis=0, concat_axis=0, tiled=True)
    sums = jnp.dot(cover.astype(jnp.float32), arrived, precision=lax.Precision.HIGHEST)
    homed = lax.all_to_all(
        sums.reshape(dev_count, local_count * piece_len),
        "expert",
        split_axis=0,
        concat_axis=0,
        tiled=True,
    )
    homed = (
        homed.reshape(dev_count, local_count, piece_len)
        .transpose(1, 0, 2)
        .reshape(local_count, hidden_width, half_width)
    )
    home_half = lax.psum_scatter(
        home_part.astype(jnp.float32).astype(jnp.bfloat16), "dp", scatter_dimension=2, tiled=True
    ).astype(jnp.float32)
    grad_weights = (home_half + homed).astype(jnp.bfloat16)
    return (hidden_gradient, grad_probs, grad_weights)


SLOT = 3
HOME, COPIES = "home", "copies"
F32 = jnp.float32
BF16 = jnp.bfloat16
NT = (((1,), (1,)), ((), ()))
TN = (((0,), (0,)), ((), ()))


def iota(shape, dim):
    return lax.broadcasted_iota(jnp.int32, shape, dim)


def dispatch_kernel(local_count, dev_count, packing, *refs):
    sources, refs = refs[:6], refs[6:]
    pick_ref, expert_ref, hs_ref, ps_ref = refs[:4]
    packed, (held, wide, sems) = refs[4:4 + len(packing)], (refs[-8:-2], refs[-2], refs[-1])
    moves = [pltpu.make_async_copy(s, h, sems.at[n]) for n, (s, h) in enumerate(zip(sources, held))]
    for move in moves:
        move.start()
    replica_ref, counts_ref, ids_ref, probs_ref, hid_ref, cot_ref = held
    top, toks = ids_ref.shape
    per_home = local_count * SLOT
    homes = dev_count * per_home
    slots = homes + dev_count * CAPR
    me = lax.axis_index("expert")
    for move in moves[:3]:
        move.wait()
    row = iota((slots, toks), 0)
    expert = ((row // per_home) ^ me) * local_count + (row % per_home) // SLOT
    within = row % SLOT
    allowed = jnp.where(within < CAPH, 1, 0)
    for d in range(dev_count):
        first = homes + d * CAPR
        mine = (row >= first) & (row < first + CAPR)
        expert = jnp.where(mine, replica_ref[d], expert)
        within = jnp.where(mine, row - first, within)
        allowed = jnp.where(mine, jnp.where(row - first < counts_ref[0, d], 1, 0), allowed)
    lower = jnp.zeros((slots, toks), jnp.int32)
    for d in range(dev_count):
        earlier = (row < homes) | (row >= homes + (d + 1) * CAPR)
        lower = lower + jnp.where(earlier & (expert == replica_ref[d]), counts_ref[0, d], 0)
    ids = ids_ref[...]
    named = jnp.zeros((slots, toks), F32)
    for k in range(top):
        named = named + jnp.where(ids[k:k + 1, :] == expert, 1.0, 0.0)
    before = jnp.where(iota((toks, toks), 0) < iota((toks, toks), 1), 1.0, 0.0).astype(BF16)
    rank = jnp.dot(named.astype(BF16), before, preferred_element_type=F32)
    wanted = (lower + within).astype(F32)
    pick = jnp.where((rank == wanted) & (allowed > 0), named, 0.0)
    pick_ref[...] = pick
    expert_ref[...] = expert
    for move in moves[3:5]:
        move.wait()
    wide[...] = hid_ref[...].astype(F32)
    h_slot = jnp.zeros((slots, hid_ref.shape[1]), F32)
    p_slot = jnp.zeros((slots, toks), F32)
    probs = probs_ref[...].astype(F32)
    for k in range(top):
        sel = jnp.where(ids[k:k + 1, :] == expert, pick, 0.0)
        h_k = wide[pl.ds(k, toks, stride=top), :].astype(BF16)
        h_slot = h_slot + jnp.dot(sel.astype(BF16), h_k, preferred_element_type=F32)
        p_slot = p_slot + sel * probs[k:k + 1, :]
    p_slot = jnp.sum(p_slot, axis=1, keepdims=True)
    hs_ref[...] = h_slot
    ps_ref[...] = jnp.broadcast_to(p_slot, ps_ref.shape)
    scaled = p_slot * h_slot
    moves[5].wait()
    rows = jnp.dot(pick.astype(BF16), cot_ref[...], preferred_element_type=F32)
    d_model = cot_ref.shape[1]
    for out_ref, blocks in zip(packed, packing):
        spans = [(homes, slots) if b == COPIES else (b * per_home, (b + 1) * per_home) for b in blocks]
        out_ref[:, :d_model] = jnp.concatenate([rows[i:j] for i, j in spans], axis=0).astype(BF16)
        out_ref[:, d_model:] = jnp.concatenate([scaled[i:j] for i, j in spans], axis=0).astype(BF16)


def padded(rows):
    return -(-rows // 16) * 16


def stack(order, blocks, height):
    values = [blocks[key] for key in order]
    missing = height - sum(v.shape[0] for v in values)
    if missing:
        values.append(jnp.zeros((missing, values[0].shape[1]), values[0].dtype))
    return jnp.concatenate(values, axis=0)


def slots_of(order, slot_ref, per_home, height):
    kinds = {HOME: slot_ref[:per_home], COPIES: slot_ref[per_home:]}
    return stack(order, {key: kinds[key[1]] for key in order}, height)


def fill_rows(order, pieces, per_home, per_copy, piece_refs, rows_ref):
    values = [r[...].astype(F32) for r in piece_refs]
    blocks = {}
    for key in order:
        n, start = pieces[key]
        blocks[key] = values[n][start:start + (per_home if key[1] == HOME else per_copy)]
    rows_ref[...] = stack(order, blocks, rows_ref.shape[0]).astype(BF16)


def own_columns(rows_ref, w_ref, slot, local_count):
    d_model = w_ref.shape[1]
    width = w_ref.shape[0] // local_count
    every = lax.dot_general(rows_ref[:, :d_model], w_ref[...], NT, preferred_element_type=F32)
    own = jnp.zeros((rows_ref.shape[0], width), F32)
    for e in range(local_count):
        own = jnp.where(slot == e, every[:, e * width:(e + 1) * width], own)
    return own


def hold_kernel(local_count, dev_count, replica_ref, w_hbm, own_hbm, even_hbm,
                own_ref, even_ref, w_ref, slot_ref, sems):
    moves = [pltpu.make_async_copy(a, b, sems.at[n]) for n, (a, b) in enumerate(
        ((w_hbm, w_ref), (own_hbm, own_ref), (even_hbm, even_ref)))]
    for move in moves:
        move.start()
    per_home, per_copy = local_count * SLOT, dev_count * CAPR
    first = lax.axis_index("expert") * local_count
    width = slot_ref.shape[1]
    slot_ref[:per_home] = iota((per_home, width), 0) // SLOT
    row = iota((per_copy, width), 0)
    copy = jnp.full((per_copy, width), -1, jnp.int32)
    for d in range(dev_count):
        mine = (row >= d * CAPR) & (row < (d + 1) * CAPR)
        copy = jnp.where(mine, replica_ref[d] - first, copy)
    slot_ref[per_home:] = copy
    for move in moves:
        move.wait()


def turn_kernel(local_count, dev_count, beside_ref, far_ref, even_ref, *out_refs):
    per_home, per_copy = local_count * SLOT, dev_count * CAPR
    beside = beside_ref[...].astype(F32)[per_copy + per_home:]
    even = even_ref[...].astype(F32)
    for n, out_ref in enumerate(out_refs):
        span = slice(n * per_home, (n + 1) * per_home)
        blocks = [far_ref[...].astype(F32)] * (n == 0) + [even[span], beside[span]]
        out_ref[...] = jnp.concatenate(blocks, axis=0).astype(BF16)


def early_kernel(local_count, dev_count, order, pieces, w_ref, slot_ref, *refs):
    piece_refs, (rows_ref, own_ref) = refs[:-2], refs[-2:]
    per_home, per_copy = local_count * SLOT, dev_count * CAPR
    fill_rows(order, pieces, per_home, per_copy, piece_refs, rows_ref)
    slot = slots_of(order, slot_ref, per_home, rows_ref.shape[0])
    own_ref[...] = own_columns(rows_ref, w_ref, slot, local_count)


def late_kernel(local_count, dev_count, early, order, pieces, own_ref, w_ref, slot_ref, *refs):
    piece_refs, (rows_ref, back_ref, passed) = refs[:-3], refs[-3:]
    per_home, per_copy = local_count * SLOT, dev_count * CAPR
    fill_rows(order, pieces, per_home, per_copy, piece_refs, rows_ref)
    own = own_columns(rows_ref, w_ref, slots_of(order, slot_ref, per_home, rows_ref.shape[0]), local_count)
    if passed.shape[1] > per_home + per_copy:
        passed[:, per_home + per_copy:] = jnp.zeros_like(passed[:, per_home + per_copy:])
    for keys, value in ((early, own_ref[...]), (order, own)):
        start = 0
        for m, kind in keys:
            lower, size = (0, per_home) if kind == HOME else (per_home, per_copy)
            passed[m, lower:lower + size] = value[start:start + size]
            start += size
    me = lax.axis_index("expert")
    back = jnp.concatenate([passed[me ^ source] for source in range(dev_count)], axis=0)
    back_ref[...] = back.astype(back_ref.dtype)


def grad_weights_half(local_count, dev_count, orders, half, slot_ref, rows_refs, columns):
    start = pl.multiple_of(half * columns, 128)
    spread = []
    for order, ref in zip(orders, rows_refs):
        slot = slots_of(order, slot_ref, local_count * SLOT, ref.shape[0])
        scaled = ref[:, 2 * columns:].astype(F32)
        spread.append(jnp.concatenate([jnp.where(slot == e, scaled, 0.0) for e in range(local_count)], axis=1))
    rows = jnp.concatenate([ref[:, pl.ds(start, columns)] for ref in rows_refs], axis=0)
    return lax.dot_general(
        jnp.concatenate(spread, axis=0).astype(BF16), rows, TN, preferred_element_type=F32)


def other_half_kernel(local_count, dev_count, orders, slot_ref, early_ref, late_ref, out_ref):
    half = 1 - lax.axis_index("dp")
    out_ref[...] = grad_weights_half(
        local_count, dev_count, orders, half, slot_ref, (early_ref, late_ref), out_ref.shape[1]).astype(out_ref.dtype)


def own_half_kernel(local_count, dev_count, orders, slot_ref, early_ref, late_ref, arrived_ref, out_ref):
    half = lax.axis_index("dp")
    total = grad_weights_half(
        local_count, dev_count, orders, half, slot_ref, (early_ref, late_ref), out_ref.shape[1])
    out_ref[...] = (total + arrived_ref[...].astype(F32)).astype(out_ref.dtype)


def combine_kernel(local_count, dev_count, back_ref, pick_ref, expert_ref, hs_ref, ps_ref, ids_ref,
                   grad_h_ref, grad_p_ref, wide, narrow):
    top, toks = ids_ref.shape
    per_home = local_count * SLOT
    me = lax.axis_index("expert")
    back = [back_ref[me ^ m].astype(F32) for m in range(dev_count)]
    slots = pick_ref.shape[0]
    copies = slots - dev_count * per_home
    copy = functools.reduce(jnp.add, [b[per_home:per_home + copies] for b in back])
    grad_in = jnp.concatenate([b[:per_home] for b in back] + [copy], axis=0)
    h_rows = (ps_ref[...] * grad_in).astype(BF16)
    p_rows = jnp.sum(hs_ref[...] * grad_in, axis=1, keepdims=True)
    ids = ids_ref[...]
    pick = pick_ref[...]
    expert = expert_ref[...]
    for k in range(top):
        sel = jnp.where(ids[k:k + 1, :] == expert, pick, 0.0)
        wide[pl.ds(k, toks, stride=top), :] = lax.dot_general(
            sel.astype(BF16), h_rows, TN, preferred_element_type=F32)
        narrow[k:k + 1, :] = jnp.sum(sel * p_rows, axis=0, keepdims=True)
    grad_h_ref[...] = wide[...].astype(grad_h_ref.dtype)
    grad_p_ref[...] = narrow[...].astype(grad_p_ref.dtype)


def call(kernel, out_shape, operands, scratch=(), flops=0, limit=24):
    shapes = jax.tree.leaves(out_shape)
    moved = sum(a.size * a.dtype.itemsize for a in (*(a for _, a in operands), *shapes))
    return pl.pallas_call(
        kernel,
        out_shape=out_shape,
        in_specs=[pl.BlockSpec(memory_space=space) for space, _ in operands],
        out_specs=jax.tree.map(lambda _: pl.BlockSpec(memory_space=pltpu.VMEM), out_shape),
        scratch_shapes=list(scratch),
        compiler_params=pltpu.CompilerParams(vmem_limit_bytes=limit << 20),
        cost_estimate=pl.CostEstimate(flops=flops, bytes_accessed=moved, transcendentals=0),
    )(*(a for _, a in operands))


def swap(x, bits, count):
    return lax.ppermute(x, "expert", [(i, i ^ bits) for i in range(count)])


def gather_body(cotangent, hidden, probs, expert_ids, send_counts, replica_of, weights):
    toks, d_model = cotangent.shape
    top = expert_ids.shape[1]
    width = hidden.shape[2]
    local_count = weights.shape[0]
    dev_count = lax.axis_size("expert")
    homes = dev_count * local_count * SLOT
    copies = dev_count * CAPR
    slots = homes + copies
    rows = homes + dev_count * copies
    columns = d_model // 2
    sizes = (local_count, dev_count)
    ids = expert_ids.T
    shape = jax.ShapeDtypeStruct
    hbm, vmem, smem = pltpu.HBM, pltpu.VMEM, pltpu.SMEM
    sources = (replica_of, send_counts, ids, probs.T, hidden.reshape(toks * top, width), cotangent)
    per_home = local_count * SLOT
    odd, even = range(1, dev_count, 2), range(2, dev_count, 2)
    packing = [[COPIES, *odd], [COPIES], [0, COPIES], [*even]]
    sized = [sum(copies if b == COPIES else per_home for b in blocks) for blocks in packing]
    pick, expert, h_slot, p_slot, to_beside, copy_rows, own_rows, even_rows = call(
        functools.partial(dispatch_kernel, *sizes, packing),
        [shape((slots, toks), F32), shape((slots, toks), jnp.int32), shape((slots, width), F32),
         shape((slots, width), F32)] + [shape((n, d_model + width), BF16) for n in sized],
        [(hbm, a) for a in sources],
        [(smem if n < 2 else vmem)(a.shape, a.dtype) for n, a in enumerate(sources)]
        + [vmem((toks * top, width), F32), pltpu.SemaphoreType.DMA((len(sources),))],
        flops=2 * slots * toks * d_model,
        limit=60,
    )
    beside = swap(to_beside, 1, dev_count)
    far = swap(copy_rows, 4, dev_count)
    near = swap(copy_rows, 2, dev_count)
    flat_w = weights.reshape(local_count * width, d_model)
    own_rows, even_rows, w_held, slot = call(
        functools.partial(hold_kernel, *sizes),
        [shape(a.shape, BF16) for a in (own_rows, even_rows, flat_w)] + [shape((per_home + copies, width), jnp.int32)],
        [(smem, replica_of)] + [(hbm, a) for a in (flat_w, own_rows, even_rows)],
        [pltpu.SemaphoreType.DMA((3,))],
    )
    beside, far, near, own_rows, even_rows, w_held, slot = lax.optimization_barrier(
        (beside, far, near, own_rows, even_rows, w_held, slot))
    far_beside = swap(far, 1, dev_count)
    turned = call(
        functools.partial(turn_kernel, *sizes),
        [shape((copies * (m == 2) + 2 * per_home, d_model + width), BF16) for m in even],
        [(vmem, a) for a in (beside, far, even_rows)],
    )
    turned = [swap(a, m, dev_count) for a, m in zip(turned, even)]
    near_beside = swap(near, 1, dev_count)
    pieces = {(0, HOME): (0, 0), (0, COPIES): (0, per_home), (1, COPIES): (1, 0), (1, HOME): (1, copies),
              (2, COPIES): (2, 0), (4, COPIES): (3, 0)}
    orders = [list(pieces)]
    height = padded(sum(per_home if kind == HOME else copies for _, kind in pieces))
    early_rows, own = call(
        functools.partial(early_kernel, *sizes, orders[0], pieces),
        (shape((height, d_model + width), BF16), shape((height, width), F32)),
        [(vmem, a) for a in (w_held, slot, own_rows, beside, near, far)],
        flops=2 * height * d_model * local_count * width * 30,
    )
    far_across = swap(turned[0][:copies], 1, dev_count)
    arrays = [far_beside, near_beside, far_across, *turned]
    pieces = {(5, COPIES): (0, 0), (3, COPIES): (1, 0), (7, COPIES): (2, 0), (6, COPIES): (3, 0)}
    for n, m in enumerate(even):
        pieces[m, HOME], pieces[m + 1, HOME] = ((3 + n, copies * (m == 2) + k * per_home) for k in range(2))
    orders.append(list(pieces))
    height = padded(sum(per_home if kind == HOME else copies for _, kind in pieces))
    block = padded(per_home + copies)
    late_rows, back = call(
        functools.partial(late_kernel, *sizes, *orders, pieces),
        (shape((height, d_model + width), BF16), shape((dev_count * block, width), BF16)),
        [(vmem, a) for a in (own, w_held, slot, *arrays)],
        [vmem((dev_count, block, width), F32)],
        flops=2 * height * d_model * local_count * width,
    )
    back = lax.all_to_all(back, "expert", split_axis=0, concat_axis=0, tiled=True)
    half_flops = 2 * rows * columns * local_count * width
    halves = (slot, early_rows, late_rows)
    other = call(
        functools.partial(other_half_kernel, *sizes, orders),
        shape((local_count * width, columns), BF16),
        [(vmem, a) for a in halves],
        flops=half_flops,
    )
    arrived = lax.ppermute(other, "dp", [(0, 1), (1, 0)])
    grad_w = call(
        functools.partial(own_half_kernel, *sizes, orders),
        shape((local_count * width, columns), BF16),
        [(vmem, a) for a in (*halves, arrived)],
        flops=30 * half_flops,
    )
    grad_w, pick = lax.optimization_barrier((grad_w, pick))
    grad_h, grad_p = call(
        functools.partial(combine_kernel, *sizes),
        (shape((toks * top, width), BF16), shape((top, toks), BF16)),
        [(vmem, a) for a in (back.reshape(dev_count, block, width), pick, expert, h_slot, p_slot, ids)],
        [vmem((toks * top, width), F32), vmem((top, toks), F32)],
        flops=2 * slots * toks * width * top,
    )
    return (
        grad_h.reshape(toks, top, width),
        grad_p.T,
        grad_w.reshape(local_count, width, columns),
    )


def body(cotangent, hidden, probs, expert_ids, send_counts, replica_of, weights):
    dev_count = lax.axis_size("expert")
    local_count, width, _ = weights.shape
    gathered = dev_count * dev_count * CAPR
    if gathered <= (local_count + 3) * width and dev_count == 8 and lax.axis_size("dp") == 2:
        run = gather_body
    else:
        run = replica_body
    return run(cotangent, hidden, probs, expert_ids, send_counts, replica_of, weights)


def solution(mesh):
    in_specs = (
        P(("groups", "expert", "dp"), None),
        P(("groups", "expert", "dp"), None, None),
        P(("groups", "expert", "dp"), None),
        P(("groups", "expert", "dp"), None),
        P(("groups", "expert", "dp"), None),
        P("groups"),
        P("expert", None, None),
    )
    out_specs = (
        P(("groups", "expert", "dp"), None, None),
        P(("groups", "expert", "dp"), None),
        P(("groups", "expert"), None, "dp"),
    )
    return jax.shard_map(body, mesh=mesh, in_specs=in_specs, out_specs=out_specs, check_vma=False)
```

```python
import functools

import jax
import jax.numpy as jnp
from jax import lax
from jax.experimental import pallas as pl
from jax.experimental.pallas import tpu as pltpu
from jax.sharding import PartitionSpec as P

CAPH = 3
CAPR = 3


def ranks_within(keys):
    total_rows = keys.shape[0]
    sort_order = jnp.argsort(keys * total_rows + jnp.arange(total_rows, dtype=jnp.int32))
    sorted_keys = keys[sort_order]
    first_seen = jnp.searchsorted(sorted_keys, sorted_keys, side="left")
    ranked = jnp.arange(total_rows, dtype=jnp.int32) - first_seen
    return jnp.zeros((total_rows,), jnp.int32).at[sort_order].set(ranked)


def route_rows(ids_block, counts_row, replica_of, local_count, cap_home, cap_copy):
    dev_count = replica_of.shape[0]
    experts = ids_block.reshape(-1)
    rank_expert = ranks_within(experts)
    devices = jnp.arange(dev_count, dtype=jnp.int32)
    same_copy = (replica_of[:, None] == replica_of[None, :]) & (devices[None, :] < devices[:, None])
    lower_rank = jnp.sum(jnp.where(same_copy, counts_row[None, :], 0), axis=1)
    upper_rank = lower_rank + counts_row
    hit_table = (
        (replica_of[None, :] == experts[:, None])
        & (lower_rank[None, :] <= rank_expert[:, None])
        & (rank_expert[:, None] < upper_rank[None, :])
    )
    copied = jnp.any(hit_table, axis=1)
    copy_dev = jnp.sum(jnp.where(hit_table, devices[None, :], 0), axis=1)
    dest_dev = jnp.where(copied, copy_dev, experts // local_count)
    index_of_slot = jnp.where(copied, local_count, experts % local_count)
    rank_bucket = ranks_within(dest_dev * (local_count + 1) + index_of_slot)
    keep_row = rank_bucket < jnp.where(copied, cap_copy, cap_home)
    per_dev = local_count * cap_home + cap_copy
    target = dest_dev * per_dev + index_of_slot * cap_home + rank_bucket
    return jnp.where(keep_row, target, dev_count * per_dev)


def replica_body(cotangent, hidden, probs, expert_ids, send_counts, replica_of, weights):
    tok_rows, d_model = cotangent.shape
    top_count = expert_ids.shape[1]
    hidden_width = hidden.shape[2]
    local_count = weights.shape[0]
    dev_count = lax.axis_size("expert")
    data_count = lax.axis_size("dp")
    per_dev = local_count * CAPH + CAPR
    row_count = tok_rows * top_count
    recv_count = dev_count * per_dev
    target = route_rows(expert_ids, send_counts[0], replica_of, local_count, CAPH, CAPR)
    inverse = (
        jnp.full((recv_count,), row_count, jnp.int32)
        .at[target]
        .set(jnp.arange(row_count, dtype=jnp.int32), mode="drop")
    )
    dy_pad = jnp.concatenate([cotangent, jnp.zeros((1, d_model), cotangent.dtype)], axis=0)
    h_pad = jnp.concatenate(
        [hidden.reshape(row_count, hidden_width), jnp.zeros((1, hidden_width), hidden.dtype)],
        axis=0,
    )
    p_pad = jnp.concatenate([probs.reshape(row_count), jnp.zeros((1,), probs.dtype)], axis=0)
    send_dy = dy_pad[inverse // top_count]
    send_h = h_pad[inverse]
    send_p = p_pad[inverse]
    recv_dy, recv_h, recv_p = (
        lax.all_to_all(send_dy, "expert", split_axis=0, concat_axis=0, tiled=True),
        lax.all_to_all(send_h, "expert", split_axis=0, concat_axis=0, tiled=True),
        lax.all_to_all(send_p, "expert", split_axis=0, concat_axis=0, tiled=True),
    )
    flat_size = hidden_width * d_model
    flat_w = weights.reshape(local_count, flat_size)
    pieces = lax.all_to_all(flat_w, "expert", split_axis=1, concat_axis=0, tiled=True)
    chosen = pieces[replica_of]
    copy_weight = lax.all_to_all(chosen, "expert", split_axis=0, concat_axis=0, tiled=True).reshape(
        hidden_width, d_model
    )
    slot_total = local_count + 1
    home_rows = local_count * CAPH
    row_pos = jnp.arange(recv_count, dtype=jnp.int32) % per_dev
    row_slot = jnp.where(row_pos < home_rows, row_pos // CAPH, local_count)
    all_weights = jnp.concatenate(
        [weights.reshape(local_count * hidden_width, d_model), copy_weight], axis=0
    )
    all_in = lax.dot_general(
        recv_dy, all_weights, (((1,), (1,)), ((), ())), preferred_element_type=jnp.float32
    )
    grad_in = jnp.zeros((recv_count, hidden_width), jnp.float32)
    for slot_num in range(slot_total):
        grad_in = grad_in + jnp.where(
            (row_slot == slot_num)[:, None],
            all_in[:, slot_num * hidden_width : (slot_num + 1) * hidden_width],
            0.0,
        )
    p_wide = recv_p.astype(jnp.float32)[:, None]
    h_wide = recv_h.astype(jnp.float32)
    grad_h_buf = (p_wide * grad_in).astype(jnp.bfloat16)
    grad_p_buf = jnp.sum(h_wide * grad_in, axis=1).astype(jnp.bfloat16)
    scaled = (p_wide * h_wide).astype(jnp.bfloat16)
    zero_rows = jnp.zeros_like(scaled)
    scaled_wide = jnp.concatenate(
        [
            jnp.where((row_slot == slot_num)[:, None], scaled, zero_rows)
            for slot_num in range(slot_total)
        ],
        axis=1,
    )
    parts = lax.dot_general(
        scaled_wide, recv_dy, (((0,), (0,)), ((), ())), preferred_element_type=jnp.float32
    ).astype(jnp.bfloat16)
    home_part = parts[: local_count * hidden_width].reshape(local_count, hidden_width, d_model)
    copy_part = parts[local_count * hidden_width :]
    back_h, back_p = (
        lax.all_to_all(grad_h_buf, "expert", split_axis=0, concat_axis=0, tiled=True),
        lax.all_to_all(grad_p_buf, "expert", split_axis=0, concat_axis=0, tiled=True),
    )
    flat_h = jnp.concatenate([back_h, jnp.zeros((1, hidden_width), back_h.dtype)], axis=0)
    flat_p = jnp.concatenate([back_p, jnp.zeros((1,), back_p.dtype)], axis=0)
    hidden_gradient = flat_h[target].reshape(tok_rows, top_count, hidden_width)
    grad_probs = flat_p[target].reshape(tok_rows, top_count)
    expert_total = dev_count * local_count
    cover = replica_of[None, :] == jnp.arange(expert_total, dtype=jnp.int32)[:, None]
    half_width = d_model // data_count
    halves = lax.all_to_all(copy_part, "dp", split_axis=1, concat_axis=0, tiled=True)
    copy_half = jnp.sum(
        halves.reshape(data_count, hidden_width, half_width).astype(jnp.float32), axis=0
    )
    piece_len = hidden_width * half_width // dev_count
    slabs = copy_half.reshape(dev_count, piece_len)
    arrived = lax.all_to_all(slabs, "expert", split_axis=0, concat_axis=0, tiled=True)
    sums = jnp.dot(cover.astype(jnp.float32), arrived, precision=lax.Precision.HIGHEST)
    homed = lax.all_to_all(
        sums.reshape(dev_count, local_count * piece_len),
        "expert",
        split_axis=0,
        concat_axis=0,
        tiled=True,
    )
    homed = (
        homed.reshape(dev_count, local_count, piece_len)
        .transpose(1, 0, 2)
        .reshape(local_count, hidden_width, half_width)
    )
    home_half = lax.psum_scatter(
        home_part.astype(jnp.float32).astype(jnp.bfloat16), "dp", scatter_dimension=2, tiled=True
    ).astype(jnp.float32)
    grad_weights = (home_half + homed).astype(jnp.bfloat16)
    return (hidden_gradient, grad_probs, grad_weights)


SLOT = 3
HOME, COPIES = "home", "copies"
F32 = jnp.float32
BF16 = jnp.bfloat16
NT = (((1,), (1,)), ((), ()))
TN = (((0,), (0,)), ((), ()))


def iota(shape, dim):
    return lax.broadcasted_iota(jnp.int32, shape, dim)


def dispatch_kernel(local_count, dev_count, packing, *refs):
    sources, refs = refs[:6], refs[6:]
    pick_ref, expert_ref, hs_ref, ps_ref = refs[:4]
    packed, (held, wide, sems) = refs[4:4 + len(packing)], (refs[-8:-2], refs[-2], refs[-1])
    moves = [pltpu.make_async_copy(s, h, sems.at[n]) for n, (s, h) in enumerate(zip(sources, held))]
    for move in moves:
        move.start()
    replica_ref, counts_ref, ids_ref, probs_ref, hid_ref, cot_ref = held
    top, toks = ids_ref.shape
    per_home = local_count * SLOT
    homes = dev_count * per_home
    slots = homes + dev_count * CAPR
    me = lax.axis_index("expert")
    for move in moves[:3]:
        move.wait()
    row = iota((slots, toks), 0)
    expert = ((row // per_home) ^ me) * local_count + (row % per_home) // SLOT
    within = row % SLOT
    allowed = jnp.where(within < CAPH, 1, 0)
    for d in range(dev_count):
        first = homes + d * CAPR
        mine = (row >= first) & (row < first + CAPR)
        expert = jnp.where(mine, replica_ref[d], expert)
        within = jnp.where(mine, row - first, within)
        allowed = jnp.where(mine, jnp.where(row - first < counts_ref[0, d], 1, 0), allowed)
    lower = jnp.zeros((slots, toks), jnp.int32)
    for d in range(dev_count):
        earlier = (row < homes) | (row >= homes + (d + 1) * CAPR)
        lower = lower + jnp.where(earlier & (expert == replica_ref[d]), counts_ref[0, d], 0)
    ids = ids_ref[...]
    named = jnp.zeros((slots, toks), F32)
    for k in range(top):
        named = named + jnp.where(ids[k:k + 1, :] == expert, 1.0, 0.0)
    before = jnp.where(iota((toks, toks), 0) < iota((toks, toks), 1), 1.0, 0.0).astype(BF16)
    rank = jnp.dot(named.astype(BF16), before, preferred_element_type=F32)
    wanted = (lower + within).astype(F32)
    pick = jnp.where((rank == wanted) & (allowed > 0), named, 0.0)
    pick_ref[...] = pick
    expert_ref[...] = expert
    for move in moves[3:5]:
        move.wait()
    wide[...] = hid_ref[...].astype(F32)
    p_slot = jnp.zeros((slots, toks), F32)
    probs = probs_ref[...].astype(F32)
    chosen, values = [], []
    for k in range(top):
        sel = jnp.where(ids[k:k + 1, :] == expert, pick, 0.0)
        chosen.append(sel.astype(BF16))
        values.append(wide[pl.ds(k, toks, stride=top), :].astype(BF16))
        p_slot = p_slot + sel * probs[k:k + 1, :]
    h_slot = jnp.dot(
        jnp.concatenate(chosen, axis=1), jnp.concatenate(values, axis=0), preferred_element_type=F32)
    p_slot = jnp.sum(p_slot, axis=1, keepdims=True)
    hs_ref[...] = h_slot
    ps_ref[...] = jnp.broadcast_to(p_slot, ps_ref.shape)
    scaled = p_slot * h_slot
    moves[5].wait()
    rows = jnp.dot(pick.astype(BF16), cot_ref[...], preferred_element_type=F32)
    d_model = cot_ref.shape[1]
    for out_ref, blocks in zip(packed, packing):
        spans = [(homes, slots) if b == COPIES else (b * per_home, (b + 1) * per_home) for b in blocks]
        out_ref[:, :d_model] = jnp.concatenate([rows[i:j] for i, j in spans], axis=0).astype(BF16)
        out_ref[:, d_model:] = jnp.concatenate([scaled[i:j] for i, j in spans], axis=0).astype(BF16)


def padded(rows):
    return -(-rows // 16) * 16


def stack(order, blocks, height):
    values = [blocks[key] for key in order]
    missing = height - sum(v.shape[0] for v in values)
    if missing:
        values.append(jnp.zeros((missing, values[0].shape[1]), values[0].dtype))
    return jnp.concatenate(values, axis=0)


def slots_of(order, slot_ref, per_home, height):
    kinds = {HOME: slot_ref[:per_home], COPIES: slot_ref[per_home:]}
    return stack(order, {key: kinds[key[1]] for key in order}, height)


def fill_rows(order, pieces, per_home, per_copy, piece_refs, rows_ref):
    values = [r[...].astype(F32) for r in piece_refs]
    blocks = {}
    for key in order:
        n, start = pieces[key]
        blocks[key] = values[n][start:start + (per_home if key[1] == HOME else per_copy)]
    rows_ref[...] = stack(order, blocks, rows_ref.shape[0]).astype(BF16)


def own_columns(rows_ref, w_ref, slot, local_count):
    d_model = w_ref.shape[1]
    width = w_ref.shape[0] // local_count
    every = lax.dot_general(rows_ref[:, :d_model], w_ref[...], NT, preferred_element_type=F32)
    own = jnp.zeros((rows_ref.shape[0], width), F32)
    for e in range(local_count):
        own = jnp.where(slot == e, every[:, e * width:(e + 1) * width], own)
    return own


def hold_kernel(local_count, dev_count, replica_ref, w_hbm, own_hbm, even_hbm,
                own_ref, even_ref, w_ref, slot_ref, sems):
    moves = [pltpu.make_async_copy(a, b, sems.at[n]) for n, (a, b) in enumerate(
        ((w_hbm, w_ref), (own_hbm, own_ref), (even_hbm, even_ref)))]
    for move in moves:
        move.start()
    per_home, per_copy = local_count * SLOT, dev_count * CAPR
    first = lax.axis_index("expert") * local_count
    width = slot_ref.shape[1]
    slot_ref[:per_home] = iota((per_home, width), 0) // SLOT
    row = iota((per_copy, width), 0)
    copy = jnp.full((per_copy, width), -1, jnp.int32)
    for d in range(dev_count):
        mine = (row >= d * CAPR) & (row < (d + 1) * CAPR)
        copy = jnp.where(mine, replica_ref[d] - first, copy)
    slot_ref[per_home:] = copy
    for move in moves:
        move.wait()


def turn_kernel(local_count, dev_count, beside_ref, even_ref, *line_refs):
    per_home, per_copy = local_count * SLOT, dev_count * CAPR
    beside = beside_ref[...].astype(F32)[per_copy + per_home:]
    even = even_ref[...].astype(F32)
    for n, line_ref in enumerate(line_refs):
        span = slice(n * per_home, (n + 1) * per_home)
        line_ref[...] = jnp.concatenate([even[span], beside[span]], axis=0).astype(BF16)


def early_kernel(local_count, dev_count, order, pieces, w_ref, slot_ref, *refs):
    piece_refs, (rows_ref, own_ref) = refs[:-2], refs[-2:]
    per_home, per_copy = local_count * SLOT, dev_count * CAPR
    fill_rows(order, pieces, per_home, per_copy, piece_refs, rows_ref)
    slot = slots_of(order, slot_ref, per_home, rows_ref.shape[0])
    own_ref[...] = own_columns(rows_ref, w_ref, slot, local_count)


def late_kernel(local_count, dev_count, early, order, pieces, own_ref, w_ref, slot_ref, *refs):
    piece_refs, (rows_ref, back_ref, passed) = refs[:-3], refs[-3:]
    per_home, per_copy = local_count * SLOT, dev_count * CAPR
    fill_rows(order, pieces, per_home, per_copy, piece_refs, rows_ref)
    own = own_columns(rows_ref, w_ref, slots_of(order, slot_ref, per_home, rows_ref.shape[0]), local_count)
    if passed.shape[1] > per_home + per_copy:
        passed[:, per_home + per_copy:] = jnp.zeros_like(passed[:, per_home + per_copy:])
    for keys, value in ((early, own_ref[...]), (order, own)):
        start = 0
        for m, kind in keys:
            lower, size = (0, per_home) if kind == HOME else (per_home, per_copy)
            passed[m, lower:lower + size] = value[start:start + size]
            start += size
    me = lax.axis_index("expert")
    back = jnp.concatenate([passed[me ^ source] for source in range(dev_count)], axis=0)
    back_ref[...] = back.astype(back_ref.dtype)


def grad_weights_half(local_count, dev_count, orders, half, slot_ref, rows_refs, columns):
    start = pl.multiple_of(half * columns, 128)
    spread = []
    for order, ref in zip(orders, rows_refs):
        slot = slots_of(order, slot_ref, local_count * SLOT, ref.shape[0])
        scaled = ref[:, 2 * columns:].astype(F32)
        spread.append(jnp.concatenate([jnp.where(slot == e, scaled, 0.0) for e in range(local_count)], axis=1))
    rows = jnp.concatenate([ref[:, pl.ds(start, columns)] for ref in rows_refs], axis=0)
    return lax.dot_general(
        jnp.concatenate(spread, axis=0).astype(BF16), rows, TN, preferred_element_type=F32)


def other_half_kernel(local_count, dev_count, orders, slot_ref, early_ref, late_ref, out_ref):
    half = 1 - lax.axis_index("dp")
    out_ref[...] = grad_weights_half(
        local_count, dev_count, orders, half, slot_ref, (early_ref, late_ref), out_ref.shape[1]).astype(out_ref.dtype)


def own_half_kernel(local_count, dev_count, orders, slot_ref, early_ref, late_ref, arrived_ref, out_ref):
    half = lax.axis_index("dp")
    total = grad_weights_half(
        local_count, dev_count, orders, half, slot_ref, (early_ref, late_ref), out_ref.shape[1])
    out_ref[...] = (total + arrived_ref[...].astype(F32)).astype(out_ref.dtype)


def combine_kernel(local_count, dev_count, back_ref, pick_ref, expert_ref, hs_ref, ps_ref, ids_ref,
                   grad_h_ref, grad_p_ref, wide, narrow):
    top, toks = ids_ref.shape
    per_home = local_count * SLOT
    me = lax.axis_index("expert")
    back = [back_ref[me ^ m].astype(F32) for m in range(dev_count)]
    slots = pick_ref.shape[0]
    copies = slots - dev_count * per_home
    copy = functools.reduce(jnp.add, [b[per_home:per_home + copies] for b in back])
    grad_in = jnp.concatenate([b[:per_home] for b in back] + [copy], axis=0)
    h_rows = (ps_ref[...] * grad_in).astype(BF16)
    p_rows = jnp.sum(hs_ref[...] * grad_in, axis=1, keepdims=True)
    ids = ids_ref[...]
    pick = pick_ref[...]
    expert = expert_ref[...]
    for k in range(top):
        sel = jnp.where(ids[k:k + 1, :] == expert, pick, 0.0)
        wide[pl.ds(k, toks, stride=top), :] = lax.dot_general(
            sel.astype(BF16), h_rows, TN, preferred_element_type=F32)
        narrow[k:k + 1, :] = jnp.sum(sel * p_rows, axis=0, keepdims=True)
    grad_h_ref[...] = wide[...].astype(grad_h_ref.dtype)
    grad_p_ref[...] = narrow[...].astype(grad_p_ref.dtype)


def call(kernel, out_shape, operands, scratch=(), flops=0, limit=24):
    shapes = jax.tree.leaves(out_shape)
    moved = sum(a.size * a.dtype.itemsize for a in (*(a for _, a in operands), *shapes))
    return pl.pallas_call(
        kernel,
        out_shape=out_shape,
        in_specs=[pl.BlockSpec(memory_space=space) for space, _ in operands],
        out_specs=jax.tree.map(lambda _: pl.BlockSpec(memory_space=pltpu.VMEM), out_shape),
        scratch_shapes=list(scratch),
        compiler_params=pltpu.CompilerParams(vmem_limit_bytes=limit << 20),
        cost_estimate=pl.CostEstimate(flops=flops, bytes_accessed=moved, transcendentals=0),
    )(*(a for _, a in operands))


def swap(x, bits, count):
    return lax.ppermute(x, "expert", [(i, i ^ bits) for i in range(count)])


def gather_body(cotangent, hidden, probs, expert_ids, send_counts, replica_of, weights):
    toks, d_model = cotangent.shape
    top = expert_ids.shape[1]
    width = hidden.shape[2]
    local_count = weights.shape[0]
    dev_count = lax.axis_size("expert")
    homes = dev_count * local_count * SLOT
    copies = dev_count * CAPR
    slots = homes + copies
    rows = homes + dev_count * copies
    columns = d_model // 2
    sizes = (local_count, dev_count)
    ids = expert_ids.T
    shape = jax.ShapeDtypeStruct
    hbm, vmem, smem = pltpu.HBM, pltpu.VMEM, pltpu.SMEM
    sources = (replica_of, send_counts, ids, probs.T, hidden.reshape(toks * top, width), cotangent)
    per_home = local_count * SLOT
    odd, even = range(1, dev_count, 2), range(2, dev_count, 2)
    packing = [[COPIES, *odd], [COPIES], [0, COPIES], [*even]]
    sized = [sum(copies if b == COPIES else per_home for b in blocks) for blocks in packing]
    pick, expert, h_slot, p_slot, to_beside, copy_rows, own_rows, even_rows = call(
        functools.partial(dispatch_kernel, *sizes, packing),
        [shape((slots, toks), F32), shape((slots, toks), jnp.int32), shape((slots, width), F32),
         shape((slots, width), F32)] + [shape((n, d_model + width), BF16) for n in sized],
        [(hbm, a) for a in sources],
        [(smem if n < 2 else vmem)(a.shape, a.dtype) for n, a in enumerate(sources)]
        + [vmem((toks * top, width), F32), pltpu.SemaphoreType.DMA((len(sources),))],
        flops=2 * slots * toks * d_model,
        limit=60,
    )
    beside = swap(to_beside, 1, dev_count)
    far = swap(copy_rows, 4, dev_count)
    near = swap(copy_rows, 2, dev_count)
    flat_w = weights.reshape(local_count * width, d_model)
    own_rows, even_rows, w_held, slot = call(
        functools.partial(hold_kernel, *sizes),
        [shape(a.shape, BF16) for a in (own_rows, even_rows, flat_w)] + [shape((per_home + copies, width), jnp.int32)],
        [(smem, replica_of)] + [(hbm, a) for a in (flat_w, own_rows, even_rows)],
        [pltpu.SemaphoreType.DMA((3,))],
    )
    beside, far, near, own_rows, even_rows, w_held, slot = lax.optimization_barrier(
        (beside, far, near, own_rows, even_rows, w_held, slot))
    far_near = swap(far, 2, dev_count)
    lines = call(
        functools.partial(turn_kernel, *sizes),
        [shape((n, d_model + width), BF16) for n in [2 * per_home] * len(even)],
        [(vmem, a) for a in (beside, even_rows)],
    )
    far_beside, near_beside = swap(far, 1, dev_count), swap(near, 1, dev_count)
    lines = [swap(a, m, dev_count) for a, m in zip(lines, even)]
    pieces = {(0, HOME): (0, 0), (0, COPIES): (0, per_home), (1, COPIES): (1, 0), (1, HOME): (1, copies),
              (2, COPIES): (2, 0), (4, COPIES): (3, 0)}
    orders = [list(pieces)]
    height = padded(sum(per_home if kind == HOME else copies for _, kind in pieces))
    early_rows, own = call(
        functools.partial(early_kernel, *sizes, orders[0], pieces),
        (shape((height, d_model + width), BF16), shape((height, width), F32)),
        [(vmem, a) for a in (w_held, slot, own_rows, beside, near, far)],
        flops=2 * height * d_model * local_count * width * 30,
    )
    far_across = swap(far_near, 1, dev_count)
    arrays = [far_beside, near_beside, far_near, far_across, *lines]
    pieces = {(5, COPIES): (0, 0), (3, COPIES): (1, 0), (6, COPIES): (2, 0), (7, COPIES): (3, 0)}
    for n, m in enumerate(even):
        pieces[m, HOME], pieces[m + 1, HOME] = ((4 + n, k * per_home) for k in range(2))
    orders.append(list(pieces))
    height = padded(sum(per_home if kind == HOME else copies for _, kind in pieces))
    block = padded(per_home + copies)
    late_rows, back = call(
        functools.partial(late_kernel, *sizes, *orders, pieces),
        (shape((height, d_model + width), BF16), shape((dev_count * block, width), BF16)),
        [(vmem, a) for a in (own, w_held, slot, *arrays)],
        [vmem((dev_count, block, width), F32)],
        flops=2 * height * d_model * local_count * width,
    )
    back = lax.all_to_all(back, "expert", split_axis=0, concat_axis=0, tiled=True)
    half_flops = 2 * rows * columns * local_count * width
    halves = (slot, early_rows, late_rows)
    other = call(
        functools.partial(other_half_kernel, *sizes, orders),
        shape((local_count * width, columns), BF16),
        [(vmem, a) for a in halves],
        flops=half_flops,
    )
    arrived = lax.ppermute(other, "dp", [(0, 1), (1, 0)])
    grad_w = call(
        functools.partial(own_half_kernel, *sizes, orders),
        shape((local_count * width, columns), BF16),
        [(vmem, a) for a in (*halves, arrived)],
        flops=30 * half_flops,
    )
    grad_w, pick = lax.optimization_barrier((grad_w, pick))
    grad_h, grad_p = call(
        functools.partial(combine_kernel, *sizes),
        (shape((toks * top, width), BF16), shape((top, toks), BF16)),
        [(vmem, a) for a in (back.reshape(dev_count, block, width), pick, expert, h_slot, p_slot, ids)],
        [vmem((toks * top, width), F32), vmem((top, toks), F32)],
        flops=2 * slots * toks * width * top,
    )
    return (
        grad_h.reshape(toks, top, width),
        grad_p.T,
        grad_w.reshape(local_count, width, columns),
    )


def body(cotangent, hidden, probs, expert_ids, send_counts, replica_of, weights):
    dev_count = lax.axis_size("expert")
    local_count, width, _ = weights.shape
    gathered = dev_count * dev_count * CAPR
    if gathered <= (local_count + 3) * width and dev_count == 8 and lax.axis_size("dp") == 2:
        run = gather_body
    else:
        run = replica_body
    return run(cotangent, hidden, probs, expert_ids, send_counts, replica_of, weights)


def solution(mesh):
    in_specs = (
        P(("groups", "expert", "dp"), None),
        P(("groups", "expert", "dp"), None, None),
        P(("groups", "expert", "dp"), None),
        P(("groups", "expert", "dp"), None),
        P(("groups", "expert", "dp"), None),
        P("groups"),
        P("expert", None, None),
    )
    out_specs = (
        P(("groups", "expert", "dp"), None, None),
        P(("groups", "expert", "dp"), None),
        P(("groups", "expert"), None, "dp"),
    )
    return jax.shard_map(body, mesh=mesh, in_specs=in_specs, out_specs=out_specs, check_vma=False)
```

```python
import functools

import jax
import jax.numpy as jnp
from jax import lax
from jax.experimental import pallas as pl
from jax.experimental.pallas import tpu as pltpu
from jax.sharding import PartitionSpec as P

CAPH = 3
CAPR = 3


def ranks_within(keys):
    total_rows = keys.shape[0]
    sort_order = jnp.argsort(keys * total_rows + jnp.arange(total_rows, dtype=jnp.int32))
    sorted_keys = keys[sort_order]
    first_seen = jnp.searchsorted(sorted_keys, sorted_keys, side="left")
    ranked = jnp.arange(total_rows, dtype=jnp.int32) - first_seen
    return jnp.zeros((total_rows,), jnp.int32).at[sort_order].set(ranked)


def route_rows(ids_block, counts_row, replica_of, local_count, cap_home, cap_copy):
    dev_count = replica_of.shape[0]
    experts = ids_block.reshape(-1)
    rank_expert = ranks_within(experts)
    devices = jnp.arange(dev_count, dtype=jnp.int32)
    same_copy = (replica_of[:, None] == replica_of[None, :]) & (devices[None, :] < devices[:, None])
    lower_rank = jnp.sum(jnp.where(same_copy, counts_row[None, :], 0), axis=1)
    upper_rank = lower_rank + counts_row
    hit_table = (
        (replica_of[None, :] == experts[:, None])
        & (lower_rank[None, :] <= rank_expert[:, None])
        & (rank_expert[:, None] < upper_rank[None, :])
    )
    copied = jnp.any(hit_table, axis=1)
    copy_dev = jnp.sum(jnp.where(hit_table, devices[None, :], 0), axis=1)
    dest_dev = jnp.where(copied, copy_dev, experts // local_count)
    index_of_slot = jnp.where(copied, local_count, experts % local_count)
    rank_bucket = ranks_within(dest_dev * (local_count + 1) + index_of_slot)
    keep_row = rank_bucket < jnp.where(copied, cap_copy, cap_home)
    per_dev = local_count * cap_home + cap_copy
    target = dest_dev * per_dev + index_of_slot * cap_home + rank_bucket
    return jnp.where(keep_row, target, dev_count * per_dev)


def replica_body(cotangent, hidden, probs, expert_ids, send_counts, replica_of, weights):
    tok_rows, d_model = cotangent.shape
    top_count = expert_ids.shape[1]
    hidden_width = hidden.shape[2]
    local_count = weights.shape[0]
    dev_count = lax.axis_size("expert")
    data_count = lax.axis_size("dp")
    per_dev = local_count * CAPH + CAPR
    row_count = tok_rows * top_count
    recv_count = dev_count * per_dev
    target = route_rows(expert_ids, send_counts[0], replica_of, local_count, CAPH, CAPR)
    inverse = (
        jnp.full((recv_count,), row_count, jnp.int32)
        .at[target]
        .set(jnp.arange(row_count, dtype=jnp.int32), mode="drop")
    )
    dy_pad = jnp.concatenate([cotangent, jnp.zeros((1, d_model), cotangent.dtype)], axis=0)
    h_pad = jnp.concatenate(
        [hidden.reshape(row_count, hidden_width), jnp.zeros((1, hidden_width), hidden.dtype)],
        axis=0,
    )
    p_pad = jnp.concatenate([probs.reshape(row_count), jnp.zeros((1,), probs.dtype)], axis=0)
    send_dy = dy_pad[inverse // top_count]
    send_h = h_pad[inverse]
    send_p = p_pad[inverse]
    recv_dy, recv_h, recv_p = (
        lax.all_to_all(send_dy, "expert", split_axis=0, concat_axis=0, tiled=True),
        lax.all_to_all(send_h, "expert", split_axis=0, concat_axis=0, tiled=True),
        lax.all_to_all(send_p, "expert", split_axis=0, concat_axis=0, tiled=True),
    )
    flat_size = hidden_width * d_model
    flat_w = weights.reshape(local_count, flat_size)
    pieces = lax.all_to_all(flat_w, "expert", split_axis=1, concat_axis=0, tiled=True)
    chosen = pieces[replica_of]
    copy_weight = lax.all_to_all(chosen, "expert", split_axis=0, concat_axis=0, tiled=True).reshape(
        hidden_width, d_model
    )
    slot_total = local_count + 1
    home_rows = local_count * CAPH
    row_pos = jnp.arange(recv_count, dtype=jnp.int32) % per_dev
    row_slot = jnp.where(row_pos < home_rows, row_pos // CAPH, local_count)
    all_weights = jnp.concatenate(
        [weights.reshape(local_count * hidden_width, d_model), copy_weight], axis=0
    )
    all_in = lax.dot_general(
        recv_dy, all_weights, (((1,), (1,)), ((), ())), preferred_element_type=jnp.float32
    )
    grad_in = jnp.zeros((recv_count, hidden_width), jnp.float32)
    for slot_num in range(slot_total):
        grad_in = grad_in + jnp.where(
            (row_slot == slot_num)[:, None],
            all_in[:, slot_num * hidden_width : (slot_num + 1) * hidden_width],
            0.0,
        )
    p_wide = recv_p.astype(jnp.float32)[:, None]
    h_wide = recv_h.astype(jnp.float32)
    grad_h_buf = (p_wide * grad_in).astype(jnp.bfloat16)
    grad_p_buf = jnp.sum(h_wide * grad_in, axis=1).astype(jnp.bfloat16)
    scaled = (p_wide * h_wide).astype(jnp.bfloat16)
    zero_rows = jnp.zeros_like(scaled)
    scaled_wide = jnp.concatenate(
        [
            jnp.where((row_slot == slot_num)[:, None], scaled, zero_rows)
            for slot_num in range(slot_total)
        ],
        axis=1,
    )
    parts = lax.dot_general(
        scaled_wide, recv_dy, (((0,), (0,)), ((), ())), preferred_element_type=jnp.float32
    ).astype(jnp.bfloat16)
    home_part = parts[: local_count * hidden_width].reshape(local_count, hidden_width, d_model)
    copy_part = parts[local_count * hidden_width :]
    back_h, back_p = (
        lax.all_to_all(grad_h_buf, "expert", split_axis=0, concat_axis=0, tiled=True),
        lax.all_to_all(grad_p_buf, "expert", split_axis=0, concat_axis=0, tiled=True),
    )
    flat_h = jnp.concatenate([back_h, jnp.zeros((1, hidden_width), back_h.dtype)], axis=0)
    flat_p = jnp.concatenate([back_p, jnp.zeros((1,), back_p.dtype)], axis=0)
    hidden_gradient = flat_h[target].reshape(tok_rows, top_count, hidden_width)
    grad_probs = flat_p[target].reshape(tok_rows, top_count)
    expert_total = dev_count * local_count
    cover = replica_of[None, :] == jnp.arange(expert_total, dtype=jnp.int32)[:, None]
    half_width = d_model // data_count
    halves = lax.all_to_all(copy_part, "dp", split_axis=1, concat_axis=0, tiled=True)
    copy_half = jnp.sum(
        halves.reshape(data_count, hidden_width, half_width).astype(jnp.float32), axis=0
    )
    piece_len = hidden_width * half_width // dev_count
    slabs = copy_half.reshape(dev_count, piece_len)
    arrived = lax.all_to_all(slabs, "expert", split_axis=0, concat_axis=0, tiled=True)
    sums = jnp.dot(cover.astype(jnp.float32), arrived, precision=lax.Precision.HIGHEST)
    homed = lax.all_to_all(
        sums.reshape(dev_count, local_count * piece_len),
        "expert",
        split_axis=0,
        concat_axis=0,
        tiled=True,
    )
    homed = (
        homed.reshape(dev_count, local_count, piece_len)
        .transpose(1, 0, 2)
        .reshape(local_count, hidden_width, half_width)
    )
    home_half = lax.psum_scatter(
        home_part.astype(jnp.float32).astype(jnp.bfloat16), "dp", scatter_dimension=2, tiled=True
    ).astype(jnp.float32)
    grad_weights = (home_half + homed).astype(jnp.bfloat16)
    return (hidden_gradient, grad_probs, grad_weights)


SLOT = 3
HOME, COPIES = "home", "copies"
F32 = jnp.float32
BF16 = jnp.bfloat16
NT = (((1,), (1,)), ((), ()))
TN = (((0,), (0,)), ((), ()))


def iota(shape, dim):
    return lax.broadcasted_iota(jnp.int32, shape, dim)


def dispatch_kernel(local_count, dev_count, packing, *refs):
    sources, refs = refs[:6], refs[6:]
    pick_ref, expert_ref, hs_ref, ps_ref = refs[:4]
    packed, (held, wide, sems) = refs[4:4 + len(packing)], (refs[-8:-2], refs[-2], refs[-1])
    moves = [pltpu.make_async_copy(s, h, sems.at[n]) for n, (s, h) in enumerate(zip(sources, held))]
    for move in moves:
        move.start()
    replica_ref, counts_ref, ids_ref, probs_ref, hid_ref, cot_ref = held
    top, toks = ids_ref.shape
    per_home = local_count * SLOT
    homes = dev_count * per_home
    slots = homes + dev_count * CAPR
    me = lax.axis_index("expert")
    for move in moves[:3]:
        move.wait()
    row = iota((slots, toks), 0)
    expert = ((row // per_home) ^ me) * local_count + (row % per_home) // SLOT
    within = row % SLOT
    allowed = jnp.where(within < CAPH, 1, 0)
    for d in range(dev_count):
        first = homes + d * CAPR
        mine = (row >= first) & (row < first + CAPR)
        expert = jnp.where(mine, replica_ref[d], expert)
        within = jnp.where(mine, row - first, within)
        allowed = jnp.where(mine, jnp.where(row - first < counts_ref[0, d], 1, 0), allowed)
    lower = jnp.zeros((slots, toks), jnp.int32)
    for d in range(dev_count):
        earlier = (row < homes) | (row >= homes + (d + 1) * CAPR)
        lower = lower + jnp.where(earlier & (expert == replica_ref[d]), counts_ref[0, d], 0)
    ids = ids_ref[...]
    named = jnp.zeros((slots, toks), F32)
    for k in range(top):
        named = named + jnp.where(ids[k:k + 1, :] == expert, 1.0, 0.0)
    before = jnp.where(iota((toks, toks), 0) < iota((toks, toks), 1), 1.0, 0.0).astype(BF16)
    rank = jnp.dot(named.astype(BF16), before, preferred_element_type=F32)
    wanted = (lower + within).astype(F32)
    pick = jnp.where((rank == wanted) & (allowed > 0), named, 0.0)
    pick_ref[...] = pick
    expert_ref[...] = expert
    for move in moves[3:5]:
        move.wait()
    wide[...] = hid_ref[...].astype(F32)
    p_slot = jnp.zeros((slots, toks), F32)
    probs = probs_ref[...].astype(F32)
    chosen, values = [], []
    for k in range(top):
        sel = jnp.where(ids[k:k + 1, :] == expert, pick, 0.0)
        chosen.append(sel.astype(BF16))
        values.append(wide[pl.ds(k, toks, stride=top), :].astype(BF16))
        p_slot = p_slot + sel * probs[k:k + 1, :]
    h_slot = jnp.dot(
        jnp.concatenate(chosen, axis=1), jnp.concatenate(values, axis=0), preferred_element_type=F32)
    p_slot = jnp.sum(p_slot, axis=1, keepdims=True)
    hs_ref[...] = h_slot
    ps_ref[...] = jnp.broadcast_to(p_slot, ps_ref.shape)
    scaled = p_slot * h_slot
    moves[5].wait()
    rows = jnp.dot(pick.astype(BF16), cot_ref[...], preferred_element_type=F32)
    d_model = cot_ref.shape[1]
    for out_ref, blocks in zip(packed, packing):
        spans = [(homes, slots) if b == COPIES else (b * per_home, (b + 1) * per_home) for b in blocks]
        out_ref[:, :d_model] = jnp.concatenate([rows[i:j] for i, j in spans], axis=0).astype(BF16)
        out_ref[:, d_model:] = jnp.concatenate([scaled[i:j] for i, j in spans], axis=0).astype(BF16)


def padded(rows):
    return -(-rows // 16) * 16


def stack(order, blocks, height):
    values = [blocks[key] for key in order]
    missing = height - sum(v.shape[0] for v in values)
    if missing:
        values.append(jnp.zeros((missing, values[0].shape[1]), values[0].dtype))
    return jnp.concatenate(values, axis=0)


def slots_of(order, slot_ref, per_home, height):
    kinds = {HOME: slot_ref[:per_home], COPIES: slot_ref[per_home:]}
    return stack(order, {key: kinds[key[1]] for key in order}, height)


def fill_rows(order, pieces, per_home, per_copy, piece_refs, rows_ref):
    values = [r[...].astype(F32) for r in piece_refs]
    blocks = {}
    for key in order:
        n, start = pieces[key]
        blocks[key] = values[n][start:start + (per_home if key[1] == HOME else per_copy)]
    rows_ref[...] = stack(order, blocks, rows_ref.shape[0]).astype(BF16)


def own_columns(rows_ref, w_ref, slot, local_count):
    d_model = w_ref.shape[1]
    width = w_ref.shape[0] // local_count
    every = lax.dot_general(rows_ref[:, :d_model], w_ref[...], NT, preferred_element_type=F32)
    own = jnp.zeros((rows_ref.shape[0], width), F32)
    for e in range(local_count):
        own = jnp.where(slot == e, every[:, e * width:(e + 1) * width], own)
    return own


def hold_kernel(local_count, dev_count, replica_ref, w_hbm, own_hbm, even_hbm,
                own_ref, even_ref, w_ref, slot_ref, sems):
    moves = [pltpu.make_async_copy(a, b, sems.at[n]) for n, (a, b) in enumerate(
        ((w_hbm, w_ref), (own_hbm, own_ref), (even_hbm, even_ref)))]
    for move in moves:
        move.start()
    per_home, per_copy = local_count * SLOT, dev_count * CAPR
    first = lax.axis_index("expert") * local_count
    width = slot_ref.shape[1]
    slot_ref[:per_home] = iota((per_home, width), 0) // SLOT
    row = iota((per_copy, width), 0)
    copy = jnp.full((per_copy, width), -1, jnp.int32)
    for d in range(dev_count):
        mine = (row >= d * CAPR) & (row < (d + 1) * CAPR)
        copy = jnp.where(mine, replica_ref[d] - first, copy)
    slot_ref[per_home:] = copy
    for move in moves:
        move.wait()


def turn_kernel(local_count, dev_count, beside_ref, even_ref, *line_refs):
    per_home, per_copy = local_count * SLOT, dev_count * CAPR
    beside = beside_ref[...].astype(F32)[per_copy + per_home:]
    even = even_ref[...].astype(F32)
    for n, line_ref in enumerate(line_refs):
        span = slice(n * per_home, (n + 1) * per_home)
        line_ref[...] = jnp.concatenate([even[span], beside[span]], axis=0).astype(BF16)


def early_kernel(local_count, dev_count, order, pieces, w_ref, slot_ref, *refs):
    piece_refs, (rows_ref, own_ref) = refs[:-2], refs[-2:]
    per_home, per_copy = local_count * SLOT, dev_count * CAPR
    fill_rows(order, pieces, per_home, per_copy, piece_refs, rows_ref)
    slot = slots_of(order, slot_ref, per_home, rows_ref.shape[0])
    own_ref[...] = own_columns(rows_ref, w_ref, slot, local_count)


def late_kernel(local_count, dev_count, early, order, pieces, own_ref, w_ref, slot_ref, *refs):
    piece_refs, (rows_ref, back_ref, passed) = refs[:-3], refs[-3:]
    per_home, per_copy = local_count * SLOT, dev_count * CAPR
    fill_rows(order, pieces, per_home, per_copy, piece_refs, rows_ref)
    own = own_columns(rows_ref, w_ref, slots_of(order, slot_ref, per_home, rows_ref.shape[0]), local_count)
    if passed.shape[1] > per_home + per_copy:
        passed[:, per_home + per_copy:] = jnp.zeros_like(passed[:, per_home + per_copy:])
    for keys, value in ((early, own_ref[...]), (order, own)):
        start = 0
        for m, kind in keys:
            lower, size = (0, per_home) if kind == HOME else (per_home, per_copy)
            passed[m, lower:lower + size] = value[start:start + size]
            start += size
    me = lax.axis_index("expert")
    back = jnp.concatenate([passed[me ^ source] for source in range(dev_count)], axis=0)
    back_ref[...] = back.astype(back_ref.dtype)


def grad_weights_half(local_count, dev_count, orders, half, slot_ref, rows_refs, columns):
    start = pl.multiple_of(half * columns, 128)
    spread = []
    for order, ref in zip(orders, rows_refs):
        slot = slots_of(order, slot_ref, local_count * SLOT, ref.shape[0])
        scaled = ref[:, 2 * columns:].astype(F32)
        spread.append(jnp.concatenate([jnp.where(slot == e, scaled, 0.0) for e in range(local_count)], axis=1))
    rows = jnp.concatenate([ref[:, pl.ds(start, columns)] for ref in rows_refs], axis=0)
    return lax.dot_general(
        jnp.concatenate(spread, axis=0).astype(BF16), rows, TN, preferred_element_type=F32)


def other_half_kernel(local_count, dev_count, orders, slot_ref, early_ref, late_ref, out_ref):
    half = 1 - lax.axis_index("dp")
    out_ref[...] = grad_weights_half(
        local_count, dev_count, orders, half, slot_ref, (early_ref, late_ref), out_ref.shape[1]).astype(out_ref.dtype)


def own_half_kernel(local_count, dev_count, orders, slot_ref, early_ref, late_ref, arrived_ref, out_ref):
    half = lax.axis_index("dp")
    total = grad_weights_half(
        local_count, dev_count, orders, half, slot_ref, (early_ref, late_ref), out_ref.shape[1])
    out_ref[...] = (total + arrived_ref[...].astype(F32)).astype(out_ref.dtype)


def combine_kernel(local_count, dev_count, back_ref, pick_ref, expert_ref, hs_ref, ps_ref, ids_ref,
                   grad_h_ref, grad_p_ref, wide, narrow):
    top, toks = ids_ref.shape
    per_home = local_count * SLOT
    me = lax.axis_index("expert")
    back = [back_ref[me ^ m].astype(F32) for m in range(dev_count)]
    slots = pick_ref.shape[0]
    copies = slots - dev_count * per_home
    copy = functools.reduce(jnp.add, [b[per_home:per_home + copies] for b in back])
    grad_in = jnp.concatenate([b[:per_home] for b in back] + [copy], axis=0)
    h_rows = (ps_ref[...] * grad_in).astype(BF16)
    p_rows = jnp.sum(hs_ref[...] * grad_in, axis=1, keepdims=True)
    ids = ids_ref[...]
    pick = pick_ref[...]
    expert = expert_ref[...]
    for k in range(top):
        sel = jnp.where(ids[k:k + 1, :] == expert, pick, 0.0)
        wide[pl.ds(k, toks, stride=top), :] = lax.dot_general(
            sel.astype(BF16), h_rows, TN, preferred_element_type=F32)
        narrow[k:k + 1, :] = jnp.sum(sel * p_rows, axis=0, keepdims=True)
    grad_h_ref[...] = wide[...].astype(grad_h_ref.dtype)
    grad_p_ref[...] = narrow[...].astype(grad_p_ref.dtype)


def call(kernel, out_shape, operands, scratch=(), flops=0, limit=24):
    shapes = jax.tree.leaves(out_shape)
    moved = sum(a.size * a.dtype.itemsize for a in (*(a for _, a in operands), *shapes))
    return pl.pallas_call(
        kernel,
        out_shape=out_shape,
        in_specs=[pl.BlockSpec(memory_space=space) for space, _ in operands],
        out_specs=jax.tree.map(lambda _: pl.BlockSpec(memory_space=pltpu.VMEM), out_shape),
        scratch_shapes=list(scratch),
        compiler_params=pltpu.CompilerParams(vmem_limit_bytes=limit << 20),
        cost_estimate=pl.CostEstimate(flops=flops, bytes_accessed=moved, transcendentals=0),
    )(*(a for _, a in operands))


def swap(x, bits, count):
    return lax.ppermute(x, "expert", [(i, i ^ bits) for i in range(count)])


def gather_body(cotangent, hidden, probs, expert_ids, send_counts, replica_of, weights):
    toks, d_model = cotangent.shape
    top = expert_ids.shape[1]
    width = hidden.shape[2]
    local_count = weights.shape[0]
    dev_count = lax.axis_size("expert")
    homes = dev_count * local_count * SLOT
    copies = dev_count * CAPR
    slots = homes + copies
    rows = homes + dev_count * copies
    columns = d_model // 2
    sizes = (local_count, dev_count)
    ids = expert_ids.T
    shape = jax.ShapeDtypeStruct
    hbm, vmem, smem = pltpu.HBM, pltpu.VMEM, pltpu.SMEM
    sources = (replica_of, send_counts, ids, probs.T, hidden.reshape(toks * top, width), cotangent)
    per_home = local_count * SLOT
    odd, even = range(1, dev_count, 2), range(2, dev_count, 2)
    packing = [[COPIES, *odd], [COPIES], [0, COPIES], [*even]]
    sized = [sum(copies if b == COPIES else per_home for b in blocks) for blocks in packing]
    pick, expert, h_slot, p_slot, to_beside, copy_rows, own_rows, even_rows = call(
        functools.partial(dispatch_kernel, *sizes, packing),
        [shape((slots, toks), F32), shape((slots, toks), jnp.int32), shape((slots, width), F32),
         shape((slots, width), F32)] + [shape((n, d_model + width), BF16) for n in sized],
        [(hbm, a) for a in sources],
        [(smem if n < 2 else vmem)(a.shape, a.dtype) for n, a in enumerate(sources)]
        + [vmem((toks * top, width), F32), pltpu.SemaphoreType.DMA((len(sources),))],
        flops=2 * slots * toks * d_model,
        limit=60,
    )
    beside = swap(to_beside, 1, dev_count)
    far = swap(copy_rows, 4, dev_count)
    near = swap(copy_rows, 2, dev_count)
    flat_w = weights.reshape(local_count * width, d_model)
    own_rows, even_rows, w_held, slot = call(
        functools.partial(hold_kernel, *sizes),
        [shape(a.shape, BF16) for a in (own_rows, even_rows, flat_w)] + [shape((per_home + copies, width), jnp.int32)],
        [(smem, replica_of)] + [(hbm, a) for a in (flat_w, own_rows, even_rows)],
        [pltpu.SemaphoreType.DMA((3,))],
    )
    beside, far, near, own_rows, even_rows, w_held, slot = lax.optimization_barrier(
        (beside, far, near, own_rows, even_rows, w_held, slot))
    far_near = swap(far, 2, dev_count)
    lines = call(
        functools.partial(turn_kernel, *sizes),
        [shape((n, d_model + width), BF16) for n in [2 * per_home] * len(even)],
        [(vmem, a) for a in (beside, even_rows)],
    )
    far_beside, near_beside = swap(far, 1, dev_count), swap(near, 1, dev_count)
    lines = [swap(a, m, dev_count) for a, m in zip(lines, even)]
    pieces = {(0, HOME): (0, 0), (0, COPIES): (0, per_home), (1, COPIES): (1, 0), (1, HOME): (1, copies),
              (2, COPIES): (2, 0), (4, COPIES): (3, 0), (5, COPIES): (4, 0), (3, COPIES): (5, 0)}
    orders = [list(pieces)]
    height = padded(sum(per_home if kind == HOME else copies for _, kind in pieces))
    early_rows, own = call(
        functools.partial(early_kernel, *sizes, orders[0], pieces),
        (shape((height, d_model + width), BF16), shape((height, width), F32)),
        [(vmem, a) for a in (w_held, slot, own_rows, beside, near, far, far_beside, near_beside)],
        flops=2 * height * d_model * local_count * width * 30,
    )
    far_across = swap(far_near, 1, dev_count)
    arrays = [far_near, far_across, *lines]
    pieces = {(6, COPIES): (0, 0), (7, COPIES): (1, 0)}
    for n, m in enumerate(even):
        pieces[m, HOME], pieces[m + 1, HOME] = ((2 + n, k * per_home) for k in range(2))
    orders.append(list(pieces))
    height = padded(sum(per_home if kind == HOME else copies for _, kind in pieces))
    block = padded(per_home + copies)
    late_rows, back = call(
        functools.partial(late_kernel, *sizes, *orders, pieces),
        (shape((height, d_model + width), BF16), shape((dev_count * block, width), BF16)),
        [(vmem, a) for a in (own, w_held, slot, *arrays)],
        [vmem((dev_count, block, width), F32)],
        flops=2 * height * d_model * local_count * width,
    )
    back = lax.all_to_all(back, "expert", split_axis=0, concat_axis=0, tiled=True)
    half_flops = 2 * rows * columns * local_count * width
    halves = (slot, early_rows, late_rows)
    other = call(
        functools.partial(other_half_kernel, *sizes, orders),
        shape((local_count * width, columns), BF16),
        [(vmem, a) for a in halves],
        flops=half_flops,
    )
    arrived = lax.ppermute(other, "dp", [(0, 1), (1, 0)])
    grad_w = call(
        functools.partial(own_half_kernel, *sizes, orders),
        shape((local_count * width, columns), BF16),
        [(vmem, a) for a in (*halves, arrived)],
        flops=30 * half_flops,
    )
    grad_w, pick = lax.optimization_barrier((grad_w, pick))
    grad_h, grad_p = call(
        functools.partial(combine_kernel, *sizes),
        (shape((toks * top, width), BF16), shape((top, toks), BF16)),
        [(vmem, a) for a in (back.reshape(dev_count, block, width), pick, expert, h_slot, p_slot, ids)],
        [vmem((toks * top, width), F32), vmem((top, toks), F32)],
        flops=2 * slots * toks * width * top,
    )
    return (
        grad_h.reshape(toks, top, width),
        grad_p.T,
        grad_w.reshape(local_count, width, columns),
    )


def body(cotangent, hidden, probs, expert_ids, send_counts, replica_of, weights):
    dev_count = lax.axis_size("expert")
    local_count, width, _ = weights.shape
    gathered = dev_count * dev_count * CAPR
    if gathered <= (local_count + 3) * width and dev_count == 8 and lax.axis_size("dp") == 2:
        run = gather_body
    else:
        run = replica_body
    return run(cotangent, hidden, probs, expert_ids, send_counts, replica_of, weights)


def solution(mesh):
    in_specs = (
        P(("groups", "expert", "dp"), None),
        P(("groups", "expert", "dp"), None, None),
        P(("groups", "expert", "dp"), None),
        P(("groups", "expert", "dp"), None),
        P(("groups", "expert", "dp"), None),
        P("groups"),
        P("expert", None, None),
    )
    out_specs = (
        P(("groups", "expert", "dp"), None, None),
        P(("groups", "expert", "dp"), None),
        P(("groups", "expert"), None, "dp"),
    )
    return jax.shard_map(body, mesh=mesh, in_specs=in_specs, out_specs=out_specs, check_vma=False)
```

```python
import functools

import jax
import jax.numpy as jnp
from jax import lax
from jax.experimental import pallas as pl
from jax.experimental.pallas import tpu as pltpu
from jax.sharding import PartitionSpec as P

CAPH = 3
CAPR = 3


def ranks_within(keys):
    total_rows = keys.shape[0]
    sort_order = jnp.argsort(keys * total_rows + jnp.arange(total_rows, dtype=jnp.int32))
    sorted_keys = keys[sort_order]
    first_seen = jnp.searchsorted(sorted_keys, sorted_keys, side="left")
    ranked = jnp.arange(total_rows, dtype=jnp.int32) - first_seen
    return jnp.zeros((total_rows,), jnp.int32).at[sort_order].set(ranked)


def route_rows(ids_block, counts_row, replica_of, local_count, cap_home, cap_copy):
    dev_count = replica_of.shape[0]
    experts = ids_block.reshape(-1)
    rank_expert = ranks_within(experts)
    devices = jnp.arange(dev_count, dtype=jnp.int32)
    same_copy = (replica_of[:, None] == replica_of[None, :]) & (devices[None, :] < devices[:, None])
    lower_rank = jnp.sum(jnp.where(same_copy, counts_row[None, :], 0), axis=1)
    upper_rank = lower_rank + counts_row
    hit_table = (
        (replica_of[None, :] == experts[:, None])
        & (lower_rank[None, :] <= rank_expert[:, None])
        & (rank_expert[:, None] < upper_rank[None, :])
    )
    copied = jnp.any(hit_table, axis=1)
    copy_dev = jnp.sum(jnp.where(hit_table, devices[None, :], 0), axis=1)
    dest_dev = jnp.where(copied, copy_dev, experts // local_count)
    index_of_slot = jnp.where(copied, local_count, experts % local_count)
    rank_bucket = ranks_within(dest_dev * (local_count + 1) + index_of_slot)
    keep_row = rank_bucket < jnp.where(copied, cap_copy, cap_home)
    per_dev = local_count * cap_home + cap_copy
    target = dest_dev * per_dev + index_of_slot * cap_home + rank_bucket
    return jnp.where(keep_row, target, dev_count * per_dev)


def replica_body(cotangent, hidden, probs, expert_ids, send_counts, replica_of, weights):
    tok_rows, d_model = cotangent.shape
    top_count = expert_ids.shape[1]
    hidden_width = hidden.shape[2]
    local_count = weights.shape[0]
    dev_count = lax.axis_size("expert")
    data_count = lax.axis_size("dp")
    per_dev = local_count * CAPH + CAPR
    row_count = tok_rows * top_count
    recv_count = dev_count * per_dev
    target = route_rows(expert_ids, send_counts[0], replica_of, local_count, CAPH, CAPR)
    inverse = (
        jnp.full((recv_count,), row_count, jnp.int32)
        .at[target]
        .set(jnp.arange(row_count, dtype=jnp.int32), mode="drop")
    )
    dy_pad = jnp.concatenate([cotangent, jnp.zeros((1, d_model), cotangent.dtype)], axis=0)
    h_pad = jnp.concatenate(
        [hidden.reshape(row_count, hidden_width), jnp.zeros((1, hidden_width), hidden.dtype)],
        axis=0,
    )
    p_pad = jnp.concatenate([probs.reshape(row_count), jnp.zeros((1,), probs.dtype)], axis=0)
    send_dy = dy_pad[inverse // top_count]
    send_h = h_pad[inverse]
    send_p = p_pad[inverse]
    recv_dy, recv_h, recv_p = (
        lax.all_to_all(send_dy, "expert", split_axis=0, concat_axis=0, tiled=True),
        lax.all_to_all(send_h, "expert", split_axis=0, concat_axis=0, tiled=True),
        lax.all_to_all(send_p, "expert", split_axis=0, concat_axis=0, tiled=True),
    )
    flat_size = hidden_width * d_model
    flat_w = weights.reshape(local_count, flat_size)
    pieces = lax.all_to_all(flat_w, "expert", split_axis=1, concat_axis=0, tiled=True)
    chosen = pieces[replica_of]
    copy_weight = lax.all_to_all(chosen, "expert", split_axis=0, concat_axis=0, tiled=True).reshape(
        hidden_width, d_model
    )
    slot_total = local_count + 1
    home_rows = local_count * CAPH
    row_pos = jnp.arange(recv_count, dtype=jnp.int32) % per_dev
    row_slot = jnp.where(row_pos < home_rows, row_pos // CAPH, local_count)
    all_weights = jnp.concatenate(
        [weights.reshape(local_count * hidden_width, d_model), copy_weight], axis=0
    )
    all_in = lax.dot_general(
        recv_dy, all_weights, (((1,), (1,)), ((), ())), preferred_element_type=jnp.float32
    )
    grad_in = jnp.zeros((recv_count, hidden_width), jnp.float32)
    for slot_num in range(slot_total):
        grad_in = grad_in + jnp.where(
            (row_slot == slot_num)[:, None],
            all_in[:, slot_num * hidden_width : (slot_num + 1) * hidden_width],
            0.0,
        )
    p_wide = recv_p.astype(jnp.float32)[:, None]
    h_wide = recv_h.astype(jnp.float32)
    grad_h_buf = (p_wide * grad_in).astype(jnp.bfloat16)
    grad_p_buf = jnp.sum(h_wide * grad_in, axis=1).astype(jnp.bfloat16)
    scaled = (p_wide * h_wide).astype(jnp.bfloat16)
    zero_rows = jnp.zeros_like(scaled)
    scaled_wide = jnp.concatenate(
        [
            jnp.where((row_slot == slot_num)[:, None], scaled, zero_rows)
            for slot_num in range(slot_total)
        ],
        axis=1,
    )
    parts = lax.dot_general(
        scaled_wide, recv_dy, (((0,), (0,)), ((), ())), preferred_element_type=jnp.float32
    ).astype(jnp.bfloat16)
    home_part = parts[: local_count * hidden_width].reshape(local_count, hidden_width, d_model)
    copy_part = parts[local_count * hidden_width :]
    back_h, back_p = (
        lax.all_to_all(grad_h_buf, "expert", split_axis=0, concat_axis=0, tiled=True),
        lax.all_to_all(grad_p_buf, "expert", split_axis=0, concat_axis=0, tiled=True),
    )
    flat_h = jnp.concatenate([back_h, jnp.zeros((1, hidden_width), back_h.dtype)], axis=0)
    flat_p = jnp.concatenate([back_p, jnp.zeros((1,), back_p.dtype)], axis=0)
    hidden_gradient = flat_h[target].reshape(tok_rows, top_count, hidden_width)
    grad_probs = flat_p[target].reshape(tok_rows, top_count)
    expert_total = dev_count * local_count
    cover = replica_of[None, :] == jnp.arange(expert_total, dtype=jnp.int32)[:, None]
    half_width = d_model // data_count
    halves = lax.all_to_all(copy_part, "dp", split_axis=1, concat_axis=0, tiled=True)
    copy_half = jnp.sum(
        halves.reshape(data_count, hidden_width, half_width).astype(jnp.float32), axis=0
    )
    piece_len = hidden_width * half_width // dev_count
    slabs = copy_half.reshape(dev_count, piece_len)
    arrived = lax.all_to_all(slabs, "expert", split_axis=0, concat_axis=0, tiled=True)
    sums = jnp.dot(cover.astype(jnp.float32), arrived, precision=lax.Precision.HIGHEST)
    homed = lax.all_to_all(
        sums.reshape(dev_count, local_count * piece_len),
        "expert",
        split_axis=0,
        concat_axis=0,
        tiled=True,
    )
    homed = (
        homed.reshape(dev_count, local_count, piece_len)
        .transpose(1, 0, 2)
        .reshape(local_count, hidden_width, half_width)
    )
    home_half = lax.psum_scatter(
        home_part.astype(jnp.float32).astype(jnp.bfloat16), "dp", scatter_dimension=2, tiled=True
    ).astype(jnp.float32)
    grad_weights = (home_half + homed).astype(jnp.bfloat16)
    return (hidden_gradient, grad_probs, grad_weights)


SLOT = 3
HOME, COPIES = "home", "copies"
F32 = jnp.float32
BF16 = jnp.bfloat16
NT = (((1,), (1,)), ((), ()))
TN = (((0,), (0,)), ((), ()))


def iota(shape, dim):
    return lax.broadcasted_iota(jnp.int32, shape, dim)


def dispatch_kernel(local_count, dev_count, packing, *refs):
    sources, refs = refs[:6], refs[6:]
    pick_ref, expert_ref, hs_ref, ps_ref = refs[:4]
    packed, (held, wide, sems) = refs[4:4 + len(packing)], (refs[-8:-2], refs[-2], refs[-1])
    moves = [pltpu.make_async_copy(s, h, sems.at[n]) for n, (s, h) in enumerate(zip(sources, held))]
    for move in moves:
        move.start()
    replica_ref, counts_ref, ids_ref, probs_ref, hid_ref, cot_ref = held
    top, toks = ids_ref.shape
    per_home = local_count * SLOT
    homes = dev_count * per_home
    slots = homes + dev_count * CAPR
    me = lax.axis_index("expert")
    for move in moves[:3]:
        move.wait()
    row = iota((slots, toks), 0)
    expert = ((row // per_home) ^ me) * local_count + (row % per_home) // SLOT
    within = row % SLOT
    allowed = jnp.where(within < CAPH, 1, 0)
    for d in range(dev_count):
        first = homes + d * CAPR
        mine = (row >= first) & (row < first + CAPR)
        expert = jnp.where(mine, replica_ref[d], expert)
        within = jnp.where(mine, row - first, within)
        allowed = jnp.where(mine, jnp.where(row - first < counts_ref[0, d], 1, 0), allowed)
    lower = jnp.zeros((slots, toks), jnp.int32)
    for d in range(dev_count):
        earlier = (row < homes) | (row >= homes + (d + 1) * CAPR)
        lower = lower + jnp.where(earlier & (expert == replica_ref[d]), counts_ref[0, d], 0)
    ids = ids_ref[...]
    named = jnp.zeros((slots, toks), F32)
    for k in range(top):
        named = named + jnp.where(ids[k:k + 1, :] == expert, 1.0, 0.0)
    before = jnp.where(iota((toks, toks), 0) < iota((toks, toks), 1), 1.0, 0.0).astype(BF16)
    rank = jnp.dot(named.astype(BF16), before, preferred_element_type=F32)
    wanted = (lower + within).astype(F32)
    pick = jnp.where((rank == wanted) & (allowed > 0), named, 0.0)
    pick_ref[...] = pick
    expert_ref[...] = expert
    for move in moves[3:5]:
        move.wait()
    wide[...] = hid_ref[...].astype(F32)
    p_slot = jnp.zeros((slots, toks), F32)
    probs = probs_ref[...].astype(F32)
    chosen, values = [], []
    for k in range(top):
        sel = jnp.where(ids[k:k + 1, :] == expert, pick, 0.0)
        chosen.append(sel.astype(BF16))
        values.append(wide[pl.ds(k, toks, stride=top), :].astype(BF16))
        p_slot = p_slot + sel * probs[k:k + 1, :]
    h_slot = jnp.dot(
        jnp.concatenate(chosen, axis=1), jnp.concatenate(values, axis=0), preferred_element_type=F32)
    p_slot = jnp.sum(p_slot, axis=1, keepdims=True)
    hs_ref[...] = h_slot
    ps_ref[...] = jnp.broadcast_to(p_slot, ps_ref.shape)
    scaled = p_slot * h_slot
    moves[5].wait()
    rows = jnp.dot(pick.astype(BF16), cot_ref[...], preferred_element_type=F32)
    d_model = cot_ref.shape[1]
    for out_ref, blocks in zip(packed, packing):
        spans = [(homes, slots) if b == COPIES else (b * per_home, (b + 1) * per_home) for b in blocks]
        out_ref[:, :d_model] = jnp.concatenate([rows[i:j] for i, j in spans], axis=0).astype(BF16)
        out_ref[:, d_model:] = jnp.concatenate([scaled[i:j] for i, j in spans], axis=0).astype(BF16)


def padded(rows):
    return -(-rows // 16) * 16


def stack(order, blocks, height):
    values = [blocks[key] for key in order]
    missing = height - sum(v.shape[0] for v in values)
    if missing:
        values.append(jnp.zeros((missing, values[0].shape[1]), values[0].dtype))
    return jnp.concatenate(values, axis=0)


def slots_of(order, slot_ref, per_home, height):
    kinds = {HOME: slot_ref[:per_home], COPIES: slot_ref[per_home:]}
    return stack(order, {key: kinds[key[1]] for key in order}, height)


def fill_rows(order, pieces, per_home, per_copy, piece_refs, rows_ref):
    values = [r[...].astype(F32) for r in piece_refs]
    blocks = {}
    for key in order:
        n, start = pieces[key]
        blocks[key] = values[n][start:start + (per_home if key[1] == HOME else per_copy)]
    rows_ref[...] = stack(order, blocks, rows_ref.shape[0]).astype(BF16)


def own_columns(rows_ref, w_ref, slot, local_count):
    d_model = w_ref.shape[1]
    width = w_ref.shape[0] // local_count
    every = lax.dot_general(rows_ref[:, :d_model], w_ref[...], NT, preferred_element_type=F32)
    own = jnp.zeros((rows_ref.shape[0], width), F32)
    for e in range(local_count):
        own = jnp.where(slot == e, every[:, e * width:(e + 1) * width], own)
    return own


def hold_kernel(local_count, dev_count, replica_ref, w_hbm, own_hbm, even_hbm,
                own_ref, even_ref, w_ref, slot_ref, sems):
    moves = [pltpu.make_async_copy(a, b, sems.at[n]) for n, (a, b) in enumerate(
        ((w_hbm, w_ref), (own_hbm, own_ref), (even_hbm, even_ref)))]
    for move in moves:
        move.start()
    per_home, per_copy = local_count * SLOT, dev_count * CAPR
    first = lax.axis_index("expert") * local_count
    width = slot_ref.shape[1]
    slot_ref[:per_home] = iota((per_home, width), 0) // SLOT
    row = iota((per_copy, width), 0)
    copy = jnp.full((per_copy, width), -1, jnp.int32)
    for d in range(dev_count):
        mine = (row >= d * CAPR) & (row < (d + 1) * CAPR)
        copy = jnp.where(mine, replica_ref[d] - first, copy)
    slot_ref[per_home:] = copy
    for move in moves:
        move.wait()


def turn_kernel(local_count, dev_count, beside_ref, even_ref, *line_refs):
    per_home, per_copy = local_count * SLOT, dev_count * CAPR
    beside = beside_ref[...].astype(F32)[per_copy + per_home:]
    even = even_ref[...].astype(F32)
    for n, line_ref in enumerate(line_refs):
        span = slice(n * per_home, (n + 1) * per_home)
        line_ref[...] = jnp.concatenate([even[span], beside[span]], axis=0).astype(BF16)


def early_kernel(local_count, dev_count, order, pieces, w_ref, slot_ref, *refs):
    piece_refs, (rows_ref, own_ref) = refs[:-2], refs[-2:]
    per_home, per_copy = local_count * SLOT, dev_count * CAPR
    fill_rows(order, pieces, per_home, per_copy, piece_refs, rows_ref)
    slot = slots_of(order, slot_ref, per_home, rows_ref.shape[0])
    own_ref[...] = own_columns(rows_ref, w_ref, slot, local_count)


def late_kernel(local_count, dev_count, early, order, pieces, own_ref, w_ref, slot_ref, *refs):
    piece_refs, (rows_ref, back_ref, passed) = refs[:-3], refs[-3:]
    per_home, per_copy = local_count * SLOT, dev_count * CAPR
    fill_rows(order, pieces, per_home, per_copy, piece_refs, rows_ref)
    own = own_columns(rows_ref, w_ref, slots_of(order, slot_ref, per_home, rows_ref.shape[0]), local_count)
    if passed.shape[1] > per_home + per_copy:
        passed[:, per_home + per_copy:] = jnp.zeros_like(passed[:, per_home + per_copy:])
    for keys, value in ((early, own_ref[...]), (order, own)):
        start = 0
        for m, kind in keys:
            lower, size = (0, per_home) if kind == HOME else (per_home, per_copy)
            passed[m, lower:lower + size] = value[start:start + size]
            start += size
    me = lax.axis_index("expert")
    back = jnp.concatenate([passed[me ^ source] for source in range(dev_count)], axis=0)
    back_ref[...] = back.astype(back_ref.dtype)


def grad_weights_half(local_count, dev_count, orders, half, slot_ref, rows_refs, columns):
    start = pl.multiple_of(half * columns, 128)
    spread = []
    for order, ref in zip(orders, rows_refs):
        slot = slots_of(order, slot_ref, local_count * SLOT, ref.shape[0])
        scaled = ref[:, 2 * columns:].astype(F32)
        spread.append(jnp.concatenate([jnp.where(slot == e, scaled, 0.0) for e in range(local_count)], axis=1))
    rows = jnp.concatenate([ref[:, pl.ds(start, columns)] for ref in rows_refs], axis=0)
    return lax.dot_general(
        jnp.concatenate(spread, axis=0).astype(BF16), rows, TN, preferred_element_type=F32)


def other_half_kernel(local_count, dev_count, orders, slot_ref, early_ref, late_ref, out_ref):
    half = 1 - lax.axis_index("dp")
    out_ref[...] = grad_weights_half(
        local_count, dev_count, orders, half, slot_ref, (early_ref, late_ref), out_ref.shape[1]).astype(out_ref.dtype)


def own_half_kernel(local_count, dev_count, orders, slot_ref, early_ref, late_ref, arrived_ref, out_ref):
    half = lax.axis_index("dp")
    total = grad_weights_half(
        local_count, dev_count, orders, half, slot_ref, (early_ref, late_ref), out_ref.shape[1])
    out_ref[...] = (total + arrived_ref[...].astype(F32)).astype(out_ref.dtype)


def combine_kernel(local_count, dev_count, back_ref, pick_ref, expert_ref, hs_ref, ps_ref, ids_ref,
                   grad_h_ref, grad_p_ref, wide, narrow):
    top, toks = ids_ref.shape
    per_home = local_count * SLOT
    me = lax.axis_index("expert")
    back = [back_ref[me ^ m].astype(F32) for m in range(dev_count)]
    slots = pick_ref.shape[0]
    copies = slots - dev_count * per_home
    copy = functools.reduce(jnp.add, [b[per_home:per_home + copies] for b in back])
    grad_in = jnp.concatenate([b[:per_home] for b in back] + [copy], axis=0)
    h_rows = (ps_ref[...] * grad_in).astype(BF16)
    p_rows = jnp.sum(hs_ref[...] * grad_in, axis=1, keepdims=True)
    ids = ids_ref[...]
    pick = pick_ref[...]
    expert = expert_ref[...]
    for k in range(top):
        sel = jnp.where(ids[k:k + 1, :] == expert, pick, 0.0)
        wide[pl.ds(k, toks, stride=top), :] = lax.dot_general(
            sel.astype(BF16), h_rows, TN, preferred_element_type=F32)
        narrow[k:k + 1, :] = jnp.sum(sel * p_rows, axis=0, keepdims=True)
    grad_h_ref[...] = wide[...].astype(grad_h_ref.dtype)
    grad_p_ref[...] = narrow[...].astype(grad_p_ref.dtype)


def call(kernel, out_shape, operands, scratch=(), flops=0, limit=24):
    shapes = jax.tree.leaves(out_shape)
    moved = sum(a.size * a.dtype.itemsize for a in (*(a for _, a in operands), *shapes))
    return pl.pallas_call(
        kernel,
        out_shape=out_shape,
        in_specs=[pl.BlockSpec(memory_space=space) for space, _ in operands],
        out_specs=jax.tree.map(lambda _: pl.BlockSpec(memory_space=pltpu.VMEM), out_shape),
        scratch_shapes=list(scratch),
        compiler_params=pltpu.CompilerParams(vmem_limit_bytes=limit << 20),
        cost_estimate=pl.CostEstimate(flops=flops, bytes_accessed=moved, transcendentals=0),
    )(*(a for _, a in operands))


def swap(x, bits, count):
    return lax.ppermute(x, "expert", [(i, i ^ bits) for i in range(count)])


def gather_body(cotangent, hidden, probs, expert_ids, send_counts, replica_of, weights):
    toks, d_model = cotangent.shape
    top = expert_ids.shape[1]
    width = hidden.shape[2]
    local_count = weights.shape[0]
    dev_count = lax.axis_size("expert")
    homes = dev_count * local_count * SLOT
    copies = dev_count * CAPR
    slots = homes + copies
    rows = homes + dev_count * copies
    columns = d_model // 2
    sizes = (local_count, dev_count)
    ids = expert_ids.T
    shape = jax.ShapeDtypeStruct
    hbm, vmem, smem = pltpu.HBM, pltpu.VMEM, pltpu.SMEM
    sources = (replica_of, send_counts, ids, probs.T, hidden.reshape(toks * top, width), cotangent)
    per_home = local_count * SLOT
    odd, even = range(1, dev_count, 2), range(2, dev_count, 2)
    packing = [[COPIES, *odd], [COPIES], [0, COPIES], [*even]]
    sized = [sum(copies if b == COPIES else per_home for b in blocks) for blocks in packing]
    pick, expert, h_slot, p_slot, to_beside, copy_rows, own_rows, even_rows = call(
        functools.partial(dispatch_kernel, *sizes, packing),
        [shape((slots, toks), F32), shape((slots, toks), jnp.int32), shape((slots, width), F32),
         shape((slots, width), F32)] + [shape((n, d_model + width), BF16) for n in sized],
        [(hbm, a) for a in sources],
        [(smem if n < 2 else vmem)(a.shape, a.dtype) for n, a in enumerate(sources)]
        + [vmem((toks * top, width), F32), pltpu.SemaphoreType.DMA((len(sources),))],
        flops=2 * slots * toks * d_model,
        limit=60,
    )
    beside = swap(to_beside, 1, dev_count)
    near = swap(copy_rows, 2, dev_count)
    far = swap(copy_rows, 4, dev_count)
    flat_w = weights.reshape(local_count * width, d_model)
    own_rows, even_rows, w_held, slot = call(
        functools.partial(hold_kernel, *sizes),
        [shape(a.shape, BF16) for a in (own_rows, even_rows, flat_w)] + [shape((per_home + copies, width), jnp.int32)],
        [(smem, replica_of)] + [(hbm, a) for a in (flat_w, own_rows, even_rows)],
        [pltpu.SemaphoreType.DMA((3,))],
    )
    near, far, beside, own_rows, even_rows, w_held, slot = lax.optimization_barrier(
        (near, far, beside, own_rows, even_rows, w_held, slot))
    far_near = swap(far, 2, dev_count)
    lines = call(
        functools.partial(turn_kernel, *sizes),
        [shape((n, d_model + width), BF16) for n in [2 * per_home] * len(even)],
        [(vmem, a) for a in (beside, even_rows)],
    )
    far_beside, near_beside = swap(far, 1, dev_count), swap(near, 1, dev_count)
    lines = [swap(a, m, dev_count) for a, m in zip(lines, even)]
    pieces = {(0, HOME): (0, 0), (0, COPIES): (0, per_home), (1, COPIES): (1, 0), (1, HOME): (1, copies),
              (2, COPIES): (2, 0), (4, COPIES): (3, 0), (5, COPIES): (4, 0), (3, COPIES): (5, 0)}
    orders = [list(pieces)]
    height = padded(sum(per_home if kind == HOME else copies for _, kind in pieces))
    early_rows, own = call(
        functools.partial(early_kernel, *sizes, orders[0], pieces),
        (shape((height, d_model + width), BF16), shape((height, width), F32)),
        [(vmem, a) for a in (w_held, slot, own_rows, beside, near, far, far_beside, near_beside)],
        flops=2 * height * d_model * local_count * width * 30,
    )
    far_across = swap(far_near, 1, dev_count)
    arrays = [far_near, far_across, *lines[::-1]]
    pieces = {(6, COPIES): (0, 0), (7, COPIES): (1, 0)}
    for n, m in enumerate(even[::-1]):
        pieces[m, HOME], pieces[m + 1, HOME] = ((2 + n, k * per_home) for k in range(2))
    orders.append(list(pieces))
    height = padded(sum(per_home if kind == HOME else copies for _, kind in pieces))
    block = padded(per_home + copies)
    late_rows, back = call(
        functools.partial(late_kernel, *sizes, *orders, pieces),
        (shape((height, d_model + width), BF16), shape((dev_count * block, width), BF16)),
        [(vmem, a) for a in (own, w_held, slot, *arrays)],
        [vmem((dev_count, block, width), F32)],
        flops=2 * height * d_model * local_count * width,
    )
    back = lax.all_to_all(back, "expert", split_axis=0, concat_axis=0, tiled=True)
    half_flops = 2 * rows * columns * local_count * width
    halves = (slot, early_rows, late_rows)
    other = call(
        functools.partial(other_half_kernel, *sizes, orders),
        shape((local_count * width, columns), BF16),
        [(vmem, a) for a in halves],
        flops=half_flops,
    )
    arrived = lax.ppermute(other, "dp", [(0, 1), (1, 0)])
    grad_w = call(
        functools.partial(own_half_kernel, *sizes, orders),
        shape((local_count * width, columns), BF16),
        [(vmem, a) for a in (*halves, arrived)],
        flops=30 * half_flops,
    )
    grad_w, pick = lax.optimization_barrier((grad_w, pick))
    grad_h, grad_p = call(
        functools.partial(combine_kernel, *sizes),
        (shape((toks * top, width), BF16), shape((top, toks), BF16)),
        [(vmem, a) for a in (back.reshape(dev_count, block, width), pick, expert, h_slot, p_slot, ids)],
        [vmem((toks * top, width), F32), vmem((top, toks), F32)],
        flops=2 * slots * toks * width * top,
    )
    return (
        grad_h.reshape(toks, top, width),
        grad_p.T,
        grad_w.reshape(local_count, width, columns),
    )


def body(cotangent, hidden, probs, expert_ids, send_counts, replica_of, weights):
    dev_count = lax.axis_size("expert")
    local_count, width, _ = weights.shape
    gathered = dev_count * dev_count * CAPR
    if gathered <= (local_count + 3) * width and dev_count == 8 and lax.axis_size("dp") == 2:
        run = gather_body
    else:
        run = replica_body
    return run(cotangent, hidden, probs, expert_ids, send_counts, replica_of, weights)


def solution(mesh):
    in_specs = (
        P(("groups", "expert", "dp"), None),
        P(("groups", "expert", "dp"), None, None),
        P(("groups", "expert", "dp"), None),
        P(("groups", "expert", "dp"), None),
        P(("groups", "expert", "dp"), None),
        P("groups"),
        P("expert", None, None),
    )
    out_specs = (
        P(("groups", "expert", "dp"), None, None),
        P(("groups", "expert", "dp"), None),
        P(("groups", "expert"), None, "dp"),
    )
    return jax.shard_map(body, mesh=mesh, in_specs=in_specs, out_specs=out_specs, check_vma=False)
```

```python
import functools

import jax
import jax.numpy as jnp
from jax import lax
from jax.experimental import pallas as pl
from jax.experimental.pallas import tpu as pltpu
from jax.sharding import PartitionSpec as P

CAPH = 3
CAPR = 3


def ranks_within(keys):
    total_rows = keys.shape[0]
    sort_order = jnp.argsort(keys * total_rows + jnp.arange(total_rows, dtype=jnp.int32))
    sorted_keys = keys[sort_order]
    first_seen = jnp.searchsorted(sorted_keys, sorted_keys, side="left")
    ranked = jnp.arange(total_rows, dtype=jnp.int32) - first_seen
    return jnp.zeros((total_rows,), jnp.int32).at[sort_order].set(ranked)


def route_rows(ids_block, counts_row, replica_of, local_count, cap_home, cap_copy):
    dev_count = replica_of.shape[0]
    experts = ids_block.reshape(-1)
    rank_expert = ranks_within(experts)
    devices = jnp.arange(dev_count, dtype=jnp.int32)
    same_copy = (replica_of[:, None] == replica_of[None, :]) & (devices[None, :] < devices[:, None])
    lower_rank = jnp.sum(jnp.where(same_copy, counts_row[None, :], 0), axis=1)
    upper_rank = lower_rank + counts_row
    hit_table = (
        (replica_of[None, :] == experts[:, None])
        & (lower_rank[None, :] <= rank_expert[:, None])
        & (rank_expert[:, None] < upper_rank[None, :])
    )
    copied = jnp.any(hit_table, axis=1)
    copy_dev = jnp.sum(jnp.where(hit_table, devices[None, :], 0), axis=1)
    dest_dev = jnp.where(copied, copy_dev, experts // local_count)
    index_of_slot = jnp.where(copied, local_count, experts % local_count)
    rank_bucket = ranks_within(dest_dev * (local_count + 1) + index_of_slot)
    keep_row = rank_bucket < jnp.where(copied, cap_copy, cap_home)
    per_dev = local_count * cap_home + cap_copy
    target = dest_dev * per_dev + index_of_slot * cap_home + rank_bucket
    return jnp.where(keep_row, target, dev_count * per_dev)


def replica_body(cotangent, hidden, probs, expert_ids, send_counts, replica_of, weights):
    tok_rows, d_model = cotangent.shape
    top_count = expert_ids.shape[1]
    hidden_width = hidden.shape[2]
    local_count = weights.shape[0]
    dev_count = lax.axis_size("expert")
    data_count = lax.axis_size("dp")
    per_dev = local_count * CAPH + CAPR
    row_count = tok_rows * top_count
    recv_count = dev_count * per_dev
    target = route_rows(expert_ids, send_counts[0], replica_of, local_count, CAPH, CAPR)
    inverse = (
        jnp.full((recv_count,), row_count, jnp.int32)
        .at[target]
        .set(jnp.arange(row_count, dtype=jnp.int32), mode="drop")
    )
    dy_pad = jnp.concatenate([cotangent, jnp.zeros((1, d_model), cotangent.dtype)], axis=0)
    h_pad = jnp.concatenate(
        [hidden.reshape(row_count, hidden_width), jnp.zeros((1, hidden_width), hidden.dtype)],
        axis=0,
    )
    p_pad = jnp.concatenate([probs.reshape(row_count), jnp.zeros((1,), probs.dtype)], axis=0)
    send_dy = dy_pad[inverse // top_count]
    send_h = h_pad[inverse]
    send_p = p_pad[inverse]
    recv_dy, recv_h, recv_p = (
        lax.all_to_all(send_dy, "expert", split_axis=0, concat_axis=0, tiled=True),
        lax.all_to_all(send_h, "expert", split_axis=0, concat_axis=0, tiled=True),
        lax.all_to_all(send_p, "expert", split_axis=0, concat_axis=0, tiled=True),
    )
    flat_size = hidden_width * d_model
    flat_w = weights.reshape(local_count, flat_size)
    pieces = lax.all_to_all(flat_w, "expert", split_axis=1, concat_axis=0, tiled=True)
    chosen = pieces[replica_of]
    copy_weight = lax.all_to_all(chosen, "expert", split_axis=0, concat_axis=0, tiled=True).reshape(
        hidden_width, d_model
    )
    slot_total = local_count + 1
    home_rows = local_count * CAPH
    row_pos = jnp.arange(recv_count, dtype=jnp.int32) % per_dev
    row_slot = jnp.where(row_pos < home_rows, row_pos // CAPH, local_count)
    all_weights = jnp.concatenate(
        [weights.reshape(local_count * hidden_width, d_model), copy_weight], axis=0
    )
    all_in = lax.dot_general(
        recv_dy, all_weights, (((1,), (1,)), ((), ())), preferred_element_type=jnp.float32
    )
    grad_in = jnp.zeros((recv_count, hidden_width), jnp.float32)
    for slot_num in range(slot_total):
        grad_in = grad_in + jnp.where(
            (row_slot == slot_num)[:, None],
            all_in[:, slot_num * hidden_width : (slot_num + 1) * hidden_width],
            0.0,
        )
    p_wide = recv_p.astype(jnp.float32)[:, None]
    h_wide = recv_h.astype(jnp.float32)
    grad_h_buf = (p_wide * grad_in).astype(jnp.bfloat16)
    grad_p_buf = jnp.sum(h_wide * grad_in, axis=1).astype(jnp.bfloat16)
    scaled = (p_wide * h_wide).astype(jnp.bfloat16)
    zero_rows = jnp.zeros_like(scaled)
    scaled_wide = jnp.concatenate(
        [
            jnp.where((row_slot == slot_num)[:, None], scaled, zero_rows)
            for slot_num in range(slot_total)
        ],
        axis=1,
    )
    parts = lax.dot_general(
        scaled_wide, recv_dy, (((0,), (0,)), ((), ())), preferred_element_type=jnp.float32
    ).astype(jnp.bfloat16)
    home_part = parts[: local_count * hidden_width].reshape(local_count, hidden_width, d_model)
    copy_part = parts[local_count * hidden_width :]
    back_h, back_p = (
        lax.all_to_all(grad_h_buf, "expert", split_axis=0, concat_axis=0, tiled=True),
        lax.all_to_all(grad_p_buf, "expert", split_axis=0, concat_axis=0, tiled=True),
    )
    flat_h = jnp.concatenate([back_h, jnp.zeros((1, hidden_width), back_h.dtype)], axis=0)
    flat_p = jnp.concatenate([back_p, jnp.zeros((1,), back_p.dtype)], axis=0)
    hidden_gradient = flat_h[target].reshape(tok_rows, top_count, hidden_width)
    grad_probs = flat_p[target].reshape(tok_rows, top_count)
    expert_total = dev_count * local_count
    cover = replica_of[None, :] == jnp.arange(expert_total, dtype=jnp.int32)[:, None]
    half_width = d_model // data_count
    halves = lax.all_to_all(copy_part, "dp", split_axis=1, concat_axis=0, tiled=True)
    copy_half = jnp.sum(
        halves.reshape(data_count, hidden_width, half_width).astype(jnp.float32), axis=0
    )
    piece_len = hidden_width * half_width // dev_count
    slabs = copy_half.reshape(dev_count, piece_len)
    arrived = lax.all_to_all(slabs, "expert", split_axis=0, concat_axis=0, tiled=True)
    sums = jnp.dot(cover.astype(jnp.float32), arrived, precision=lax.Precision.HIGHEST)
    homed = lax.all_to_all(
        sums.reshape(dev_count, local_count * piece_len),
        "expert",
        split_axis=0,
        concat_axis=0,
        tiled=True,
    )
    homed = (
        homed.reshape(dev_count, local_count, piece_len)
        .transpose(1, 0, 2)
        .reshape(local_count, hidden_width, half_width)
    )
    home_half = lax.psum_scatter(
        home_part.astype(jnp.float32).astype(jnp.bfloat16), "dp", scatter_dimension=2, tiled=True
    ).astype(jnp.float32)
    grad_weights = (home_half + homed).astype(jnp.bfloat16)
    return (hidden_gradient, grad_probs, grad_weights)


SLOT = 3
HOME, COPIES = "home", "copies"
F32 = jnp.float32
BF16 = jnp.bfloat16
NT = (((1,), (1,)), ((), ()))
TN = (((0,), (0,)), ((), ()))


def iota(shape, dim):
    return lax.broadcasted_iota(jnp.int32, shape, dim)


def dispatch_kernel(local_count, dev_count, packing, *refs):
    sources, refs = refs[:6], refs[6:]
    pick_ref, expert_ref, hs_ref, ps_ref = refs[:4]
    packed, (held, wide, sems) = refs[4:4 + len(packing)], (refs[-8:-2], refs[-2], refs[-1])
    moves = [pltpu.make_async_copy(s, h, sems.at[n]) for n, (s, h) in enumerate(zip(sources, held))]
    for move in moves:
        move.start()
    replica_ref, counts_ref, ids_ref, probs_ref, hid_ref, cot_ref = held
    top, toks = ids_ref.shape
    per_home = local_count * SLOT
    homes = dev_count * per_home
    slots = homes + dev_count * CAPR
    me = lax.axis_index("expert")
    for move in moves[:3]:
        move.wait()
    row = iota((slots, toks), 0)
    expert = ((row // per_home) ^ me) * local_count + (row % per_home) // SLOT
    within = row % SLOT
    allowed = jnp.where(within < CAPH, 1, 0)
    for d in range(dev_count):
        first = homes + d * CAPR
        mine = (row >= first) & (row < first + CAPR)
        expert = jnp.where(mine, replica_ref[d], expert)
        within = jnp.where(mine, row - first, within)
        allowed = jnp.where(mine, jnp.where(row - first < counts_ref[0, d], 1, 0), allowed)
    lower = jnp.zeros((slots, toks), jnp.int32)
    for d in range(dev_count):
        earlier = (row < homes) | (row >= homes + (d + 1) * CAPR)
        lower = lower + jnp.where(earlier & (expert == replica_ref[d]), counts_ref[0, d], 0)
    ids = ids_ref[...]
    named = jnp.zeros((slots, toks), F32)
    for k in range(top):
        named = named + jnp.where(ids[k:k + 1, :] == expert, 1.0, 0.0)
    before = jnp.where(iota((toks, toks), 0) < iota((toks, toks), 1), 1.0, 0.0).astype(BF16)
    rank = jnp.dot(named.astype(BF16), before, preferred_element_type=F32)
    wanted = (lower + within).astype(F32)
    pick = jnp.where((rank == wanted) & (allowed > 0), named, 0.0)
    pick_ref[...] = pick
    expert_ref[...] = expert
    for move in moves[3:5]:
        move.wait()
    wide[...] = hid_ref[...].astype(F32)
    p_slot = jnp.zeros((slots, toks), F32)
    probs = probs_ref[...].astype(F32)
    chosen, values = [], []
    for k in range(top):
        sel = jnp.where(ids[k:k + 1, :] == expert, pick, 0.0)
        chosen.append(sel.astype(BF16))
        values.append(wide[pl.ds(k, toks, stride=top), :].astype(BF16))
        p_slot = p_slot + sel * probs[k:k + 1, :]
    h_slot = jnp.dot(
        jnp.concatenate(chosen, axis=1), jnp.concatenate(values, axis=0), preferred_element_type=F32)
    p_slot = jnp.sum(p_slot, axis=1, keepdims=True)
    hs_ref[...] = h_slot
    ps_ref[...] = jnp.broadcast_to(p_slot, ps_ref.shape)
    scaled = p_slot * h_slot
    moves[5].wait()
    rows = jnp.dot(pick.astype(BF16), cot_ref[...], preferred_element_type=F32)
    d_model = cot_ref.shape[1]
    for out_ref, blocks in zip(packed, packing):
        spans = [(homes, slots) if b == COPIES else (b * per_home, (b + 1) * per_home) for b in blocks]
        out_ref[:, :d_model] = jnp.concatenate([rows[i:j] for i, j in spans], axis=0).astype(BF16)
        out_ref[:, d_model:] = jnp.concatenate([scaled[i:j] for i, j in spans], axis=0).astype(BF16)


def padded(rows):
    return -(-rows // 16) * 16


def stack(order, blocks, height):
    values = [blocks[key] for key in order]
    missing = height - sum(v.shape[0] for v in values)
    if missing:
        values.append(jnp.zeros((missing, values[0].shape[1]), values[0].dtype))
    return jnp.concatenate(values, axis=0)


def fold_width(columns):
    return -(-columns // 256) * 128


def folded(rows):
    count, columns = rows.shape
    left = fold_width(columns)
    right = [rows[:, left:], jnp.zeros((count, 2 * left - columns), rows.dtype)]
    return jnp.concatenate([rows[:, :left], jnp.concatenate(right, axis=1)], axis=0)


def unfolded(rows, columns):
    count, left = rows.shape
    if left == columns:
        return rows
    return jnp.concatenate([rows[:count // 2], rows[count // 2:, :columns - left]], axis=1)


def slots_of(order, slot_ref, per_home, height):
    kinds = {HOME: slot_ref[:per_home], COPIES: slot_ref[per_home:]}
    return stack(order, {key: kinds[key[1]] for key in order}, height)


def fill_rows(order, pieces, per_home, per_copy, piece_refs, rows_ref):
    values = [unfolded(r[...].astype(F32), rows_ref.shape[1]) for r in piece_refs]
    blocks = {}
    for key in order:
        n, start = pieces[key]
        blocks[key] = values[n][start:start + (per_home if key[1] == HOME else per_copy)]
    rows_ref[...] = stack(order, blocks, rows_ref.shape[0]).astype(BF16)


def own_columns(rows_ref, w_ref, slot, local_count):
    d_model = w_ref.shape[1]
    width = w_ref.shape[0] // local_count
    every = lax.dot_general(rows_ref[:, :d_model], w_ref[...], NT, preferred_element_type=F32)
    own = jnp.zeros((rows_ref.shape[0], width), F32)
    for e in range(local_count):
        own = jnp.where(slot == e, every[:, e * width:(e + 1) * width], own)
    return own


def hold_kernel(local_count, dev_count, replica_ref, w_hbm, own_hbm, even_hbm,
                own_ref, even_ref, w_ref, slot_ref, sems):
    moves = [pltpu.make_async_copy(a, b, sems.at[n]) for n, (a, b) in enumerate(
        ((w_hbm, w_ref), (own_hbm, own_ref), (even_hbm, even_ref)))]
    for move in moves:
        move.start()
    per_home, per_copy = local_count * SLOT, dev_count * CAPR
    first = lax.axis_index("expert") * local_count
    width = slot_ref.shape[1]
    slot_ref[:per_home] = iota((per_home, width), 0) // SLOT
    row = iota((per_copy, width), 0)
    copy = jnp.full((per_copy, width), -1, jnp.int32)
    for d in range(dev_count):
        mine = (row >= d * CAPR) & (row < (d + 1) * CAPR)
        copy = jnp.where(mine, replica_ref[d] - first, copy)
    slot_ref[per_home:] = copy
    for move in moves:
        move.wait()


def turn_kernel(local_count, dev_count, beside_ref, even_ref, *line_refs):
    per_home, per_copy = local_count * SLOT, dev_count * CAPR
    beside = beside_ref[...].astype(F32)[per_copy + per_home:]
    even = even_ref[...].astype(F32)
    for n, line_ref in enumerate(line_refs):
        span = slice(n * per_home, (n + 1) * per_home)
        line_ref[...] = folded(jnp.concatenate([even[span], beside[span]], axis=0)).astype(BF16)


def early_kernel(local_count, dev_count, order, pieces, w_ref, slot_ref, *refs):
    piece_refs, (rows_ref, own_ref) = refs[:-2], refs[-2:]
    per_home, per_copy = local_count * SLOT, dev_count * CAPR
    fill_rows(order, pieces, per_home, per_copy, piece_refs, rows_ref)
    slot = slots_of(order, slot_ref, per_home, rows_ref.shape[0])
    own_ref[...] = own_columns(rows_ref, w_ref, slot, local_count)


def late_kernel(local_count, dev_count, early, order, pieces, own_ref, w_ref, slot_ref, *refs):
    piece_refs, (rows_ref, back_ref, passed) = refs[:-3], refs[-3:]
    per_home, per_copy = local_count * SLOT, dev_count * CAPR
    fill_rows(order, pieces, per_home, per_copy, piece_refs, rows_ref)
    own = own_columns(rows_ref, w_ref, slots_of(order, slot_ref, per_home, rows_ref.shape[0]), local_count)
    if passed.shape[1] > per_home + per_copy:
        passed[:, per_home + per_copy:] = jnp.zeros_like(passed[:, per_home + per_copy:])
    for keys, value in ((early, own_ref[...]), (order, own)):
        start = 0
        for m, kind in keys:
            lower, size = (0, per_home) if kind == HOME else (per_home, per_copy)
            passed[m, lower:lower + size] = value[start:start + size]
            start += size
    me = lax.axis_index("expert")
    back = jnp.concatenate([passed[me ^ source] for source in range(dev_count)], axis=0)
    back_ref[...] = back.astype(back_ref.dtype)


def grad_weights_half(local_count, dev_count, orders, half, slot_ref, rows_refs, columns):
    start = pl.multiple_of(half * columns, 128)
    spread = []
    for order, ref in zip(orders, rows_refs):
        slot = slots_of(order, slot_ref, local_count * SLOT, ref.shape[0])
        scaled = ref[:, 2 * columns:].astype(F32)
        spread.append(jnp.concatenate([jnp.where(slot == e, scaled, 0.0) for e in range(local_count)], axis=1))
    rows = jnp.concatenate([ref[:, pl.ds(start, columns)] for ref in rows_refs], axis=0)
    return lax.dot_general(
        jnp.concatenate(spread, axis=0).astype(BF16), rows, TN, preferred_element_type=F32)


def other_half_kernel(local_count, dev_count, orders, slot_ref, early_ref, late_ref, out_ref):
    half = 1 - lax.axis_index("dp")
    out_ref[...] = grad_weights_half(
        local_count, dev_count, orders, half, slot_ref, (early_ref, late_ref), out_ref.shape[1]).astype(out_ref.dtype)


def own_half_kernel(local_count, dev_count, orders, slot_ref, early_ref, late_ref, arrived_ref, out_ref):
    half = lax.axis_index("dp")
    total = grad_weights_half(
        local_count, dev_count, orders, half, slot_ref, (early_ref, late_ref), out_ref.shape[1])
    out_ref[...] = (total + arrived_ref[...].astype(F32)).astype(out_ref.dtype)


def combine_kernel(local_count, dev_count, back_ref, pick_ref, expert_ref, hs_ref, ps_ref, ids_ref,
                   grad_h_ref, grad_p_ref, wide, narrow):
    top, toks = ids_ref.shape
    per_home = local_count * SLOT
    me = lax.axis_index("expert")
    back = [back_ref[me ^ m].astype(F32) for m in range(dev_count)]
    slots = pick_ref.shape[0]
    copies = slots - dev_count * per_home
    copy = functools.reduce(jnp.add, [b[per_home:per_home + copies] for b in back])
    grad_in = jnp.concatenate([b[:per_home] for b in back] + [copy], axis=0)
    h_rows = (ps_ref[...] * grad_in).astype(BF16)
    p_rows = jnp.sum(hs_ref[...] * grad_in, axis=1, keepdims=True)
    ids = ids_ref[...]
    pick = pick_ref[...]
    expert = expert_ref[...]
    for k in range(top):
        sel = jnp.where(ids[k:k + 1, :] == expert, pick, 0.0)
        wide[pl.ds(k, toks, stride=top), :] = lax.dot_general(
            sel.astype(BF16), h_rows, TN, preferred_element_type=F32)
        narrow[k:k + 1, :] = jnp.sum(sel * p_rows, axis=0, keepdims=True)
    grad_h_ref[...] = wide[...].astype(grad_h_ref.dtype)
    grad_p_ref[...] = narrow[...].astype(grad_p_ref.dtype)


def call(kernel, out_shape, operands, scratch=(), flops=0, limit=24):
    shapes = jax.tree.leaves(out_shape)
    moved = sum(a.size * a.dtype.itemsize for a in (*(a for _, a in operands), *shapes))
    return pl.pallas_call(
        kernel,
        out_shape=out_shape,
        in_specs=[pl.BlockSpec(memory_space=space) for space, _ in operands],
        out_specs=jax.tree.map(lambda _: pl.BlockSpec(memory_space=pltpu.VMEM), out_shape),
        scratch_shapes=list(scratch),
        compiler_params=pltpu.CompilerParams(vmem_limit_bytes=limit << 20),
        cost_estimate=pl.CostEstimate(flops=flops, bytes_accessed=moved, transcendentals=0),
    )(*(a for _, a in operands))


def swap(x, bits, count):
    return lax.ppermute(x, "expert", [(i, i ^ bits) for i in range(count)])


def gather_body(cotangent, hidden, probs, expert_ids, send_counts, replica_of, weights):
    toks, d_model = cotangent.shape
    top = expert_ids.shape[1]
    width = hidden.shape[2]
    local_count = weights.shape[0]
    dev_count = lax.axis_size("expert")
    homes = dev_count * local_count * SLOT
    copies = dev_count * CAPR
    slots = homes + copies
    rows = homes + dev_count * copies
    columns = d_model // 2
    sizes = (local_count, dev_count)
    ids = expert_ids.T
    shape = jax.ShapeDtypeStruct
    hbm, vmem, smem = pltpu.HBM, pltpu.VMEM, pltpu.SMEM
    sources = (replica_of, send_counts, ids, probs.T, hidden.reshape(toks * top, width), cotangent)
    per_home = local_count * SLOT
    odd, even = range(1, dev_count, 2), range(2, dev_count, 2)
    packing = [[COPIES, *odd], [COPIES], [0, COPIES], [*even]]
    sized = [sum(copies if b == COPIES else per_home for b in blocks) for blocks in packing]
    pick, expert, h_slot, p_slot, to_beside, copy_rows, own_rows, even_rows = call(
        functools.partial(dispatch_kernel, *sizes, packing),
        [shape((slots, toks), F32), shape((slots, toks), jnp.int32), shape((slots, width), F32),
         shape((slots, width), F32)] + [shape((n, d_model + width), BF16) for n in sized],
        [(hbm, a) for a in sources],
        [(smem if n < 2 else vmem)(a.shape, a.dtype) for n, a in enumerate(sources)]
        + [vmem((toks * top, width), F32), pltpu.SemaphoreType.DMA((len(sources),))],
        flops=2 * slots * toks * d_model,
        limit=60,
    )
    beside = swap(to_beside, 1, dev_count)
    near = swap(copy_rows, 2, dev_count)
    far = swap(copy_rows, 4, dev_count)
    flat_w = weights.reshape(local_count * width, d_model)
    own_rows, even_rows, w_held, slot = call(
        functools.partial(hold_kernel, *sizes),
        [shape(a.shape, BF16) for a in (own_rows, even_rows, flat_w)] + [shape((per_home + copies, width), jnp.int32)],
        [(smem, replica_of)] + [(hbm, a) for a in (flat_w, own_rows, even_rows)],
        [pltpu.SemaphoreType.DMA((3,))],
    )
    near, far, beside, own_rows, even_rows, w_held, slot = lax.optimization_barrier(
        (near, far, beside, own_rows, even_rows, w_held, slot))
    far_near = swap(far, 2, dev_count)
    lines = call(
        functools.partial(turn_kernel, *sizes),
        [shape((4 * per_home, fold_width(d_model + width)), BF16)] * len(even),
        [(vmem, a) for a in (beside, even_rows)],
    )
    far_beside, near_beside = swap(far, 1, dev_count), swap(near, 1, dev_count)
    lines = [swap(a, m, dev_count) for a, m in zip(lines, even)]
    pieces = {(0, HOME): (0, 0), (0, COPIES): (0, per_home), (1, COPIES): (1, 0), (1, HOME): (1, copies),
              (2, COPIES): (2, 0), (4, COPIES): (3, 0), (5, COPIES): (4, 0), (3, COPIES): (5, 0)}
    orders = [list(pieces)]
    height = padded(sum(per_home if kind == HOME else copies for _, kind in pieces))
    early_rows, own = call(
        functools.partial(early_kernel, *sizes, orders[0], pieces),
        (shape((height, d_model + width), BF16), shape((height, width), F32)),
        [(vmem, a) for a in (w_held, slot, own_rows, beside, near, far, far_beside, near_beside)],
        flops=2 * height * d_model * local_count * width * 30,
    )
    far_across = swap(far_near, 1, dev_count)
    arrays = [far_near, far_across, *lines[::-1]]
    pieces = {(6, COPIES): (0, 0), (7, COPIES): (1, 0)}
    for n, m in enumerate(even[::-1]):
        pieces[m, HOME], pieces[m + 1, HOME] = ((2 + n, k * per_home) for k in range(2))
    orders.append(list(pieces))
    height = padded(sum(per_home if kind == HOME else copies for _, kind in pieces))
    block = padded(per_home + copies)
    late_rows, back = call(
        functools.partial(late_kernel, *sizes, *orders, pieces),
        (shape((height, d_model + width), BF16), shape((dev_count * block, width), BF16)),
        [(vmem, a) for a in (own, w_held, slot, *arrays)],
        [vmem((dev_count, block, width), F32)],
        flops=2 * height * d_model * local_count * width,
    )
    back = lax.all_to_all(back, "expert", split_axis=0, concat_axis=0, tiled=True)
    half_flops = 2 * rows * columns * local_count * width
    halves = (slot, early_rows, late_rows)
    other = call(
        functools.partial(other_half_kernel, *sizes, orders),
        shape((local_count * width, columns), BF16),
        [(vmem, a) for a in halves],
        flops=half_flops,
    )
    arrived = lax.ppermute(other, "dp", [(0, 1), (1, 0)])
    grad_w = call(
        functools.partial(own_half_kernel, *sizes, orders),
        shape((local_count * width, columns), BF16),
        [(vmem, a) for a in (*halves, arrived)],
        flops=30 * half_flops,
    )
    grad_w, pick = lax.optimization_barrier((grad_w, pick))
    grad_h, grad_p = call(
        functools.partial(combine_kernel, *sizes),
        (shape((toks * top, width), BF16), shape((top, toks), BF16)),
        [(vmem, a) for a in (back.reshape(dev_count, block, width), pick, expert, h_slot, p_slot, ids)],
        [vmem((toks * top, width), F32), vmem((top, toks), F32)],
        flops=2 * slots * toks * width * top,
    )
    return (
        grad_h.reshape(toks, top, width),
        grad_p.T,
        grad_w.reshape(local_count, width, columns),
    )


def body(cotangent, hidden, probs, expert_ids, send_counts, replica_of, weights):
    dev_count = lax.axis_size("expert")
    local_count, width, _ = weights.shape
    gathered = dev_count * dev_count * CAPR
    if gathered <= (local_count + 3) * width and dev_count == 8 and lax.axis_size("dp") == 2:
        run = gather_body
    else:
        run = replica_body
    return run(cotangent, hidden, probs, expert_ids, send_counts, replica_of, weights)


def solution(mesh):
    in_specs = (
        P(("groups", "expert", "dp"), None),
        P(("groups", "expert", "dp"), None, None),
        P(("groups", "expert", "dp"), None),
        P(("groups", "expert", "dp"), None),
        P(("groups", "expert", "dp"), None),
        P("groups"),
        P("expert", None, None),
    )
    out_specs = (
        P(("groups", "expert", "dp"), None, None),
        P(("groups", "expert", "dp"), None),
        P(("groups", "expert"), None, "dp"),
    )
    return jax.shard_map(body, mesh=mesh, in_specs=in_specs, out_specs=out_specs, check_vma=False)
```

```python
import functools

import jax
import jax.numpy as jnp
from jax import lax
from jax.experimental import pallas as pl
from jax.experimental.pallas import tpu as pltpu
from jax.sharding import PartitionSpec as P

CAPH = 3
CAPR = 3


def ranks_within(keys):
    total_rows = keys.shape[0]
    sort_order = jnp.argsort(keys * total_rows + jnp.arange(total_rows, dtype=jnp.int32))
    sorted_keys = keys[sort_order]
    first_seen = jnp.searchsorted(sorted_keys, sorted_keys, side="left")
    ranked = jnp.arange(total_rows, dtype=jnp.int32) - first_seen
    return jnp.zeros((total_rows,), jnp.int32).at[sort_order].set(ranked)


def route_rows(ids_block, counts_row, replica_of, local_count, cap_home, cap_copy):
    dev_count = replica_of.shape[0]
    experts = ids_block.reshape(-1)
    rank_expert = ranks_within(experts)
    devices = jnp.arange(dev_count, dtype=jnp.int32)
    same_copy = (replica_of[:, None] == replica_of[None, :]) & (devices[None, :] < devices[:, None])
    lower_rank = jnp.sum(jnp.where(same_copy, counts_row[None, :], 0), axis=1)
    upper_rank = lower_rank + counts_row
    hit_table = (
        (replica_of[None, :] == experts[:, None])
        & (lower_rank[None, :] <= rank_expert[:, None])
        & (rank_expert[:, None] < upper_rank[None, :])
    )
    copied = jnp.any(hit_table, axis=1)
    copy_dev = jnp.sum(jnp.where(hit_table, devices[None, :], 0), axis=1)
    dest_dev = jnp.where(copied, copy_dev, experts // local_count)
    index_of_slot = jnp.where(copied, local_count, experts % local_count)
    rank_bucket = ranks_within(dest_dev * (local_count + 1) + index_of_slot)
    keep_row = rank_bucket < jnp.where(copied, cap_copy, cap_home)
    per_dev = local_count * cap_home + cap_copy
    target = dest_dev * per_dev + index_of_slot * cap_home + rank_bucket
    return jnp.where(keep_row, target, dev_count * per_dev)


def replica_body(cotangent, hidden, probs, expert_ids, send_counts, replica_of, weights):
    tok_rows, d_model = cotangent.shape
    top_count = expert_ids.shape[1]
    hidden_width = hidden.shape[2]
    local_count = weights.shape[0]
    dev_count = lax.axis_size("expert")
    data_count = lax.axis_size("dp")
    per_dev = local_count * CAPH + CAPR
    row_count = tok_rows * top_count
    recv_count = dev_count * per_dev
    target = route_rows(expert_ids, send_counts[0], replica_of, local_count, CAPH, CAPR)
    inverse = (
        jnp.full((recv_count,), row_count, jnp.int32)
        .at[target]
        .set(jnp.arange(row_count, dtype=jnp.int32), mode="drop")
    )
    dy_pad = jnp.concatenate([cotangent, jnp.zeros((1, d_model), cotangent.dtype)], axis=0)
    h_pad = jnp.concatenate(
        [hidden.reshape(row_count, hidden_width), jnp.zeros((1, hidden_width), hidden.dtype)],
        axis=0,
    )
    p_pad = jnp.concatenate([probs.reshape(row_count), jnp.zeros((1,), probs.dtype)], axis=0)
    send_dy = dy_pad[inverse // top_count]
    send_h = h_pad[inverse]
    send_p = p_pad[inverse]
    recv_dy, recv_h, recv_p = (
        lax.all_to_all(send_dy, "expert", split_axis=0, concat_axis=0, tiled=True),
        lax.all_to_all(send_h, "expert", split_axis=0, concat_axis=0, tiled=True),
        lax.all_to_all(send_p, "expert", split_axis=0, concat_axis=0, tiled=True),
    )
    flat_size = hidden_width * d_model
    flat_w = weights.reshape(local_count, flat_size)
    pieces = lax.all_to_all(flat_w, "expert", split_axis=1, concat_axis=0, tiled=True)
    chosen = pieces[replica_of]
    copy_weight = lax.all_to_all(chosen, "expert", split_axis=0, concat_axis=0, tiled=True).reshape(
        hidden_width, d_model
    )
    slot_total = local_count + 1
    home_rows = local_count * CAPH
    row_pos = jnp.arange(recv_count, dtype=jnp.int32) % per_dev
    row_slot = jnp.where(row_pos < home_rows, row_pos // CAPH, local_count)
    all_weights = jnp.concatenate(
        [weights.reshape(local_count * hidden_width, d_model), copy_weight], axis=0
    )
    all_in = lax.dot_general(
        recv_dy, all_weights, (((1,), (1,)), ((), ())), preferred_element_type=jnp.float32
    )
    grad_in = jnp.zeros((recv_count, hidden_width), jnp.float32)
    for slot_num in range(slot_total):
        grad_in = grad_in + jnp.where(
            (row_slot == slot_num)[:, None],
            all_in[:, slot_num * hidden_width : (slot_num + 1) * hidden_width],
            0.0,
        )
    p_wide = recv_p.astype(jnp.float32)[:, None]
    h_wide = recv_h.astype(jnp.float32)
    grad_h_buf = (p_wide * grad_in).astype(jnp.bfloat16)
    grad_p_buf = jnp.sum(h_wide * grad_in, axis=1).astype(jnp.bfloat16)
    scaled = (p_wide * h_wide).astype(jnp.bfloat16)
    zero_rows = jnp.zeros_like(scaled)
    scaled_wide = jnp.concatenate(
        [
            jnp.where((row_slot == slot_num)[:, None], scaled, zero_rows)
            for slot_num in range(slot_total)
        ],
        axis=1,
    )
    parts = lax.dot_general(
        scaled_wide, recv_dy, (((0,), (0,)), ((), ())), preferred_element_type=jnp.float32
    ).astype(jnp.bfloat16)
    home_part = parts[: local_count * hidden_width].reshape(local_count, hidden_width, d_model)
    copy_part = parts[local_count * hidden_width :]
    back_h, back_p = (
        lax.all_to_all(grad_h_buf, "expert", split_axis=0, concat_axis=0, tiled=True),
        lax.all_to_all(grad_p_buf, "expert", split_axis=0, concat_axis=0, tiled=True),
    )
    flat_h = jnp.concatenate([back_h, jnp.zeros((1, hidden_width), back_h.dtype)], axis=0)
    flat_p = jnp.concatenate([back_p, jnp.zeros((1,), back_p.dtype)], axis=0)
    hidden_gradient = flat_h[target].reshape(tok_rows, top_count, hidden_width)
    grad_probs = flat_p[target].reshape(tok_rows, top_count)
    expert_total = dev_count * local_count
    cover = replica_of[None, :] == jnp.arange(expert_total, dtype=jnp.int32)[:, None]
    half_width = d_model // data_count
    halves = lax.all_to_all(copy_part, "dp", split_axis=1, concat_axis=0, tiled=True)
    copy_half = jnp.sum(
        halves.reshape(data_count, hidden_width, half_width).astype(jnp.float32), axis=0
    )
    piece_len = hidden_width * half_width // dev_count
    slabs = copy_half.reshape(dev_count, piece_len)
    arrived = lax.all_to_all(slabs, "expert", split_axis=0, concat_axis=0, tiled=True)
    sums = jnp.dot(cover.astype(jnp.float32), arrived, precision=lax.Precision.HIGHEST)
    homed = lax.all_to_all(
        sums.reshape(dev_count, local_count * piece_len),
        "expert",
        split_axis=0,
        concat_axis=0,
        tiled=True,
    )
    homed = (
        homed.reshape(dev_count, local_count, piece_len)
        .transpose(1, 0, 2)
        .reshape(local_count, hidden_width, half_width)
    )
    home_half = lax.psum_scatter(
        home_part.astype(jnp.float32).astype(jnp.bfloat16), "dp", scatter_dimension=2, tiled=True
    ).astype(jnp.float32)
    grad_weights = (home_half + homed).astype(jnp.bfloat16)
    return (hidden_gradient, grad_probs, grad_weights)


SLOT = 3
HOME, COPIES = "home", "copies"
F32 = jnp.float32
BF16 = jnp.bfloat16
NT = (((1,), (1,)), ((), ()))
TN = (((0,), (0,)), ((), ()))


def iota(shape, dim):
    return lax.broadcasted_iota(jnp.int32, shape, dim)


def dispatch_kernel(local_count, dev_count, packing, *refs):
    sources, refs = refs[:6], refs[6:]
    pick_ref, expert_ref, hs_ref, ps_ref = refs[:4]
    packed, (held, wide, sems) = refs[4:4 + len(packing)], (refs[-8:-2], refs[-2], refs[-1])
    moves = [pltpu.make_async_copy(s, h, sems.at[n]) for n, (s, h) in enumerate(zip(sources, held))]
    for move in moves:
        move.start()
    replica_ref, counts_ref, ids_ref, probs_ref, hid_ref, cot_ref = held
    top, toks = ids_ref.shape
    per_home = local_count * SLOT
    homes = dev_count * per_home
    slots = homes + dev_count * CAPR
    me = lax.axis_index("expert")
    for move in moves[:3]:
        move.wait()
    row = iota((slots, toks), 0)
    expert = ((row // per_home) ^ me) * local_count + (row % per_home) // SLOT
    within = row % SLOT
    allowed = jnp.where(within < CAPH, 1, 0)
    for d in range(dev_count):
        first = homes + d * CAPR
        mine = (row >= first) & (row < first + CAPR)
        expert = jnp.where(mine, replica_ref[d], expert)
        within = jnp.where(mine, row - first, within)
        allowed = jnp.where(mine, jnp.where(row - first < counts_ref[0, d], 1, 0), allowed)
    lower = jnp.zeros((slots, toks), jnp.int32)
    for d in range(dev_count):
        earlier = (row < homes) | (row >= homes + (d + 1) * CAPR)
        lower = lower + jnp.where(earlier & (expert == replica_ref[d]), counts_ref[0, d], 0)
    ids = ids_ref[...]
    named = jnp.zeros((slots, toks), F32)
    for k in range(top):
        named = named + jnp.where(ids[k:k + 1, :] == expert, 1.0, 0.0)
    before = jnp.where(iota((toks, toks), 0) < iota((toks, toks), 1), 1.0, 0.0).astype(BF16)
    rank = jnp.dot(named.astype(BF16), before, preferred_element_type=F32)
    wanted = (lower + within).astype(F32)
    pick = jnp.where((rank == wanted) & (allowed > 0), named, 0.0)
    pick_ref[...] = pick
    expert_ref[...] = expert
    for move in moves[3:5]:
        move.wait()
    wide[...] = hid_ref[...].astype(F32)
    p_slot = jnp.zeros((slots, toks), F32)
    probs = probs_ref[...].astype(F32)
    chosen, values = [], []
    for k in range(top):
        sel = jnp.where(ids[k:k + 1, :] == expert, pick, 0.0)
        chosen.append(sel.astype(BF16))
        values.append(wide[pl.ds(k, toks, stride=top), :].astype(BF16))
        p_slot = p_slot + sel * probs[k:k + 1, :]
    h_slot = jnp.dot(
        jnp.concatenate(chosen, axis=1), jnp.concatenate(values, axis=0), preferred_element_type=F32)
    p_slot = jnp.sum(p_slot, axis=1, keepdims=True)
    hs_ref[...] = h_slot
    ps_ref[...] = jnp.broadcast_to(p_slot, ps_ref.shape)
    scaled = p_slot * h_slot
    moves[5].wait()
    rows = jnp.dot(pick.astype(BF16), cot_ref[...], preferred_element_type=F32)
    d_model = cot_ref.shape[1]
    for out_ref, blocks in zip(packed, packing):
        spans = [(homes, slots) if b == COPIES else (b * per_home, (b + 1) * per_home) for b in blocks]
        out_ref[:, :d_model] = jnp.concatenate([rows[i:j] for i, j in spans], axis=0).astype(BF16)
        out_ref[:, d_model:] = jnp.concatenate([scaled[i:j] for i, j in spans], axis=0).astype(BF16)


def padded(rows):
    return -(-rows // 16) * 16


def stack(order, blocks, height):
    values = [blocks[key] for key in order]
    missing = height - sum(v.shape[0] for v in values)
    if missing:
        values.append(jnp.zeros((missing, values[0].shape[1]), values[0].dtype))
    return jnp.concatenate(values, axis=0)


def fold_width(columns):
    return -(-columns // 256) * 128


def folded(rows):
    count, columns = rows.shape
    left = fold_width(columns)
    right = [rows[:, left:], jnp.zeros((count, 2 * left - columns), rows.dtype)]
    return jnp.concatenate([rows[:, :left], jnp.concatenate(right, axis=1)], axis=0)


def unfolded(rows, columns):
    count, left = rows.shape
    if left == columns:
        return rows
    return jnp.concatenate([rows[:count // 2], rows[count // 2:, :columns - left]], axis=1)


def slots_of(order, slot_ref, per_home, height):
    kinds = {HOME: slot_ref[:per_home], COPIES: slot_ref[per_home:]}
    return stack(order, {key: kinds[key[1]] for key in order}, height)


def fill_rows(order, pieces, per_home, per_copy, piece_refs, rows_ref):
    values = [unfolded(r[...].astype(F32), rows_ref.shape[1]) for r in piece_refs]
    blocks = {}
    for key in order:
        n, start = pieces[key]
        blocks[key] = values[n][start:start + (per_home if key[1] == HOME else per_copy)]
    rows_ref[...] = stack(order, blocks, rows_ref.shape[0]).astype(BF16)


def own_columns(rows_ref, w_ref, slot, local_count):
    d_model = w_ref.shape[1]
    width = w_ref.shape[0] // local_count
    every = lax.dot_general(rows_ref[:, :d_model], w_ref[...], NT, preferred_element_type=F32)
    own = jnp.zeros((rows_ref.shape[0], width), F32)
    for e in range(local_count):
        own = jnp.where(slot == e, every[:, e * width:(e + 1) * width], own)
    return own


def hold_kernel(local_count, dev_count, replica_ref, w_hbm, own_hbm, even_hbm,
                own_ref, even_ref, w_ref, slot_ref, sems):
    moves = [pltpu.make_async_copy(a, b, sems.at[n]) for n, (a, b) in enumerate(
        ((w_hbm, w_ref), (own_hbm, own_ref), (even_hbm, even_ref)))]
    for move in moves:
        move.start()
    per_home, per_copy = local_count * SLOT, dev_count * CAPR
    first = lax.axis_index("expert") * local_count
    width = slot_ref.shape[1]
    slot_ref[:per_home] = iota((per_home, width), 0) // SLOT
    row = iota((per_copy, width), 0)
    copy = jnp.full((per_copy, width), -1, jnp.int32)
    for d in range(dev_count):
        mine = (row >= d * CAPR) & (row < (d + 1) * CAPR)
        copy = jnp.where(mine, replica_ref[d] - first, copy)
    slot_ref[per_home:] = copy
    for move in moves:
        move.wait()


def turn_kernel(local_count, dev_count, beside_ref, even_ref, *line_refs):
    per_home, per_copy = local_count * SLOT, dev_count * CAPR
    beside = beside_ref[...].astype(F32)[per_copy + per_home:]
    even = even_ref[...].astype(F32)
    for n, line_ref in enumerate(line_refs):
        span = slice(n * per_home, (n + 1) * per_home)
        line_ref[...] = folded(jnp.concatenate([even[span], beside[span]], axis=0)).astype(BF16)


def early_kernel(local_count, dev_count, order, pieces, w_ref, slot_ref, *refs):
    piece_refs, (rows_ref, own_ref) = refs[:-2], refs[-2:]
    per_home, per_copy = local_count * SLOT, dev_count * CAPR
    fill_rows(order, pieces, per_home, per_copy, piece_refs, rows_ref)
    slot = slots_of(order, slot_ref, per_home, rows_ref.shape[0])
    own_ref[...] = own_columns(rows_ref, w_ref, slot, local_count)


def late_kernel(local_count, dev_count, early, order, pieces, own_ref, w_ref, slot_ref, *refs):
    piece_refs, (rows_ref, back_ref, passed) = refs[:-3], refs[-3:]
    per_home, per_copy = local_count * SLOT, dev_count * CAPR
    fill_rows(order, pieces, per_home, per_copy, piece_refs, rows_ref)
    own = own_columns(rows_ref, w_ref, slots_of(order, slot_ref, per_home, rows_ref.shape[0]), local_count)
    if passed.shape[1] > per_home + per_copy:
        passed[:, per_home + per_copy:] = jnp.zeros_like(passed[:, per_home + per_copy:])
    for keys, value in ((early, own_ref[...]), (order, own)):
        start = 0
        for m, kind in keys:
            lower, size = (0, per_home) if kind == HOME else (per_home, per_copy)
            passed[m, lower:lower + size] = value[start:start + size]
            start += size
    me = lax.axis_index("expert")
    back = jnp.concatenate([passed[me ^ source] for source in range(dev_count)], axis=0)
    back_ref[...] = back.astype(back_ref.dtype)


def grad_weights_half(local_count, dev_count, orders, half, slot_ref, rows_refs, columns):
    start = pl.multiple_of(half * columns, 128)
    spread = []
    for order, ref in zip(orders, rows_refs):
        slot = slots_of(order, slot_ref, local_count * SLOT, ref.shape[0])
        scaled = ref[:, 2 * columns:].astype(F32)
        spread.append(jnp.concatenate([jnp.where(slot == e, scaled, 0.0) for e in range(local_count)], axis=1))
    rows = jnp.concatenate([ref[:, pl.ds(start, columns)] for ref in rows_refs], axis=0)
    return lax.dot_general(
        jnp.concatenate(spread, axis=0).astype(BF16), rows, TN, preferred_element_type=F32)


def other_half_kernel(local_count, dev_count, orders, slot_ref, early_ref, late_ref, out_ref):
    half = 1 - lax.axis_index("dp")
    out_ref[...] = grad_weights_half(
        local_count, dev_count, orders, half, slot_ref, (early_ref, late_ref), out_ref.shape[1]).astype(out_ref.dtype)


def own_half_kernel(local_count, dev_count, orders, slot_ref, early_ref, late_ref, arrived_ref, out_ref):
    half = lax.axis_index("dp")
    total = grad_weights_half(
        local_count, dev_count, orders, half, slot_ref, (early_ref, late_ref), out_ref.shape[1])
    out_ref[...] = (total + arrived_ref[...].astype(F32)).astype(out_ref.dtype)


def combine_kernel(local_count, dev_count, back_ref, pick_ref, expert_ref, hs_ref, ps_ref, ids_ref,
                   grad_h_ref, grad_p_ref, wide, narrow):
    top, toks = ids_ref.shape
    per_home = local_count * SLOT
    me = lax.axis_index("expert")
    back = [back_ref[me ^ m].astype(F32) for m in range(dev_count)]
    slots = pick_ref.shape[0]
    copies = slots - dev_count * per_home
    copy = functools.reduce(jnp.add, [b[per_home:per_home + copies] for b in back])
    grad_in = jnp.concatenate([b[:per_home] for b in back] + [copy], axis=0)
    h_rows = (ps_ref[...] * grad_in).astype(BF16)
    p_rows = jnp.sum(hs_ref[...] * grad_in, axis=1, keepdims=True)
    ids = ids_ref[...]
    pick = pick_ref[...]
    expert = expert_ref[...]
    for k in range(top):
        sel = jnp.where(ids[k:k + 1, :] == expert, pick, 0.0)
        wide[pl.ds(k, toks, stride=top), :] = lax.dot_general(
            sel.astype(BF16), h_rows, TN, preferred_element_type=F32)
        narrow[k:k + 1, :] = jnp.sum(sel * p_rows, axis=0, keepdims=True)
    grad_h_ref[...] = wide[...].astype(grad_h_ref.dtype)
    grad_p_ref[...] = narrow[...].astype(grad_p_ref.dtype)


def call(kernel, out_shape, operands, scratch=(), flops=0, limit=24):
    shapes = jax.tree.leaves(out_shape)
    moved = sum(a.size * a.dtype.itemsize for a in (*(a for _, a in operands), *shapes))
    return pl.pallas_call(
        kernel,
        out_shape=out_shape,
        in_specs=[pl.BlockSpec(memory_space=space) for space, _ in operands],
        out_specs=jax.tree.map(lambda _: pl.BlockSpec(memory_space=pltpu.VMEM), out_shape),
        scratch_shapes=list(scratch),
        compiler_params=pltpu.CompilerParams(vmem_limit_bytes=limit << 20),
        cost_estimate=pl.CostEstimate(flops=flops, bytes_accessed=moved, transcendentals=0),
    )(*(a for _, a in operands))


def swap(x, bits, count):
    return lax.ppermute(x, "expert", [(i, i ^ bits) for i in range(count)])


def gather_body(cotangent, hidden, probs, expert_ids, send_counts, replica_of, weights):
    toks, d_model = cotangent.shape
    top = expert_ids.shape[1]
    width = hidden.shape[2]
    local_count = weights.shape[0]
    dev_count = lax.axis_size("expert")
    homes = dev_count * local_count * SLOT
    copies = dev_count * CAPR
    slots = homes + copies
    rows = homes + dev_count * copies
    columns = d_model // 2
    sizes = (local_count, dev_count)
    ids = expert_ids.T
    shape = jax.ShapeDtypeStruct
    hbm, vmem, smem = pltpu.HBM, pltpu.VMEM, pltpu.SMEM
    sources = (replica_of, send_counts, ids, probs.T, hidden.reshape(toks * top, width), cotangent)
    per_home = local_count * SLOT
    odd, even = range(1, dev_count, 2), range(2, dev_count, 2)
    packing = [[COPIES, *odd], [COPIES], [0, COPIES], [*even]]
    sized = [sum(copies if b == COPIES else per_home for b in blocks) for blocks in packing]
    pick, expert, h_slot, p_slot, to_beside, copy_rows, own_rows, even_rows = call(
        functools.partial(dispatch_kernel, *sizes, packing),
        [shape((slots, toks), F32), shape((slots, toks), jnp.int32), shape((slots, width), F32),
         shape((slots, width), F32)] + [shape((n, d_model + width), BF16) for n in sized],
        [(hbm, a) for a in sources],
        [(smem if n < 2 else vmem)(a.shape, a.dtype) for n, a in enumerate(sources)]
        + [vmem((toks * top, width), F32), pltpu.SemaphoreType.DMA((len(sources),))],
        flops=2 * slots * toks * d_model,
        limit=60,
    )
    beside = swap(to_beside, 1, dev_count)
    near = swap(copy_rows, 2, dev_count)
    far = swap(copy_rows, 4, dev_count)
    flat_w = weights.reshape(local_count * width, d_model)
    own_rows, even_rows, w_held, slot = call(
        functools.partial(hold_kernel, *sizes),
        [shape(a.shape, BF16) for a in (own_rows, even_rows, flat_w)] + [shape((per_home + copies, width), jnp.int32)],
        [(smem, replica_of)] + [(hbm, a) for a in (flat_w, own_rows, even_rows)],
        [pltpu.SemaphoreType.DMA((3,))],
    )
    near, far, beside, own_rows, even_rows, w_held, slot = lax.optimization_barrier(
        (near, far, beside, own_rows, even_rows, w_held, slot))
    far_near = swap(far, 2, dev_count)
    lines = call(
        functools.partial(turn_kernel, *sizes),
        [shape((4 * per_home, fold_width(d_model + width)), BF16)] * len(even),
        [(vmem, a) for a in (beside, even_rows)],
    )
    far_beside, near_beside = swap(far, 1, dev_count), swap(near, 1, dev_count)
    lines = [swap(a, m, dev_count) for a, m in zip(lines, even)]
    pieces = {(0, HOME): (0, 0), (0, COPIES): (0, per_home), (1, COPIES): (1, 0), (1, HOME): (1, copies),
              (2, COPIES): (2, 0), (4, COPIES): (3, 0), (5, COPIES): (4, 0), (3, COPIES): (5, 0)}
    orders = [list(pieces)]
    height = padded(sum(per_home if kind == HOME else copies for _, kind in pieces))
    early_rows, own = call(
        functools.partial(early_kernel, *sizes, orders[0], pieces),
        (shape((height, d_model + width), BF16), shape((height, width), F32)),
        [(vmem, a) for a in (w_held, slot, own_rows, beside, near, far, far_beside, near_beside)],
        flops=2 * height * d_model * local_count * width,
    )
    far_across = swap(far_near, 1, dev_count)
    arrays = [far_near, far_across, *lines[::-1]]
    pieces = {(6, COPIES): (0, 0), (7, COPIES): (1, 0)}
    for n, m in enumerate(even[::-1]):
        pieces[m, HOME], pieces[m + 1, HOME] = ((2 + n, k * per_home) for k in range(2))
    orders.append(list(pieces))
    height = padded(sum(per_home if kind == HOME else copies for _, kind in pieces))
    block = padded(per_home + copies)
    late_rows, back = call(
        functools.partial(late_kernel, *sizes, *orders, pieces),
        (shape((height, d_model + width), BF16), shape((dev_count * block, width), BF16)),
        [(vmem, a) for a in (own, w_held, slot, *arrays)],
        [vmem((dev_count, block, width), F32)],
        flops=2 * height * d_model * local_count * width,
    )
    back = lax.all_to_all(back, "expert", split_axis=0, concat_axis=0, tiled=True)
    half_flops = 2 * rows * columns * local_count * width
    halves = (slot, early_rows, late_rows)
    other = call(
        functools.partial(other_half_kernel, *sizes, orders),
        shape((local_count * width, columns), BF16),
        [(vmem, a) for a in halves],
        flops=half_flops,
    )
    arrived = lax.ppermute(other, "dp", [(0, 1), (1, 0)])
    grad_w = call(
        functools.partial(own_half_kernel, *sizes, orders),
        shape((local_count * width, columns), BF16),
        [(vmem, a) for a in (*halves, arrived)],
        flops=30 * half_flops,
    )
    grad_w, pick = lax.optimization_barrier((grad_w, pick))
    grad_h, grad_p = call(
        functools.partial(combine_kernel, *sizes),
        (shape((toks * top, width), BF16), shape((top, toks), BF16)),
        [(vmem, a) for a in (back.reshape(dev_count, block, width), pick, expert, h_slot, p_slot, ids)],
        [vmem((toks * top, width), F32), vmem((top, toks), F32)],
        flops=2 * slots * toks * width * top,
    )
    return (
        grad_h.reshape(toks, top, width),
        grad_p.T,
        grad_w.reshape(local_count, width, columns),
    )


def body(cotangent, hidden, probs, expert_ids, send_counts, replica_of, weights):
    dev_count = lax.axis_size("expert")
    local_count, width, _ = weights.shape
    gathered = dev_count * dev_count * CAPR
    if gathered <= (local_count + 3) * width and dev_count == 8 and lax.axis_size("dp") == 2:
        run = gather_body
    else:
        run = replica_body
    return run(cotangent, hidden, probs, expert_ids, send_counts, replica_of, weights)


def solution(mesh):
    in_specs = (
        P(("groups", "expert", "dp"), None),
        P(("groups", "expert", "dp"), None, None),
        P(("groups", "expert", "dp"), None),
        P(("groups", "expert", "dp"), None),
        P(("groups", "expert", "dp"), None),
        P("groups"),
        P("expert", None, None),
    )
    out_specs = (
        P(("groups", "expert", "dp"), None, None),
        P(("groups", "expert", "dp"), None),
        P(("groups", "expert"), None, "dp"),
    )
    return jax.shard_map(body, mesh=mesh, in_specs=in_specs, out_specs=out_specs, check_vma=False)
```

```python
import functools

import jax
import jax.numpy as jnp
from jax import lax
from jax.experimental import pallas as pl
from jax.experimental.pallas import tpu as pltpu
from jax.sharding import PartitionSpec as P

CAPH = 3
CAPR = 3


def ranks_within(keys):
    total_rows = keys.shape[0]
    sort_order = jnp.argsort(keys * total_rows + jnp.arange(total_rows, dtype=jnp.int32))
    sorted_keys = keys[sort_order]
    first_seen = jnp.searchsorted(sorted_keys, sorted_keys, side="left")
    ranked = jnp.arange(total_rows, dtype=jnp.int32) - first_seen
    return jnp.zeros((total_rows,), jnp.int32).at[sort_order].set(ranked)


def route_rows(ids_block, counts_row, replica_of, local_count, cap_home, cap_copy):
    dev_count = replica_of.shape[0]
    experts = ids_block.reshape(-1)
    rank_expert = ranks_within(experts)
    devices = jnp.arange(dev_count, dtype=jnp.int32)
    same_copy = (replica_of[:, None] == replica_of[None, :]) & (devices[None, :] < devices[:, None])
    lower_rank = jnp.sum(jnp.where(same_copy, counts_row[None, :], 0), axis=1)
    upper_rank = lower_rank + counts_row
    hit_table = (
        (replica_of[None, :] == experts[:, None])
        & (lower_rank[None, :] <= rank_expert[:, None])
        & (rank_expert[:, None] < upper_rank[None, :])
    )
    copied = jnp.any(hit_table, axis=1)
    copy_dev = jnp.sum(jnp.where(hit_table, devices[None, :], 0), axis=1)
    dest_dev = jnp.where(copied, copy_dev, experts // local_count)
    index_of_slot = jnp.where(copied, local_count, experts % local_count)
    rank_bucket = ranks_within(dest_dev * (local_count + 1) + index_of_slot)
    keep_row = rank_bucket < jnp.where(copied, cap_copy, cap_home)
    per_dev = local_count * cap_home + cap_copy
    target = dest_dev * per_dev + index_of_slot * cap_home + rank_bucket
    return jnp.where(keep_row, target, dev_count * per_dev)


def replica_body(cotangent, hidden, probs, expert_ids, send_counts, replica_of, weights):
    tok_rows, d_model = cotangent.shape
    top_count = expert_ids.shape[1]
    hidden_width = hidden.shape[2]
    local_count = weights.shape[0]
    dev_count = lax.axis_size("expert")
    data_count = lax.axis_size("dp")
    per_dev = local_count * CAPH + CAPR
    row_count = tok_rows * top_count
    recv_count = dev_count * per_dev
    target = route_rows(expert_ids, send_counts[0], replica_of, local_count, CAPH, CAPR)
    inverse = (
        jnp.full((recv_count,), row_count, jnp.int32)
        .at[target]
        .set(jnp.arange(row_count, dtype=jnp.int32), mode="drop")
    )
    dy_pad = jnp.concatenate([cotangent, jnp.zeros((1, d_model), cotangent.dtype)], axis=0)
    h_pad = jnp.concatenate(
        [hidden.reshape(row_count, hidden_width), jnp.zeros((1, hidden_width), hidden.dtype)],
        axis=0,
    )
    p_pad = jnp.concatenate([probs.reshape(row_count), jnp.zeros((1,), probs.dtype)], axis=0)
    send_dy = dy_pad[inverse // top_count]
    send_h = h_pad[inverse]
    send_p = p_pad[inverse]
    recv_dy, recv_h, recv_p = (
        lax.all_to_all(send_dy, "expert", split_axis=0, concat_axis=0, tiled=True),
        lax.all_to_all(send_h, "expert", split_axis=0, concat_axis=0, tiled=True),
        lax.all_to_all(send_p, "expert", split_axis=0, concat_axis=0, tiled=True),
    )
    flat_size = hidden_width * d_model
    flat_w = weights.reshape(local_count, flat_size)
    pieces = lax.all_to_all(flat_w, "expert", split_axis=1, concat_axis=0, tiled=True)
    chosen = pieces[replica_of]
    copy_weight = lax.all_to_all(chosen, "expert", split_axis=0, concat_axis=0, tiled=True).reshape(
        hidden_width, d_model
    )
    slot_total = local_count + 1
    home_rows = local_count * CAPH
    row_pos = jnp.arange(recv_count, dtype=jnp.int32) % per_dev
    row_slot = jnp.where(row_pos < home_rows, row_pos // CAPH, local_count)
    all_weights = jnp.concatenate(
        [weights.reshape(local_count * hidden_width, d_model), copy_weight], axis=0
    )
    all_in = lax.dot_general(
        recv_dy, all_weights, (((1,), (1,)), ((), ())), preferred_element_type=jnp.float32
    )
    grad_in = jnp.zeros((recv_count, hidden_width), jnp.float32)
    for slot_num in range(slot_total):
        grad_in = grad_in + jnp.where(
            (row_slot == slot_num)[:, None],
            all_in[:, slot_num * hidden_width : (slot_num + 1) * hidden_width],
            0.0,
        )
    p_wide = recv_p.astype(jnp.float32)[:, None]
    h_wide = recv_h.astype(jnp.float32)
    grad_h_buf = (p_wide * grad_in).astype(jnp.bfloat16)
    grad_p_buf = jnp.sum(h_wide * grad_in, axis=1).astype(jnp.bfloat16)
    scaled = (p_wide * h_wide).astype(jnp.bfloat16)
    zero_rows = jnp.zeros_like(scaled)
    scaled_wide = jnp.concatenate(
        [
            jnp.where((row_slot == slot_num)[:, None], scaled, zero_rows)
            for slot_num in range(slot_total)
        ],
        axis=1,
    )
    parts = lax.dot_general(
        scaled_wide, recv_dy, (((0,), (0,)), ((), ())), preferred_element_type=jnp.float32
    ).astype(jnp.bfloat16)
    home_part = parts[: local_count * hidden_width].reshape(local_count, hidden_width, d_model)
    copy_part = parts[local_count * hidden_width :]
    back_h, back_p = (
        lax.all_to_all(grad_h_buf, "expert", split_axis=0, concat_axis=0, tiled=True),
        lax.all_to_all(grad_p_buf, "expert", split_axis=0, concat_axis=0, tiled=True),
    )
    flat_h = jnp.concatenate([back_h, jnp.zeros((1, hidden_width), back_h.dtype)], axis=0)
    flat_p = jnp.concatenate([back_p, jnp.zeros((1,), back_p.dtype)], axis=0)
    hidden_gradient = flat_h[target].reshape(tok_rows, top_count, hidden_width)
    grad_probs = flat_p[target].reshape(tok_rows, top_count)
    expert_total = dev_count * local_count
    cover = replica_of[None, :] == jnp.arange(expert_total, dtype=jnp.int32)[:, None]
    half_width = d_model // data_count
    halves = lax.all_to_all(copy_part, "dp", split_axis=1, concat_axis=0, tiled=True)
    copy_half = jnp.sum(
        halves.reshape(data_count, hidden_width, half_width).astype(jnp.float32), axis=0
    )
    piece_len = hidden_width * half_width // dev_count
    slabs = copy_half.reshape(dev_count, piece_len)
    arrived = lax.all_to_all(slabs, "expert", split_axis=0, concat_axis=0, tiled=True)
    sums = jnp.dot(cover.astype(jnp.float32), arrived, precision=lax.Precision.HIGHEST)
    homed = lax.all_to_all(
        sums.reshape(dev_count, local_count * piece_len),
        "expert",
        split_axis=0,
        concat_axis=0,
        tiled=True,
    )
    homed = (
        homed.reshape(dev_count, local_count, piece_len)
        .transpose(1, 0, 2)
        .reshape(local_count, hidden_width, half_width)
    )
    home_half = lax.psum_scatter(
        home_part.astype(jnp.float32).astype(jnp.bfloat16), "dp", scatter_dimension=2, tiled=True
    ).astype(jnp.float32)
    grad_weights = (home_half + homed).astype(jnp.bfloat16)
    return (hidden_gradient, grad_probs, grad_weights)


SLOT = 3
HOME, COPIES = "home", "copies"
F32 = jnp.float32
BF16 = jnp.bfloat16
NT = (((1,), (1,)), ((), ()))
TN = (((0,), (0,)), ((), ()))


def iota(shape, dim):
    return lax.broadcasted_iota(jnp.int32, shape, dim)


def dispatch_kernel(local_count, dev_count, packing, *refs):
    sources, refs = refs[:6], refs[6:]
    pick_ref, expert_ref, hs_ref, ps_ref = refs[:4]
    packed, (held, wide, sems) = refs[4:4 + len(packing)], (refs[-8:-2], refs[-2], refs[-1])
    moves = [pltpu.make_async_copy(s, h, sems.at[n]) for n, (s, h) in enumerate(zip(sources, held))]
    for move in moves:
        move.start()
    replica_ref, counts_ref, ids_ref, probs_ref, hid_ref, cot_ref = held
    top, toks = ids_ref.shape
    per_home = local_count * SLOT
    homes = dev_count * per_home
    slots = homes + dev_count * CAPR
    me = lax.axis_index("expert")
    row = iota((slots, toks), 0)
    expert = ((row // per_home) ^ me) * local_count + (row % per_home) // SLOT
    within = row % SLOT
    allowed = jnp.where(within < CAPH, 1, 0)
    before = jnp.where(iota((toks, toks), 0) < iota((toks, toks), 1), 1.0, 0.0).astype(BF16)
    for move in moves[:3]:
        move.wait()
    for d in range(dev_count):
        first = homes + d * CAPR
        mine = (row >= first) & (row < first + CAPR)
        expert = jnp.where(mine, replica_ref[d], expert)
        within = jnp.where(mine, row - first, within)
        allowed = jnp.where(mine, jnp.where(row - first < counts_ref[0, d], 1, 0), allowed)
    lower = jnp.zeros((slots, toks), jnp.int32)
    for d in range(dev_count):
        earlier = (row < homes) | (row >= homes + (d + 1) * CAPR)
        lower = lower + jnp.where(earlier & (expert == replica_ref[d]), counts_ref[0, d], 0)
    ids = ids_ref[...]
    named = jnp.zeros((slots, toks), F32)
    for k in range(top):
        named = named + jnp.where(ids[k:k + 1, :] == expert, 1.0, 0.0)
    rank = jnp.dot(named.astype(BF16), before, preferred_element_type=F32)
    wanted = (lower + within).astype(F32)
    pick = jnp.where((rank == wanted) & (allowed > 0), named, 0.0)
    pick_ref[...] = pick
    expert_ref[...] = expert
    for move in moves[3:5]:
        move.wait()
    wide[...] = hid_ref[...].astype(F32)
    p_slot = jnp.zeros((slots, toks), F32)
    probs = probs_ref[...].astype(F32)
    chosen, values = [], []
    for k in range(top):
        sel = jnp.where(ids[k:k + 1, :] == expert, pick, 0.0)
        chosen.append(sel.astype(BF16))
        values.append(wide[pl.ds(k, toks, stride=top), :].astype(BF16))
        p_slot = p_slot + sel * probs[k:k + 1, :]
    h_slot = jnp.dot(
        jnp.concatenate(chosen, axis=1), jnp.concatenate(values, axis=0), preferred_element_type=F32)
    p_slot = jnp.sum(p_slot, axis=1, keepdims=True)
    hs_ref[...] = h_slot
    ps_ref[...] = jnp.broadcast_to(p_slot, ps_ref.shape)
    scaled = p_slot * h_slot
    moves[5].wait()
    rows = jnp.dot(pick.astype(BF16), cot_ref[...], preferred_element_type=F32)
    d_model = cot_ref.shape[1]
    for out_ref, blocks in zip(packed, packing):
        spans = [(homes, slots) if b == COPIES else (b * per_home, (b + 1) * per_home) for b in blocks]
        out_ref[:, :d_model] = jnp.concatenate([rows[i:j] for i, j in spans], axis=0).astype(BF16)
        out_ref[:, d_model:] = jnp.concatenate([scaled[i:j] for i, j in spans], axis=0).astype(BF16)


def padded(rows):
    return -(-rows // 16) * 16


def stack(order, blocks, height):
    values = [blocks[key] for key in order]
    missing = height - sum(v.shape[0] for v in values)
    if missing:
        values.append(jnp.zeros((missing, values[0].shape[1]), values[0].dtype))
    return jnp.concatenate(values, axis=0)


def fold_width(columns):
    return -(-columns // 256) * 128


def folded(rows):
    count, columns = rows.shape
    left = fold_width(columns)
    right = [rows[:, left:], jnp.zeros((count, 2 * left - columns), rows.dtype)]
    return jnp.concatenate([rows[:, :left], jnp.concatenate(right, axis=1)], axis=0)


def unfolded(rows, columns):
    count, left = rows.shape
    if left == columns:
        return rows
    return jnp.concatenate([rows[:count // 2], rows[count // 2:, :columns - left]], axis=1)


def slots_of(order, slot_ref, per_home, height):
    kinds = {HOME: slot_ref[:per_home], COPIES: slot_ref[per_home:]}
    return stack(order, {key: kinds[key[1]] for key in order}, height)


def fill_rows(order, pieces, per_home, per_copy, piece_refs, rows_ref):
    values = [unfolded(r[...].astype(F32), rows_ref.shape[1]) for r in piece_refs]
    blocks = {}
    for key in order:
        n, start = pieces[key]
        blocks[key] = values[n][start:start + (per_home if key[1] == HOME else per_copy)]
    rows_ref[...] = stack(order, blocks, rows_ref.shape[0]).astype(BF16)


def own_columns(rows_ref, w_ref, slot, local_count):
    d_model = w_ref.shape[1]
    width = w_ref.shape[0] // local_count
    every = lax.dot_general(rows_ref[:, :d_model], w_ref[...], NT, preferred_element_type=F32)
    own = jnp.zeros((rows_ref.shape[0], width), F32)
    for e in range(local_count):
        own = jnp.where(slot == e, every[:, e * width:(e + 1) * width], own)
    return own


def hold_kernel(local_count, dev_count, replica_ref, w_hbm, own_hbm, even_hbm,
                own_ref, even_ref, w_ref, slot_ref, sems):
    moves = [pltpu.make_async_copy(a, b, sems.at[n]) for n, (a, b) in enumerate(
        ((w_hbm, w_ref), (own_hbm, own_ref), (even_hbm, even_ref)))]
    for move in moves:
        move.start()
    per_home, per_copy = local_count * SLOT, dev_count * CAPR
    first = lax.axis_index("expert") * local_count
    width = slot_ref.shape[1]
    slot_ref[:per_home] = iota((per_home, width), 0) // SLOT
    row = iota((per_copy, width), 0)
    copy = jnp.full((per_copy, width), -1, jnp.int32)
    for d in range(dev_count):
        mine = (row >= d * CAPR) & (row < (d + 1) * CAPR)
        copy = jnp.where(mine, replica_ref[d] - first, copy)
    slot_ref[per_home:] = copy
    for move in moves:
        move.wait()


def turn_kernel(local_count, dev_count, beside_ref, even_ref, *line_refs):
    per_home, per_copy = local_count * SLOT, dev_count * CAPR
    beside = beside_ref[...].astype(F32)[per_copy + per_home:]
    even = even_ref[...].astype(F32)
    for n, line_ref in enumerate(line_refs):
        span = slice(n * per_home, (n + 1) * per_home)
        line_ref[...] = folded(jnp.concatenate([even[span], beside[span]], axis=0)).astype(BF16)


def early_kernel(local_count, dev_count, order, pieces, w_ref, slot_ref, *refs):
    piece_refs, (rows_ref, own_ref) = refs[:-2], refs[-2:]
    per_home, per_copy = local_count * SLOT, dev_count * CAPR
    fill_rows(order, pieces, per_home, per_copy, piece_refs, rows_ref)
    slot = slots_of(order, slot_ref, per_home, rows_ref.shape[0])
    own_ref[...] = own_columns(rows_ref, w_ref, slot, local_count)


def late_kernel(local_count, dev_count, early, order, pieces, own_ref, w_ref, slot_ref, *refs):
    piece_refs, (rows_ref, back_ref, passed) = refs[:-3], refs[-3:]
    per_home, per_copy = local_count * SLOT, dev_count * CAPR
    fill_rows(order, pieces, per_home, per_copy, piece_refs, rows_ref)
    own = own_columns(rows_ref, w_ref, slots_of(order, slot_ref, per_home, rows_ref.shape[0]), local_count)
    if passed.shape[1] > per_home + per_copy:
        passed[:, per_home + per_copy:] = jnp.zeros_like(passed[:, per_home + per_copy:])
    for keys, value in ((early, own_ref[...]), (order, own)):
        start = 0
        for m, kind in keys:
            lower, size = (0, per_home) if kind == HOME else (per_home, per_copy)
            passed[m, lower:lower + size] = value[start:start + size]
            start += size
    me = lax.axis_index("expert")
    back = jnp.concatenate([passed[me ^ source] for source in range(dev_count)], axis=0)
    back_ref[...] = back.astype(back_ref.dtype)


def grad_weights_half(local_count, dev_count, orders, half, slot_ref, rows_refs, columns):
    start = pl.multiple_of(half * columns, 128)
    spread = []
    for order, ref in zip(orders, rows_refs):
        slot = slots_of(order, slot_ref, local_count * SLOT, ref.shape[0])
        scaled = ref[:, 2 * columns:].astype(F32)
        spread.append(jnp.concatenate([jnp.where(slot == e, scaled, 0.0) for e in range(local_count)], axis=1))
    rows = jnp.concatenate([ref[:, pl.ds(start, columns)] for ref in rows_refs], axis=0)
    return lax.dot_general(
        jnp.concatenate(spread, axis=0).astype(BF16), rows, TN, preferred_element_type=F32)


def other_half_kernel(local_count, dev_count, orders, slot_ref, early_ref, late_ref, out_ref):
    half = 1 - lax.axis_index("dp")
    out_ref[...] = grad_weights_half(
        local_count, dev_count, orders, half, slot_ref, (early_ref, late_ref), out_ref.shape[1]).astype(out_ref.dtype)


def own_half_kernel(local_count, dev_count, orders, slot_ref, early_ref, late_ref, arrived_ref, out_ref):
    half = lax.axis_index("dp")
    total = grad_weights_half(
        local_count, dev_count, orders, half, slot_ref, (early_ref, late_ref), out_ref.shape[1])
    out_ref[...] = (total + arrived_ref[...].astype(F32)).astype(out_ref.dtype)


def combine_kernel(local_count, dev_count, back_ref, pick_ref, expert_ref, hs_ref, ps_ref, ids_ref,
                   grad_h_ref, grad_p_ref, wide, narrow):
    top, toks = ids_ref.shape
    per_home = local_count * SLOT
    me = lax.axis_index("expert")
    back = [back_ref[me ^ m].astype(F32) for m in range(dev_count)]
    slots = pick_ref.shape[0]
    copies = slots - dev_count * per_home
    copy = functools.reduce(jnp.add, [b[per_home:per_home + copies] for b in back])
    grad_in = jnp.concatenate([b[:per_home] for b in back] + [copy], axis=0)
    h_rows = (ps_ref[...] * grad_in).astype(BF16)
    p_rows = jnp.sum(hs_ref[...] * grad_in, axis=1, keepdims=True)
    ids = ids_ref[...]
    pick = pick_ref[...]
    expert = expert_ref[...]
    sels = [jnp.where(ids[k:k + 1, :] == expert, pick, 0.0) for k in range(top)]
    rows = lax.dot_general(
        jnp.concatenate([sel.astype(BF16) for sel in sels], axis=1), h_rows, TN, preferred_element_type=F32)
    for k, sel in enumerate(sels):
        wide[pl.ds(k, toks, stride=top), :] = rows[k * toks:(k + 1) * toks]
        narrow[k:k + 1, :] = jnp.sum(sel * p_rows, axis=0, keepdims=True)
    grad_h_ref[...] = wide[...].astype(grad_h_ref.dtype)
    grad_p_ref[...] = narrow[...].astype(grad_p_ref.dtype)


def call(kernel, out_shape, operands, scratch=(), flops=0, limit=24):
    shapes = jax.tree.leaves(out_shape)
    moved = sum(a.size * a.dtype.itemsize for a in (*(a for _, a in operands), *shapes))
    return pl.pallas_call(
        kernel,
        out_shape=out_shape,
        in_specs=[pl.BlockSpec(memory_space=space) for space, _ in operands],
        out_specs=jax.tree.map(lambda _: pl.BlockSpec(memory_space=pltpu.VMEM), out_shape),
        scratch_shapes=list(scratch),
        compiler_params=pltpu.CompilerParams(vmem_limit_bytes=limit << 20),
        cost_estimate=pl.CostEstimate(flops=flops, bytes_accessed=moved, transcendentals=0),
    )(*(a for _, a in operands))


def swap(x, bits, count):
    return lax.ppermute(x, "expert", [(i, i ^ bits) for i in range(count)])


def gather_body(cotangent, hidden, probs, expert_ids, send_counts, replica_of, weights):
    toks, d_model = cotangent.shape
    top = expert_ids.shape[1]
    width = hidden.shape[2]
    local_count = weights.shape[0]
    dev_count = lax.axis_size("expert")
    homes = dev_count * local_count * SLOT
    copies = dev_count * CAPR
    slots = homes + copies
    rows = homes + dev_count * copies
    columns = d_model // 2
    sizes = (local_count, dev_count)
    ids = expert_ids.T
    shape = jax.ShapeDtypeStruct
    hbm, vmem, smem = pltpu.HBM, pltpu.VMEM, pltpu.SMEM
    sources = (replica_of, send_counts, ids, probs.T, hidden.reshape(toks * top, width), cotangent)
    per_home = local_count * SLOT
    odd, even = range(1, dev_count, 2), range(2, dev_count, 2)
    packing = [[COPIES, *odd], [COPIES], [0, COPIES], [*even]]
    sized = [sum(copies if b == COPIES else per_home for b in blocks) for blocks in packing]
    pick, expert, h_slot, p_slot, to_beside, copy_rows, own_rows, even_rows = call(
        functools.partial(dispatch_kernel, *sizes, packing),
        [shape((slots, toks), F32), shape((slots, toks), jnp.int32), shape((slots, width), F32),
         shape((slots, width), F32)] + [shape((n, d_model + width), BF16) for n in sized],
        [(hbm, a) for a in sources],
        [(smem if n < 2 else vmem)(a.shape, a.dtype) for n, a in enumerate(sources)]
        + [vmem((toks * top, width), F32), pltpu.SemaphoreType.DMA((len(sources),))],
        flops=2 * slots * toks * d_model,
        limit=60,
    )
    beside = swap(to_beside, 1, dev_count)
    near = swap(copy_rows, 2, dev_count)
    far = swap(copy_rows, 4, dev_count)
    flat_w = weights.reshape(local_count * width, d_model)
    own_rows, even_rows, w_held, slot = call(
        functools.partial(hold_kernel, *sizes),
        [shape(a.shape, BF16) for a in (own_rows, even_rows, flat_w)] + [shape((per_home + copies, width), jnp.int32)],
        [(smem, replica_of)] + [(hbm, a) for a in (flat_w, own_rows, even_rows)],
        [pltpu.SemaphoreType.DMA((3,))],
    )
    near, far, beside, own_rows, even_rows, w_held, slot = lax.optimization_barrier(
        (near, far, beside, own_rows, even_rows, w_held, slot))
    far_near = swap(far, 2, dev_count)
    lines = call(
        functools.partial(turn_kernel, *sizes),
        [shape((4 * per_home, fold_width(d_model + width)), BF16)] * len(even),
        [(vmem, a) for a in (beside, even_rows)],
    )
    far_beside, near_beside = swap(far, 1, dev_count), swap(near, 1, dev_count)
    lines = [swap(a, m, dev_count) for a, m in zip(lines, even)]
    pieces = {(0, HOME): (0, 0), (0, COPIES): (0, per_home), (1, COPIES): (1, 0), (1, HOME): (1, copies),
              (2, COPIES): (2, 0), (4, COPIES): (3, 0), (5, COPIES): (4, 0), (3, COPIES): (5, 0),
              (even[-1], HOME): (6, 0), (even[-1] + 1, HOME): (6, per_home)}
    orders = [list(pieces)]
    height = padded(sum(per_home if kind == HOME else copies for _, kind in pieces))
    early_rows, own = call(
        functools.partial(early_kernel, *sizes, orders[0], pieces),
        (shape((height, d_model + width), BF16), shape((height, width), F32)),
        [(vmem, a) for a in (w_held, slot, own_rows, beside, near, far, far_beside, near_beside, lines[-1])],
        flops=2 * height * d_model * local_count * width,
    )
    far_across = swap(far_near, 1, dev_count)
    arrays = [far_near, far_across, *lines[-2::-1]]
    pieces = {(6, COPIES): (0, 0), (7, COPIES): (1, 0)}
    for n, m in enumerate(even[-2::-1]):
        pieces[m, HOME], pieces[m + 1, HOME] = ((2 + n, k * per_home) for k in range(2))
    orders.append(list(pieces))
    height = padded(sum(per_home if kind == HOME else copies for _, kind in pieces))
    block = padded(per_home + copies)
    late_rows, back = call(
        functools.partial(late_kernel, *sizes, *orders, pieces),
        (shape((height, d_model + width), BF16), shape((dev_count * block, width), BF16)),
        [(vmem, a) for a in (own, w_held, slot, *arrays)],
        [vmem((dev_count, block, width), F32)],
        flops=2 * height * d_model * local_count * width,
    )
    back = lax.all_to_all(back, "expert", split_axis=0, concat_axis=0, tiled=True)
    half_flops = 2 * rows * columns * local_count * width
    halves = (slot, early_rows, late_rows)
    other = call(
        functools.partial(other_half_kernel, *sizes, orders),
        shape((local_count * width, columns), BF16),
        [(vmem, a) for a in halves],
        flops=half_flops,
    )
    arrived = lax.ppermute(other, "dp", [(0, 1), (1, 0)])
    grad_w = call(
        functools.partial(own_half_kernel, *sizes, orders),
        shape((local_count * width, columns), BF16),
        [(vmem, a) for a in (*halves, arrived)],
        flops=30 * half_flops,
    )
    grad_w, pick = lax.optimization_barrier((grad_w, pick))
    grad_h, grad_p = call(
        functools.partial(combine_kernel, *sizes),
        (shape((toks * top, width), BF16), shape((top, toks), BF16)),
        [(vmem, a) for a in (back.reshape(dev_count, block, width), pick, expert, h_slot, p_slot, ids)],
        [vmem((toks * top, width), F32), vmem((top, toks), F32)],
        flops=2 * slots * toks * width * top,
    )
    return (
        grad_h.reshape(toks, top, width),
        grad_p.T,
        grad_w.reshape(local_count, width, columns),
    )


def body(cotangent, hidden, probs, expert_ids, send_counts, replica_of, weights):
    dev_count = lax.axis_size("expert")
    local_count, width, _ = weights.shape
    gathered = dev_count * dev_count * CAPR
    if gathered <= (local_count + 3) * width and dev_count == 8 and lax.axis_size("dp") == 2:
        run = gather_body
    else:
        run = replica_body
    return run(cotangent, hidden, probs, expert_ids, send_counts, replica_of, weights)


def solution(mesh):
    in_specs = (
        P(("groups", "expert", "dp"), None),
        P(("groups", "expert", "dp"), None, None),
        P(("groups", "expert", "dp"), None),
        P(("groups", "expert", "dp"), None),
        P(("groups", "expert", "dp"), None),
        P("groups"),
        P("expert", None, None),
    )
    out_specs = (
        P(("groups", "expert", "dp"), None, None),
        P(("groups", "expert", "dp"), None),
        P(("groups", "expert"), None, "dp"),
    )
    return jax.shard_map(body, mesh=mesh, in_specs=in_specs, out_specs=out_specs, check_vma=False)
```

```python
import functools

import jax
import jax.numpy as jnp
from jax import lax
from jax.experimental import pallas as pl
from jax.experimental.pallas import tpu as pltpu
from jax.sharding import PartitionSpec as P

CAPH = 3
CAPR = 3


def ranks_within(keys):
    total_rows = keys.shape[0]
    sort_order = jnp.argsort(keys * total_rows + jnp.arange(total_rows, dtype=jnp.int32))
    sorted_keys = keys[sort_order]
    first_seen = jnp.searchsorted(sorted_keys, sorted_keys, side="left")
    ranked = jnp.arange(total_rows, dtype=jnp.int32) - first_seen
    return jnp.zeros((total_rows,), jnp.int32).at[sort_order].set(ranked)


def route_rows(ids_block, counts_row, replica_of, local_count, cap_home, cap_copy):
    dev_count = replica_of.shape[0]
    experts = ids_block.reshape(-1)
    rank_expert = ranks_within(experts)
    devices = jnp.arange(dev_count, dtype=jnp.int32)
    same_copy = (replica_of[:, None] == replica_of[None, :]) & (devices[None, :] < devices[:, None])
    lower_rank = jnp.sum(jnp.where(same_copy, counts_row[None, :], 0), axis=1)
    upper_rank = lower_rank + counts_row
    hit_table = (
        (replica_of[None, :] == experts[:, None])
        & (lower_rank[None, :] <= rank_expert[:, None])
        & (rank_expert[:, None] < upper_rank[None, :])
    )
    copied = jnp.any(hit_table, axis=1)
    copy_dev = jnp.sum(jnp.where(hit_table, devices[None, :], 0), axis=1)
    dest_dev = jnp.where(copied, copy_dev, experts // local_count)
    index_of_slot = jnp.where(copied, local_count, experts % local_count)
    rank_bucket = ranks_within(dest_dev * (local_count + 1) + index_of_slot)
    keep_row = rank_bucket < jnp.where(copied, cap_copy, cap_home)
    per_dev = local_count * cap_home + cap_copy
    target = dest_dev * per_dev + index_of_slot * cap_home + rank_bucket
    return jnp.where(keep_row, target, dev_count * per_dev)


def replica_body(cotangent, hidden, probs, expert_ids, send_counts, replica_of, weights):
    tok_rows, d_model = cotangent.shape
    top_count = expert_ids.shape[1]
    hidden_width = hidden.shape[2]
    local_count = weights.shape[0]
    dev_count = lax.axis_size("expert")
    data_count = lax.axis_size("dp")
    per_dev = local_count * CAPH + CAPR
    row_count = tok_rows * top_count
    recv_count = dev_count * per_dev
    target = route_rows(expert_ids, send_counts[0], replica_of, local_count, CAPH, CAPR)
    inverse = (
        jnp.full((recv_count,), row_count, jnp.int32)
        .at[target]
        .set(jnp.arange(row_count, dtype=jnp.int32), mode="drop")
    )
    dy_pad = jnp.concatenate([cotangent, jnp.zeros((1, d_model), cotangent.dtype)], axis=0)
    h_pad = jnp.concatenate(
        [hidden.reshape(row_count, hidden_width), jnp.zeros((1, hidden_width), hidden.dtype)],
        axis=0,
    )
    p_pad = jnp.concatenate([probs.reshape(row_count), jnp.zeros((1,), probs.dtype)], axis=0)
    send_dy = dy_pad[inverse // top_count]
    send_h = h_pad[inverse]
    send_p = p_pad[inverse]
    recv_dy, recv_h, recv_p = (
        lax.all_to_all(send_dy, "expert", split_axis=0, concat_axis=0, tiled=True),
        lax.all_to_all(send_h, "expert", split_axis=0, concat_axis=0, tiled=True),
        lax.all_to_all(send_p, "expert", split_axis=0, concat_axis=0, tiled=True),
    )
    flat_size = hidden_width * d_model
    flat_w = weights.reshape(local_count, flat_size)
    pieces = lax.all_to_all(flat_w, "expert", split_axis=1, concat_axis=0, tiled=True)
    chosen = pieces[replica_of]
    copy_weight = lax.all_to_all(chosen, "expert", split_axis=0, concat_axis=0, tiled=True).reshape(
        hidden_width, d_model
    )
    slot_total = local_count + 1
    home_rows = local_count * CAPH
    row_pos = jnp.arange(recv_count, dtype=jnp.int32) % per_dev
    row_slot = jnp.where(row_pos < home_rows, row_pos // CAPH, local_count)
    all_weights = jnp.concatenate(
        [weights.reshape(local_count * hidden_width, d_model), copy_weight], axis=0
    )
    all_in = lax.dot_general(
        recv_dy, all_weights, (((1,), (1,)), ((), ())), preferred_element_type=jnp.float32
    )
    grad_in = jnp.zeros((recv_count, hidden_width), jnp.float32)
    for slot_num in range(slot_total):
        grad_in = grad_in + jnp.where(
            (row_slot == slot_num)[:, None],
            all_in[:, slot_num * hidden_width : (slot_num + 1) * hidden_width],
            0.0,
        )
    p_wide = recv_p.astype(jnp.float32)[:, None]
    h_wide = recv_h.astype(jnp.float32)
    grad_h_buf = (p_wide * grad_in).astype(jnp.bfloat16)
    grad_p_buf = jnp.sum(h_wide * grad_in, axis=1).astype(jnp.bfloat16)
    scaled = (p_wide * h_wide).astype(jnp.bfloat16)
    zero_rows = jnp.zeros_like(scaled)
    scaled_wide = jnp.concatenate(
        [
            jnp.where((row_slot == slot_num)[:, None], scaled, zero_rows)
            for slot_num in range(slot_total)
        ],
        axis=1,
    )
    parts = lax.dot_general(
        scaled_wide, recv_dy, (((0,), (0,)), ((), ())), preferred_element_type=jnp.float32
    ).astype(jnp.bfloat16)
    home_part = parts[: local_count * hidden_width].reshape(local_count, hidden_width, d_model)
    copy_part = parts[local_count * hidden_width :]
    back_h, back_p = (
        lax.all_to_all(grad_h_buf, "expert", split_axis=0, concat_axis=0, tiled=True),
        lax.all_to_all(grad_p_buf, "expert", split_axis=0, concat_axis=0, tiled=True),
    )
    flat_h = jnp.concatenate([back_h, jnp.zeros((1, hidden_width), back_h.dtype)], axis=0)
    flat_p = jnp.concatenate([back_p, jnp.zeros((1,), back_p.dtype)], axis=0)
    hidden_gradient = flat_h[target].reshape(tok_rows, top_count, hidden_width)
    grad_probs = flat_p[target].reshape(tok_rows, top_count)
    expert_total = dev_count * local_count
    cover = replica_of[None, :] == jnp.arange(expert_total, dtype=jnp.int32)[:, None]
    half_width = d_model // data_count
    halves = lax.all_to_all(copy_part, "dp", split_axis=1, concat_axis=0, tiled=True)
    copy_half = jnp.sum(
        halves.reshape(data_count, hidden_width, half_width).astype(jnp.float32), axis=0
    )
    piece_len = hidden_width * half_width // dev_count
    slabs = copy_half.reshape(dev_count, piece_len)
    arrived = lax.all_to_all(slabs, "expert", split_axis=0, concat_axis=0, tiled=True)
    sums = jnp.dot(cover.astype(jnp.float32), arrived, precision=lax.Precision.HIGHEST)
    homed = lax.all_to_all(
        sums.reshape(dev_count, local_count * piece_len),
        "expert",
        split_axis=0,
        concat_axis=0,
        tiled=True,
    )
    homed = (
        homed.reshape(dev_count, local_count, piece_len)
        .transpose(1, 0, 2)
        .reshape(local_count, hidden_width, half_width)
    )
    home_half = lax.psum_scatter(
        home_part.astype(jnp.float32).astype(jnp.bfloat16), "dp", scatter_dimension=2, tiled=True
    ).astype(jnp.float32)
    grad_weights = (home_half + homed).astype(jnp.bfloat16)
    return (hidden_gradient, grad_probs, grad_weights)


SLOT = 3
HOME, COPIES = "home", "copies"
F32 = jnp.float32
BF16 = jnp.bfloat16
NT = (((1,), (1,)), ((), ()))
TN = (((0,), (0,)), ((), ()))


def iota(shape, dim):
    return lax.broadcasted_iota(jnp.int32, shape, dim)


def dispatch_kernel(local_count, dev_count, packing, *refs):
    sources, refs = refs[:6], refs[6:]
    pick_ref, expert_ref, hs_ref, ps_ref = refs[:4]
    packed, (held, wide, sems) = refs[4:4 + len(packing)], (refs[-8:-2], refs[-2], refs[-1])
    moves = [pltpu.make_async_copy(s, h, sems.at[n]) for n, (s, h) in enumerate(zip(sources, held))]
    for move in moves:
        move.start()
    replica_ref, counts_ref, ids_ref, probs_ref, hid_ref, cot_ref = held
    top, toks = ids_ref.shape
    per_home = local_count * SLOT
    homes = dev_count * per_home
    slots = homes + dev_count * CAPR
    me = lax.axis_index("expert")
    row = iota((slots, toks), 0)
    expert = ((row // per_home) ^ me) * local_count + (row % per_home) // SLOT
    within = row % SLOT
    allowed = jnp.where(within < CAPH, 1, 0)
    before = jnp.where(iota((toks, toks), 0) < iota((toks, toks), 1), 1.0, 0.0).astype(BF16)
    for move in moves[:3]:
        move.wait()
    for d in range(dev_count):
        first = homes + d * CAPR
        mine = (row >= first) & (row < first + CAPR)
        expert = jnp.where(mine, replica_ref[d], expert)
        within = jnp.where(mine, row - first, within)
        allowed = jnp.where(mine, jnp.where(row - first < counts_ref[0, d], 1, 0), allowed)
    lower = jnp.zeros((slots, toks), jnp.int32)
    for d in range(dev_count):
        earlier = (row < homes) | (row >= homes + (d + 1) * CAPR)
        lower = lower + jnp.where(earlier & (expert == replica_ref[d]), counts_ref[0, d], 0)
    ids = ids_ref[...]
    named = jnp.zeros((slots, toks), F32)
    for k in range(top):
        named = named + jnp.where(ids[k:k + 1, :] == expert, 1.0, 0.0)
    rank = jnp.dot(named.astype(BF16), before, preferred_element_type=F32)
    wanted = (lower + within).astype(F32)
    pick = jnp.where((rank == wanted) & (allowed > 0), named, 0.0)
    pick_ref[...] = pick
    expert_ref[...] = expert
    for move in moves[3:5]:
        move.wait()
    wide[...] = hid_ref[...].astype(F32)
    p_slot = jnp.zeros((slots, toks), F32)
    probs = probs_ref[...].astype(F32)
    chosen, values = [], []
    for k in range(top):
        sel = jnp.where(ids[k:k + 1, :] == expert, pick, 0.0)
        chosen.append(sel.astype(BF16))
        values.append(wide[pl.ds(k, toks, stride=top), :].astype(BF16))
        p_slot = p_slot + sel * probs[k:k + 1, :]
    h_slot = jnp.dot(
        jnp.concatenate(chosen, axis=1), jnp.concatenate(values, axis=0), preferred_element_type=F32)
    p_slot = jnp.sum(p_slot, axis=1, keepdims=True)
    hs_ref[...] = h_slot
    ps_ref[...] = jnp.broadcast_to(p_slot, ps_ref.shape)
    scaled = p_slot * h_slot
    moves[5].wait()
    rows = jnp.dot(pick.astype(BF16), cot_ref[...], preferred_element_type=F32)
    d_model = cot_ref.shape[1]
    for out_ref, blocks in zip(packed, packing):
        spans = [(homes, slots) if b == COPIES else (b * per_home, (b + 1) * per_home) for b in blocks]
        out_ref[:, :d_model] = jnp.concatenate([rows[i:j] for i, j in spans], axis=0).astype(BF16)
        out_ref[:, d_model:] = jnp.concatenate([scaled[i:j] for i, j in spans], axis=0).astype(BF16)


def padded(rows):
    return -(-rows // 16) * 16


def stack(order, blocks, height):
    values = [blocks[key] for key in order]
    missing = height - sum(v.shape[0] for v in values)
    if missing:
        values.append(jnp.zeros((missing, values[0].shape[1]), values[0].dtype))
    return jnp.concatenate(values, axis=0)


def fold_width(columns):
    return -(-columns // 256) * 128


def folded(rows):
    count, columns = rows.shape
    left = fold_width(columns)
    right = [rows[:, left:], jnp.zeros((count, 2 * left - columns), rows.dtype)]
    return jnp.concatenate([rows[:, :left], jnp.concatenate(right, axis=1)], axis=0)


def unfolded(rows, columns):
    count, left = rows.shape
    if left == columns:
        return rows
    return jnp.concatenate([rows[:count // 2], rows[count // 2:, :columns - left]], axis=1)


def slots_of(order, slot_ref, per_home, height):
    kinds = {HOME: slot_ref[:per_home], COPIES: slot_ref[per_home:]}
    return stack(order, {key: kinds[key[1]] for key in order}, height)


def fill_rows(order, pieces, per_home, per_copy, piece_refs, rows_ref):
    values = [unfolded(r[...].astype(F32), rows_ref.shape[1]) for r in piece_refs]
    blocks = {}
    for key in order:
        n, start = pieces[key]
        blocks[key] = values[n][start:start + (per_home if key[1] == HOME else per_copy)]
    rows_ref[...] = stack(order, blocks, rows_ref.shape[0]).astype(BF16)


def own_columns(rows_ref, w_ref, slot, local_count):
    d_model = w_ref.shape[1]
    width = w_ref.shape[0] // local_count
    every = lax.dot_general(rows_ref[:, :d_model], w_ref[...], NT, preferred_element_type=F32)
    own = jnp.zeros((rows_ref.shape[0], width), F32)
    for e in range(local_count):
        own = jnp.where(slot == e, every[:, e * width:(e + 1) * width], own)
    return own


def hold_kernel(local_count, dev_count, replica_ref, w_hbm, own_hbm, even_hbm,
                own_ref, even_ref, w_ref, slot_ref, sems):
    moves = [pltpu.make_async_copy(a, b, sems.at[n]) for n, (a, b) in enumerate(
        ((w_hbm, w_ref), (own_hbm, own_ref), (even_hbm, even_ref)))]
    for move in moves:
        move.start()
    per_home, per_copy = local_count * SLOT, dev_count * CAPR
    first = lax.axis_index("expert") * local_count
    width = slot_ref.shape[1]
    slot_ref[:per_home] = iota((per_home, width), 0) // SLOT
    row = iota((per_copy, width), 0)
    copy = jnp.full((per_copy, width), -1, jnp.int32)
    for d in range(dev_count):
        mine = (row >= d * CAPR) & (row < (d + 1) * CAPR)
        copy = jnp.where(mine, replica_ref[d] - first, copy)
    slot_ref[per_home:] = copy
    for move in moves:
        move.wait()


def turn_kernel(local_count, dev_count, beside_ref, even_ref, *line_refs):
    per_home, per_copy = local_count * SLOT, dev_count * CAPR
    beside = beside_ref[...].astype(F32)[per_home:]
    even = even_ref[...].astype(F32)
    for n, line_ref in enumerate(line_refs):
        span = slice(n * per_home, (n + 1) * per_home)
        line_ref[...] = folded(jnp.concatenate([even[span], beside[span]], axis=0)).astype(BF16)


def early_kernel(local_count, dev_count, order, pieces, w_ref, slot_ref, *refs):
    piece_refs, (rows_ref, own_ref) = refs[:-2], refs[-2:]
    per_home, per_copy = local_count * SLOT, dev_count * CAPR
    fill_rows(order, pieces, per_home, per_copy, piece_refs, rows_ref)
    slot = slots_of(order, slot_ref, per_home, rows_ref.shape[0])
    own_ref[...] = own_columns(rows_ref, w_ref, slot, local_count)


def late_kernel(local_count, dev_count, early, order, pieces, own_ref, w_ref, slot_ref, *refs):
    piece_refs, (rows_ref, back_ref, passed) = refs[:-3], refs[-3:]
    per_home, per_copy = local_count * SLOT, dev_count * CAPR
    fill_rows(order, pieces, per_home, per_copy, piece_refs, rows_ref)
    own = own_columns(rows_ref, w_ref, slots_of(order, slot_ref, per_home, rows_ref.shape[0]), local_count)
    if passed.shape[1] > per_home + per_copy:
        passed[:, per_home + per_copy:] = jnp.zeros_like(passed[:, per_home + per_copy:])
    for keys, value in ((early, own_ref[...]), (order, own)):
        start = 0
        for m, kind in keys:
            lower, size = (0, per_home) if kind == HOME else (per_home, per_copy)
            passed[m, lower:lower + size] = value[start:start + size]
            start += size
    me = lax.axis_index("expert")
    back = jnp.concatenate([passed[me ^ source] for source in range(dev_count)], axis=0)
    back_ref[...] = back.astype(back_ref.dtype)


def grad_weights_half(local_count, dev_count, orders, half, slot_ref, rows_refs, columns):
    start = pl.multiple_of(half * columns, 128)
    spread = []
    for order, ref in zip(orders, rows_refs):
        slot = slots_of(order, slot_ref, local_count * SLOT, ref.shape[0])
        scaled = ref[:, 2 * columns:].astype(F32)
        spread.append(jnp.concatenate([jnp.where(slot == e, scaled, 0.0) for e in range(local_count)], axis=1))
    rows = jnp.concatenate([ref[:, pl.ds(start, columns)] for ref in rows_refs], axis=0)
    return lax.dot_general(
        jnp.concatenate(spread, axis=0).astype(BF16), rows, TN, preferred_element_type=F32)


def other_half_kernel(local_count, dev_count, orders, slot_ref, early_ref, late_ref, out_ref):
    half = 1 - lax.axis_index("dp")
    out_ref[...] = grad_weights_half(
        local_count, dev_count, orders, half, slot_ref, (early_ref, late_ref), out_ref.shape[1]).astype(out_ref.dtype)


def own_half_kernel(local_count, dev_count, orders, slot_ref, early_ref, late_ref, arrived_ref, out_ref):
    half = lax.axis_index("dp")
    total = grad_weights_half(
        local_count, dev_count, orders, half, slot_ref, (early_ref, late_ref), out_ref.shape[1])
    out_ref[...] = (total + arrived_ref[...].astype(F32)).astype(out_ref.dtype)


def combine_kernel(local_count, dev_count, back_ref, pick_ref, expert_ref, hs_ref, ps_ref, ids_ref,
                   grad_h_ref, grad_p_ref, wide, narrow):
    top, toks = ids_ref.shape
    per_home = local_count * SLOT
    me = lax.axis_index("expert")
    back = [back_ref[me ^ m].astype(F32) for m in range(dev_count)]
    slots = pick_ref.shape[0]
    copies = slots - dev_count * per_home
    copy = functools.reduce(jnp.add, [b[per_home:per_home + copies] for b in back])
    grad_in = jnp.concatenate([b[:per_home] for b in back] + [copy], axis=0)
    h_rows = (ps_ref[...] * grad_in).astype(BF16)
    p_rows = jnp.sum(hs_ref[...] * grad_in, axis=1, keepdims=True)
    ids = ids_ref[...]
    pick = pick_ref[...]
    expert = expert_ref[...]
    sels = [jnp.where(ids[k:k + 1, :] == expert, pick, 0.0) for k in range(top)]
    rows = lax.dot_general(
        jnp.concatenate([sel.astype(BF16) for sel in sels], axis=1), h_rows, TN, preferred_element_type=F32)
    for k, sel in enumerate(sels):
        wide[pl.ds(k, toks, stride=top), :] = rows[k * toks:(k + 1) * toks]
        narrow[k:k + 1, :] = jnp.sum(sel * p_rows, axis=0, keepdims=True)
    grad_h_ref[...] = wide[...].astype(grad_h_ref.dtype)
    grad_p_ref[...] = narrow[...].astype(grad_p_ref.dtype)


def call(kernel, out_shape, operands, scratch=(), flops=0, limit=24):
    shapes = jax.tree.leaves(out_shape)
    moved = sum(a.size * a.dtype.itemsize for a in (*(a for _, a in operands), *shapes))
    return pl.pallas_call(
        kernel,
        out_shape=out_shape,
        in_specs=[pl.BlockSpec(memory_space=space) for space, _ in operands],
        out_specs=jax.tree.map(lambda _: pl.BlockSpec(memory_space=pltpu.VMEM), out_shape),
        scratch_shapes=list(scratch),
        compiler_params=pltpu.CompilerParams(vmem_limit_bytes=limit << 20),
        cost_estimate=pl.CostEstimate(flops=flops, bytes_accessed=moved, transcendentals=0),
    )(*(a for _, a in operands))


def swap(x, bits, count):
    return lax.ppermute(x, "expert", [(i, i ^ bits) for i in range(count)])


def gather_body(cotangent, hidden, probs, expert_ids, send_counts, replica_of, weights):
    toks, d_model = cotangent.shape
    top = expert_ids.shape[1]
    width = hidden.shape[2]
    local_count = weights.shape[0]
    dev_count = lax.axis_size("expert")
    homes = dev_count * local_count * SLOT
    copies = dev_count * CAPR
    slots = homes + copies
    rows = homes + dev_count * copies
    columns = d_model // 2
    sizes = (local_count, dev_count)
    ids = expert_ids.T
    shape = jax.ShapeDtypeStruct
    hbm, vmem, smem = pltpu.HBM, pltpu.VMEM, pltpu.SMEM
    sources = (replica_of, send_counts, ids, probs.T, hidden.reshape(toks * top, width), cotangent)
    per_home = local_count * SLOT
    odd, even = range(1, dev_count, 2), range(2, dev_count, 2)
    packing = [[*odd], [COPIES], [0, COPIES], [*even]]
    sized = [sum(copies if b == COPIES else per_home for b in blocks) for blocks in packing]
    pick, expert, h_slot, p_slot, to_beside, copy_rows, own_rows, even_rows = call(
        functools.partial(dispatch_kernel, *sizes, packing),
        [shape((slots, toks), F32), shape((slots, toks), jnp.int32), shape((slots, width), F32),
         shape((slots, width), F32)] + [shape((n, d_model + width), BF16) for n in sized],
        [(hbm, a) for a in sources],
        [(smem if n < 2 else vmem)(a.shape, a.dtype) for n, a in enumerate(sources)]
        + [vmem((toks * top, width), F32), pltpu.SemaphoreType.DMA((len(sources),))],
        flops=2 * slots * toks * d_model,
        limit=60,
    )
    near, far, beside = (swap(copy_rows, bits, dev_count) for bits in (2, 4, 1))
    line = swap(to_beside, 1, dev_count)
    flat_w = weights.reshape(local_count * width, d_model)
    own_rows, even_rows, w_held, slot = call(
        functools.partial(hold_kernel, *sizes),
        [shape(a.shape, BF16) for a in (own_rows, even_rows, flat_w)] + [shape((per_home + copies, width), jnp.int32)],
        [(smem, replica_of)] + [(hbm, a) for a in (flat_w, own_rows, even_rows)],
        [pltpu.SemaphoreType.DMA((3,))],
    )
    near, far, line, beside, own_rows, even_rows, w_held, slot = lax.optimization_barrier(
        (near, far, line, beside, own_rows, even_rows, w_held, slot))
    far_near = swap(far, 2, dev_count)
    lines = call(
        functools.partial(turn_kernel, *sizes),
        [shape((4 * per_home, fold_width(d_model + width)), BF16)] * len(even),
        [(vmem, a) for a in (line, even_rows)],
    )
    far_beside, near_beside = swap(far, 1, dev_count), swap(near, 1, dev_count)
    lines = [swap(a, m, dev_count) for a, m in zip(lines, even)]
    pieces = {(0, HOME): (0, 0), (0, COPIES): (0, per_home), (1, COPIES): (1, 0), (1, HOME): (7, 0),
              (2, COPIES): (2, 0), (4, COPIES): (3, 0), (5, COPIES): (4, 0), (3, COPIES): (5, 0),
              (even[-1], HOME): (6, 0), (even[-1] + 1, HOME): (6, per_home)}
    orders = [list(pieces)]
    height = padded(sum(per_home if kind == HOME else copies for _, kind in pieces))
    early_rows, own = call(
        functools.partial(early_kernel, *sizes, orders[0], pieces),
        (shape((height, d_model + width), BF16), shape((height, width), F32)),
        [(vmem, a) for a in (w_held, slot, own_rows, beside, near, far, far_beside, near_beside, lines[-1], line)],
        flops=2 * height * d_model * local_count * width,
    )
    far_across = swap(far_near, 1, dev_count)
    arrays = [far_near, far_across, *lines[:-1]]
    pieces = {(6, COPIES): (0, 0), (7, COPIES): (1, 0)}
    for n, m in enumerate(even[:-1]):
        pieces[m, HOME], pieces[m + 1, HOME] = ((2 + n, k * per_home) for k in range(2))
    orders.append(list(pieces))
    height = padded(sum(per_home if kind == HOME else copies for _, kind in pieces))
    block = padded(per_home + copies)
    late_rows, back = call(
        functools.partial(late_kernel, *sizes, *orders, pieces),
        (shape((height, d_model + width), BF16), shape((dev_count * block, width), BF16)),
        [(vmem, a) for a in (own, w_held, slot, *arrays)],
        [vmem((dev_count, block, width), F32)],
        flops=2 * height * d_model * local_count * width,
    )
    back = lax.all_to_all(back, "expert", split_axis=0, concat_axis=0, tiled=True)
    half_flops = 2 * rows * columns * local_count * width
    halves = (slot, early_rows, late_rows)
    other = call(
        functools.partial(other_half_kernel, *sizes, orders),
        shape((local_count * width, columns), BF16),
        [(vmem, a) for a in halves],
        flops=half_flops,
    )
    arrived = lax.ppermute(other, "dp", [(0, 1), (1, 0)])
    grad_w = call(
        functools.partial(own_half_kernel, *sizes, orders),
        shape((local_count * width, columns), BF16),
        [(vmem, a) for a in (*halves, arrived)],
        flops=30 * half_flops,
    )
    grad_w, pick = lax.optimization_barrier((grad_w, pick))
    grad_h, grad_p = call(
        functools.partial(combine_kernel, *sizes),
        (shape((toks * top, width), BF16), shape((top, toks), BF16)),
        [(vmem, a) for a in (back.reshape(dev_count, block, width), pick, expert, h_slot, p_slot, ids)],
        [vmem((toks * top, width), F32), vmem((top, toks), F32)],
        flops=2 * slots * toks * width * top,
    )
    return (
        grad_h.reshape(toks, top, width),
        grad_p.T,
        grad_w.reshape(local_count, width, columns),
    )


def body(cotangent, hidden, probs, expert_ids, send_counts, replica_of, weights):
    dev_count = lax.axis_size("expert")
    local_count, width, _ = weights.shape
    gathered = dev_count * dev_count * CAPR
    if gathered <= (local_count + 3) * width and dev_count == 8 and lax.axis_size("dp") == 2:
        run = gather_body
    else:
        run = replica_body
    return run(cotangent, hidden, probs, expert_ids, send_counts, replica_of, weights)


def solution(mesh):
    in_specs = (
        P(("groups", "expert", "dp"), None),
        P(("groups", "expert", "dp"), None, None),
        P(("groups", "expert", "dp"), None),
        P(("groups", "expert", "dp"), None),
        P(("groups", "expert", "dp"), None),
        P("groups"),
        P("expert", None, None),
    )
    out_specs = (
        P(("groups", "expert", "dp"), None, None),
        P(("groups", "expert", "dp"), None),
        P(("groups", "expert"), None, "dp"),
    )
    return jax.shard_map(body, mesh=mesh, in_specs=in_specs, out_specs=out_specs, check_vma=False)
```

```python
import functools

import jax
import jax.numpy as jnp
from jax import lax
from jax.experimental import pallas as pl
from jax.experimental.pallas import tpu as pltpu
from jax.sharding import PartitionSpec as P

CAPH = 3
CAPR = 3


def ranks_within(keys):
    total_rows = keys.shape[0]
    sort_order = jnp.argsort(keys * total_rows + jnp.arange(total_rows, dtype=jnp.int32))
    sorted_keys = keys[sort_order]
    first_seen = jnp.searchsorted(sorted_keys, sorted_keys, side="left")
    ranked = jnp.arange(total_rows, dtype=jnp.int32) - first_seen
    return jnp.zeros((total_rows,), jnp.int32).at[sort_order].set(ranked)


def route_rows(ids_block, counts_row, replica_of, local_count, cap_home, cap_copy):
    dev_count = replica_of.shape[0]
    experts = ids_block.reshape(-1)
    rank_expert = ranks_within(experts)
    devices = jnp.arange(dev_count, dtype=jnp.int32)
    same_copy = (replica_of[:, None] == replica_of[None, :]) & (devices[None, :] < devices[:, None])
    lower_rank = jnp.sum(jnp.where(same_copy, counts_row[None, :], 0), axis=1)
    upper_rank = lower_rank + counts_row
    hit_table = (
        (replica_of[None, :] == experts[:, None])
        & (lower_rank[None, :] <= rank_expert[:, None])
        & (rank_expert[:, None] < upper_rank[None, :])
    )
    copied = jnp.any(hit_table, axis=1)
    copy_dev = jnp.sum(jnp.where(hit_table, devices[None, :], 0), axis=1)
    dest_dev = jnp.where(copied, copy_dev, experts // local_count)
    index_of_slot = jnp.where(copied, local_count, experts % local_count)
    rank_bucket = ranks_within(dest_dev * (local_count + 1) + index_of_slot)
    keep_row = rank_bucket < jnp.where(copied, cap_copy, cap_home)
    per_dev = local_count * cap_home + cap_copy
    target = dest_dev * per_dev + index_of_slot * cap_home + rank_bucket
    return jnp.where(keep_row, target, dev_count * per_dev)


def replica_body(cotangent, hidden, probs, expert_ids, send_counts, replica_of, weights):
    tok_rows, d_model = cotangent.shape
    top_count = expert_ids.shape[1]
    hidden_width = hidden.shape[2]
    local_count = weights.shape[0]
    dev_count = lax.axis_size("expert")
    data_count = lax.axis_size("dp")
    per_dev = local_count * CAPH + CAPR
    row_count = tok_rows * top_count
    recv_count = dev_count * per_dev
    target = route_rows(expert_ids, send_counts[0], replica_of, local_count, CAPH, CAPR)
    inverse = (
        jnp.full((recv_count,), row_count, jnp.int32)
        .at[target]
        .set(jnp.arange(row_count, dtype=jnp.int32), mode="drop")
    )
    dy_pad = jnp.concatenate([cotangent, jnp.zeros((1, d_model), cotangent.dtype)], axis=0)
    h_pad = jnp.concatenate(
        [hidden.reshape(row_count, hidden_width), jnp.zeros((1, hidden_width), hidden.dtype)],
        axis=0,
    )
    p_pad = jnp.concatenate([probs.reshape(row_count), jnp.zeros((1,), probs.dtype)], axis=0)
    send_dy = dy_pad[inverse // top_count]
    send_h = h_pad[inverse]
    send_p = p_pad[inverse]
    recv_dy, recv_h, recv_p = (
        lax.all_to_all(send_dy, "expert", split_axis=0, concat_axis=0, tiled=True),
        lax.all_to_all(send_h, "expert", split_axis=0, concat_axis=0, tiled=True),
        lax.all_to_all(send_p, "expert", split_axis=0, concat_axis=0, tiled=True),
    )
    flat_size = hidden_width * d_model
    flat_w = weights.reshape(local_count, flat_size)
    pieces = lax.all_to_all(flat_w, "expert", split_axis=1, concat_axis=0, tiled=True)
    chosen = pieces[replica_of]
    copy_weight = lax.all_to_all(chosen, "expert", split_axis=0, concat_axis=0, tiled=True).reshape(
        hidden_width, d_model
    )
    slot_total = local_count + 1
    home_rows = local_count * CAPH
    row_pos = jnp.arange(recv_count, dtype=jnp.int32) % per_dev
    row_slot = jnp.where(row_pos < home_rows, row_pos // CAPH, local_count)
    all_weights = jnp.concatenate(
        [weights.reshape(local_count * hidden_width, d_model), copy_weight], axis=0
    )
    all_in = lax.dot_general(
        recv_dy, all_weights, (((1,), (1,)), ((), ())), preferred_element_type=jnp.float32
    )
    grad_in = jnp.zeros((recv_count, hidden_width), jnp.float32)
    for slot_num in range(slot_total):
        grad_in = grad_in + jnp.where(
            (row_slot == slot_num)[:, None],
            all_in[:, slot_num * hidden_width : (slot_num + 1) * hidden_width],
            0.0,
        )
    p_wide = recv_p.astype(jnp.float32)[:, None]
    h_wide = recv_h.astype(jnp.float32)
    grad_h_buf = (p_wide * grad_in).astype(jnp.bfloat16)
    grad_p_buf = jnp.sum(h_wide * grad_in, axis=1).astype(jnp.bfloat16)
    scaled = (p_wide * h_wide).astype(jnp.bfloat16)
    zero_rows = jnp.zeros_like(scaled)
    scaled_wide = jnp.concatenate(
        [
            jnp.where((row_slot == slot_num)[:, None], scaled, zero_rows)
            for slot_num in range(slot_total)
        ],
        axis=1,
    )
    parts = lax.dot_general(
        scaled_wide, recv_dy, (((0,), (0,)), ((), ())), preferred_element_type=jnp.float32
    ).astype(jnp.bfloat16)
    home_part = parts[: local_count * hidden_width].reshape(local_count, hidden_width, d_model)
    copy_part = parts[local_count * hidden_width :]
    back_h, back_p = (
        lax.all_to_all(grad_h_buf, "expert", split_axis=0, concat_axis=0, tiled=True),
        lax.all_to_all(grad_p_buf, "expert", split_axis=0, concat_axis=0, tiled=True),
    )
    flat_h = jnp.concatenate([back_h, jnp.zeros((1, hidden_width), back_h.dtype)], axis=0)
    flat_p = jnp.concatenate([back_p, jnp.zeros((1,), back_p.dtype)], axis=0)
    hidden_gradient = flat_h[target].reshape(tok_rows, top_count, hidden_width)
    grad_probs = flat_p[target].reshape(tok_rows, top_count)
    expert_total = dev_count * local_count
    cover = replica_of[None, :] == jnp.arange(expert_total, dtype=jnp.int32)[:, None]
    half_width = d_model // data_count
    halves = lax.all_to_all(copy_part, "dp", split_axis=1, concat_axis=0, tiled=True)
    copy_half = jnp.sum(
        halves.reshape(data_count, hidden_width, half_width).astype(jnp.float32), axis=0
    )
    piece_len = hidden_width * half_width // dev_count
    slabs = copy_half.reshape(dev_count, piece_len)
    arrived = lax.all_to_all(slabs, "expert", split_axis=0, concat_axis=0, tiled=True)
    sums = jnp.dot(cover.astype(jnp.float32), arrived, precision=lax.Precision.HIGHEST)
    homed = lax.all_to_all(
        sums.reshape(dev_count, local_count * piece_len),
        "expert",
        split_axis=0,
        concat_axis=0,
        tiled=True,
    )
    homed = (
        homed.reshape(dev_count, local_count, piece_len)
        .transpose(1, 0, 2)
        .reshape(local_count, hidden_width, half_width)
    )
    home_half = lax.psum_scatter(
        home_part.astype(jnp.float32).astype(jnp.bfloat16), "dp", scatter_dimension=2, tiled=True
    ).astype(jnp.float32)
    grad_weights = (home_half + homed).astype(jnp.bfloat16)
    return (hidden_gradient, grad_probs, grad_weights)


SLOT = 3
HOME, COPIES = "home", "copies"
F32 = jnp.float32
BF16 = jnp.bfloat16
NT = (((1,), (1,)), ((), ()))
TN = (((0,), (0,)), ((), ()))


def iota(shape, dim):
    return lax.broadcasted_iota(jnp.int32, shape, dim)


def dispatch_kernel(local_count, dev_count, packing, *refs):
    sources, refs = refs[:6], refs[6:]
    pick_ref, expert_ref, hs_ref, ps_ref = refs[:4]
    packed, (held, wide, sems) = refs[4:4 + len(packing)], (refs[-8:-2], refs[-2], refs[-1])
    moves = [pltpu.make_async_copy(s, h, sems.at[n]) for n, (s, h) in enumerate(zip(sources, held))]
    for move in moves:
        move.start()
    replica_ref, counts_ref, ids_ref, probs_ref, hid_ref, cot_ref = held
    top, toks = ids_ref.shape
    per_home = local_count * SLOT
    homes = dev_count * per_home
    slots = homes + dev_count * CAPR
    me = lax.axis_index("expert")
    row = iota((slots, toks), 0)
    expert = ((row // per_home) ^ me) * local_count + (row % per_home) // SLOT
    within = row % SLOT
    allowed = jnp.where(within < CAPH, 1, 0)
    before = jnp.where(iota((toks, toks), 0) < iota((toks, toks), 1), 1.0, 0.0).astype(BF16)
    for move in moves[:3]:
        move.wait()
    for d in range(dev_count):
        first = homes + d * CAPR
        mine = (row >= first) & (row < first + CAPR)
        expert = jnp.where(mine, replica_ref[d], expert)
        within = jnp.where(mine, row - first, within)
        allowed = jnp.where(mine, jnp.where(row - first < counts_ref[0, d], 1, 0), allowed)
    lower = jnp.zeros((slots, toks), jnp.int32)
    for d in range(dev_count):
        earlier = (row < homes) | (row >= homes + (d + 1) * CAPR)
        lower = lower + jnp.where(earlier & (expert == replica_ref[d]), counts_ref[0, d], 0)
    ids = ids_ref[...]
    named = jnp.zeros((slots, toks), F32)
    for k in range(top):
        named = named + jnp.where(ids[k:k + 1, :] == expert, 1.0, 0.0)
    rank = jnp.dot(named.astype(BF16), before, preferred_element_type=F32)
    wanted = (lower + within).astype(F32)
    pick = jnp.where((rank == wanted) & (allowed > 0), named, 0.0)
    pick_ref[...] = pick
    expert_ref[...] = expert
    for move in moves[3:5]:
        move.wait()
    wide[...] = hid_ref[...].astype(F32)
    p_slot = jnp.zeros((slots, toks), F32)
    probs = probs_ref[...].astype(F32)
    chosen, values = [], []
    for k in range(top):
        sel = jnp.where(ids[k:k + 1, :] == expert, pick, 0.0)
        chosen.append(sel.astype(BF16))
        values.append(wide[pl.ds(k, toks, stride=top), :].astype(BF16))
        p_slot = p_slot + sel * probs[k:k + 1, :]
    h_slot = jnp.dot(
        jnp.concatenate(chosen, axis=1), jnp.concatenate(values, axis=0), preferred_element_type=F32)
    p_slot = jnp.sum(p_slot, axis=1, keepdims=True)
    hs_ref[...] = h_slot
    ps_ref[...] = jnp.broadcast_to(p_slot, ps_ref.shape)
    scaled = p_slot * h_slot
    moves[5].wait()
    rows = jnp.dot(pick.astype(BF16), cot_ref[...], preferred_element_type=F32)
    d_model = cot_ref.shape[1]
    for out_ref, blocks in zip(packed, packing):
        spans = [(homes, slots) if b == COPIES else (b * per_home, (b + 1) * per_home) for b in blocks]
        out_ref[:, :d_model] = jnp.concatenate([rows[i:j] for i, j in spans], axis=0).astype(BF16)
        out_ref[:, d_model:] = jnp.concatenate([scaled[i:j] for i, j in spans], axis=0).astype(BF16)


def padded(rows):
    return -(-rows // 16) * 16


def stack(order, blocks, height):
    values = [blocks[key] for key in order]
    missing = height - sum(v.shape[0] for v in values)
    if missing:
        values.append(jnp.zeros((missing, values[0].shape[1]), values[0].dtype))
    return jnp.concatenate(values, axis=0)


def fold_width(columns):
    return -(-columns // 256) * 128


def folded(rows):
    count, columns = rows.shape
    left = fold_width(columns)
    right = [rows[:, left:], jnp.zeros((count, 2 * left - columns), rows.dtype)]
    return jnp.concatenate([rows[:, :left], jnp.concatenate(right, axis=1)], axis=0)


def unfolded(rows, columns):
    count, left = rows.shape
    if left == columns:
        return rows
    return jnp.concatenate([rows[:count // 2], rows[count // 2:, :columns - left]], axis=1)


def slots_of(order, slot_ref, per_home, height):
    kinds = {HOME: slot_ref[:per_home], COPIES: slot_ref[per_home:]}
    return stack(order, {key: kinds[key[1]] for key in order}, height)


def fill_rows(order, pieces, per_home, per_copy, piece_refs, rows_ref):
    values = [unfolded(r[...].astype(F32), rows_ref.shape[1]) for r in piece_refs]
    blocks = {}
    for key in order:
        n, start = pieces[key]
        blocks[key] = values[n][start:start + (per_home if key[1] == HOME else per_copy)]
    rows_ref[...] = stack(order, blocks, rows_ref.shape[0]).astype(BF16)


def own_columns(rows_ref, w_ref, slot, local_count):
    d_model = w_ref.shape[1]
    width = w_ref.shape[0] // local_count
    every = lax.dot_general(rows_ref[:, :d_model], w_ref[...], NT, preferred_element_type=F32)
    own = jnp.zeros((rows_ref.shape[0], width), F32)
    for e in range(local_count):
        own = jnp.where(slot == e, every[:, e * width:(e + 1) * width], own)
    return own


def hold_kernel(local_count, dev_count, replica_ref, w_hbm, own_hbm, even_hbm,
                own_ref, even_ref, w_ref, slot_ref, sems):
    moves = [pltpu.make_async_copy(a, b, sems.at[n]) for n, (a, b) in enumerate(
        ((w_hbm, w_ref), (own_hbm, own_ref), (even_hbm, even_ref)))]
    for move in moves:
        move.start()
    per_home, per_copy = local_count * SLOT, dev_count * CAPR
    first = lax.axis_index("expert") * local_count
    width = slot_ref.shape[1]
    slot_ref[:per_home] = iota((per_home, width), 0) // SLOT
    row = iota((per_copy, width), 0)
    copy = jnp.full((per_copy, width), -1, jnp.int32)
    for d in range(dev_count):
        mine = (row >= d * CAPR) & (row < (d + 1) * CAPR)
        copy = jnp.where(mine, replica_ref[d] - first, copy)
    slot_ref[per_home:] = copy
    for move in moves:
        move.wait()


def turn_kernel(local_count, dev_count, line_ref, far_ref, near_ref, even_ref, near_out, beside_out, *line_outs):
    per_home = local_count * SLOT
    far, line, even = far_ref[...].astype(F32), line_ref[...].astype(F32)[per_home:], even_ref[...].astype(F32)
    beside_out[...] = jnp.concatenate([far, near_ref[...].astype(F32)], axis=0).astype(BF16)
    for n, out_ref in enumerate((near_out, *line_outs)):
        span = slice(n * per_home, (n + 1) * per_home)
        rows = jnp.concatenate([far] * (n == 0) + [even[span], line[span]], axis=0)
        out_ref[...] = (folded(rows) if n else rows).astype(BF16)


def early_kernel(local_count, dev_count, order, pieces, w_ref, slot_ref, *refs):
    piece_refs, (rows_ref, own_ref) = refs[:-2], refs[-2:]
    per_home, per_copy = local_count * SLOT, dev_count * CAPR
    fill_rows(order, pieces, per_home, per_copy, piece_refs, rows_ref)
    slot = slots_of(order, slot_ref, per_home, rows_ref.shape[0])
    own_ref[...] = own_columns(rows_ref, w_ref, slot, local_count)


def late_kernel(local_count, dev_count, early, order, pieces, own_ref, w_ref, slot_ref, *refs):
    piece_refs, (rows_ref, back_ref, passed) = refs[:-3], refs[-3:]
    per_home, per_copy = local_count * SLOT, dev_count * CAPR
    fill_rows(order, pieces, per_home, per_copy, piece_refs, rows_ref)
    own = own_columns(rows_ref, w_ref, slots_of(order, slot_ref, per_home, rows_ref.shape[0]), local_count)
    if passed.shape[1] > per_home + per_copy:
        passed[:, per_home + per_copy:] = jnp.zeros_like(passed[:, per_home + per_copy:])
    for keys, value in ((early, own_ref[...]), (order, own)):
        start = 0
        for m, kind in keys:
            lower, size = (0, per_home) if kind == HOME else (per_home, per_copy)
            passed[m, lower:lower + size] = value[start:start + size]
            start += size
    me = lax.axis_index("expert")
    back = jnp.concatenate([passed[me ^ source] for source in range(dev_count)], axis=0)
    back_ref[...] = back.astype(back_ref.dtype)


def grad_weights_half(local_count, dev_count, orders, half, slot_ref, rows_refs, columns):
    start = pl.multiple_of(half * columns, 128)
    spread = []
    for order, ref in zip(orders, rows_refs):
        slot = slots_of(order, slot_ref, local_count * SLOT, ref.shape[0])
        scaled = ref[:, 2 * columns:].astype(F32)
        spread.append(jnp.concatenate([jnp.where(slot == e, scaled, 0.0) for e in range(local_count)], axis=1))
    rows = jnp.concatenate([ref[:, pl.ds(start, columns)] for ref in rows_refs], axis=0)
    return lax.dot_general(
        jnp.concatenate(spread, axis=0).astype(BF16), rows, TN, preferred_element_type=F32)


def other_half_kernel(local_count, dev_count, orders, slot_ref, early_ref, late_ref, out_ref):
    half = 1 - lax.axis_index("dp")
    out_ref[...] = grad_weights_half(
        local_count, dev_count, orders, half, slot_ref, (early_ref, late_ref), out_ref.shape[1]).astype(out_ref.dtype)


def own_half_kernel(local_count, dev_count, orders, slot_ref, early_ref, late_ref, arrived_ref, out_ref):
    half = lax.axis_index("dp")
    total = grad_weights_half(
        local_count, dev_count, orders, half, slot_ref, (early_ref, late_ref), out_ref.shape[1])
    out_ref[...] = (total + arrived_ref[...].astype(F32)).astype(out_ref.dtype)


def combine_kernel(local_count, dev_count, back_ref, pick_ref, expert_ref, hs_ref, ps_ref, ids_ref,
                   grad_h_ref, grad_p_ref, wide, narrow):
    top, toks = ids_ref.shape
    per_home = local_count * SLOT
    me = lax.axis_index("expert")
    back = [back_ref[me ^ m].astype(F32) for m in range(dev_count)]
    slots = pick_ref.shape[0]
    copies = slots - dev_count * per_home
    copy = functools.reduce(jnp.add, [b[per_home:per_home + copies] for b in back])
    grad_in = jnp.concatenate([b[:per_home] for b in back] + [copy], axis=0)
    h_rows = (ps_ref[...] * grad_in).astype(BF16)
    p_rows = jnp.sum(hs_ref[...] * grad_in, axis=1, keepdims=True)
    ids = ids_ref[...]
    pick = pick_ref[...]
    expert = expert_ref[...]
    sels = [jnp.where(ids[k:k + 1, :] == expert, pick, 0.0) for k in range(top)]
    rows = lax.dot_general(
        jnp.concatenate([sel.astype(BF16) for sel in sels], axis=1), h_rows, TN, preferred_element_type=F32)
    for k, sel in enumerate(sels):
        wide[pl.ds(k, toks, stride=top), :] = rows[k * toks:(k + 1) * toks]
        narrow[k:k + 1, :] = jnp.sum(sel * p_rows, axis=0, keepdims=True)
    grad_h_ref[...] = wide[...].astype(grad_h_ref.dtype)
    grad_p_ref[...] = narrow[...].astype(grad_p_ref.dtype)


def call(kernel, out_shape, operands, scratch=(), flops=0, limit=24):
    shapes = jax.tree.leaves(out_shape)
    moved = sum(a.size * a.dtype.itemsize for a in (*(a for _, a in operands), *shapes))
    return pl.pallas_call(
        kernel,
        out_shape=out_shape,
        in_specs=[pl.BlockSpec(memory_space=space) for space, _ in operands],
        out_specs=jax.tree.map(lambda _: pl.BlockSpec(memory_space=pltpu.VMEM), out_shape),
        scratch_shapes=list(scratch),
        compiler_params=pltpu.CompilerParams(vmem_limit_bytes=limit << 20),
        cost_estimate=pl.CostEstimate(flops=flops, bytes_accessed=moved, transcendentals=0),
    )(*(a for _, a in operands))


def swap(x, bits, count):
    return lax.ppermute(x, "expert", [(i, i ^ bits) for i in range(count)])


def gather_body(cotangent, hidden, probs, expert_ids, send_counts, replica_of, weights):
    toks, d_model = cotangent.shape
    top = expert_ids.shape[1]
    width = hidden.shape[2]
    local_count = weights.shape[0]
    dev_count = lax.axis_size("expert")
    homes = dev_count * local_count * SLOT
    copies = dev_count * CAPR
    slots = homes + copies
    rows = homes + dev_count * copies
    columns = d_model // 2
    sizes = (local_count, dev_count)
    ids = expert_ids.T
    shape = jax.ShapeDtypeStruct
    hbm, vmem, smem = pltpu.HBM, pltpu.VMEM, pltpu.SMEM
    sources = (replica_of, send_counts, ids, probs.T, hidden.reshape(toks * top, width), cotangent)
    per_home = local_count * SLOT
    odd, even = range(1, dev_count, 2), range(2, dev_count, 2)
    packing = [[*odd], [COPIES], [0, COPIES], [*even]]
    sized = [sum(copies if b == COPIES else per_home for b in blocks) for blocks in packing]
    pick, expert, h_slot, p_slot, to_beside, copy_rows, own_rows, even_rows = call(
        functools.partial(dispatch_kernel, *sizes, packing),
        [shape((slots, toks), F32), shape((slots, toks), jnp.int32), shape((slots, width), F32),
         shape((slots, width), F32)] + [shape((n, d_model + width), BF16) for n in sized],
        [(hbm, a) for a in sources],
        [(smem if n < 2 else vmem)(a.shape, a.dtype) for n, a in enumerate(sources)]
        + [vmem((toks * top, width), F32), pltpu.SemaphoreType.DMA((len(sources),))],
        flops=2 * slots * toks * d_model,
        limit=60,
    )
    near, far, beside = (swap(copy_rows, bits, dev_count) for bits in (2, 4, 1))
    line = swap(to_beside, 1, dev_count)
    flat_w = weights.reshape(local_count * width, d_model)
    own_rows, even_rows, w_held, slot = call(
        functools.partial(hold_kernel, *sizes),
        [shape(a.shape, BF16) for a in (own_rows, even_rows, flat_w)] + [shape((per_home + copies, width), jnp.int32)],
        [(smem, replica_of)] + [(hbm, a) for a in (flat_w, own_rows, even_rows)],
        [pltpu.SemaphoreType.DMA((3,))],
    )
    near, far, line, beside, own_rows, even_rows, w_held, slot = lax.optimization_barrier(
        (near, far, line, beside, own_rows, even_rows, w_held, slot))
    to_near, to_beside, *lines = call(
        functools.partial(turn_kernel, *sizes),
        [shape((copies + 2 * per_home, d_model + width), BF16), shape((2 * copies, d_model + width), BF16)]
        + [shape((4 * per_home, fold_width(d_model + width)), BF16)] * (len(even) - 1),
        [(vmem, a) for a in (line, far, near, even_rows)],
    )
    far_near, onward = swap(to_near, 2, dev_count), swap(to_beside, 1, dev_count)
    lines = [swap(a, m, dev_count) for a, m in zip(lines, even[1:])]
    pieces = {(0, HOME): (0, 0), (0, COPIES): (0, per_home), (1, COPIES): (1, 0), (1, HOME): (6, 0),
              (2, COPIES): (2, 0), (4, COPIES): (3, 0), (5, COPIES): (4, 0), (3, COPIES): (4, copies),
              (even[-1], HOME): (5, 0), (even[-1] + 1, HOME): (5, per_home)}
    orders = [list(pieces)]
    height = padded(sum(per_home if kind == HOME else copies for _, kind in pieces))
    early_rows, own = call(
        functools.partial(early_kernel, *sizes, orders[0], pieces),
        (shape((height, d_model + width), BF16), shape((height, width), F32)),
        [(vmem, a) for a in (w_held, slot, own_rows, beside, near, far, onward, lines[-1], line)],
        flops=2 * height * d_model * local_count * width * 30,
    )
    far_across = swap(far_near[:copies], 1, dev_count)
    arrays = [far_near, far_across, *lines[:-1]]
    pieces = {(6, COPIES): (0, 0), (2, HOME): (0, copies), (3, HOME): (0, copies + per_home), (7, COPIES): (1, 0)}
    for n, m in enumerate(even[1:-1]):
        pieces[m, HOME], pieces[m + 1, HOME] = ((2 + n, k * per_home) for k in range(2))
    orders.append(list(pieces))
    height = padded(sum(per_home if kind == HOME else copies for _, kind in pieces))
    block = padded(per_home + copies)
    late_rows, back = call(
        functools.partial(late_kernel, *sizes, *orders, pieces),
        (shape((height, d_model + width), BF16), shape((dev_count * block, width), BF16)),
        [(vmem, a) for a in (own, w_held, slot, *arrays)],
        [vmem((dev_count, block, width), F32)],
        flops=2 * height * d_model * local_count * width,
    )
    back = lax.all_to_all(back, "expert", split_axis=0, concat_axis=0, tiled=True)
    half_flops = 2 * rows * columns * local_count * width
    halves = (slot, early_rows, late_rows)
    other = call(
        functools.partial(other_half_kernel, *sizes, orders),
        shape((local_count * width, columns), BF16),
        [(vmem, a) for a in halves],
        flops=half_flops,
    )
    arrived = lax.ppermute(other, "dp", [(0, 1), (1, 0)])
    grad_w = call(
        functools.partial(own_half_kernel, *sizes, orders),
        shape((local_count * width, columns), BF16),
        [(vmem, a) for a in (*halves, arrived)],
        flops=30 * half_flops,
    )
    grad_w, pick = lax.optimization_barrier((grad_w, pick))
    grad_h, grad_p = call(
        functools.partial(combine_kernel, *sizes),
        (shape((toks * top, width), BF16), shape((top, toks), BF16)),
        [(vmem, a) for a in (back.reshape(dev_count, block, width), pick, expert, h_slot, p_slot, ids)],
        [vmem((toks * top, width), F32), vmem((top, toks), F32)],
        flops=2 * slots * toks * width * top,
    )
    return (
        grad_h.reshape(toks, top, width),
        grad_p.T,
        grad_w.reshape(local_count, width, columns),
    )


def body(cotangent, hidden, probs, expert_ids, send_counts, replica_of, weights):
    dev_count = lax.axis_size("expert")
    local_count, width, _ = weights.shape
    gathered = dev_count * dev_count * CAPR
    if gathered <= (local_count + 3) * width and dev_count == 8 and lax.axis_size("dp") == 2:
        run = gather_body
    else:
        run = replica_body
    return run(cotangent, hidden, probs, expert_ids, send_counts, replica_of, weights)


def solution(mesh):
    in_specs = (
        P(("groups", "expert", "dp"), None),
        P(("groups", "expert", "dp"), None, None),
        P(("groups", "expert", "dp"), None),
        P(("groups", "expert", "dp"), None),
        P(("groups", "expert", "dp"), None),
        P("groups"),
        P("expert", None, None),
    )
    out_specs = (
        P(("groups", "expert", "dp"), None, None),
        P(("groups", "expert", "dp"), None),
        P(("groups", "expert"), None, "dp"),
    )
    return jax.shard_map(body, mesh=mesh, in_specs=in_specs, out_specs=out_specs, check_vma=False)
```

```python
import functools

import jax
import jax.numpy as jnp
from jax import lax
from jax.experimental import pallas as pl
from jax.experimental.pallas import tpu as pltpu
from jax.sharding import PartitionSpec as P

CAPH = 3
CAPR = 3


def ranks_within(keys):
    total_rows = keys.shape[0]
    sort_order = jnp.argsort(keys * total_rows + jnp.arange(total_rows, dtype=jnp.int32))
    sorted_keys = keys[sort_order]
    first_seen = jnp.searchsorted(sorted_keys, sorted_keys, side="left")
    ranked = jnp.arange(total_rows, dtype=jnp.int32) - first_seen
    return jnp.zeros((total_rows,), jnp.int32).at[sort_order].set(ranked)


def route_rows(ids_block, counts_row, replica_of, local_count, cap_home, cap_copy):
    dev_count = replica_of.shape[0]
    experts = ids_block.reshape(-1)
    rank_expert = ranks_within(experts)
    devices = jnp.arange(dev_count, dtype=jnp.int32)
    same_copy = (replica_of[:, None] == replica_of[None, :]) & (devices[None, :] < devices[:, None])
    lower_rank = jnp.sum(jnp.where(same_copy, counts_row[None, :], 0), axis=1)
    upper_rank = lower_rank + counts_row
    hit_table = (
        (replica_of[None, :] == experts[:, None])
        & (lower_rank[None, :] <= rank_expert[:, None])
        & (rank_expert[:, None] < upper_rank[None, :])
    )
    copied = jnp.any(hit_table, axis=1)
    copy_dev = jnp.sum(jnp.where(hit_table, devices[None, :], 0), axis=1)
    dest_dev = jnp.where(copied, copy_dev, experts // local_count)
    index_of_slot = jnp.where(copied, local_count, experts % local_count)
    rank_bucket = ranks_within(dest_dev * (local_count + 1) + index_of_slot)
    keep_row = rank_bucket < jnp.where(copied, cap_copy, cap_home)
    per_dev = local_count * cap_home + cap_copy
    target = dest_dev * per_dev + index_of_slot * cap_home + rank_bucket
    return jnp.where(keep_row, target, dev_count * per_dev)


def replica_body(cotangent, hidden, probs, expert_ids, send_counts, replica_of, weights):
    tok_rows, d_model = cotangent.shape
    top_count = expert_ids.shape[1]
    hidden_width = hidden.shape[2]
    local_count = weights.shape[0]
    dev_count = lax.axis_size("expert")
    data_count = lax.axis_size("dp")
    per_dev = local_count * CAPH + CAPR
    row_count = tok_rows * top_count
    recv_count = dev_count * per_dev
    target = route_rows(expert_ids, send_counts[0], replica_of, local_count, CAPH, CAPR)
    inverse = (
        jnp.full((recv_count,), row_count, jnp.int32)
        .at[target]
        .set(jnp.arange(row_count, dtype=jnp.int32), mode="drop")
    )
    dy_pad = jnp.concatenate([cotangent, jnp.zeros((1, d_model), cotangent.dtype)], axis=0)
    h_pad = jnp.concatenate(
        [hidden.reshape(row_count, hidden_width), jnp.zeros((1, hidden_width), hidden.dtype)],
        axis=0,
    )
    p_pad = jnp.concatenate([probs.reshape(row_count), jnp.zeros((1,), probs.dtype)], axis=0)
    send_dy = dy_pad[inverse // top_count]
    send_h = h_pad[inverse]
    send_p = p_pad[inverse]
    recv_dy, recv_h, recv_p = (
        lax.all_to_all(send_dy, "expert", split_axis=0, concat_axis=0, tiled=True),
        lax.all_to_all(send_h, "expert", split_axis=0, concat_axis=0, tiled=True),
        lax.all_to_all(send_p, "expert", split_axis=0, concat_axis=0, tiled=True),
    )
    flat_size = hidden_width * d_model
    flat_w = weights.reshape(local_count, flat_size)
    pieces = lax.all_to_all(flat_w, "expert", split_axis=1, concat_axis=0, tiled=True)
    chosen = pieces[replica_of]
    copy_weight = lax.all_to_all(chosen, "expert", split_axis=0, concat_axis=0, tiled=True).reshape(
        hidden_width, d_model
    )
    slot_total = local_count + 1
    home_rows = local_count * CAPH
    row_pos = jnp.arange(recv_count, dtype=jnp.int32) % per_dev
    row_slot = jnp.where(row_pos < home_rows, row_pos // CAPH, local_count)
    all_weights = jnp.concatenate(
        [weights.reshape(local_count * hidden_width, d_model), copy_weight], axis=0
    )
    all_in = lax.dot_general(
        recv_dy, all_weights, (((1,), (1,)), ((), ())), preferred_element_type=jnp.float32
    )
    grad_in = jnp.zeros((recv_count, hidden_width), jnp.float32)
    for slot_num in range(slot_total):
        grad_in = grad_in + jnp.where(
            (row_slot == slot_num)[:, None],
            all_in[:, slot_num * hidden_width : (slot_num + 1) * hidden_width],
            0.0,
        )
    p_wide = recv_p.astype(jnp.float32)[:, None]
    h_wide = recv_h.astype(jnp.float32)
    grad_h_buf = (p_wide * grad_in).astype(jnp.bfloat16)
    grad_p_buf = jnp.sum(h_wide * grad_in, axis=1).astype(jnp.bfloat16)
    scaled = (p_wide * h_wide).astype(jnp.bfloat16)
    zero_rows = jnp.zeros_like(scaled)
    scaled_wide = jnp.concatenate(
        [
            jnp.where((row_slot == slot_num)[:, None], scaled, zero_rows)
            for slot_num in range(slot_total)
        ],
        axis=1,
    )
    parts = lax.dot_general(
        scaled_wide, recv_dy, (((0,), (0,)), ((), ())), preferred_element_type=jnp.float32
    ).astype(jnp.bfloat16)
    home_part = parts[: local_count * hidden_width].reshape(local_count, hidden_width, d_model)
    copy_part = parts[local_count * hidden_width :]
    back_h, back_p = (
        lax.all_to_all(grad_h_buf, "expert", split_axis=0, concat_axis=0, tiled=True),
        lax.all_to_all(grad_p_buf, "expert", split_axis=0, concat_axis=0, tiled=True),
    )
    flat_h = jnp.concatenate([back_h, jnp.zeros((1, hidden_width), back_h.dtype)], axis=0)
    flat_p = jnp.concatenate([back_p, jnp.zeros((1,), back_p.dtype)], axis=0)
    hidden_gradient = flat_h[target].reshape(tok_rows, top_count, hidden_width)
    grad_probs = flat_p[target].reshape(tok_rows, top_count)
    expert_total = dev_count * local_count
    cover = replica_of[None, :] == jnp.arange(expert_total, dtype=jnp.int32)[:, None]
    half_width = d_model // data_count
    halves = lax.all_to_all(copy_part, "dp", split_axis=1, concat_axis=0, tiled=True)
    copy_half = jnp.sum(
        halves.reshape(data_count, hidden_width, half_width).astype(jnp.float32), axis=0
    )
    piece_len = hidden_width * half_width // dev_count
    slabs = copy_half.reshape(dev_count, piece_len)
    arrived = lax.all_to_all(slabs, "expert", split_axis=0, concat_axis=0, tiled=True)
    sums = jnp.dot(cover.astype(jnp.float32), arrived, precision=lax.Precision.HIGHEST)
    homed = lax.all_to_all(
        sums.reshape(dev_count, local_count * piece_len),
        "expert",
        split_axis=0,
        concat_axis=0,
        tiled=True,
    )
    homed = (
        homed.reshape(dev_count, local_count, piece_len)
        .transpose(1, 0, 2)
        .reshape(local_count, hidden_width, half_width)
    )
    home_half = lax.psum_scatter(
        home_part.astype(jnp.float32).astype(jnp.bfloat16), "dp", scatter_dimension=2, tiled=True
    ).astype(jnp.float32)
    grad_weights = (home_half + homed).astype(jnp.bfloat16)
    return (hidden_gradient, grad_probs, grad_weights)


SLOT = 3
HOME, COPIES = "home", "copies"
F32 = jnp.float32
BF16 = jnp.bfloat16
NT = (((1,), (1,)), ((), ()))
TN = (((0,), (0,)), ((), ()))


def iota(shape, dim):
    return lax.broadcasted_iota(jnp.int32, shape, dim)


def dispatch_kernel(local_count, dev_count, packing, *refs):
    sources, refs = refs[:6], refs[6:]
    pick_ref, expert_ref, hs_ref, ps_ref = refs[:4]
    packed, (held, wide, sems) = refs[4:4 + len(packing)], (refs[-8:-2], refs[-2], refs[-1])
    moves = [pltpu.make_async_copy(s, h, sems.at[n]) for n, (s, h) in enumerate(zip(sources, held))]
    for move in moves:
        move.start()
    replica_ref, counts_ref, ids_ref, probs_ref, hid_ref, cot_ref = held
    top, toks = ids_ref.shape
    per_home = local_count * SLOT
    homes = dev_count * per_home
    slots = homes + dev_count * CAPR
    me = lax.axis_index("expert")
    row = iota((slots, toks), 0)
    expert = ((row // per_home) ^ me) * local_count + (row % per_home) // SLOT
    within = row % SLOT
    allowed = jnp.where(within < CAPH, 1, 0)
    before = jnp.where(iota((toks, toks), 0) < iota((toks, toks), 1), 1.0, 0.0).astype(BF16)
    for move in moves[:3]:
        move.wait()
    for d in range(dev_count):
        first = homes + d * CAPR
        mine = (row >= first) & (row < first + CAPR)
        expert = jnp.where(mine, replica_ref[d], expert)
        within = jnp.where(mine, row - first, within)
        allowed = jnp.where(mine, jnp.where(row - first < counts_ref[0, d], 1, 0), allowed)
    lower = jnp.zeros((slots, toks), jnp.int32)
    for d in range(dev_count):
        earlier = (row < homes) | (row >= homes + (d + 1) * CAPR)
        lower = lower + jnp.where(earlier & (expert == replica_ref[d]), counts_ref[0, d], 0)
    ids = ids_ref[...]
    named = jnp.zeros((slots, toks), F32)
    for k in range(top):
        named = named + jnp.where(ids[k:k + 1, :] == expert, 1.0, 0.0)
    rank = jnp.dot(named.astype(BF16), before, preferred_element_type=F32)
    wanted = (lower + within).astype(F32)
    pick = jnp.where((rank == wanted) & (allowed > 0), named, 0.0)
    pick_ref[...] = pick
    expert_ref[...] = expert
    for move in moves[3:5]:
        move.wait()
    wide[...] = hid_ref[...].astype(F32)
    p_slot = jnp.zeros((slots, toks), F32)
    probs = probs_ref[...].astype(F32)
    chosen, values = [], []
    for k in range(top):
        sel = jnp.where(ids[k:k + 1, :] == expert, pick, 0.0)
        chosen.append(sel.astype(BF16))
        values.append(wide[pl.ds(k, toks, stride=top), :].astype(BF16))
        p_slot = p_slot + sel * probs[k:k + 1, :]
    h_slot = jnp.dot(
        jnp.concatenate(chosen, axis=1), jnp.concatenate(values, axis=0), preferred_element_type=F32)
    p_slot = jnp.sum(p_slot, axis=1, keepdims=True)
    hs_ref[...] = h_slot
    ps_ref[...] = jnp.broadcast_to(p_slot, ps_ref.shape)
    scaled = p_slot * h_slot
    moves[5].wait()
    rows = jnp.dot(pick.astype(BF16), cot_ref[...], preferred_element_type=F32)
    d_model = cot_ref.shape[1]
    for out_ref, blocks in zip(packed, packing):
        spans = [(homes, slots) if b == COPIES else (b * per_home, (b + 1) * per_home) for b in blocks]
        out_ref[:, :d_model] = jnp.concatenate([rows[i:j] for i, j in spans], axis=0).astype(BF16)
        out_ref[:, d_model:] = jnp.concatenate([scaled[i:j] for i, j in spans], axis=0).astype(BF16)


def padded(rows):
    return -(-rows // 16) * 16


def stack(order, blocks, height):
    values = [blocks[key] for key in order]
    missing = height - sum(v.shape[0] for v in values)
    if missing:
        values.append(jnp.zeros((missing, values[0].shape[1]), values[0].dtype))
    return jnp.concatenate(values, axis=0)


def fold_width(columns):
    return -(-columns // 256) * 128


def folded(rows):
    count, columns = rows.shape
    left = fold_width(columns)
    right = [rows[:, left:], jnp.zeros((count, 2 * left - columns), rows.dtype)]
    return jnp.concatenate([rows[:, :left], jnp.concatenate(right, axis=1)], axis=0)


def unfolded(rows, columns):
    count, left = rows.shape
    if left == columns:
        return rows
    return jnp.concatenate([rows[:count // 2], rows[count // 2:, :columns - left]], axis=1)


def slots_of(order, slot_ref, per_home, height):
    kinds = {HOME: slot_ref[:per_home], COPIES: slot_ref[per_home:]}
    return stack(order, {key: kinds[key[1]] for key in order}, height)


def fill_rows(order, pieces, per_home, per_copy, piece_refs, rows_ref):
    values = [unfolded(r[...].astype(F32), rows_ref.shape[1]) for r in piece_refs]
    blocks = {}
    for key in order:
        n, start = pieces[key]
        blocks[key] = values[n][start:start + (per_home if key[1] == HOME else per_copy)]
    rows_ref[...] = stack(order, blocks, rows_ref.shape[0]).astype(BF16)


def own_columns(rows_ref, w_ref, slot, local_count):
    d_model = w_ref.shape[1]
    width = w_ref.shape[0] // local_count
    every = lax.dot_general(rows_ref[:, :d_model], w_ref[...], NT, preferred_element_type=F32)
    own = jnp.zeros((rows_ref.shape[0], width), F32)
    for e in range(local_count):
        own = jnp.where(slot == e, every[:, e * width:(e + 1) * width], own)
    return own


def hold_kernel(local_count, dev_count, replica_ref, w_hbm, own_hbm, even_hbm,
                own_ref, even_ref, w_ref, slot_ref, sems):
    moves = [pltpu.make_async_copy(a, b, sems.at[n]) for n, (a, b) in enumerate(
        ((w_hbm, w_ref), (own_hbm, own_ref), (even_hbm, even_ref)))]
    for move in moves:
        move.start()
    per_home, per_copy = local_count * SLOT, dev_count * CAPR
    first = lax.axis_index("expert") * local_count
    width = slot_ref.shape[1]
    slot_ref[:per_home] = iota((per_home, width), 0) // SLOT
    row = iota((per_copy, width), 0)
    copy = jnp.full((per_copy, width), -1, jnp.int32)
    for d in range(dev_count):
        mine = (row >= d * CAPR) & (row < (d + 1) * CAPR)
        copy = jnp.where(mine, replica_ref[d] - first, copy)
    slot_ref[per_home:] = copy
    for move in moves:
        move.wait()


def turn_kernel(local_count, dev_count, line_ref, far_ref, near_ref, even_ref, beside_out, *line_outs):
    per_home = local_count * SLOT
    beside_out[...] = jnp.concatenate([far_ref[...].astype(F32), near_ref[...].astype(F32)], axis=0).astype(BF16)
    line, even = line_ref[...].astype(F32)[per_home:], even_ref[...].astype(F32)
    for n, out_ref in enumerate(line_outs):
        span = slice(n * per_home, (n + 1) * per_home)
        out_ref[...] = folded(jnp.concatenate([even[span], line[span]], axis=0)).astype(BF16)


def early_kernel(local_count, dev_count, order, pieces, w_ref, slot_ref, *refs):
    piece_refs, (rows_ref, own_ref) = refs[:-2], refs[-2:]
    per_home, per_copy = local_count * SLOT, dev_count * CAPR
    fill_rows(order, pieces, per_home, per_copy, piece_refs, rows_ref)
    slot = slots_of(order, slot_ref, per_home, rows_ref.shape[0])
    own_ref[...] = own_columns(rows_ref, w_ref, slot, local_count)


def late_kernel(local_count, dev_count, early, order, pieces, own_ref, w_ref, slot_ref, *refs):
    piece_refs, (rows_ref, back_ref, passed) = refs[:-3], refs[-3:]
    per_home, per_copy = local_count * SLOT, dev_count * CAPR
    fill_rows(order, pieces, per_home, per_copy, piece_refs, rows_ref)
    own = own_columns(rows_ref, w_ref, slots_of(order, slot_ref, per_home, rows_ref.shape[0]), local_count)
    if passed.shape[1] > per_home + per_copy:
        passed[:, per_home + per_copy:] = jnp.zeros_like(passed[:, per_home + per_copy:])
    for keys, value in ((early, own_ref[...]), (order, own)):
        start = 0
        for m, kind in keys:
            lower, size = (0, per_home) if kind == HOME else (per_home, per_copy)
            passed[m, lower:lower + size] = value[start:start + size]
            start += size
    me = lax.axis_index("expert")
    back = jnp.concatenate([passed[me ^ source] for source in range(dev_count)], axis=0)
    back_ref[...] = back.astype(back_ref.dtype)


def grad_weights_half(local_count, dev_count, orders, half, slot_ref, rows_refs, columns):
    start = pl.multiple_of(half * columns, 128)
    spread = []
    for order, ref in zip(orders, rows_refs):
        slot = slots_of(order, slot_ref, local_count * SLOT, ref.shape[0])
        scaled = ref[:, 2 * columns:].astype(F32)
        spread.append(jnp.concatenate([jnp.where(slot == e, scaled, 0.0) for e in range(local_count)], axis=1))
    rows = jnp.concatenate([ref[:, pl.ds(start, columns)] for ref in rows_refs], axis=0)
    return lax.dot_general(
        jnp.concatenate(spread, axis=0).astype(BF16), rows, TN, preferred_element_type=F32)


def other_half_kernel(local_count, dev_count, orders, slot_ref, early_ref, late_ref, out_ref):
    half = 1 - lax.axis_index("dp")
    out_ref[...] = grad_weights_half(
        local_count, dev_count, orders, half, slot_ref, (early_ref, late_ref), out_ref.shape[1]).astype(out_ref.dtype)


def own_half_kernel(local_count, dev_count, orders, slot_ref, early_ref, late_ref, arrived_ref, out_ref):
    half = lax.axis_index("dp")
    total = grad_weights_half(
        local_count, dev_count, orders, half, slot_ref, (early_ref, late_ref), out_ref.shape[1])
    out_ref[...] = (total + arrived_ref[...].astype(F32)).astype(out_ref.dtype)


def combine_kernel(local_count, dev_count, back_ref, pick_ref, expert_ref, hs_ref, ps_ref, ids_ref,
                   grad_h_ref, grad_p_ref, wide, narrow):
    top, toks = ids_ref.shape
    per_home = local_count * SLOT
    me = lax.axis_index("expert")
    back = [back_ref[me ^ m].astype(F32) for m in range(dev_count)]
    slots = pick_ref.shape[0]
    copies = slots - dev_count * per_home
    copy = functools.reduce(jnp.add, [b[per_home:per_home + copies] for b in back])
    grad_in = jnp.concatenate([b[:per_home] for b in back] + [copy], axis=0)
    h_rows = (ps_ref[...] * grad_in).astype(BF16)
    p_rows = jnp.sum(hs_ref[...] * grad_in, axis=1, keepdims=True)
    ids = ids_ref[...]
    pick = pick_ref[...]
    expert = expert_ref[...]
    sels = [jnp.where(ids[k:k + 1, :] == expert, pick, 0.0) for k in range(top)]
    rows = lax.dot_general(
        jnp.concatenate([sel.astype(BF16) for sel in sels], axis=1), h_rows, TN, preferred_element_type=F32)
    for k, sel in enumerate(sels):
        wide[pl.ds(k, toks, stride=top), :] = rows[k * toks:(k + 1) * toks]
        narrow[k:k + 1, :] = jnp.sum(sel * p_rows, axis=0, keepdims=True)
    grad_h_ref[...] = wide[...].astype(grad_h_ref.dtype)
    grad_p_ref[...] = narrow[...].astype(grad_p_ref.dtype)


def call(kernel, out_shape, operands, scratch=(), flops=0, limit=24):
    shapes = jax.tree.leaves(out_shape)
    moved = sum(a.size * a.dtype.itemsize for a in (*(a for _, a in operands), *shapes))
    return pl.pallas_call(
        kernel,
        out_shape=out_shape,
        in_specs=[pl.BlockSpec(memory_space=space) for space, _ in operands],
        out_specs=jax.tree.map(lambda _: pl.BlockSpec(memory_space=pltpu.VMEM), out_shape),
        scratch_shapes=list(scratch),
        compiler_params=pltpu.CompilerParams(vmem_limit_bytes=limit << 20),
        cost_estimate=pl.CostEstimate(flops=flops, bytes_accessed=moved, transcendentals=0),
    )(*(a for _, a in operands))


def swap(x, bits, count):
    return lax.ppermute(x, "expert", [(i, i ^ bits) for i in range(count)])


def gather_body(cotangent, hidden, probs, expert_ids, send_counts, replica_of, weights):
    toks, d_model = cotangent.shape
    top = expert_ids.shape[1]
    width = hidden.shape[2]
    local_count = weights.shape[0]
    dev_count = lax.axis_size("expert")
    homes = dev_count * local_count * SLOT
    copies = dev_count * CAPR
    slots = homes + copies
    rows = homes + dev_count * copies
    columns = d_model // 2
    sizes = (local_count, dev_count)
    ids = expert_ids.T
    shape = jax.ShapeDtypeStruct
    hbm, vmem, smem = pltpu.HBM, pltpu.VMEM, pltpu.SMEM
    sources = (replica_of, send_counts, ids, probs.T, hidden.reshape(toks * top, width), cotangent)
    per_home = local_count * SLOT
    odd, even = range(1, dev_count, 2), range(2, dev_count, 2)
    packing = [[*odd], [COPIES], [0, COPIES], [*even]]
    sized = [sum(copies if b == COPIES else per_home for b in blocks) for blocks in packing]
    pick, expert, h_slot, p_slot, to_beside, copy_rows, own_rows, even_rows = call(
        functools.partial(dispatch_kernel, *sizes, packing),
        [shape((slots, toks), F32), shape((slots, toks), jnp.int32), shape((slots, width), F32),
         shape((slots, width), F32)] + [shape((n, d_model + width), BF16) for n in sized],
        [(hbm, a) for a in sources],
        [(smem if n < 2 else vmem)(a.shape, a.dtype) for n, a in enumerate(sources)]
        + [vmem((toks * top, width), F32), pltpu.SemaphoreType.DMA((len(sources),))],
        flops=2 * slots * toks * d_model,
        limit=60,
    )
    near, far, beside = (swap(copy_rows, bits, dev_count) for bits in (2, 4, 1))
    line = swap(to_beside, 1, dev_count)
    flat_w = weights.reshape(local_count * width, d_model)
    own_rows, even_rows, w_held, slot = call(
        functools.partial(hold_kernel, *sizes),
        [shape(a.shape, BF16) for a in (own_rows, even_rows, flat_w)] + [shape((per_home + copies, width), jnp.int32)],
        [(smem, replica_of)] + [(hbm, a) for a in (flat_w, own_rows, even_rows)],
        [pltpu.SemaphoreType.DMA((3,))],
    )
    near, far, line, beside, own_rows, even_rows, w_held, slot = lax.optimization_barrier(
        (near, far, line, beside, own_rows, even_rows, w_held, slot))
    far_near = swap(far, 2, dev_count)
    to_beside, *lines = call(
        functools.partial(turn_kernel, *sizes),
        [shape((2 * copies, d_model + width), BF16)]
        + [shape((4 * per_home, fold_width(d_model + width)), BF16)] * len(even),
        [(vmem, a) for a in (line, far, near, even_rows)],
    )
    onward = swap(to_beside, 1, dev_count)
    lines = [swap(a, m, dev_count) for a, m in zip(lines, even)]
    pieces = {(0, HOME): (0, 0), (0, COPIES): (0, per_home), (1, COPIES): (1, 0), (1, HOME): (6, 0),
              (2, COPIES): (2, 0), (4, COPIES): (3, 0), (5, COPIES): (4, 0), (3, COPIES): (4, copies),
              (even[-1], HOME): (5, 0), (even[-1] + 1, HOME): (5, per_home)}
    orders = [list(pieces)]
    height = padded(sum(per_home if kind == HOME else copies for _, kind in pieces))
    early_rows, own = call(
        functools.partial(early_kernel, *sizes, orders[0], pieces),
        (shape((height, d_model + width), BF16), shape((height, width), F32)),
        [(vmem, a) for a in (w_held, slot, own_rows, beside, near, far, onward, lines[-1], line)],
        flops=2 * height * d_model * local_count * width * 4,
    )
    far_across = swap(far_near, 1, dev_count)
    arrays = [far_near, far_across, *lines[-2::-1]]
    pieces = {(6, COPIES): (0, 0), (7, COPIES): (1, 0)}
    for n, m in enumerate(even[-2::-1]):
        pieces[m, HOME], pieces[m + 1, HOME] = ((2 + n, k * per_home) for k in range(2))
    orders.append(list(pieces))
    height = padded(sum(per_home if kind == HOME else copies for _, kind in pieces))
    block = padded(per_home + copies)
    late_rows, back = call(
        functools.partial(late_kernel, *sizes, *orders, pieces),
        (shape((height, d_model + width), BF16), shape((dev_count * block, width), BF16)),
        [(vmem, a) for a in (own, w_held, slot, *arrays)],
        [vmem((dev_count, block, width), F32)],
        flops=2 * height * d_model * local_count * width,
    )
    back = lax.all_to_all(back, "expert", split_axis=0, concat_axis=0, tiled=True)
    half_flops = 2 * rows * columns * local_count * width
    halves = (slot, early_rows, late_rows)
    other = call(
        functools.partial(other_half_kernel, *sizes, orders),
        shape((local_count * width, columns), BF16),
        [(vmem, a) for a in halves],
        flops=half_flops,
    )
    arrived = lax.ppermute(other, "dp", [(0, 1), (1, 0)])
    grad_w = call(
        functools.partial(own_half_kernel, *sizes, orders),
        shape((local_count * width, columns), BF16),
        [(vmem, a) for a in (*halves, arrived)],
        flops=30 * half_flops,
    )
    grad_w, pick = lax.optimization_barrier((grad_w, pick))
    grad_h, grad_p = call(
        functools.partial(combine_kernel, *sizes),
        (shape((toks * top, width), BF16), shape((top, toks), BF16)),
        [(vmem, a) for a in (back.reshape(dev_count, block, width), pick, expert, h_slot, p_slot, ids)],
        [vmem((toks * top, width), F32), vmem((top, toks), F32)],
        flops=2 * slots * toks * width * top,
    )
    return (
        grad_h.reshape(toks, top, width),
        grad_p.T,
        grad_w.reshape(local_count, width, columns),
    )


def body(cotangent, hidden, probs, expert_ids, send_counts, replica_of, weights):
    dev_count = lax.axis_size("expert")
    local_count, width, _ = weights.shape
    gathered = dev_count * dev_count * CAPR
    if gathered <= (local_count + 3) * width and dev_count == 8 and lax.axis_size("dp") == 2:
        run = gather_body
    else:
        run = replica_body
    return run(cotangent, hidden, probs, expert_ids, send_counts, replica_of, weights)


def solution(mesh):
    in_specs = (
        P(("groups", "expert", "dp"), None),
        P(("groups", "expert", "dp"), None, None),
        P(("groups", "expert", "dp"), None),
        P(("groups", "expert", "dp"), None),
        P(("groups", "expert", "dp"), None),
        P("groups"),
        P("expert", None, None),
    )
    out_specs = (
        P(("groups", "expert", "dp"), None, None),
        P(("groups", "expert", "dp"), None),
        P(("groups", "expert"), None, "dp"),
    )
    return jax.shard_map(body, mesh=mesh, in_specs=in_specs, out_specs=out_specs, check_vma=False)
```

```python
import functools

import jax
import jax.numpy as jnp
from jax import lax
from jax.experimental import pallas as pl
from jax.experimental.pallas import tpu as pltpu
from jax.sharding import PartitionSpec as P

CAPH = 3
CAPR = 3


def ranks_within(keys):
    total_rows = keys.shape[0]
    sort_order = jnp.argsort(keys * total_rows + jnp.arange(total_rows, dtype=jnp.int32))
    sorted_keys = keys[sort_order]
    first_seen = jnp.searchsorted(sorted_keys, sorted_keys, side="left")
    ranked = jnp.arange(total_rows, dtype=jnp.int32) - first_seen
    return jnp.zeros((total_rows,), jnp.int32).at[sort_order].set(ranked)


def route_rows(ids_block, counts_row, replica_of, local_count, cap_home, cap_copy):
    dev_count = replica_of.shape[0]
    experts = ids_block.reshape(-1)
    rank_expert = ranks_within(experts)
    devices = jnp.arange(dev_count, dtype=jnp.int32)
    same_copy = (replica_of[:, None] == replica_of[None, :]) & (devices[None, :] < devices[:, None])
    lower_rank = jnp.sum(jnp.where(same_copy, counts_row[None, :], 0), axis=1)
    upper_rank = lower_rank + counts_row
    hit_table = (
        (replica_of[None, :] == experts[:, None])
        & (lower_rank[None, :] <= rank_expert[:, None])
        & (rank_expert[:, None] < upper_rank[None, :])
    )
    copied = jnp.any(hit_table, axis=1)
    copy_dev = jnp.sum(jnp.where(hit_table, devices[None, :], 0), axis=1)
    dest_dev = jnp.where(copied, copy_dev, experts // local_count)
    index_of_slot = jnp.where(copied, local_count, experts % local_count)
    rank_bucket = ranks_within(dest_dev * (local_count + 1) + index_of_slot)
    keep_row = rank_bucket < jnp.where(copied, cap_copy, cap_home)
    per_dev = local_count * cap_home + cap_copy
    target = dest_dev * per_dev + index_of_slot * cap_home + rank_bucket
    return jnp.where(keep_row, target, dev_count * per_dev)


def replica_body(cotangent, hidden, probs, expert_ids, send_counts, replica_of, weights):
    tok_rows, d_model = cotangent.shape
    top_count = expert_ids.shape[1]
    hidden_width = hidden.shape[2]
    local_count = weights.shape[0]
    dev_count = lax.axis_size("expert")
    data_count = lax.axis_size("dp")
    per_dev = local_count * CAPH + CAPR
    row_count = tok_rows * top_count
    recv_count = dev_count * per_dev
    target = route_rows(expert_ids, send_counts[0], replica_of, local_count, CAPH, CAPR)
    inverse = (
        jnp.full((recv_count,), row_count, jnp.int32)
        .at[target]
        .set(jnp.arange(row_count, dtype=jnp.int32), mode="drop")
    )
    dy_pad = jnp.concatenate([cotangent, jnp.zeros((1, d_model), cotangent.dtype)], axis=0)
    h_pad = jnp.concatenate(
        [hidden.reshape(row_count, hidden_width), jnp.zeros((1, hidden_width), hidden.dtype)],
        axis=0,
    )
    p_pad = jnp.concatenate([probs.reshape(row_count), jnp.zeros((1,), probs.dtype)], axis=0)
    send_dy = dy_pad[inverse // top_count]
    send_h = h_pad[inverse]
    send_p = p_pad[inverse]
    recv_dy, recv_h, recv_p = (
        lax.all_to_all(send_dy, "expert", split_axis=0, concat_axis=0, tiled=True),
        lax.all_to_all(send_h, "expert", split_axis=0, concat_axis=0, tiled=True),
        lax.all_to_all(send_p, "expert", split_axis=0, concat_axis=0, tiled=True),
    )
    flat_size = hidden_width * d_model
    flat_w = weights.reshape(local_count, flat_size)
    pieces = lax.all_to_all(flat_w, "expert", split_axis=1, concat_axis=0, tiled=True)
    chosen = pieces[replica_of]
    copy_weight = lax.all_to_all(chosen, "expert", split_axis=0, concat_axis=0, tiled=True).reshape(
        hidden_width, d_model
    )
    slot_total = local_count + 1
    home_rows = local_count * CAPH
    row_pos = jnp.arange(recv_count, dtype=jnp.int32) % per_dev
    row_slot = jnp.where(row_pos < home_rows, row_pos // CAPH, local_count)
    all_weights = jnp.concatenate(
        [weights.reshape(local_count * hidden_width, d_model), copy_weight], axis=0
    )
    all_in = lax.dot_general(
        recv_dy, all_weights, (((1,), (1,)), ((), ())), preferred_element_type=jnp.float32
    )
    grad_in = jnp.zeros((recv_count, hidden_width), jnp.float32)
    for slot_num in range(slot_total):
        grad_in = grad_in + jnp.where(
            (row_slot == slot_num)[:, None],
            all_in[:, slot_num * hidden_width : (slot_num + 1) * hidden_width],
            0.0,
        )
    p_wide = recv_p.astype(jnp.float32)[:, None]
    h_wide = recv_h.astype(jnp.float32)
    grad_h_buf = (p_wide * grad_in).astype(jnp.bfloat16)
    grad_p_buf = jnp.sum(h_wide * grad_in, axis=1).astype(jnp.bfloat16)
    scaled = (p_wide * h_wide).astype(jnp.bfloat16)
    zero_rows = jnp.zeros_like(scaled)
    scaled_wide = jnp.concatenate(
        [
            jnp.where((row_slot == slot_num)[:, None], scaled, zero_rows)
            for slot_num in range(slot_total)
        ],
        axis=1,
    )
    parts = lax.dot_general(
        scaled_wide, recv_dy, (((0,), (0,)), ((), ())), preferred_element_type=jnp.float32
    ).astype(jnp.bfloat16)
    home_part = parts[: local_count * hidden_width].reshape(local_count, hidden_width, d_model)
    copy_part = parts[local_count * hidden_width :]
    back_h, back_p = (
        lax.all_to_all(grad_h_buf, "expert", split_axis=0, concat_axis=0, tiled=True),
        lax.all_to_all(grad_p_buf, "expert", split_axis=0, concat_axis=0, tiled=True),
    )
    flat_h = jnp.concatenate([back_h, jnp.zeros((1, hidden_width), back_h.dtype)], axis=0)
    flat_p = jnp.concatenate([back_p, jnp.zeros((1,), back_p.dtype)], axis=0)
    hidden_gradient = flat_h[target].reshape(tok_rows, top_count, hidden_width)
    grad_probs = flat_p[target].reshape(tok_rows, top_count)
    expert_total = dev_count * local_count
    cover = replica_of[None, :] == jnp.arange(expert_total, dtype=jnp.int32)[:, None]
    half_width = d_model // data_count
    halves = lax.all_to_all(copy_part, "dp", split_axis=1, concat_axis=0, tiled=True)
    copy_half = jnp.sum(
        halves.reshape(data_count, hidden_width, half_width).astype(jnp.float32), axis=0
    )
    piece_len = hidden_width * half_width // dev_count
    slabs = copy_half.reshape(dev_count, piece_len)
    arrived = lax.all_to_all(slabs, "expert", split_axis=0, concat_axis=0, tiled=True)
    sums = jnp.dot(cover.astype(jnp.float32), arrived, precision=lax.Precision.HIGHEST)
    homed = lax.all_to_all(
        sums.reshape(dev_count, local_count * piece_len),
        "expert",
        split_axis=0,
        concat_axis=0,
        tiled=True,
    )
    homed = (
        homed.reshape(dev_count, local_count, piece_len)
        .transpose(1, 0, 2)
        .reshape(local_count, hidden_width, half_width)
    )
    home_half = lax.psum_scatter(
        home_part.astype(jnp.float32).astype(jnp.bfloat16), "dp", scatter_dimension=2, tiled=True
    ).astype(jnp.float32)
    grad_weights = (home_half + homed).astype(jnp.bfloat16)
    return (hidden_gradient, grad_probs, grad_weights)


SLOT = 3
HOME, COPIES = "home", "copies"
F32 = jnp.float32
BF16 = jnp.bfloat16
NT = (((1,), (1,)), ((), ()))
TN = (((0,), (0,)), ((), ()))


def iota(shape, dim):
    return lax.broadcasted_iota(jnp.int32, shape, dim)


def dispatch_kernel(local_count, dev_count, packing, *refs):
    sources, refs = refs[:6], refs[6:]
    pick_ref, expert_ref, hs_ref, ps_ref = refs[:4]
    packed, (held, wide, sems) = refs[4:4 + len(packing)], (refs[-8:-2], refs[-2], refs[-1])
    moves = [pltpu.make_async_copy(s, h, sems.at[n]) for n, (s, h) in enumerate(zip(sources, held))]
    for move in moves:
        move.start()
    replica_ref, counts_ref, ids_ref, probs_ref, hid_ref, cot_ref = held
    top, toks = ids_ref.shape
    per_home = local_count * SLOT
    homes = dev_count * per_home
    slots = homes + dev_count * CAPR
    me = lax.axis_index("expert")
    row = iota((slots, toks), 0)
    expert = ((row // per_home) ^ me) * local_count + (row % per_home) // SLOT
    within = row % SLOT
    allowed = jnp.where(within < CAPH, 1, 0)
    before = jnp.where(iota((toks, toks), 0) < iota((toks, toks), 1), 1.0, 0.0).astype(BF16)
    for move in moves[:3]:
        move.wait()
    for d in range(dev_count):
        first = homes + d * CAPR
        mine = (row >= first) & (row < first + CAPR)
        expert = jnp.where(mine, replica_ref[d], expert)
        within = jnp.where(mine, row - first, within)
        allowed = jnp.where(mine, jnp.where(row - first < counts_ref[0, d], 1, 0), allowed)
    lower = jnp.zeros((slots, toks), jnp.int32)
    for d in range(dev_count):
        earlier = (row < homes) | (row >= homes + (d + 1) * CAPR)
        lower = lower + jnp.where(earlier & (expert == replica_ref[d]), counts_ref[0, d], 0)
    ids = ids_ref[...]
    named = jnp.zeros((slots, toks), F32)
    for k in range(top):
        named = named + jnp.where(ids[k:k + 1, :] == expert, 1.0, 0.0)
    rank = jnp.dot(named.astype(BF16), before, preferred_element_type=F32)
    wanted = (lower + within).astype(F32)
    pick = jnp.where((rank == wanted) & (allowed > 0), named, 0.0)
    pick_ref[...] = pick
    expert_ref[...] = expert
    for move in moves[3:5]:
        move.wait()
    wide[...] = hid_ref[...].astype(F32)
    p_slot = jnp.zeros((slots, toks), F32)
    probs = probs_ref[...].astype(F32)
    chosen, values = [], []
    for k in range(top):
        sel = jnp.where(ids[k:k + 1, :] == expert, pick, 0.0)
        chosen.append(sel.astype(BF16))
        values.append(wide[pl.ds(k, toks, stride=top), :].astype(BF16))
        p_slot = p_slot + sel * probs[k:k + 1, :]
    h_slot = jnp.dot(
        jnp.concatenate(chosen, axis=1), jnp.concatenate(values, axis=0), preferred_element_type=F32)
    p_slot = jnp.sum(p_slot, axis=1, keepdims=True)
    hs_ref[...] = h_slot
    ps_ref[...] = jnp.broadcast_to(p_slot, ps_ref.shape)
    scaled = p_slot * h_slot
    moves[5].wait()
    rows = jnp.dot(pick.astype(BF16), cot_ref[...], preferred_element_type=F32)
    d_model = cot_ref.shape[1]
    for out_ref, blocks in zip(packed, packing):
        spans = [(homes, slots) if b == COPIES else (b * per_home, (b + 1) * per_home) for b in blocks]
        out_ref[:, :d_model] = jnp.concatenate([rows[i:j] for i, j in spans], axis=0).astype(BF16)
        out_ref[:, d_model:] = jnp.concatenate([scaled[i:j] for i, j in spans], axis=0).astype(BF16)


def padded(rows):
    return -(-rows // 16) * 16


def stack(order, blocks, height):
    values = [blocks[key] for key in order]
    missing = height - sum(v.shape[0] for v in values)
    if missing:
        values.append(jnp.zeros((missing, values[0].shape[1]), values[0].dtype))
    return jnp.concatenate(values, axis=0)


def fold_width(columns):
    return -(-columns // 256) * 128


def folded(rows):
    count, columns = rows.shape
    left = fold_width(columns)
    right = [rows[:, left:], jnp.zeros((count, 2 * left - columns), rows.dtype)]
    return jnp.concatenate([rows[:, :left], jnp.concatenate(right, axis=1)], axis=0)


def unfolded(rows, columns):
    count, left = rows.shape
    if left == columns:
        return rows
    return jnp.concatenate([rows[:count // 2], rows[count // 2:, :columns - left]], axis=1)


def slots_of(order, slot_ref, per_home, height):
    kinds = {HOME: slot_ref[:per_home], COPIES: slot_ref[per_home:]}
    return stack(order, {key: kinds[key[1]] for key in order}, height)


def fill_rows(order, pieces, per_home, per_copy, piece_refs, rows_ref):
    values = [unfolded(r[...].astype(F32), rows_ref.shape[1]) for r in piece_refs]
    blocks = {}
    for key in order:
        n, start = pieces[key]
        blocks[key] = values[n][start:start + (per_home if key[1] == HOME else per_copy)]
    rows_ref[...] = stack(order, blocks, rows_ref.shape[0]).astype(BF16)


def own_columns(rows_ref, w_ref, slot, local_count):
    d_model = w_ref.shape[1]
    width = w_ref.shape[0] // local_count
    every = lax.dot_general(rows_ref[:, :d_model], w_ref[...], NT, preferred_element_type=F32)
    own = jnp.zeros((rows_ref.shape[0], width), F32)
    for e in range(local_count):
        own = jnp.where(slot == e, every[:, e * width:(e + 1) * width], own)
    return own


def hold_kernel(local_count, dev_count, replica_ref, w_hbm, own_hbm, even_hbm,
                own_ref, even_ref, w_ref, slot_ref, sems):
    moves = [pltpu.make_async_copy(a, b, sems.at[n]) for n, (a, b) in enumerate(
        ((w_hbm, w_ref), (own_hbm, own_ref), (even_hbm, even_ref)))]
    for move in moves:
        move.start()
    per_home, per_copy = local_count * SLOT, dev_count * CAPR
    first = lax.axis_index("expert") * local_count
    width = slot_ref.shape[1]
    slot_ref[:per_home] = iota((per_home, width), 0) // SLOT
    row = iota((per_copy, width), 0)
    copy = jnp.full((per_copy, width), -1, jnp.int32)
    for d in range(dev_count):
        mine = (row >= d * CAPR) & (row < (d + 1) * CAPR)
        copy = jnp.where(mine, replica_ref[d] - first, copy)
    slot_ref[per_home:] = copy
    for move in moves:
        move.wait()


def turn_kernel(local_count, dev_count, line_ref, far_ref, near_ref, even_ref, beside_out, *line_outs):
    per_home = local_count * SLOT
    beside_out[...] = jnp.concatenate([far_ref[...].astype(F32), near_ref[...].astype(F32)], axis=0).astype(BF16)
    line, even = line_ref[...].astype(F32)[per_home:], even_ref[...].astype(F32)
    for n, out_ref in enumerate(line_outs):
        span = slice(n * per_home, (n + 1) * per_home)
        out_ref[...] = folded(jnp.concatenate([even[span], line[span]], axis=0)).astype(BF16)


def early_kernel(local_count, dev_count, order, pieces, w_ref, slot_ref, *refs):
    piece_refs, (rows_ref, own_ref) = refs[:-2], refs[-2:]
    per_home, per_copy = local_count * SLOT, dev_count * CAPR
    fill_rows(order, pieces, per_home, per_copy, piece_refs, rows_ref)
    slot = slots_of(order, slot_ref, per_home, rows_ref.shape[0])
    own_ref[...] = own_columns(rows_ref, w_ref, slot, local_count)


def late_kernel(local_count, dev_count, early, order, pieces, own_ref, w_ref, slot_ref, *refs):
    piece_refs, (rows_ref, back_ref, passed) = refs[:-3], refs[-3:]
    per_home, per_copy = local_count * SLOT, dev_count * CAPR
    fill_rows(order, pieces, per_home, per_copy, piece_refs, rows_ref)
    own = own_columns(rows_ref, w_ref, slots_of(order, slot_ref, per_home, rows_ref.shape[0]), local_count)
    if passed.shape[1] > per_home + per_copy:
        passed[:, per_home + per_copy:] = jnp.zeros_like(passed[:, per_home + per_copy:])
    for keys, value in ((early, own_ref[...]), (order, own)):
        start = 0
        for m, kind in keys:
            lower, size = (0, per_home) if kind == HOME else (per_home, per_copy)
            passed[m, lower:lower + size] = value[start:start + size]
            start += size
    me = lax.axis_index("expert")
    back = jnp.concatenate([passed[me ^ source] for source in range(dev_count)], axis=0)
    back_ref[...] = back.astype(back_ref.dtype)


def grad_weights_half(local_count, dev_count, orders, half, slot_ref, rows_refs, columns):
    start = pl.multiple_of(half * columns, 128)
    spread = []
    for order, ref in zip(orders, rows_refs):
        slot = slots_of(order, slot_ref, local_count * SLOT, ref.shape[0])
        scaled = ref[:, 2 * columns:].astype(F32)
        spread.append(jnp.concatenate([jnp.where(slot == e, scaled, 0.0) for e in range(local_count)], axis=1))
    rows = jnp.concatenate([ref[:, pl.ds(start, columns)] for ref in rows_refs], axis=0)
    return lax.dot_general(
        jnp.concatenate(spread, axis=0).astype(BF16), rows, TN, preferred_element_type=F32)


def other_half_kernel(local_count, dev_count, orders, slot_ref, early_ref, late_ref, out_ref):
    half = 1 - lax.axis_index("dp")
    out_ref[...] = grad_weights_half(
        local_count, dev_count, orders, half, slot_ref, (early_ref, late_ref), out_ref.shape[1]).astype(out_ref.dtype)


def own_half_kernel(local_count, dev_count, orders, slot_ref, early_ref, late_ref, arrived_ref, out_ref):
    half = lax.axis_index("dp")
    total = grad_weights_half(
        local_count, dev_count, orders, half, slot_ref, (early_ref, late_ref), out_ref.shape[1])
    out_ref[...] = (total + arrived_ref[...].astype(F32)).astype(out_ref.dtype)


def combine_kernel(local_count, dev_count, back_ref, pick_ref, expert_ref, hs_ref, ps_ref, ids_ref,
                   grad_h_ref, grad_p_ref, wide, narrow):
    top, toks = ids_ref.shape
    per_home = local_count * SLOT
    me = lax.axis_index("expert")
    back = [back_ref[me ^ m].astype(F32) for m in range(dev_count)]
    slots = pick_ref.shape[0]
    copies = slots - dev_count * per_home
    copy = functools.reduce(jnp.add, [b[per_home:per_home + copies] for b in back])
    grad_in = jnp.concatenate([b[:per_home] for b in back] + [copy], axis=0)
    h_rows = (ps_ref[...] * grad_in).astype(BF16)
    p_rows = jnp.sum(hs_ref[...] * grad_in, axis=1, keepdims=True)
    ids = ids_ref[...]
    pick = pick_ref[...]
    expert = expert_ref[...]
    sels = [jnp.where(ids[k:k + 1, :] == expert, pick, 0.0) for k in range(top)]
    rows = lax.dot_general(
        jnp.concatenate([sel.astype(BF16) for sel in sels], axis=1), h_rows, TN, preferred_element_type=F32)
    for k, sel in enumerate(sels):
        wide[pl.ds(k, toks, stride=top), :] = rows[k * toks:(k + 1) * toks]
        narrow[k:k + 1, :] = jnp.sum(sel * p_rows, axis=0, keepdims=True)
    grad_h_ref[...] = wide[...].astype(grad_h_ref.dtype)
    grad_p_ref[...] = narrow[...].astype(grad_p_ref.dtype)


def call(kernel, out_shape, operands, scratch=(), flops=0, limit=24):
    shapes = jax.tree.leaves(out_shape)
    moved = sum(a.size * a.dtype.itemsize for a in (*(a for _, a in operands), *shapes))
    return pl.pallas_call(
        kernel,
        out_shape=out_shape,
        in_specs=[pl.BlockSpec(memory_space=space) for space, _ in operands],
        out_specs=jax.tree.map(lambda _: pl.BlockSpec(memory_space=pltpu.VMEM), out_shape),
        scratch_shapes=list(scratch),
        compiler_params=pltpu.CompilerParams(vmem_limit_bytes=limit << 20),
        cost_estimate=pl.CostEstimate(flops=flops, bytes_accessed=moved, transcendentals=0),
    )(*(a for _, a in operands))


def swap(x, bits, count):
    return lax.ppermute(x, "expert", [(i, i ^ bits) for i in range(count)])


def gather_body(cotangent, hidden, probs, expert_ids, send_counts, replica_of, weights):
    toks, d_model = cotangent.shape
    top = expert_ids.shape[1]
    width = hidden.shape[2]
    local_count = weights.shape[0]
    dev_count = lax.axis_size("expert")
    homes = dev_count * local_count * SLOT
    copies = dev_count * CAPR
    slots = homes + copies
    rows = homes + dev_count * copies
    columns = d_model // 2
    sizes = (local_count, dev_count)
    ids = expert_ids.T
    shape = jax.ShapeDtypeStruct
    hbm, vmem, smem = pltpu.HBM, pltpu.VMEM, pltpu.SMEM
    sources = (replica_of, send_counts, ids, probs.T, hidden.reshape(toks * top, width), cotangent)
    per_home = local_count * SLOT
    odd, even = range(1, dev_count, 2), range(2, dev_count, 2)
    packing = [[*odd], [COPIES], [0, COPIES], [*even]]
    sized = [sum(copies if b == COPIES else per_home for b in blocks) for blocks in packing]
    pick, expert, h_slot, p_slot, to_beside, copy_rows, own_rows, even_rows = call(
        functools.partial(dispatch_kernel, *sizes, packing),
        [shape((slots, toks), F32), shape((slots, toks), jnp.int32), shape((slots, width), F32),
         shape((slots, width), F32)] + [shape((n, d_model + width), BF16) for n in sized],
        [(hbm, a) for a in sources],
        [(smem if n < 2 else vmem)(a.shape, a.dtype) for n, a in enumerate(sources)]
        + [vmem((toks * top, width), F32), pltpu.SemaphoreType.DMA((len(sources),))],
        flops=2 * slots * toks * d_model,
        limit=60,
    )
    near, far, beside = (swap(copy_rows, bits, dev_count) for bits in (2, 4, 1))
    line = swap(to_beside, 1, dev_count)
    flat_w = weights.reshape(local_count * width, d_model)
    own_rows, even_rows, w_held, slot = call(
        functools.partial(hold_kernel, *sizes),
        [shape(a.shape, BF16) for a in (own_rows, even_rows, flat_w)] + [shape((per_home + copies, width), jnp.int32)],
        [(smem, replica_of)] + [(hbm, a) for a in (flat_w, own_rows, even_rows)],
        [pltpu.SemaphoreType.DMA((3,))],
    )
    near, far, line, beside, own_rows, even_rows, w_held, slot = lax.optimization_barrier(
        (near, far, line, beside, own_rows, even_rows, w_held, slot))
    far_near = swap(far, 2, dev_count)
    to_beside, *lines = call(
        functools.partial(turn_kernel, *sizes),
        [shape((2 * copies, d_model + width), BF16)]
        + [shape((4 * per_home, fold_width(d_model + width)), BF16)] * len(even),
        [(vmem, a) for a in (line, far, near, even_rows)],
    )
    onward = swap(to_beside, 1, dev_count)
    lines = [swap(a, m, dev_count) for a, m in zip(lines, even)]
    pieces = {(0, HOME): (0, 0), (0, COPIES): (0, per_home), (1, COPIES): (1, 0), (1, HOME): (5, 0),
              (2, COPIES): (2, 0), (4, COPIES): (3, 0),
              (even[-1], HOME): (4, 0), (even[-1] + 1, HOME): (4, per_home)}
    orders = [list(pieces)]
    height = padded(sum(per_home if kind == HOME else copies for _, kind in pieces))
    early_rows, own = call(
        functools.partial(early_kernel, *sizes, orders[0], pieces),
        (shape((height, d_model + width), BF16), shape((height, width), F32)),
        [(vmem, a) for a in (w_held, slot, own_rows, beside, near, far, lines[-1], line)],
        flops=2 * height * d_model * local_count * width,
    )
    far_across = swap(far_near, 1, dev_count)
    arrays = [far_near, far_across, onward, *lines[-2::-1]]
    pieces = {(6, COPIES): (0, 0), (7, COPIES): (1, 0), (5, COPIES): (2, 0), (3, COPIES): (2, copies)}
    for n, m in enumerate(even[-2::-1]):
        pieces[m, HOME], pieces[m + 1, HOME] = ((3 + n, k * per_home) for k in range(2))
    orders.append(list(pieces))
    height = padded(sum(per_home if kind == HOME else copies for _, kind in pieces))
    block = padded(per_home + copies)
    late_rows, back = call(
        functools.partial(late_kernel, *sizes, *orders, pieces),
        (shape((height, d_model + width), BF16), shape((dev_count * block, width), BF16)),
        [(vmem, a) for a in (own, w_held, slot, *arrays)],
        [vmem((dev_count, block, width), F32)],
        flops=2 * height * d_model * local_count * width,
    )
    back = lax.all_to_all(back, "expert", split_axis=0, concat_axis=0, tiled=True)
    half_flops = 2 * rows * columns * local_count * width
    halves = (slot, early_rows, late_rows)
    other = call(
        functools.partial(other_half_kernel, *sizes, orders),
        shape((local_count * width, columns), BF16),
        [(vmem, a) for a in halves],
        flops=half_flops,
    )
    arrived = lax.ppermute(other, "dp", [(0, 1), (1, 0)])
    grad_w = call(
        functools.partial(own_half_kernel, *sizes, orders),
        shape((local_count * width, columns), BF16),
        [(vmem, a) for a in (*halves, arrived)],
        flops=30 * half_flops,
    )
    grad_w, pick = lax.optimization_barrier((grad_w, pick))
    grad_h, grad_p = call(
        functools.partial(combine_kernel, *sizes),
        (shape((toks * top, width), BF16), shape((top, toks), BF16)),
        [(vmem, a) for a in (back.reshape(dev_count, block, width), pick, expert, h_slot, p_slot, ids)],
        [vmem((toks * top, width), F32), vmem((top, toks), F32)],
        flops=2 * slots * toks * width * top,
    )
    return (
        grad_h.reshape(toks, top, width),
        grad_p.T,
        grad_w.reshape(local_count, width, columns),
    )


def body(cotangent, hidden, probs, expert_ids, send_counts, replica_of, weights):
    dev_count = lax.axis_size("expert")
    local_count, width, _ = weights.shape
    gathered = dev_count * dev_count * CAPR
    if gathered <= (local_count + 3) * width and dev_count == 8 and lax.axis_size("dp") == 2:
        run = gather_body
    else:
        run = replica_body
    return run(cotangent, hidden, probs, expert_ids, send_counts, replica_of, weights)


def solution(mesh):
    in_specs = (
        P(("groups", "expert", "dp"), None),
        P(("groups", "expert", "dp"), None, None),
        P(("groups", "expert", "dp"), None),
        P(("groups", "expert", "dp"), None),
        P(("groups", "expert", "dp"), None),
        P("groups"),
        P("expert", None, None),
    )
    out_specs = (
        P(("groups", "expert", "dp"), None, None),
        P(("groups", "expert", "dp"), None),
        P(("groups", "expert"), None, "dp"),
    )
    return jax.shard_map(body, mesh=mesh, in_specs=in_specs, out_specs=out_specs, check_vma=False)
```

```python
import functools

import jax
import jax.numpy as jnp
from jax import lax
from jax.experimental import pallas as pl
from jax.experimental.pallas import tpu as pltpu
from jax.sharding import PartitionSpec as P

CAPH = 3
CAPR = 3


def ranks_within(keys):
    total_rows = keys.shape[0]
    sort_order = jnp.argsort(keys * total_rows + jnp.arange(total_rows, dtype=jnp.int32))
    sorted_keys = keys[sort_order]
    first_seen = jnp.searchsorted(sorted_keys, sorted_keys, side="left")
    ranked = jnp.arange(total_rows, dtype=jnp.int32) - first_seen
    return jnp.zeros((total_rows,), jnp.int32).at[sort_order].set(ranked)


def route_rows(ids_block, counts_row, replica_of, local_count, cap_home, cap_copy):
    dev_count = replica_of.shape[0]
    experts = ids_block.reshape(-1)
    rank_expert = ranks_within(experts)
    devices = jnp.arange(dev_count, dtype=jnp.int32)
    same_copy = (replica_of[:, None] == replica_of[None, :]) & (devices[None, :] < devices[:, None])
    lower_rank = jnp.sum(jnp.where(same_copy, counts_row[None, :], 0), axis=1)
    upper_rank = lower_rank + counts_row
    hit_table = (
        (replica_of[None, :] == experts[:, None])
        & (lower_rank[None, :] <= rank_expert[:, None])
        & (rank_expert[:, None] < upper_rank[None, :])
    )
    copied = jnp.any(hit_table, axis=1)
    copy_dev = jnp.sum(jnp.where(hit_table, devices[None, :], 0), axis=1)
    dest_dev = jnp.where(copied, copy_dev, experts // local_count)
    index_of_slot = jnp.where(copied, local_count, experts % local_count)
    rank_bucket = ranks_within(dest_dev * (local_count + 1) + index_of_slot)
    keep_row = rank_bucket < jnp.where(copied, cap_copy, cap_home)
    per_dev = local_count * cap_home + cap_copy
    target = dest_dev * per_dev + index_of_slot * cap_home + rank_bucket
    return jnp.where(keep_row, target, dev_count * per_dev)


def replica_body(cotangent, hidden, probs, expert_ids, send_counts, replica_of, weights):
    tok_rows, d_model = cotangent.shape
    top_count = expert_ids.shape[1]
    hidden_width = hidden.shape[2]
    local_count = weights.shape[0]
    dev_count = lax.axis_size("expert")
    data_count = lax.axis_size("dp")
    per_dev = local_count * CAPH + CAPR
    row_count = tok_rows * top_count
    recv_count = dev_count * per_dev
    target = route_rows(expert_ids, send_counts[0], replica_of, local_count, CAPH, CAPR)
    inverse = (
        jnp.full((recv_count,), row_count, jnp.int32)
        .at[target]
        .set(jnp.arange(row_count, dtype=jnp.int32), mode="drop")
    )
    dy_pad = jnp.concatenate([cotangent, jnp.zeros((1, d_model), cotangent.dtype)], axis=0)
    h_pad = jnp.concatenate(
        [hidden.reshape(row_count, hidden_width), jnp.zeros((1, hidden_width), hidden.dtype)],
        axis=0,
    )
    p_pad = jnp.concatenate([probs.reshape(row_count), jnp.zeros((1,), probs.dtype)], axis=0)
    send_dy = dy_pad[inverse // top_count]
    send_h = h_pad[inverse]
    send_p = p_pad[inverse]
    recv_dy, recv_h, recv_p = (
        lax.all_to_all(send_dy, "expert", split_axis=0, concat_axis=0, tiled=True),
        lax.all_to_all(send_h, "expert", split_axis=0, concat_axis=0, tiled=True),
        lax.all_to_all(send_p, "expert", split_axis=0, concat_axis=0, tiled=True),
    )
    flat_size = hidden_width * d_model
    flat_w = weights.reshape(local_count, flat_size)
    pieces = lax.all_to_all(flat_w, "expert", split_axis=1, concat_axis=0, tiled=True)
    chosen = pieces[replica_of]
    copy_weight = lax.all_to_all(chosen, "expert", split_axis=0, concat_axis=0, tiled=True).reshape(
        hidden_width, d_model
    )
    slot_total = local_count + 1
    home_rows = local_count * CAPH
    row_pos = jnp.arange(recv_count, dtype=jnp.int32) % per_dev
    row_slot = jnp.where(row_pos < home_rows, row_pos // CAPH, local_count)
    all_weights = jnp.concatenate(
        [weights.reshape(local_count * hidden_width, d_model), copy_weight], axis=0
    )
    all_in = lax.dot_general(
        recv_dy, all_weights, (((1,), (1,)), ((), ())), preferred_element_type=jnp.float32
    )
    grad_in = jnp.zeros((recv_count, hidden_width), jnp.float32)
    for slot_num in range(slot_total):
        grad_in = grad_in + jnp.where(
            (row_slot == slot_num)[:, None],
            all_in[:, slot_num * hidden_width : (slot_num + 1) * hidden_width],
            0.0,
        )
    p_wide = recv_p.astype(jnp.float32)[:, None]
    h_wide = recv_h.astype(jnp.float32)
    grad_h_buf = (p_wide * grad_in).astype(jnp.bfloat16)
    grad_p_buf = jnp.sum(h_wide * grad_in, axis=1).astype(jnp.bfloat16)
    scaled = (p_wide * h_wide).astype(jnp.bfloat16)
    zero_rows = jnp.zeros_like(scaled)
    scaled_wide = jnp.concatenate(
        [
            jnp.where((row_slot == slot_num)[:, None], scaled, zero_rows)
            for slot_num in range(slot_total)
        ],
        axis=1,
    )
    parts = lax.dot_general(
        scaled_wide, recv_dy, (((0,), (0,)), ((), ())), preferred_element_type=jnp.float32
    ).astype(jnp.bfloat16)
    home_part = parts[: local_count * hidden_width].reshape(local_count, hidden_width, d_model)
    copy_part = parts[local_count * hidden_width :]
    back_h, back_p = (
        lax.all_to_all(grad_h_buf, "expert", split_axis=0, concat_axis=0, tiled=True),
        lax.all_to_all(grad_p_buf, "expert", split_axis=0, concat_axis=0, tiled=True),
    )
    flat_h = jnp.concatenate([back_h, jnp.zeros((1, hidden_width), back_h.dtype)], axis=0)
    flat_p = jnp.concatenate([back_p, jnp.zeros((1,), back_p.dtype)], axis=0)
    hidden_gradient = flat_h[target].reshape(tok_rows, top_count, hidden_width)
    grad_probs = flat_p[target].reshape(tok_rows, top_count)
    expert_total = dev_count * local_count
    cover = replica_of[None, :] == jnp.arange(expert_total, dtype=jnp.int32)[:, None]
    half_width = d_model // data_count
    halves = lax.all_to_all(copy_part, "dp", split_axis=1, concat_axis=0, tiled=True)
    copy_half = jnp.sum(
        halves.reshape(data_count, hidden_width, half_width).astype(jnp.float32), axis=0
    )
    piece_len = hidden_width * half_width // dev_count
    slabs = copy_half.reshape(dev_count, piece_len)
    arrived = lax.all_to_all(slabs, "expert", split_axis=0, concat_axis=0, tiled=True)
    sums = jnp.dot(cover.astype(jnp.float32), arrived, precision=lax.Precision.HIGHEST)
    homed = lax.all_to_all(
        sums.reshape(dev_count, local_count * piece_len),
        "expert",
        split_axis=0,
        concat_axis=0,
        tiled=True,
    )
    homed = (
        homed.reshape(dev_count, local_count, piece_len)
        .transpose(1, 0, 2)
        .reshape(local_count, hidden_width, half_width)
    )
    home_half = lax.psum_scatter(
        home_part.astype(jnp.float32).astype(jnp.bfloat16), "dp", scatter_dimension=2, tiled=True
    ).astype(jnp.float32)
    grad_weights = (home_half + homed).astype(jnp.bfloat16)
    return (hidden_gradient, grad_probs, grad_weights)


SLOT = 3
HOME, COPIES = "home", "copies"
F32 = jnp.float32
BF16 = jnp.bfloat16
NT = (((1,), (1,)), ((), ()))
TN = (((0,), (0,)), ((), ()))


def iota(shape, dim):
    return lax.broadcasted_iota(jnp.int32, shape, dim)


def dispatch_kernel(local_count, dev_count, packing, *refs):
    sources, refs = refs[:6], refs[6:]
    pick_ref, expert_ref, hs_ref, ps_ref = refs[:4]
    packed, (held, wide, sems) = refs[4:4 + len(packing)], (refs[-8:-2], refs[-2], refs[-1])
    moves = [pltpu.make_async_copy(s, h, sems.at[n]) for n, (s, h) in enumerate(zip(sources, held))]
    for move in moves:
        move.start()
    replica_ref, counts_ref, ids_ref, probs_ref, hid_ref, cot_ref = held
    top, toks = ids_ref.shape
    per_home = local_count * SLOT
    homes = dev_count * per_home
    slots = homes + dev_count * CAPR
    me = lax.axis_index("expert")
    row = iota((slots, toks), 0)
    expert = ((row // per_home) ^ me) * local_count + (row % per_home) // SLOT
    within = row % SLOT
    allowed = jnp.where(within < CAPH, 1, 0)
    before = jnp.where(iota((toks, toks), 0) < iota((toks, toks), 1), 1.0, 0.0).astype(BF16)
    for move in moves[:3]:
        move.wait()
    for d in range(dev_count):
        first = homes + d * CAPR
        mine = (row >= first) & (row < first + CAPR)
        expert = jnp.where(mine, replica_ref[d], expert)
        within = jnp.where(mine, row - first, within)
        allowed = jnp.where(mine, jnp.where(row - first < counts_ref[0, d], 1, 0), allowed)
    lower = jnp.zeros((slots, toks), jnp.int32)
    for d in range(dev_count):
        earlier = (row < homes) | (row >= homes + (d + 1) * CAPR)
        lower = lower + jnp.where(earlier & (expert == replica_ref[d]), counts_ref[0, d], 0)
    ids = ids_ref[...]
    named = jnp.zeros((slots, toks), F32)
    for k in range(top):
        named = named + jnp.where(ids[k:k + 1, :] == expert, 1.0, 0.0)
    rank = jnp.dot(named.astype(BF16), before, preferred_element_type=F32)
    wanted = (lower + within).astype(F32)
    pick = jnp.where((rank == wanted) & (allowed > 0), named, 0.0)
    pick_ref[...] = pick
    expert_ref[...] = expert
    for move in moves[3:5]:
        move.wait()
    wide[...] = hid_ref[...].astype(F32)
    p_slot = jnp.zeros((slots, toks), F32)
    probs = probs_ref[...].astype(F32)
    chosen, values = [], []
    for k in range(top):
        sel = jnp.where(ids[k:k + 1, :] == expert, pick, 0.0)
        chosen.append(sel.astype(BF16))
        values.append(wide[pl.ds(k, toks, stride=top), :].astype(BF16))
        p_slot = p_slot + sel * probs[k:k + 1, :]
    h_slot = jnp.dot(
        jnp.concatenate(chosen, axis=1), jnp.concatenate(values, axis=0), preferred_element_type=F32)
    p_slot = jnp.sum(p_slot, axis=1, keepdims=True)
    hs_ref[...] = h_slot
    ps_ref[...] = jnp.broadcast_to(p_slot, ps_ref.shape)
    scaled = p_slot * h_slot
    moves[5].wait()
    rows = jnp.dot(pick.astype(BF16), cot_ref[...], preferred_element_type=F32)
    d_model = cot_ref.shape[1]
    for out_ref, blocks in zip(packed, packing):
        spans = [(homes, slots) if b == COPIES else (b * per_home, (b + 1) * per_home) for b in blocks]
        out_ref[:, :d_model] = jnp.concatenate([rows[i:j] for i, j in spans], axis=0).astype(BF16)
        out_ref[:, d_model:] = jnp.concatenate([scaled[i:j] for i, j in spans], axis=0).astype(BF16)


def padded(rows):
    return -(-rows // 16) * 16


def stack(order, blocks, height):
    values = [blocks[key] for key in order]
    missing = height - sum(v.shape[0] for v in values)
    if missing:
        values.append(jnp.zeros((missing, values[0].shape[1]), values[0].dtype))
    return jnp.concatenate(values, axis=0)


def fold_width(columns):
    return -(-columns // 256) * 128


def folded(rows):
    count, columns = rows.shape
    left = fold_width(columns)
    right = [rows[:, left:], jnp.zeros((count, 2 * left - columns), rows.dtype)]
    return jnp.concatenate([rows[:, :left], jnp.concatenate(right, axis=1)], axis=0)


def unfolded(rows, columns):
    count, left = rows.shape
    if left == columns:
        return rows
    return jnp.concatenate([rows[:count // 2], rows[count // 2:, :columns - left]], axis=1)


def slots_of(order, slot_ref, per_home, height):
    kinds = {HOME: slot_ref[:per_home], COPIES: slot_ref[per_home:]}
    return stack(order, {key: kinds[key[1]] for key in order}, height)


def fill_rows(order, pieces, per_home, per_copy, piece_refs, rows_ref):
    values = [unfolded(r[...].astype(F32), rows_ref.shape[1]) for r in piece_refs]
    blocks = {}
    for key in order:
        n, start = pieces[key]
        blocks[key] = values[n][start:start + (per_home if key[1] == HOME else per_copy)]
    rows_ref[...] = stack(order, blocks, rows_ref.shape[0]).astype(BF16)


def own_columns(rows_ref, w_ref, slot, local_count):
    d_model = w_ref.shape[1]
    width = w_ref.shape[0] // local_count
    every = lax.dot_general(rows_ref[:, :d_model], w_ref[...], NT, preferred_element_type=F32)
    own = jnp.zeros((rows_ref.shape[0], width), F32)
    for e in range(local_count):
        own = jnp.where(slot == e, every[:, e * width:(e + 1) * width], own)
    return own


def hold_kernel(local_count, dev_count, replica_ref, w_hbm, own_hbm, even_hbm,
                own_ref, even_ref, w_ref, slot_ref, sems):
    moves = [pltpu.make_async_copy(a, b, sems.at[n]) for n, (a, b) in enumerate(
        ((w_hbm, w_ref), (own_hbm, own_ref), (even_hbm, even_ref)))]
    for move in moves:
        move.start()
    per_home, per_copy = local_count * SLOT, dev_count * CAPR
    first = lax.axis_index("expert") * local_count
    width = slot_ref.shape[1]
    slot_ref[:per_home] = iota((per_home, width), 0) // SLOT
    row = iota((per_copy, width), 0)
    copy = jnp.full((per_copy, width), -1, jnp.int32)
    for d in range(dev_count):
        mine = (row >= d * CAPR) & (row < (d + 1) * CAPR)
        copy = jnp.where(mine, replica_ref[d] - first, copy)
    slot_ref[per_home:] = copy
    for move in moves:
        move.wait()


def turn_kernel(local_count, dev_count, beside_ref, even_ref, *line_refs):
    per_home, per_copy = local_count * SLOT, dev_count * CAPR
    beside = beside_ref[...].astype(F32)[per_home:]
    even = even_ref[...].astype(F32)
    for n, line_ref in enumerate(line_refs):
        span = slice(n * per_home, (n + 1) * per_home)
        line_ref[...] = folded(jnp.concatenate([even[span], beside[span]], axis=0)).astype(BF16)


def place(order, value, per_home, per_copy, placed):
    start = 0
    for m, kind in order:
        lower, size = (0, per_home) if kind == HOME else (per_home, per_copy)
        placed[m, lower:lower + size] = value[start:start + size]
        start += size


def early_kernel(local_count, dev_count, order, pieces, w_ref, slot_ref, *refs):
    piece_refs, (rows_ref, own_ref) = refs[:-2], refs[-2:]
    per_home, per_copy = local_count * SLOT, dev_count * CAPR
    fill_rows(order, pieces, per_home, per_copy, piece_refs, rows_ref)
    slot = slots_of(order, slot_ref, per_home, rows_ref.shape[0])
    own_ref[...] = jnp.zeros_like(own_ref)
    place(order, own_columns(rows_ref, w_ref, slot, local_count), per_home, per_copy, own_ref)


def late_kernel(local_count, dev_count, order, pieces, own_ref, w_ref, slot_ref, *refs):
    piece_refs, (rows_ref, back_ref, placed) = refs[:-3], refs[-3:]
    per_home, per_copy = local_count * SLOT, dev_count * CAPR
    placed[...] = own_ref[...]
    fill_rows(order, pieces, per_home, per_copy, piece_refs, rows_ref)
    slot = slots_of(order, slot_ref, per_home, rows_ref.shape[0])
    place(order, own_columns(rows_ref, w_ref, slot, local_count), per_home, per_copy, placed)
    me = lax.axis_index("expert")
    back = jnp.concatenate([placed[me ^ source] for source in range(dev_count)], axis=0)
    back_ref[...] = back.astype(back_ref.dtype)


def grad_weights_half(local_count, dev_count, orders, half, slot_ref, rows_refs, columns):
    start = pl.multiple_of(half * columns, 128)
    spread = []
    for order, ref in zip(orders, rows_refs):
        slot = slots_of(order, slot_ref, local_count * SLOT, ref.shape[0])
        scaled = ref[:, 2 * columns:].astype(F32)
        spread.append(jnp.concatenate([jnp.where(slot == e, scaled, 0.0) for e in range(local_count)], axis=1))
    rows = jnp.concatenate([ref[:, pl.ds(start, columns)] for ref in rows_refs], axis=0)
    return lax.dot_general(
        jnp.concatenate(spread, axis=0).astype(BF16), rows, TN, preferred_element_type=F32)


def other_half_kernel(local_count, dev_count, orders, slot_ref, early_ref, late_ref, out_ref):
    half = 1 - lax.axis_index("dp")
    out_ref[...] = grad_weights_half(
        local_count, dev_count, orders, half, slot_ref, (early_ref, late_ref), out_ref.shape[1]).astype(out_ref.dtype)


def own_half_kernel(local_count, dev_count, orders, slot_ref, early_ref, late_ref, arrived_ref, out_ref):
    half = lax.axis_index("dp")
    total = grad_weights_half(
        local_count, dev_count, orders, half, slot_ref, (early_ref, late_ref), out_ref.shape[1])
    out_ref[...] = (total + arrived_ref[...].astype(F32)).astype(out_ref.dtype)


def combine_kernel(local_count, dev_count, back_ref, pick_ref, expert_ref, hs_ref, ps_ref, ids_ref,
                   grad_h_ref, grad_p_ref, wide, narrow):
    top, toks = ids_ref.shape
    per_home = local_count * SLOT
    me = lax.axis_index("expert")
    back = [back_ref[me ^ m].astype(F32) for m in range(dev_count)]
    slots = pick_ref.shape[0]
    copies = slots - dev_count * per_home
    copy = functools.reduce(jnp.add, [b[per_home:per_home + copies] for b in back])
    grad_in = jnp.concatenate([b[:per_home] for b in back] + [copy], axis=0)
    h_rows = (ps_ref[...] * grad_in).astype(BF16)
    p_rows = jnp.sum(hs_ref[...] * grad_in, axis=1, keepdims=True)
    ids = ids_ref[...]
    pick = pick_ref[...]
    expert = expert_ref[...]
    sels = [jnp.where(ids[k:k + 1, :] == expert, pick, 0.0) for k in range(top)]
    rows = lax.dot_general(
        jnp.concatenate([sel.astype(BF16) for sel in sels], axis=1), h_rows, TN, preferred_element_type=F32)
    for k, sel in enumerate(sels):
        wide[pl.ds(k, toks, stride=top), :] = rows[k * toks:(k + 1) * toks]
        narrow[k:k + 1, :] = jnp.sum(sel * p_rows, axis=0, keepdims=True)
    grad_h_ref[...] = wide[...].astype(grad_h_ref.dtype)
    grad_p_ref[...] = narrow[...].astype(grad_p_ref.dtype)


def call(kernel, out_shape, operands, scratch=(), flops=0, limit=24):
    shapes = jax.tree.leaves(out_shape)
    moved = sum(a.size * a.dtype.itemsize for a in (*(a for _, a in operands), *shapes))
    return pl.pallas_call(
        kernel,
        out_shape=out_shape,
        in_specs=[pl.BlockSpec(memory_space=space) for space, _ in operands],
        out_specs=jax.tree.map(lambda _: pl.BlockSpec(memory_space=pltpu.VMEM), out_shape),
        scratch_shapes=list(scratch),
        compiler_params=pltpu.CompilerParams(vmem_limit_bytes=limit << 20),
        cost_estimate=pl.CostEstimate(flops=flops, bytes_accessed=moved, transcendentals=0),
    )(*(a for _, a in operands))


def swap(x, bits, count):
    return lax.ppermute(x, "expert", [(i, i ^ bits) for i in range(count)])


def gather_body(cotangent, hidden, probs, expert_ids, send_counts, replica_of, weights):
    toks, d_model = cotangent.shape
    top = expert_ids.shape[1]
    width = hidden.shape[2]
    local_count = weights.shape[0]
    dev_count = lax.axis_size("expert")
    homes = dev_count * local_count * SLOT
    copies = dev_count * CAPR
    slots = homes + copies
    rows = homes + dev_count * copies
    columns = d_model // 2
    sizes = (local_count, dev_count)
    ids = expert_ids.T
    shape = jax.ShapeDtypeStruct
    hbm, vmem, smem = pltpu.HBM, pltpu.VMEM, pltpu.SMEM
    sources = (replica_of, send_counts, ids, probs.T, hidden.reshape(toks * top, width), cotangent)
    per_home = local_count * SLOT
    odd, even = range(1, dev_count, 2), range(2, dev_count, 2)
    packing = [[*odd], [COPIES], [0, COPIES], [*even]]
    sized = [sum(copies if b == COPIES else per_home for b in blocks) for blocks in packing]
    pick, expert, h_slot, p_slot, to_beside, copy_rows, own_rows, even_rows = call(
        functools.partial(dispatch_kernel, *sizes, packing),
        [shape((slots, toks), F32), shape((slots, toks), jnp.int32), shape((slots, width), F32),
         shape((slots, width), F32)] + [shape((n, d_model + width), BF16) for n in sized],
        [(hbm, a) for a in sources],
        [(smem if n < 2 else vmem)(a.shape, a.dtype) for n, a in enumerate(sources)]
        + [vmem((toks * top, width), F32), pltpu.SemaphoreType.DMA((len(sources),))],
        flops=2 * slots * toks * d_model,
        limit=60,
    )
    near, far, beside = (swap(copy_rows, bits, dev_count) for bits in (2, 4, 1))
    line = swap(to_beside, 1, dev_count)
    flat_w = weights.reshape(local_count * width, d_model)
    own_rows, even_rows, w_held, slot = call(
        functools.partial(hold_kernel, *sizes),
        [shape(a.shape, BF16) for a in (own_rows, even_rows, flat_w)] + [shape((per_home + copies, width), jnp.int32)],
        [(smem, replica_of)] + [(hbm, a) for a in (flat_w, own_rows, even_rows)],
        [pltpu.SemaphoreType.DMA((3,))],
    )
    near, far, line, beside, own_rows, even_rows, w_held, slot = lax.optimization_barrier(
        (near, far, line, beside, own_rows, even_rows, w_held, slot))
    far_near = swap(far, 2, dev_count)
    lines = call(
        functools.partial(turn_kernel, *sizes),
        [shape((4 * per_home, fold_width(d_model + width)), BF16)] * len(even),
        [(vmem, a) for a in (line, even_rows)],
    )
    far_beside, near_beside = swap(far, 1, dev_count), swap(near, 1, dev_count)
    lines = [swap(a, m, dev_count) for a, m in zip(lines, even)]
    pieces = {(0, HOME): (0, 0), (0, COPIES): (0, per_home), (1, COPIES): (1, 0), (1, HOME): (7, 0),
              (2, COPIES): (2, 0), (4, COPIES): (3, 0), (5, COPIES): (4, 0), (3, COPIES): (5, 0),
              (even[-1], HOME): (6, 0), (even[-1] + 1, HOME): (6, per_home)}
    orders, block = [list(pieces)], padded(per_home + copies)
    height = padded(sum(per_home if kind == HOME else copies for _, kind in pieces))
    early_rows, own = call(
        functools.partial(early_kernel, *sizes, orders[0], pieces),
        (shape((height, d_model + width), BF16), shape((dev_count, block, width), F32)),
        [(vmem, a) for a in (w_held, slot, own_rows, beside, near, far, far_beside, near_beside, lines[-1], line)],
        flops=2 * height * d_model * local_count * width,
    )
    far_across = swap(far_near, 1, dev_count)
    arrays = [far_near, far_across, *lines[:-1]]
    pieces = {(6, COPIES): (0, 0), (7, COPIES): (1, 0)}
    for n, m in enumerate(even[:-1]):
        pieces[m, HOME], pieces[m + 1, HOME] = ((2 + n, k * per_home) for k in range(2))
    orders.append(list(pieces))
    height = padded(sum(per_home if kind == HOME else copies for _, kind in pieces))
    late_rows, back = call(
        functools.partial(late_kernel, *sizes, orders[1], pieces),
        (shape((height, d_model + width), BF16), shape((dev_count * block, width), BF16)),
        [(vmem, a) for a in (own, w_held, slot, *arrays)],
        [vmem((dev_count, block, width), F32)],
        flops=2 * height * d_model * local_count * width,
    )
    back = lax.all_to_all(back, "expert", split_axis=0, concat_axis=0, tiled=True)
    half_flops = 2 * rows * columns * local_count * width
    halves = (slot, early_rows, late_rows)
    other = call(
        functools.partial(other_half_kernel, *sizes, orders),
        shape((local_count * width, columns), BF16),
        [(vmem, a) for a in halves],
        flops=half_flops,
    )
    arrived = lax.ppermute(other, "dp", [(0, 1), (1, 0)])
    grad_w = call(
        functools.partial(own_half_kernel, *sizes, orders),
        shape((local_count * width, columns), BF16),
        [(vmem, a) for a in (*halves, arrived)],
        flops=30 * half_flops,
    )
    grad_w, pick = lax.optimization_barrier((grad_w, pick))
    grad_h, grad_p = call(
        functools.partial(combine_kernel, *sizes),
        (shape((toks * top, width), BF16), shape((top, toks), BF16)),
        [(vmem, a) for a in (back.reshape(dev_count, block, width), pick, expert, h_slot, p_slot, ids)],
        [vmem((toks * top, width), F32), vmem((top, toks), F32)],
        flops=2 * slots * toks * width * top,
    )
    return (
        grad_h.reshape(toks, top, width),
        grad_p.T,
        grad_w.reshape(local_count, width, columns),
    )


def body(cotangent, hidden, probs, expert_ids, send_counts, replica_of, weights):
    dev_count = lax.axis_size("expert")
    local_count, width, _ = weights.shape
    gathered = dev_count * dev_count * CAPR
    if gathered <= (local_count + 3) * width and dev_count == 8 and lax.axis_size("dp") == 2:
        run = gather_body
    else:
        run = replica_body
    return run(cotangent, hidden, probs, expert_ids, send_counts, replica_of, weights)


def solution(mesh):
    in_specs = (
        P(("groups", "expert", "dp"), None),
        P(("groups", "expert", "dp"), None, None),
        P(("groups", "expert", "dp"), None),
        P(("groups", "expert", "dp"), None),
        P(("groups", "expert", "dp"), None),
        P("groups"),
        P("expert", None, None),
    )
    out_specs = (
        P(("groups", "expert", "dp"), None, None),
        P(("groups", "expert", "dp"), None),
        P(("groups", "expert"), None, "dp"),
    )
    return jax.shard_map(body, mesh=mesh, in_specs=in_specs, out_specs=out_specs, check_vma=False)
```

```python
import functools

import jax
import jax.numpy as jnp
from jax import lax
from jax.experimental import pallas as pl
from jax.experimental.pallas import tpu as pltpu
from jax.sharding import PartitionSpec as P

CAPH = 3
CAPR = 3


def ranks_within(keys):
    total_rows = keys.shape[0]
    sort_order = jnp.argsort(keys * total_rows + jnp.arange(total_rows, dtype=jnp.int32))
    sorted_keys = keys[sort_order]
    first_seen = jnp.searchsorted(sorted_keys, sorted_keys, side="left")
    ranked = jnp.arange(total_rows, dtype=jnp.int32) - first_seen
    return jnp.zeros((total_rows,), jnp.int32).at[sort_order].set(ranked)


def route_rows(ids_block, counts_row, replica_of, local_count, cap_home, cap_copy):
    dev_count = replica_of.shape[0]
    experts = ids_block.reshape(-1)
    rank_expert = ranks_within(experts)
    devices = jnp.arange(dev_count, dtype=jnp.int32)
    same_copy = (replica_of[:, None] == replica_of[None, :]) & (devices[None, :] < devices[:, None])
    lower_rank = jnp.sum(jnp.where(same_copy, counts_row[None, :], 0), axis=1)
    upper_rank = lower_rank + counts_row
    hit_table = (
        (replica_of[None, :] == experts[:, None])
        & (lower_rank[None, :] <= rank_expert[:, None])
        & (rank_expert[:, None] < upper_rank[None, :])
    )
    copied = jnp.any(hit_table, axis=1)
    copy_dev = jnp.sum(jnp.where(hit_table, devices[None, :], 0), axis=1)
    dest_dev = jnp.where(copied, copy_dev, experts // local_count)
    index_of_slot = jnp.where(copied, local_count, experts % local_count)
    rank_bucket = ranks_within(dest_dev * (local_count + 1) + index_of_slot)
    keep_row = rank_bucket < jnp.where(copied, cap_copy, cap_home)
    per_dev = local_count * cap_home + cap_copy
    target = dest_dev * per_dev + index_of_slot * cap_home + rank_bucket
    return jnp.where(keep_row, target, dev_count * per_dev)


def replica_body(cotangent, hidden, probs, expert_ids, send_counts, replica_of, weights):
    tok_rows, d_model = cotangent.shape
    top_count = expert_ids.shape[1]
    hidden_width = hidden.shape[2]
    local_count = weights.shape[0]
    dev_count = lax.axis_size("expert")
    data_count = lax.axis_size("dp")
    per_dev = local_count * CAPH + CAPR
    row_count = tok_rows * top_count
    recv_count = dev_count * per_dev
    target = route_rows(expert_ids, send_counts[0], replica_of, local_count, CAPH, CAPR)
    inverse = (
        jnp.full((recv_count,), row_count, jnp.int32)
        .at[target]
        .set(jnp.arange(row_count, dtype=jnp.int32), mode="drop")
    )
    dy_pad = jnp.concatenate([cotangent, jnp.zeros((1, d_model), cotangent.dtype)], axis=0)
    h_pad = jnp.concatenate(
        [hidden.reshape(row_count, hidden_width), jnp.zeros((1, hidden_width), hidden.dtype)],
        axis=0,
    )
    p_pad = jnp.concatenate([probs.reshape(row_count), jnp.zeros((1,), probs.dtype)], axis=0)
    send_dy = dy_pad[inverse // top_count]
    send_h = h_pad[inverse]
    send_p = p_pad[inverse]
    recv_dy, recv_h, recv_p = (
        lax.all_to_all(send_dy, "expert", split_axis=0, concat_axis=0, tiled=True),
        lax.all_to_all(send_h, "expert", split_axis=0, concat_axis=0, tiled=True),
        lax.all_to_all(send_p, "expert", split_axis=0, concat_axis=0, tiled=True),
    )
    flat_size = hidden_width * d_model
    flat_w = weights.reshape(local_count, flat_size)
    pieces = lax.all_to_all(flat_w, "expert", split_axis=1, concat_axis=0, tiled=True)
    chosen = pieces[replica_of]
    copy_weight = lax.all_to_all(chosen, "expert", split_axis=0, concat_axis=0, tiled=True).reshape(
        hidden_width, d_model
    )
    slot_total = local_count + 1
    home_rows = local_count * CAPH
    row_pos = jnp.arange(recv_count, dtype=jnp.int32) % per_dev
    row_slot = jnp.where(row_pos < home_rows, row_pos // CAPH, local_count)
    all_weights = jnp.concatenate(
        [weights.reshape(local_count * hidden_width, d_model), copy_weight], axis=0
    )
    all_in = lax.dot_general(
        recv_dy, all_weights, (((1,), (1,)), ((), ())), preferred_element_type=jnp.float32
    )
    grad_in = jnp.zeros((recv_count, hidden_width), jnp.float32)
    for slot_num in range(slot_total):
        grad_in = grad_in + jnp.where(
            (row_slot == slot_num)[:, None],
            all_in[:, slot_num * hidden_width : (slot_num + 1) * hidden_width],
            0.0,
        )
    p_wide = recv_p.astype(jnp.float32)[:, None]
    h_wide = recv_h.astype(jnp.float32)
    grad_h_buf = (p_wide * grad_in).astype(jnp.bfloat16)
    grad_p_buf = jnp.sum(h_wide * grad_in, axis=1).astype(jnp.bfloat16)
    scaled = (p_wide * h_wide).astype(jnp.bfloat16)
    zero_rows = jnp.zeros_like(scaled)
    scaled_wide = jnp.concatenate(
        [
            jnp.where((row_slot == slot_num)[:, None], scaled, zero_rows)
            for slot_num in range(slot_total)
        ],
        axis=1,
    )
    parts = lax.dot_general(
        scaled_wide, recv_dy, (((0,), (0,)), ((), ())), preferred_element_type=jnp.float32
    ).astype(jnp.bfloat16)
    home_part = parts[: local_count * hidden_width].reshape(local_count, hidden_width, d_model)
    copy_part = parts[local_count * hidden_width :]
    back_h, back_p = (
        lax.all_to_all(grad_h_buf, "expert", split_axis=0, concat_axis=0, tiled=True),
        lax.all_to_all(grad_p_buf, "expert", split_axis=0, concat_axis=0, tiled=True),
    )
    flat_h = jnp.concatenate([back_h, jnp.zeros((1, hidden_width), back_h.dtype)], axis=0)
    flat_p = jnp.concatenate([back_p, jnp.zeros((1,), back_p.dtype)], axis=0)
    hidden_gradient = flat_h[target].reshape(tok_rows, top_count, hidden_width)
    grad_probs = flat_p[target].reshape(tok_rows, top_count)
    expert_total = dev_count * local_count
    cover = replica_of[None, :] == jnp.arange(expert_total, dtype=jnp.int32)[:, None]
    half_width = d_model // data_count
    halves = lax.all_to_all(copy_part, "dp", split_axis=1, concat_axis=0, tiled=True)
    copy_half = jnp.sum(
        halves.reshape(data_count, hidden_width, half_width).astype(jnp.float32), axis=0
    )
    piece_len = hidden_width * half_width // dev_count
    slabs = copy_half.reshape(dev_count, piece_len)
    arrived = lax.all_to_all(slabs, "expert", split_axis=0, concat_axis=0, tiled=True)
    sums = jnp.dot(cover.astype(jnp.float32), arrived, precision=lax.Precision.HIGHEST)
    homed = lax.all_to_all(
        sums.reshape(dev_count, local_count * piece_len),
        "expert",
        split_axis=0,
        concat_axis=0,
        tiled=True,
    )
    homed = (
        homed.reshape(dev_count, local_count, piece_len)
        .transpose(1, 0, 2)
        .reshape(local_count, hidden_width, half_width)
    )
    home_half = lax.psum_scatter(
        home_part.astype(jnp.float32).astype(jnp.bfloat16), "dp", scatter_dimension=2, tiled=True
    ).astype(jnp.float32)
    grad_weights = (home_half + homed).astype(jnp.bfloat16)
    return (hidden_gradient, grad_probs, grad_weights)


SLOT = 3
HOME, COPIES = "home", "copies"
F32 = jnp.float32
BF16 = jnp.bfloat16
NT = (((1,), (1,)), ((), ()))
TN = (((0,), (0,)), ((), ()))


def iota(shape, dim):
    return lax.broadcasted_iota(jnp.int32, shape, dim)


def dispatch_kernel(local_count, dev_count, packing, *refs):
    replica_ref, counts_ref, ids_ref, probs_ref, hid_hbm, cot_hbm = refs[:6]
    pick_ref, expert_ref, hs_ref, ps_ref = refs[6:10]
    packed, (hid_ref, cot_ref, wide, sems) = refs[10:-4], refs[-4:]
    moves = [pltpu.make_async_copy(s, h, sems.at[n])
             for n, (s, h) in enumerate(((hid_hbm, hid_ref), (cot_hbm, cot_ref)))]
    for move in moves:
        move.start()
    top, toks = ids_ref.shape
    per_home = local_count * SLOT
    homes = dev_count * per_home
    slots = homes + dev_count * CAPR
    me = lax.axis_index("expert")
    row = iota((slots, toks), 0)
    expert = ((row // per_home) ^ me) * local_count + (row % per_home) // SLOT
    within = row % SLOT
    allowed = jnp.where(within < CAPH, 1, 0)
    before = jnp.where(iota((toks, toks), 0) < iota((toks, toks), 1), 1.0, 0.0).astype(BF16)
    for d in range(dev_count):
        first = homes + d * CAPR
        mine = (row >= first) & (row < first + CAPR)
        expert = jnp.where(mine, replica_ref[d], expert)
        within = jnp.where(mine, row - first, within)
        allowed = jnp.where(mine, jnp.where(row - first < counts_ref[0, d], 1, 0), allowed)
    lower = jnp.zeros((slots, toks), jnp.int32)
    for d in range(dev_count):
        earlier = (row < homes) | (row >= homes + (d + 1) * CAPR)
        lower = lower + jnp.where(earlier & (expert == replica_ref[d]), counts_ref[0, d], 0)
    ids = ids_ref[...]
    named = jnp.zeros((slots, toks), F32)
    for k in range(top):
        named = named + jnp.where(ids[k:k + 1, :] == expert, 1.0, 0.0)
    rank = jnp.dot(named.astype(BF16), before, preferred_element_type=F32)
    wanted = (lower + within).astype(F32)
    pick = jnp.where((rank == wanted) & (allowed > 0), named, 0.0)
    pick_ref[...] = pick
    expert_ref[...] = expert
    moves[0].wait()
    wide[...] = hid_ref[...].astype(F32)
    p_slot = jnp.zeros((slots, toks), F32)
    probs = probs_ref[...].astype(F32)
    chosen, values = [], []
    for k in range(top):
        sel = jnp.where(ids[k:k + 1, :] == expert, pick, 0.0)
        chosen.append(sel.astype(BF16))
        values.append(wide[pl.ds(k, toks, stride=top), :].astype(BF16))
        p_slot = p_slot + sel * probs[k:k + 1, :]
    h_slot = jnp.dot(
        jnp.concatenate(chosen, axis=1), jnp.concatenate(values, axis=0), preferred_element_type=F32)
    p_slot = jnp.sum(p_slot, axis=1, keepdims=True)
    hs_ref[...] = h_slot
    ps_ref[...] = jnp.broadcast_to(p_slot, ps_ref.shape)
    scaled = p_slot * h_slot
    moves[1].wait()
    rows = jnp.dot(pick.astype(BF16), cot_ref[...], preferred_element_type=F32)
    d_model = cot_ref.shape[1]
    for out_ref, blocks in zip(packed, packing):
        spans = [(homes, slots) if b == COPIES else (b * per_home, (b + 1) * per_home) for b in blocks]
        for columns, value in ((slice(0, d_model), rows), (slice(d_model, None), scaled)):
            chosen = {span: value[span[0]:span[1]] for span in spans}
            out_ref[:, columns] = stack(spans, chosen, out_ref.shape[0]).astype(BF16)


def padded(rows):
    return -(-rows // 16) * 16


def stack(order, blocks, height):
    values = [blocks[key] for key in order]
    missing = height - sum(v.shape[0] for v in values)
    if missing:
        values.append(jnp.zeros((missing, values[0].shape[1]), values[0].dtype))
    return jnp.concatenate(values, axis=0)


def fold_width(columns):
    return -(-columns // 256) * 128


def folded(rows):
    count, columns = rows.shape
    left = fold_width(columns)
    right = [rows[:, left:], jnp.zeros((count, 2 * left - columns), rows.dtype)]
    return jnp.concatenate([rows[:, :left], jnp.concatenate(right, axis=1)], axis=0)


def unfolded(rows, columns):
    count, left = rows.shape
    if left == columns:
        return rows
    return jnp.concatenate([rows[:count // 2], rows[count // 2:, :columns - left]], axis=1)


def slots_of(order, slot_ref, per_home, height):
    kinds = {HOME: slot_ref[:per_home], COPIES: slot_ref[per_home:]}
    return stack(order, {key: kinds[key[1]] for key in order}, height)


def fill_rows(order, pieces, per_home, per_copy, piece_refs, rows_ref):
    values = [unfolded(r[...].astype(F32), rows_ref.shape[1]) for r in piece_refs]
    blocks = {}
    for key in order:
        n, start = pieces[key]
        blocks[key] = values[n][start:start + (per_home if key[1] == HOME else per_copy)]
    rows_ref[...] = stack(order, blocks, rows_ref.shape[0]).astype(BF16)


def own_columns(rows_ref, w_ref, slot, local_count):
    d_model = w_ref.shape[1]
    width = w_ref.shape[0] // local_count
    every = lax.dot_general(rows_ref[:, :d_model], w_ref[...], NT, preferred_element_type=F32)
    own = jnp.zeros((rows_ref.shape[0], width), F32)
    for e in range(local_count):
        own = jnp.where(slot == e, every[:, e * width:(e + 1) * width], own)
    return own


def hold_kernel(local_count, dev_count, replica_ref, w_hbm, own_hbm, even_hbm,
                own_ref, even_ref, w_ref, slot_ref, sems):
    moves = [pltpu.make_async_copy(a, b, sems.at[n]) for n, (a, b) in enumerate(
        ((w_hbm, w_ref), (own_hbm, own_ref), (even_hbm, even_ref)))]
    for move in moves:
        move.start()
    per_home, per_copy = local_count * SLOT, dev_count * CAPR
    first = lax.axis_index("expert") * local_count
    width = slot_ref.shape[1]
    slot_ref[:per_home] = iota((per_home, width), 0) // SLOT
    row = iota((per_copy, width), 0)
    copy = jnp.full((per_copy, width), -1, jnp.int32)
    for d in range(dev_count):
        mine = (row >= d * CAPR) & (row < (d + 1) * CAPR)
        copy = jnp.where(mine, replica_ref[d] - first, copy)
    slot_ref[per_home:] = copy
    for move in moves:
        move.wait()


def turn_kernel(local_count, dev_count, beside_ref, even_ref, *line_refs):
    per_home, per_copy = local_count * SLOT, dev_count * CAPR
    beside = beside_ref[...].astype(F32)[per_home:]
    even = even_ref[...].astype(F32)
    for n, line_ref in enumerate(line_refs):
        span = slice(n * per_home, (n + 1) * per_home)
        line_ref[...] = folded(jnp.concatenate([even[span], beside[span]], axis=0)).astype(BF16)


def place(order, value, per_home, per_copy, placed):
    start = 0
    for m, kind in order:
        lower, size = (0, per_home) if kind == HOME else (per_home, per_copy)
        placed[m, lower:lower + size] = value[start:start + size]
        start += size


def early_kernel(local_count, dev_count, order, pieces, w_ref, slot_ref, *refs):
    piece_refs, (rows_ref, own_ref) = refs[:-2], refs[-2:]
    per_home, per_copy = local_count * SLOT, dev_count * CAPR
    fill_rows(order, pieces, per_home, per_copy, piece_refs, rows_ref)
    slot = slots_of(order, slot_ref, per_home, rows_ref.shape[0])
    own_ref[...] = jnp.zeros_like(own_ref)
    place(order, own_columns(rows_ref, w_ref, slot, local_count), per_home, per_copy, own_ref)


def late_kernel(local_count, dev_count, order, pieces, own_ref, w_ref, slot_ref, *refs):
    piece_refs, (rows_ref, back_ref, placed) = refs[:-3], refs[-3:]
    per_home, per_copy = local_count * SLOT, dev_count * CAPR
    placed[...] = own_ref[...]
    fill_rows(order, pieces, per_home, per_copy, piece_refs, rows_ref)
    slot = slots_of(order, slot_ref, per_home, rows_ref.shape[0])
    place(order, own_columns(rows_ref, w_ref, slot, local_count), per_home, per_copy, placed)
    me = lax.axis_index("expert")
    back = jnp.concatenate([placed[me ^ source] for source in range(dev_count)], axis=0)
    back_ref[...] = back.astype(back_ref.dtype)


def grad_weights_half(local_count, dev_count, orders, half, slot_ref, rows_refs, columns):
    start = pl.multiple_of(half * columns, 128)
    spread = []
    for order, ref in zip(orders, rows_refs):
        slot = slots_of(order, slot_ref, local_count * SLOT, ref.shape[0])
        scaled = ref[:, 2 * columns:].astype(F32)
        spread.append(jnp.concatenate([jnp.where(slot == e, scaled, 0.0) for e in range(local_count)], axis=1))
    rows = jnp.concatenate([ref[:, pl.ds(start, columns)] for ref in rows_refs], axis=0)
    return lax.dot_general(
        jnp.concatenate(spread, axis=0).astype(BF16), rows, TN, preferred_element_type=F32)


def other_half_kernel(local_count, dev_count, orders, slot_ref, early_ref, late_ref, out_ref):
    half = 1 - lax.axis_index("dp")
    out_ref[...] = grad_weights_half(
        local_count, dev_count, orders, half, slot_ref, (early_ref, late_ref), out_ref.shape[1]).astype(out_ref.dtype)


def own_half_kernel(local_count, dev_count, orders, slot_ref, early_ref, late_ref, arrived_ref, out_ref):
    half = lax.axis_index("dp")
    total = grad_weights_half(
        local_count, dev_count, orders, half, slot_ref, (early_ref, late_ref), out_ref.shape[1])
    out_ref[...] = (total + arrived_ref[...].astype(F32)).astype(out_ref.dtype)


def combine_kernel(local_count, dev_count, back_ref, pick_ref, expert_ref, hs_ref, ps_ref, ids_ref,
                   grad_h_ref, grad_p_ref, wide, narrow):
    top, toks = ids_ref.shape
    per_home = local_count * SLOT
    me = lax.axis_index("expert")
    back = [back_ref[me ^ m].astype(F32) for m in range(dev_count)]
    slots = pick_ref.shape[0]
    copies = slots - dev_count * per_home
    copy = functools.reduce(jnp.add, [b[per_home:per_home + copies] for b in back])
    grad_in = jnp.concatenate([b[:per_home] for b in back] + [copy], axis=0)
    h_rows = (ps_ref[...] * grad_in).astype(BF16)
    p_rows = jnp.sum(hs_ref[...] * grad_in, axis=1, keepdims=True)
    ids = ids_ref[...]
    pick = pick_ref[...]
    expert = expert_ref[...]
    sels = [jnp.where(ids[k:k + 1, :] == expert, pick, 0.0) for k in range(top)]
    rows = lax.dot_general(
        jnp.concatenate([sel.astype(BF16) for sel in sels], axis=1), h_rows, TN, preferred_element_type=F32)
    for k, sel in enumerate(sels):
        wide[pl.ds(k, toks, stride=top), :] = rows[k * toks:(k + 1) * toks]
        narrow[k:k + 1, :] = jnp.sum(sel * p_rows, axis=0, keepdims=True)
    grad_h_ref[...] = wide[...].astype(grad_h_ref.dtype)
    grad_p_ref[...] = narrow[...].astype(grad_p_ref.dtype)


def call(kernel, out_shape, operands, scratch=(), flops=0, limit=24):
    shapes = jax.tree.leaves(out_shape)
    moved = sum(a.size * a.dtype.itemsize for a in (*(a for _, a in operands), *shapes))
    return pl.pallas_call(
        kernel,
        out_shape=out_shape,
        in_specs=[pl.BlockSpec(memory_space=space) for space, _ in operands],
        out_specs=jax.tree.map(lambda _: pl.BlockSpec(memory_space=pltpu.VMEM), out_shape),
        scratch_shapes=list(scratch),
        compiler_params=pltpu.CompilerParams(vmem_limit_bytes=limit << 20),
        cost_estimate=pl.CostEstimate(flops=flops, bytes_accessed=moved, transcendentals=0),
    )(*(a for _, a in operands))


def swap(x, bits, count):
    return lax.ppermute(x, "expert", [(i, i ^ bits) for i in range(count)])


def gather_body(cotangent, hidden, probs, expert_ids, send_counts, replica_of, weights):
    toks, d_model = cotangent.shape
    top = expert_ids.shape[1]
    width = hidden.shape[2]
    local_count = weights.shape[0]
    dev_count = lax.axis_size("expert")
    homes = dev_count * local_count * SLOT
    copies = dev_count * CAPR
    slots = homes + copies
    rows = homes + dev_count * copies
    columns = d_model // 2
    sizes = (local_count, dev_count)
    ids = expert_ids.T
    shape = jax.ShapeDtypeStruct
    hbm, vmem, smem = pltpu.HBM, pltpu.VMEM, pltpu.SMEM
    sources = (replica_of, send_counts, ids, probs.T, hidden.reshape(toks * top, width), cotangent)
    per_home = local_count * SLOT
    odd, even = range(1, dev_count, 2), range(2, dev_count, 2)
    packing = [[*odd], [COPIES], [0, COPIES], [*even]]
    sized = [sum(copies if b == COPIES else per_home for b in blocks) for blocks in packing]
    sized[2:] = [padded(n) for n in sized[2:]]
    pick, expert, h_slot, p_slot, to_beside, copy_rows, own_rows, even_rows = call(
        functools.partial(dispatch_kernel, *sizes, packing),
        [shape((slots, toks), F32), shape((slots, toks), jnp.int32), shape((slots, width), F32),
         shape((slots, width), F32)] + [shape((n, d_model + width), BF16) for n in sized],
        list(zip((smem, smem, vmem, vmem, hbm, hbm), sources)),
        [vmem(a.shape, a.dtype) for a in sources[4:]]
        + [vmem((toks * top, width), F32), pltpu.SemaphoreType.DMA((2,))],
        flops=2 * slots * toks * d_model,
        limit=60,
    )
    near, far, beside = (swap(copy_rows, bits, dev_count) for bits in (2, 4, 1))
    line = swap(to_beside, 1, dev_count)
    flat_w = weights.reshape(local_count * width, d_model)
    own_rows, even_rows, w_held, slot = call(
        functools.partial(hold_kernel, *sizes),
        [shape(a.shape, BF16) for a in (own_rows, even_rows, flat_w)] + [shape((per_home + copies, width), jnp.int32)],
        [(smem, replica_of)] + [(hbm, a) for a in (flat_w, own_rows, even_rows)],
        [pltpu.SemaphoreType.DMA((3,))],
    )
    near, far, line, beside, own_rows, even_rows, w_held, slot = lax.optimization_barrier(
        (near, far, line, beside, own_rows, even_rows, w_held, slot))
    far_near = swap(far, 2, dev_count)
    lines = call(
        functools.partial(turn_kernel, *sizes),
        [shape((4 * per_home, fold_width(d_model + width)), BF16)] * len(even),
        [(vmem, a) for a in (line, even_rows)],
    )
    far_beside, near_beside = swap(far, 1, dev_count), swap(near, 1, dev_count)
    lines = [swap(a, m, dev_count) for a, m in zip(lines, even)]
    pieces = {(0, HOME): (0, 0), (0, COPIES): (0, per_home), (1, COPIES): (1, 0), (1, HOME): (7, 0),
              (2, COPIES): (2, 0), (4, COPIES): (3, 0), (5, COPIES): (4, 0), (3, COPIES): (5, 0),
              (even[-1], HOME): (6, 0), (even[-1] + 1, HOME): (6, per_home)}
    orders, block = [list(pieces)], padded(per_home + copies)
    height = padded(sum(per_home if kind == HOME else copies for _, kind in pieces))
    early_rows, own = call(
        functools.partial(early_kernel, *sizes, orders[0], pieces),
        (shape((height, d_model + width), BF16), shape((dev_count, block, width), F32)),
        [(vmem, a) for a in (w_held, slot, own_rows, beside, near, far, far_beside, near_beside, lines[-1], line)],
        flops=2 * height * d_model * local_count * width,
    )
    far_across = swap(far_near, 1, dev_count)
    arrays = [far_near, far_across, *lines[:-1]]
    pieces = {(6, COPIES): (0, 0), (7, COPIES): (1, 0)}
    for n, m in enumerate(even[:-1]):
        pieces[m, HOME], pieces[m + 1, HOME] = ((2 + n, k * per_home) for k in range(2))
    orders.append(list(pieces))
    height = padded(sum(per_home if kind == HOME else copies for _, kind in pieces))
    late_rows, back = call(
        functools.partial(late_kernel, *sizes, orders[1], pieces),
        (shape((height, d_model + width), BF16), shape((dev_count * block, width), BF16)),
        [(vmem, a) for a in (own, w_held, slot, *arrays)],
        [vmem((dev_count, block, width), F32)],
        flops=2 * height * d_model * local_count * width,
    )
    back = lax.all_to_all(back, "expert", split_axis=0, concat_axis=0, tiled=True)
    half_flops = 2 * rows * columns * local_count * width
    halves = (slot, early_rows, late_rows)
    other = call(
        functools.partial(other_half_kernel, *sizes, orders),
        shape((local_count * width, columns), BF16),
        [(vmem, a) for a in halves],
        flops=half_flops,
    )
    arrived = lax.ppermute(other, "dp", [(0, 1), (1, 0)])
    grad_w = call(
        functools.partial(own_half_kernel, *sizes, orders),
        shape((local_count * width, columns), BF16),
        [(vmem, a) for a in (*halves, arrived)],
        flops=30 * half_flops,
    )
    grad_w, pick = lax.optimization_barrier((grad_w, pick))
    grad_h, grad_p = call(
        functools.partial(combine_kernel, *sizes),
        (shape((toks * top, width), BF16), shape((top, toks), BF16)),
        [(vmem, a) for a in (back.reshape(dev_count, block, width), pick, expert, h_slot, p_slot, ids)],
        [vmem((toks * top, width), F32), vmem((top, toks), F32)],
        flops=2 * slots * toks * width * top,
    )
    return (
        grad_h.reshape(toks, top, width),
        grad_p.T,
        grad_w.reshape(local_count, width, columns),
    )


def body(cotangent, hidden, probs, expert_ids, send_counts, replica_of, weights):
    dev_count = lax.axis_size("expert")
    local_count, width, _ = weights.shape
    gathered = dev_count * dev_count * CAPR
    if gathered <= (local_count + 3) * width and dev_count == 8 and lax.axis_size("dp") == 2:
        run = gather_body
    else:
        run = replica_body
    return run(cotangent, hidden, probs, expert_ids, send_counts, replica_of, weights)


def solution(mesh):
    in_specs = (
        P(("groups", "expert", "dp"), None),
        P(("groups", "expert", "dp"), None, None),
        P(("groups", "expert", "dp"), None),
        P(("groups", "expert", "dp"), None),
        P(("groups", "expert", "dp"), None),
        P("groups"),
        P("expert", None, None),
    )
    out_specs = (
        P(("groups", "expert", "dp"), None, None),
        P(("groups", "expert", "dp"), None),
        P(("groups", "expert"), None, "dp"),
    )
    return jax.shard_map(body, mesh=mesh, in_specs=in_specs, out_specs=out_specs, check_vma=False)
```

```python
import functools

import jax
import jax.numpy as jnp
from jax import lax
from jax.experimental import pallas as pl
from jax.experimental.pallas import tpu as pltpu
from jax.sharding import PartitionSpec as P

CAPH = 3
CAPR = 3


def ranks_within(keys):
    total_rows = keys.shape[0]
    sort_order = jnp.argsort(keys * total_rows + jnp.arange(total_rows, dtype=jnp.int32))
    sorted_keys = keys[sort_order]
    first_seen = jnp.searchsorted(sorted_keys, sorted_keys, side="left")
    ranked = jnp.arange(total_rows, dtype=jnp.int32) - first_seen
    return jnp.zeros((total_rows,), jnp.int32).at[sort_order].set(ranked)


def route_rows(ids_block, counts_row, replica_of, local_count, cap_home, cap_copy):
    dev_count = replica_of.shape[0]
    experts = ids_block.reshape(-1)
    rank_expert = ranks_within(experts)
    devices = jnp.arange(dev_count, dtype=jnp.int32)
    same_copy = (replica_of[:, None] == replica_of[None, :]) & (devices[None, :] < devices[:, None])
    lower_rank = jnp.sum(jnp.where(same_copy, counts_row[None, :], 0), axis=1)
    upper_rank = lower_rank + counts_row
    hit_table = (
        (replica_of[None, :] == experts[:, None])
        & (lower_rank[None, :] <= rank_expert[:, None])
        & (rank_expert[:, None] < upper_rank[None, :])
    )
    copied = jnp.any(hit_table, axis=1)
    copy_dev = jnp.sum(jnp.where(hit_table, devices[None, :], 0), axis=1)
    dest_dev = jnp.where(copied, copy_dev, experts // local_count)
    index_of_slot = jnp.where(copied, local_count, experts % local_count)
    rank_bucket = ranks_within(dest_dev * (local_count + 1) + index_of_slot)
    keep_row = rank_bucket < jnp.where(copied, cap_copy, cap_home)
    per_dev = local_count * cap_home + cap_copy
    target = dest_dev * per_dev + index_of_slot * cap_home + rank_bucket
    return jnp.where(keep_row, target, dev_count * per_dev)


def replica_body(cotangent, hidden, probs, expert_ids, send_counts, replica_of, weights):
    tok_rows, d_model = cotangent.shape
    top_count = expert_ids.shape[1]
    hidden_width = hidden.shape[2]
    local_count = weights.shape[0]
    dev_count = lax.axis_size("expert")
    data_count = lax.axis_size("dp")
    per_dev = local_count * CAPH + CAPR
    row_count = tok_rows * top_count
    recv_count = dev_count * per_dev
    target = route_rows(expert_ids, send_counts[0], replica_of, local_count, CAPH, CAPR)
    inverse = (
        jnp.full((recv_count,), row_count, jnp.int32)
        .at[target]
        .set(jnp.arange(row_count, dtype=jnp.int32), mode="drop")
    )
    dy_pad = jnp.concatenate([cotangent, jnp.zeros((1, d_model), cotangent.dtype)], axis=0)
    h_pad = jnp.concatenate(
        [hidden.reshape(row_count, hidden_width), jnp.zeros((1, hidden_width), hidden.dtype)],
        axis=0,
    )
    p_pad = jnp.concatenate([probs.reshape(row_count), jnp.zeros((1,), probs.dtype)], axis=0)
    send_dy = dy_pad[inverse // top_count]
    send_h = h_pad[inverse]
    send_p = p_pad[inverse]
    recv_dy, recv_h, recv_p = (
        lax.all_to_all(send_dy, "expert", split_axis=0, concat_axis=0, tiled=True),
        lax.all_to_all(send_h, "expert", split_axis=0, concat_axis=0, tiled=True),
        lax.all_to_all(send_p, "expert", split_axis=0, concat_axis=0, tiled=True),
    )
    flat_size = hidden_width * d_model
    flat_w = weights.reshape(local_count, flat_size)
    pieces = lax.all_to_all(flat_w, "expert", split_axis=1, concat_axis=0, tiled=True)
    chosen = pieces[replica_of]
    copy_weight = lax.all_to_all(chosen, "expert", split_axis=0, concat_axis=0, tiled=True).reshape(
        hidden_width, d_model
    )
    slot_total = local_count + 1
    home_rows = local_count * CAPH
    row_pos = jnp.arange(recv_count, dtype=jnp.int32) % per_dev
    row_slot = jnp.where(row_pos < home_rows, row_pos // CAPH, local_count)
    all_weights = jnp.concatenate(
        [weights.reshape(local_count * hidden_width, d_model), copy_weight], axis=0
    )
    all_in = lax.dot_general(
        recv_dy, all_weights, (((1,), (1,)), ((), ())), preferred_element_type=jnp.float32
    )
    grad_in = jnp.zeros((recv_count, hidden_width), jnp.float32)
    for slot_num in range(slot_total):
        grad_in = grad_in + jnp.where(
            (row_slot == slot_num)[:, None],
            all_in[:, slot_num * hidden_width : (slot_num + 1) * hidden_width],
            0.0,
        )
    p_wide = recv_p.astype(jnp.float32)[:, None]
    h_wide = recv_h.astype(jnp.float32)
    grad_h_buf = (p_wide * grad_in).astype(jnp.bfloat16)
    grad_p_buf = jnp.sum(h_wide * grad_in, axis=1).astype(jnp.bfloat16)
    scaled = (p_wide * h_wide).astype(jnp.bfloat16)
    zero_rows = jnp.zeros_like(scaled)
    scaled_wide = jnp.concatenate(
        [
            jnp.where((row_slot == slot_num)[:, None], scaled, zero_rows)
            for slot_num in range(slot_total)
        ],
        axis=1,
    )
    parts = lax.dot_general(
        scaled_wide, recv_dy, (((0,), (0,)), ((), ())), preferred_element_type=jnp.float32
    ).astype(jnp.bfloat16)
    home_part = parts[: local_count * hidden_width].reshape(local_count, hidden_width, d_model)
    copy_part = parts[local_count * hidden_width :]
    back_h, back_p = (
        lax.all_to_all(grad_h_buf, "expert", split_axis=0, concat_axis=0, tiled=True),
        lax.all_to_all(grad_p_buf, "expert", split_axis=0, concat_axis=0, tiled=True),
    )
    flat_h = jnp.concatenate([back_h, jnp.zeros((1, hidden_width), back_h.dtype)], axis=0)
    flat_p = jnp.concatenate([back_p, jnp.zeros((1,), back_p.dtype)], axis=0)
    hidden_gradient = flat_h[target].reshape(tok_rows, top_count, hidden_width)
    grad_probs = flat_p[target].reshape(tok_rows, top_count)
    expert_total = dev_count * local_count
    cover = replica_of[None, :] == jnp.arange(expert_total, dtype=jnp.int32)[:, None]
    half_width = d_model // data_count
    halves = lax.all_to_all(copy_part, "dp", split_axis=1, concat_axis=0, tiled=True)
    copy_half = jnp.sum(
        halves.reshape(data_count, hidden_width, half_width).astype(jnp.float32), axis=0
    )
    piece_len = hidden_width * half_width // dev_count
    slabs = copy_half.reshape(dev_count, piece_len)
    arrived = lax.all_to_all(slabs, "expert", split_axis=0, concat_axis=0, tiled=True)
    sums = jnp.dot(cover.astype(jnp.float32), arrived, precision=lax.Precision.HIGHEST)
    homed = lax.all_to_all(
        sums.reshape(dev_count, local_count * piece_len),
        "expert",
        split_axis=0,
        concat_axis=0,
        tiled=True,
    )
    homed = (
        homed.reshape(dev_count, local_count, piece_len)
        .transpose(1, 0, 2)
        .reshape(local_count, hidden_width, half_width)
    )
    home_half = lax.psum_scatter(
        home_part.astype(jnp.float32).astype(jnp.bfloat16), "dp", scatter_dimension=2, tiled=True
    ).astype(jnp.float32)
    grad_weights = (home_half + homed).astype(jnp.bfloat16)
    return (hidden_gradient, grad_probs, grad_weights)


SLOT = 3
HOME, COPIES = "home", "copies"
F32 = jnp.float32
BF16 = jnp.bfloat16
NT = (((1,), (1,)), ((), ()))
TN = (((0,), (0,)), ((), ()))


def iota(shape, dim):
    return lax.broadcasted_iota(jnp.int32, shape, dim)


def dispatch_kernel(local_count, dev_count, packing, *refs):
    sources, refs = refs[:6], refs[6:]
    pick_ref, expert_ref, hs_ref, ps_ref = refs[:4]
    packed, (held, wide, sems) = refs[4:4 + len(packing)], (refs[-8:-2], refs[-2], refs[-1])
    moves = [pltpu.make_async_copy(s, h, sems.at[n]) for n, (s, h) in enumerate(zip(sources, held))]
    for move in moves:
        move.start()
    replica_ref, counts_ref, ids_ref, probs_ref, hid_ref, cot_ref = held
    top, toks = ids_ref.shape
    per_home = local_count * SLOT
    homes = dev_count * per_home
    slots = homes + dev_count * CAPR
    me = lax.axis_index("expert")
    row = iota((slots, toks), 0)
    expert = ((row // per_home) ^ me) * local_count + (row % per_home) // SLOT
    within = row % SLOT
    allowed = jnp.where(within < CAPH, 1, 0)
    before = jnp.where(iota((toks, toks), 0) < iota((toks, toks), 1), 1.0, 0.0).astype(BF16)
    for move in moves[:3]:
        move.wait()
    for d in range(dev_count):
        first = homes + d * CAPR
        mine = (row >= first) & (row < first + CAPR)
        expert = jnp.where(mine, replica_ref[d], expert)
        within = jnp.where(mine, row - first, within)
        allowed = jnp.where(mine, jnp.where(row - first < counts_ref[0, d], 1, 0), allowed)
    lower = jnp.zeros((slots, toks), jnp.int32)
    for d in range(dev_count):
        earlier = (row < homes) | (row >= homes + (d + 1) * CAPR)
        lower = lower + jnp.where(earlier & (expert == replica_ref[d]), counts_ref[0, d], 0)
    ids = ids_ref[...]
    named = jnp.zeros((slots, toks), F32)
    for k in range(top):
        named = named + jnp.where(ids[k:k + 1, :] == expert, 1.0, 0.0)
    rank = jnp.dot(named.astype(BF16), before, preferred_element_type=F32)
    wanted = (lower + within).astype(F32)
    pick = jnp.where((rank == wanted) & (allowed > 0), named, 0.0)
    pick_ref[...] = pick
    expert_ref[...] = expert
    for move in moves[3:5]:
        move.wait()
    wide[...] = hid_ref[...].astype(F32)
    p_slot = jnp.zeros((slots, toks), F32)
    probs = probs_ref[...].astype(F32)
    chosen, values = [], []
    for k in range(top):
        sel = jnp.where(ids[k:k + 1, :] == expert, pick, 0.0)
        chosen.append(sel.astype(BF16))
        values.append(wide[pl.ds(k, toks, stride=top), :].astype(BF16))
        p_slot = p_slot + sel * probs[k:k + 1, :]
    h_slot = jnp.dot(
        jnp.concatenate(chosen, axis=1), jnp.concatenate(values, axis=0), preferred_element_type=F32)
    p_slot = jnp.sum(p_slot, axis=1, keepdims=True)
    hs_ref[...] = h_slot
    ps_ref[...] = jnp.broadcast_to(p_slot, ps_ref.shape)
    scaled = p_slot * h_slot
    moves[5].wait()
    rows = jnp.dot(pick.astype(BF16), cot_ref[...], preferred_element_type=F32)
    d_model = cot_ref.shape[1]
    for out_ref, blocks in zip(packed, packing):
        spans = [(homes, slots) if b == COPIES else (b * per_home, (b + 1) * per_home) for b in blocks]
        for columns, value in ((slice(0, d_model), rows), (slice(d_model, None), scaled)):
            chosen = {span: value[span[0]:span[1]] for span in spans}
            out_ref[:, columns] = stack(spans, chosen, out_ref.shape[0]).astype(BF16)


def padded(rows):
    return -(-rows // 16) * 16


def stack(order, blocks, height):
    values = [blocks[key] for key in order]
    missing = height - sum(v.shape[0] for v in values)
    if missing:
        values.append(jnp.zeros((missing, values[0].shape[1]), values[0].dtype))
    return jnp.concatenate(values, axis=0)


def fold_width(columns):
    return -(-columns // 256) * 128


def folded(rows):
    count, columns = rows.shape
    left = fold_width(columns)
    right = [rows[:, left:], jnp.zeros((count, 2 * left - columns), rows.dtype)]
    return jnp.concatenate([rows[:, :left], jnp.concatenate(right, axis=1)], axis=0)


def unfolded(rows, columns):
    count, left = rows.shape
    if left == columns:
        return rows
    return jnp.concatenate([rows[:count // 2], rows[count // 2:, :columns - left]], axis=1)


def slots_of(order, slot_ref, per_home, height):
    kinds = {HOME: slot_ref[:per_home], COPIES: slot_ref[per_home:]}
    return stack(order, {key: kinds[key[1]] for key in order}, height)


def fill_rows(order, pieces, per_home, per_copy, piece_refs, rows_ref):
    values = [unfolded(r[...].astype(F32), rows_ref.shape[1]) for r in piece_refs]
    blocks = {}
    for key in order:
        n, start = pieces[key]
        blocks[key] = values[n][start:start + (per_home if key[1] == HOME else per_copy)]
    rows_ref[...] = stack(order, blocks, rows_ref.shape[0]).astype(BF16)


def own_columns(rows_ref, w_ref, slot, local_count):
    d_model = w_ref.shape[1]
    width = w_ref.shape[0] // local_count
    every = lax.dot_general(rows_ref[:, :d_model], w_ref[...], NT, preferred_element_type=F32)
    own = jnp.zeros((rows_ref.shape[0], width), F32)
    for e in range(local_count):
        own = jnp.where(slot == e, every[:, e * width:(e + 1) * width], own)
    return own


def hold_kernel(local_count, dev_count, replica_ref, w_hbm, own_hbm, even_hbm,
                own_ref, even_ref, w_ref, slot_ref, sems):
    moves = [pltpu.make_async_copy(a, b, sems.at[n]) for n, (a, b) in enumerate(
        ((w_hbm, w_ref), (own_hbm, own_ref), (even_hbm, even_ref)))]
    for move in moves:
        move.start()
    per_home, per_copy = local_count * SLOT, dev_count * CAPR
    first = lax.axis_index("expert") * local_count
    width = slot_ref.shape[1]
    slot_ref[:per_home] = iota((per_home, width), 0) // SLOT
    row = iota((per_copy, width), 0)
    copy = jnp.full((per_copy, width), -1, jnp.int32)
    for d in range(dev_count):
        mine = (row >= d * CAPR) & (row < (d + 1) * CAPR)
        copy = jnp.where(mine, replica_ref[d] - first, copy)
    slot_ref[per_home:] = copy
    for move in moves:
        move.wait()


def turn_kernel(local_count, dev_count, beside_ref, even_ref, *line_refs):
    per_home, per_copy = local_count * SLOT, dev_count * CAPR
    beside = beside_ref[...].astype(F32)[per_home:]
    even = even_ref[...].astype(F32)
    for n, line_ref in enumerate(line_refs):
        span = slice(n * per_home, (n + 1) * per_home)
        line_ref[...] = folded(jnp.concatenate([even[span], beside[span]], axis=0)).astype(BF16)


def place(order, value, per_home, per_copy, placed):
    start = 0
    for m, kind in order:
        lower, size = (0, per_home) if kind == HOME else (per_home, per_copy)
        placed[m, lower:lower + size] = value[start:start + size]
        start += size


def early_kernel(local_count, dev_count, order, pieces, w_ref, slot_ref, *refs):
    piece_refs, (rows_ref, own_ref) = refs[:-2], refs[-2:]
    per_home, per_copy = local_count * SLOT, dev_count * CAPR
    fill_rows(order, pieces, per_home, per_copy, piece_refs, rows_ref)
    slot = slots_of(order, slot_ref, per_home, rows_ref.shape[0])
    own_ref[...] = jnp.zeros_like(own_ref)
    place(order, own_columns(rows_ref, w_ref, slot, local_count), per_home, per_copy, own_ref)


def late_kernel(local_count, dev_count, order, pieces, own_ref, w_ref, slot_ref, *refs):
    piece_refs, (rows_ref, back_ref, placed) = refs[:-3], refs[-3:]
    per_home, per_copy = local_count * SLOT, dev_count * CAPR
    placed[...] = own_ref[...]
    fill_rows(order, pieces, per_home, per_copy, piece_refs, rows_ref)
    slot = slots_of(order, slot_ref, per_home, rows_ref.shape[0])
    place(order, own_columns(rows_ref, w_ref, slot, local_count), per_home, per_copy, placed)
    me = lax.axis_index("expert")
    back = jnp.concatenate([placed[me ^ source] for source in range(dev_count)], axis=0)
    back_ref[...] = back.astype(back_ref.dtype)


def grad_weights_half(local_count, dev_count, orders, half, slot_ref, rows_refs, columns):
    start = pl.multiple_of(half * columns, 128)
    spread = []
    for order, ref in zip(orders, rows_refs):
        slot = slots_of(order, slot_ref, local_count * SLOT, ref.shape[0])
        scaled = ref[:, 2 * columns:].astype(F32)
        spread.append(jnp.concatenate([jnp.where(slot == e, scaled, 0.0) for e in range(local_count)], axis=1))
    rows = jnp.concatenate([ref[:, pl.ds(start, columns)] for ref in rows_refs], axis=0)
    return lax.dot_general(
        jnp.concatenate(spread, axis=0).astype(BF16), rows, TN, preferred_element_type=F32)


def other_half_kernel(local_count, dev_count, orders, slot_ref, early_ref, late_ref, out_ref):
    half = 1 - lax.axis_index("dp")
    out_ref[...] = grad_weights_half(
        local_count, dev_count, orders, half, slot_ref, (early_ref, late_ref), out_ref.shape[1]).astype(out_ref.dtype)


def own_half_kernel(local_count, dev_count, orders, slot_ref, early_ref, late_ref, arrived_ref, out_ref):
    half = lax.axis_index("dp")
    total = grad_weights_half(
        local_count, dev_count, orders, half, slot_ref, (early_ref, late_ref), out_ref.shape[1])
    out_ref[...] = (total + arrived_ref[...].astype(F32)).astype(out_ref.dtype)


def combine_kernel(local_count, dev_count, back_ref, pick_ref, expert_ref, hs_ref, ps_ref, ids_ref,
                   grad_h_ref, grad_p_ref, wide, narrow):
    top, toks = ids_ref.shape
    per_home = local_count * SLOT
    me = lax.axis_index("expert")
    back = [back_ref[me ^ m].astype(F32) for m in range(dev_count)]
    slots = pick_ref.shape[0]
    copies = slots - dev_count * per_home
    copy = functools.reduce(jnp.add, [b[per_home:per_home + copies] for b in back])
    grad_in = jnp.concatenate([b[:per_home] for b in back] + [copy], axis=0)
    h_rows = (ps_ref[...] * grad_in).astype(BF16)
    p_rows = jnp.sum(hs_ref[...] * grad_in, axis=1, keepdims=True)
    ids = ids_ref[...]
    pick = pick_ref[...]
    expert = expert_ref[...]
    sels = [jnp.where(ids[k:k + 1, :] == expert, pick, 0.0) for k in range(top)]
    rows = lax.dot_general(
        jnp.concatenate([sel.astype(BF16) for sel in sels], axis=1), h_rows, TN, preferred_element_type=F32)
    for k, sel in enumerate(sels):
        wide[pl.ds(k, toks, stride=top), :] = rows[k * toks:(k + 1) * toks]
        narrow[k:k + 1, :] = jnp.sum(sel * p_rows, axis=0, keepdims=True)
    grad_h_ref[...] = wide[...].astype(grad_h_ref.dtype)
    grad_p_ref[...] = narrow[...].astype(grad_p_ref.dtype)


def call(kernel, out_shape, operands, scratch=(), flops=0, limit=24):
    shapes = jax.tree.leaves(out_shape)
    moved = sum(a.size * a.dtype.itemsize for a in (*(a for _, a in operands), *shapes))
    return pl.pallas_call(
        kernel,
        out_shape=out_shape,
        in_specs=[pl.BlockSpec(memory_space=space) for space, _ in operands],
        out_specs=jax.tree.map(lambda _: pl.BlockSpec(memory_space=pltpu.VMEM), out_shape),
        scratch_shapes=list(scratch),
        compiler_params=pltpu.CompilerParams(vmem_limit_bytes=limit << 20),
        cost_estimate=pl.CostEstimate(flops=flops, bytes_accessed=moved, transcendentals=0),
    )(*(a for _, a in operands))


def swap(x, bits, count):
    return lax.ppermute(x, "expert", [(i, i ^ bits) for i in range(count)])


def gather_body(cotangent, hidden, probs, expert_ids, send_counts, replica_of, weights):
    toks, d_model = cotangent.shape
    top = expert_ids.shape[1]
    width = hidden.shape[2]
    local_count = weights.shape[0]
    dev_count = lax.axis_size("expert")
    homes = dev_count * local_count * SLOT
    copies = dev_count * CAPR
    slots = homes + copies
    rows = homes + dev_count * copies
    columns = d_model // 2
    sizes = (local_count, dev_count)
    ids = expert_ids.T
    shape = jax.ShapeDtypeStruct
    hbm, vmem, smem = pltpu.HBM, pltpu.VMEM, pltpu.SMEM
    sources = (replica_of, send_counts, ids, probs.T, hidden.reshape(toks * top, width), cotangent)
    per_home = local_count * SLOT
    odd, even = range(1, dev_count, 2), range(2, dev_count, 2)
    packing = [[*odd], [COPIES], [0, COPIES], [*even]]
    sized = [sum(copies if b == COPIES else per_home for b in blocks) for blocks in packing]
    sized[2:] = [padded(n) for n in sized[2:]]
    pick, expert, h_slot, p_slot, to_beside, copy_rows, own_rows, even_rows = call(
        functools.partial(dispatch_kernel, *sizes, packing),
        [shape((slots, toks), F32), shape((slots, toks), jnp.int32), shape((slots, width), F32),
         shape((slots, width), F32)] + [shape((n, d_model + width), BF16) for n in sized],
        [(hbm, a) for a in sources],
        [(smem if n < 2 else vmem)(a.shape, a.dtype) for n, a in enumerate(sources)]
        + [vmem((toks * top, width), F32), pltpu.SemaphoreType.DMA((len(sources),))],
        flops=2 * slots * toks * d_model,
        limit=60,
    )
    near, far, beside = (swap(copy_rows, bits, dev_count) for bits in (2, 4, 1))
    line = swap(to_beside, 1, dev_count)
    flat_w = weights.reshape(local_count * width, d_model)
    own_rows, even_rows, w_held, slot = call(
        functools.partial(hold_kernel, *sizes),
        [shape(a.shape, BF16) for a in (own_rows, even_rows, flat_w)] + [shape((per_home + copies, width), jnp.int32)],
        [(smem, replica_of)] + [(hbm, a) for a in (flat_w, own_rows, even_rows)],
        [pltpu.SemaphoreType.DMA((3,))],
    )
    near, far, line, beside, own_rows, even_rows, w_held, slot = lax.optimization_barrier(
        (near, far, line, beside, own_rows, even_rows, w_held, slot))
    far_near = swap(far, 2, dev_count)
    lines = call(
        functools.partial(turn_kernel, *sizes),
        [shape((4 * per_home, fold_width(d_model + width)), BF16)] * len(even),
        [(vmem, a) for a in (line, even_rows)],
    )
    far_beside, near_beside = swap(far, 1, dev_count), swap(near, 1, dev_count)
    lines = [swap(a, m, dev_count) for a, m in zip(lines, even)]
    pieces = {(0, HOME): (0, 0), (0, COPIES): (0, per_home), (1, COPIES): (1, 0), (1, HOME): (7, 0),
              (2, COPIES): (2, 0), (4, COPIES): (3, 0), (5, COPIES): (4, 0), (3, COPIES): (5, 0),
              (even[-1], HOME): (6, 0), (even[-1] + 1, HOME): (6, per_home)}
    orders, block = [list(pieces)], padded(per_home + copies)
    height = padded(sum(per_home if kind == HOME else copies for _, kind in pieces))
    early_rows, own = call(
        functools.partial(early_kernel, *sizes, orders[0], pieces),
        (shape((height, d_model + width), BF16), shape((dev_count, block, width), F32)),
        [(vmem, a) for a in (w_held, slot, own_rows, beside, near, far, far_beside, near_beside, lines[-1], line)],
        flops=2 * height * d_model * local_count * width,
    )
    far_across = swap(far_near, 1, dev_count)
    arrays = [far_near, far_across, *lines[:-1]]
    pieces = {(6, COPIES): (0, 0), (7, COPIES): (1, 0)}
    for n, m in enumerate(even[:-1]):
        pieces[m, HOME], pieces[m + 1, HOME] = ((2 + n, k * per_home) for k in range(2))
    orders.append(list(pieces))
    height = padded(sum(per_home if kind == HOME else copies for _, kind in pieces))
    late_rows, back = call(
        functools.partial(late_kernel, *sizes, orders[1], pieces),
        (shape((height, d_model + width), BF16), shape((dev_count * block, width), BF16)),
        [(vmem, a) for a in (own, w_held, slot, *arrays)],
        [vmem((dev_count, block, width), F32)],
        flops=2 * height * d_model * local_count * width,
    )
    back = lax.all_to_all(back, "expert", split_axis=0, concat_axis=0, tiled=True)
    half_flops = 2 * rows * columns * local_count * width
    halves = (slot, early_rows, late_rows)
    other = call(
        functools.partial(other_half_kernel, *sizes, orders),
        shape((local_count * width, columns), BF16),
        [(vmem, a) for a in halves],
        flops=half_flops,
    )
    arrived = lax.ppermute(other, "dp", [(0, 1), (1, 0)])
    grad_w = call(
        functools.partial(own_half_kernel, *sizes, orders),
        shape((local_count * width, columns), BF16),
        [(vmem, a) for a in (*halves, arrived)],
        flops=30 * half_flops,
    )
    grad_w, pick = lax.optimization_barrier((grad_w, pick))
    grad_h, grad_p = call(
        functools.partial(combine_kernel, *sizes),
        (shape((toks * top, width), BF16), shape((top, toks), BF16)),
        [(vmem, a) for a in (back.reshape(dev_count, block, width), pick, expert, h_slot, p_slot, ids)],
        [vmem((toks * top, width), F32), vmem((top, toks), F32)],
        flops=2 * slots * toks * width * top,
    )
    return (
        grad_h.reshape(toks, top, width),
        grad_p.T,
        grad_w.reshape(local_count, width, columns),
    )


def body(cotangent, hidden, probs, expert_ids, send_counts, replica_of, weights):
    dev_count = lax.axis_size("expert")
    local_count, width, _ = weights.shape
    gathered = dev_count * dev_count * CAPR
    if gathered <= (local_count + 3) * width and dev_count == 8 and lax.axis_size("dp") == 2:
        run = gather_body
    else:
        run = replica_body
    return run(cotangent, hidden, probs, expert_ids, send_counts, replica_of, weights)


def solution(mesh):
    in_specs = (
        P(("groups", "expert", "dp"), None),
        P(("groups", "expert", "dp"), None, None),
        P(("groups", "expert", "dp"), None),
        P(("groups", "expert", "dp"), None),
        P(("groups", "expert", "dp"), None),
        P("groups"),
        P("expert", None, None),
    )
    out_specs = (
        P(("groups", "expert", "dp"), None, None),
        P(("groups", "expert", "dp"), None),
        P(("groups", "expert"), None, "dp"),
    )
    return jax.shard_map(body, mesh=mesh, in_specs=in_specs, out_specs=out_specs, check_vma=False)
```

```python
import functools

import jax
import jax.numpy as jnp
from jax import lax
from jax.experimental import pallas as pl
from jax.experimental.pallas import tpu as pltpu
from jax.sharding import PartitionSpec as P

CAPH = 3
CAPR = 3


def ranks_within(keys):
    total_rows = keys.shape[0]
    sort_order = jnp.argsort(keys * total_rows + jnp.arange(total_rows, dtype=jnp.int32))
    sorted_keys = keys[sort_order]
    first_seen = jnp.searchsorted(sorted_keys, sorted_keys, side="left")
    ranked = jnp.arange(total_rows, dtype=jnp.int32) - first_seen
    return jnp.zeros((total_rows,), jnp.int32).at[sort_order].set(ranked)


def route_rows(ids_block, counts_row, replica_of, local_count, cap_home, cap_copy):
    dev_count = replica_of.shape[0]
    experts = ids_block.reshape(-1)
    rank_expert = ranks_within(experts)
    devices = jnp.arange(dev_count, dtype=jnp.int32)
    same_copy = (replica_of[:, None] == replica_of[None, :]) & (devices[None, :] < devices[:, None])
    lower_rank = jnp.sum(jnp.where(same_copy, counts_row[None, :], 0), axis=1)
    upper_rank = lower_rank + counts_row
    hit_table = (
        (replica_of[None, :] == experts[:, None])
        & (lower_rank[None, :] <= rank_expert[:, None])
        & (rank_expert[:, None] < upper_rank[None, :])
    )
    copied = jnp.any(hit_table, axis=1)
    copy_dev = jnp.sum(jnp.where(hit_table, devices[None, :], 0), axis=1)
    dest_dev = jnp.where(copied, copy_dev, experts // local_count)
    index_of_slot = jnp.where(copied, local_count, experts % local_count)
    rank_bucket = ranks_within(dest_dev * (local_count + 1) + index_of_slot)
    keep_row = rank_bucket < jnp.where(copied, cap_copy, cap_home)
    per_dev = local_count * cap_home + cap_copy
    target = dest_dev * per_dev + index_of_slot * cap_home + rank_bucket
    return jnp.where(keep_row, target, dev_count * per_dev)


def replica_body(cotangent, hidden, probs, expert_ids, send_counts, replica_of, weights):
    tok_rows, d_model = cotangent.shape
    top_count = expert_ids.shape[1]
    hidden_width = hidden.shape[2]
    local_count = weights.shape[0]
    dev_count = lax.axis_size("expert")
    data_count = lax.axis_size("dp")
    per_dev = local_count * CAPH + CAPR
    row_count = tok_rows * top_count
    recv_count = dev_count * per_dev
    target = route_rows(expert_ids, send_counts[0], replica_of, local_count, CAPH, CAPR)
    inverse = (
        jnp.full((recv_count,), row_count, jnp.int32)
        .at[target]
        .set(jnp.arange(row_count, dtype=jnp.int32), mode="drop")
    )
    dy_pad = jnp.concatenate([cotangent, jnp.zeros((1, d_model), cotangent.dtype)], axis=0)
    h_pad = jnp.concatenate(
        [hidden.reshape(row_count, hidden_width), jnp.zeros((1, hidden_width), hidden.dtype)],
        axis=0,
    )
    p_pad = jnp.concatenate([probs.reshape(row_count), jnp.zeros((1,), probs.dtype)], axis=0)
    send_dy = dy_pad[inverse // top_count]
    send_h = h_pad[inverse]
    send_p = p_pad[inverse]
    recv_dy, recv_h, recv_p = (
        lax.all_to_all(send_dy, "expert", split_axis=0, concat_axis=0, tiled=True),
        lax.all_to_all(send_h, "expert", split_axis=0, concat_axis=0, tiled=True),
        lax.all_to_all(send_p, "expert", split_axis=0, concat_axis=0, tiled=True),
    )
    flat_size = hidden_width * d_model
    flat_w = weights.reshape(local_count, flat_size)
    pieces = lax.all_to_all(flat_w, "expert", split_axis=1, concat_axis=0, tiled=True)
    chosen = pieces[replica_of]
    copy_weight = lax.all_to_all(chosen, "expert", split_axis=0, concat_axis=0, tiled=True).reshape(
        hidden_width, d_model
    )
    slot_total = local_count + 1
    home_rows = local_count * CAPH
    row_pos = jnp.arange(recv_count, dtype=jnp.int32) % per_dev
    row_slot = jnp.where(row_pos < home_rows, row_pos // CAPH, local_count)
    all_weights = jnp.concatenate(
        [weights.reshape(local_count * hidden_width, d_model), copy_weight], axis=0
    )
    all_in = lax.dot_general(
        recv_dy, all_weights, (((1,), (1,)), ((), ())), preferred_element_type=jnp.float32
    )
    grad_in = jnp.zeros((recv_count, hidden_width), jnp.float32)
    for slot_num in range(slot_total):
        grad_in = grad_in + jnp.where(
            (row_slot == slot_num)[:, None],
            all_in[:, slot_num * hidden_width : (slot_num + 1) * hidden_width],
            0.0,
        )
    p_wide = recv_p.astype(jnp.float32)[:, None]
    h_wide = recv_h.astype(jnp.float32)
    grad_h_buf = (p_wide * grad_in).astype(jnp.bfloat16)
    grad_p_buf = jnp.sum(h_wide * grad_in, axis=1).astype(jnp.bfloat16)
    scaled = (p_wide * h_wide).astype(jnp.bfloat16)
    zero_rows = jnp.zeros_like(scaled)
    scaled_wide = jnp.concatenate(
        [
            jnp.where((row_slot == slot_num)[:, None], scaled, zero_rows)
            for slot_num in range(slot_total)
        ],
        axis=1,
    )
    parts = lax.dot_general(
        scaled_wide, recv_dy, (((0,), (0,)), ((), ())), preferred_element_type=jnp.float32
    ).astype(jnp.bfloat16)
    home_part = parts[: local_count * hidden_width].reshape(local_count, hidden_width, d_model)
    copy_part = parts[local_count * hidden_width :]
    back_h, back_p = (
        lax.all_to_all(grad_h_buf, "expert", split_axis=0, concat_axis=0, tiled=True),
        lax.all_to_all(grad_p_buf, "expert", split_axis=0, concat_axis=0, tiled=True),
    )
    flat_h = jnp.concatenate([back_h, jnp.zeros((1, hidden_width), back_h.dtype)], axis=0)
    flat_p = jnp.concatenate([back_p, jnp.zeros((1,), back_p.dtype)], axis=0)
    hidden_gradient = flat_h[target].reshape(tok_rows, top_count, hidden_width)
    grad_probs = flat_p[target].reshape(tok_rows, top_count)
    expert_total = dev_count * local_count
    cover = replica_of[None, :] == jnp.arange(expert_total, dtype=jnp.int32)[:, None]
    half_width = d_model // data_count
    halves = lax.all_to_all(copy_part, "dp", split_axis=1, concat_axis=0, tiled=True)
    copy_half = jnp.sum(
        halves.reshape(data_count, hidden_width, half_width).astype(jnp.float32), axis=0
    )
    piece_len = hidden_width * half_width // dev_count
    slabs = copy_half.reshape(dev_count, piece_len)
    arrived = lax.all_to_all(slabs, "expert", split_axis=0, concat_axis=0, tiled=True)
    sums = jnp.dot(cover.astype(jnp.float32), arrived, precision=lax.Precision.HIGHEST)
    homed = lax.all_to_all(
        sums.reshape(dev_count, local_count * piece_len),
        "expert",
        split_axis=0,
        concat_axis=0,
        tiled=True,
    )
    homed = (
        homed.reshape(dev_count, local_count, piece_len)
        .transpose(1, 0, 2)
        .reshape(local_count, hidden_width, half_width)
    )
    home_half = lax.psum_scatter(
        home_part.astype(jnp.float32).astype(jnp.bfloat16), "dp", scatter_dimension=2, tiled=True
    ).astype(jnp.float32)
    grad_weights = (home_half + homed).astype(jnp.bfloat16)
    return (hidden_gradient, grad_probs, grad_weights)


SLOT = 3
HOME, COPIES = "home", "copies"
F32 = jnp.float32
BF16 = jnp.bfloat16
NT = (((1,), (1,)), ((), ()))
TN = (((0,), (0,)), ((), ()))


def iota(shape, dim):
    return lax.broadcasted_iota(jnp.int32, shape, dim)


def dispatch_kernel(local_count, dev_count, packing, *refs):
    sources, refs = refs[:6], refs[6:]
    pick_ref, expert_ref, hs_ref, ps_ref = refs[:4]
    packed, (held, wide, sems) = refs[4:4 + len(packing)], (refs[-8:-2], refs[-2], refs[-1])
    moves = [pltpu.make_async_copy(s, h, sems.at[n]) for n, (s, h) in enumerate(zip(sources, held))]
    for move in moves:
        move.start()
    replica_ref, counts_ref, ids_ref, probs_ref, hid_ref, cot_ref = held
    top, toks = ids_ref.shape
    per_home = local_count * SLOT
    homes = dev_count * per_home
    slots = homes + dev_count * CAPR
    me = lax.axis_index("expert")
    row = iota((slots, toks), 0)
    expert = ((row // per_home) ^ me) * local_count + (row % per_home) // SLOT
    within = row % SLOT
    allowed = jnp.where(within < CAPH, 1, 0)
    before = jnp.where(iota((toks, toks), 0) < iota((toks, toks), 1), 1.0, 0.0).astype(BF16)
    for move in moves[:3]:
        move.wait()
    for d in range(dev_count):
        first = homes + d * CAPR
        mine = (row >= first) & (row < first + CAPR)
        expert = jnp.where(mine, replica_ref[d], expert)
        within = jnp.where(mine, row - first, within)
        allowed = jnp.where(mine, jnp.where(row - first < counts_ref[0, d], 1, 0), allowed)
    lower = jnp.zeros((slots, toks), jnp.int32)
    for d in range(dev_count):
        earlier = (row < homes) | (row >= homes + (d + 1) * CAPR)
        lower = lower + jnp.where(earlier & (expert == replica_ref[d]), counts_ref[0, d], 0)
    ids = ids_ref[...]
    named = jnp.zeros((slots, toks), F32)
    for k in range(top):
        named = named + jnp.where(ids[k:k + 1, :] == expert, 1.0, 0.0)
    rank = jnp.dot(named.astype(BF16), before, preferred_element_type=F32)
    wanted = (lower + within).astype(F32)
    pick = jnp.where((rank == wanted) & (allowed > 0), named, 0.0)
    pick_ref[...] = pick
    expert_ref[...] = expert
    for move in moves[3:5]:
        move.wait()
    wide[...] = hid_ref[...].astype(F32)
    p_slot = jnp.zeros((slots, toks), F32)
    probs = probs_ref[...].astype(F32)
    chosen, values = [], []
    for k in range(top):
        sel = jnp.where(ids[k:k + 1, :] == expert, pick, 0.0)
        chosen.append(sel.astype(BF16))
        values.append(wide[pl.ds(k, toks, stride=top), :].astype(BF16))
        p_slot = p_slot + sel * probs[k:k + 1, :]
    h_slot = jnp.dot(
        jnp.concatenate(chosen, axis=1), jnp.concatenate(values, axis=0), preferred_element_type=F32)
    p_slot = jnp.sum(p_slot, axis=1, keepdims=True)
    hs_ref[...] = h_slot
    ps_ref[...] = jnp.broadcast_to(p_slot, ps_ref.shape)
    scaled = p_slot * h_slot
    moves[5].wait()
    rows = jnp.dot(pick.astype(BF16), cot_ref[...], preferred_element_type=F32)
    d_model = cot_ref.shape[1]
    for out_ref, blocks in zip(packed, packing):
        spans = [(homes, slots) if b == COPIES else (b * per_home, (b + 1) * per_home) for b in blocks]
        for columns, value in ((slice(0, d_model), rows), (slice(d_model, None), scaled)):
            chosen = {span: value[span[0]:span[1]] for span in spans}
            out_ref[:, columns] = stack(spans, chosen, out_ref.shape[0]).astype(BF16)


def padded(rows):
    return -(-rows // 16) * 16


def stack(order, blocks, height):
    values = [blocks[key] for key in order]
    missing = height - sum(v.shape[0] for v in values)
    if missing:
        values.append(jnp.zeros((missing, values[0].shape[1]), values[0].dtype))
    return jnp.concatenate(values, axis=0)


def fold_width(columns):
    return -(-columns // 256) * 128


def folded(rows):
    count, columns = rows.shape
    left = fold_width(columns)
    right = [rows[:, left:], jnp.zeros((count, 2 * left - columns), rows.dtype)]
    return jnp.concatenate([rows[:, :left], jnp.concatenate(right, axis=1)], axis=0)


def unfolded(rows, columns):
    count, left = rows.shape
    if left == columns:
        return rows
    return jnp.concatenate([rows[:count // 2], rows[count // 2:, :columns - left]], axis=1)


def slots_of(order, slot_ref, per_home, height):
    kinds = {HOME: slot_ref[:per_home], COPIES: slot_ref[per_home:]}
    return stack(order, {key: kinds[key[1]] for key in order}, height)


def fill_rows(order, pieces, per_home, per_copy, piece_refs, rows_ref):
    values = [unfolded(r[...].astype(F32), rows_ref.shape[1]) for r in piece_refs]
    blocks = {}
    for key in order:
        n, start = pieces[key]
        blocks[key] = values[n][start:start + (per_home if key[1] == HOME else per_copy)]
    rows_ref[...] = stack(order, blocks, rows_ref.shape[0]).astype(BF16)


def own_columns(rows_ref, w_ref, slot, local_count):
    d_model = w_ref.shape[1]
    width = w_ref.shape[0] // local_count
    every = lax.dot_general(rows_ref[:, :d_model], w_ref[...], NT, preferred_element_type=F32)
    own = jnp.zeros((rows_ref.shape[0], width), F32)
    for e in range(local_count):
        own = jnp.where(slot == e, every[:, e * width:(e + 1) * width], own)
    return own


def hold_kernel(local_count, dev_count, replica_ref, w_hbm, own_hbm, even_hbm,
                own_ref, even_ref, w_ref, slot_ref, sems):
    moves = [pltpu.make_async_copy(a, b, sems.at[n]) for n, (a, b) in enumerate(
        ((w_hbm, w_ref), (own_hbm, own_ref), (even_hbm, even_ref)))]
    for move in moves:
        move.start()
    per_home, per_copy = local_count * SLOT, dev_count * CAPR
    first = lax.axis_index("expert") * local_count
    width = slot_ref.shape[1]
    slot_ref[:per_home] = iota((per_home, width), 0) // SLOT
    row = iota((per_copy, width), 0)
    copy = jnp.full((per_copy, width), -1, jnp.int32)
    for d in range(dev_count):
        mine = (row >= d * CAPR) & (row < (d + 1) * CAPR)
        copy = jnp.where(mine, replica_ref[d] - first, copy)
    slot_ref[per_home:] = copy
    for move in moves:
        move.wait()


def turn_kernel(local_count, dev_count, line_ref, far_ref, near_ref, even_ref, beside_out, *line_outs):
    per_home = local_count * SLOT
    beside_out[...] = jnp.concatenate([far_ref[...].astype(F32), near_ref[...].astype(F32)], axis=0).astype(BF16)
    line, even = line_ref[...].astype(F32)[per_home:], even_ref[...].astype(F32)
    for n, out_ref in enumerate(line_outs):
        span = slice(n * per_home, (n + 1) * per_home)
        out_ref[...] = folded(jnp.concatenate([even[span], line[span]], axis=0)).astype(BF16)


def early_kernel(local_count, dev_count, order, pieces, w_ref, slot_ref, *refs):
    piece_refs, (rows_ref, own_ref) = refs[:-2], refs[-2:]
    per_home, per_copy = local_count * SLOT, dev_count * CAPR
    fill_rows(order, pieces, per_home, per_copy, piece_refs, rows_ref)
    slot = slots_of(order, slot_ref, per_home, rows_ref.shape[0])
    own_ref[...] = own_columns(rows_ref, w_ref, slot, local_count)


def late_kernel(local_count, dev_count, early, order, pieces, own_ref, w_ref, slot_ref, *refs):
    piece_refs, (rows_ref, back_ref, passed) = refs[:-3], refs[-3:]
    per_home, per_copy = local_count * SLOT, dev_count * CAPR
    fill_rows(order, pieces, per_home, per_copy, piece_refs, rows_ref)
    own = own_columns(rows_ref, w_ref, slots_of(order, slot_ref, per_home, rows_ref.shape[0]), local_count)
    if passed.shape[1] > per_home + per_copy:
        passed[:, per_home + per_copy:] = jnp.zeros_like(passed[:, per_home + per_copy:])
    for keys, value in ((early, own_ref[...]), (order, own)):
        start = 0
        for m, kind in keys:
            lower, size = (0, per_home) if kind == HOME else (per_home, per_copy)
            passed[m, lower:lower + size] = value[start:start + size]
            start += size
    me = lax.axis_index("expert")
    back = jnp.concatenate([passed[me ^ source] for source in range(dev_count)], axis=0)
    back_ref[...] = back.astype(back_ref.dtype)


def grad_weights_half(local_count, dev_count, orders, half, slot_ref, rows_refs, columns):
    start = pl.multiple_of(half * columns, 128)
    spread = []
    for order, ref in zip(orders, rows_refs):
        slot = slots_of(order, slot_ref, local_count * SLOT, ref.shape[0])
        scaled = ref[:, 2 * columns:].astype(F32)
        spread.append(jnp.concatenate([jnp.where(slot == e, scaled, 0.0) for e in range(local_count)], axis=1))
    rows = jnp.concatenate([ref[:, pl.ds(start, columns)] for ref in rows_refs], axis=0)
    return lax.dot_general(
        jnp.concatenate(spread, axis=0).astype(BF16), rows, TN, preferred_element_type=F32)


def other_half_kernel(local_count, dev_count, orders, slot_ref, early_ref, late_ref, out_ref):
    half = 1 - lax.axis_index("dp")
    out_ref[...] = grad_weights_half(
        local_count, dev_count, orders, half, slot_ref, (early_ref, late_ref), out_ref.shape[1]).astype(out_ref.dtype)


def own_half_kernel(local_count, dev_count, orders, slot_ref, early_ref, late_ref, arrived_ref, out_ref):
    half = lax.axis_index("dp")
    total = grad_weights_half(
        local_count, dev_count, orders, half, slot_ref, (early_ref, late_ref), out_ref.shape[1])
    out_ref[...] = (total + arrived_ref[...].astype(F32)).astype(out_ref.dtype)


def combine_kernel(local_count, dev_count, back_ref, pick_ref, expert_ref, hs_ref, ps_ref, ids_ref,
                   grad_h_ref, grad_p_ref, wide, narrow):
    top, toks = ids_ref.shape
    per_home = local_count * SLOT
    me = lax.axis_index("expert")
    back = [back_ref[me ^ m].astype(F32) for m in range(dev_count)]
    slots = pick_ref.shape[0]
    copies = slots - dev_count * per_home
    copy = functools.reduce(jnp.add, [b[per_home:per_home + copies] for b in back])
    grad_in = jnp.concatenate([b[:per_home] for b in back] + [copy], axis=0)
    h_rows = (ps_ref[...] * grad_in).astype(BF16)
    p_rows = jnp.sum(hs_ref[...] * grad_in, axis=1, keepdims=True)
    ids = ids_ref[...]
    pick = pick_ref[...]
    expert = expert_ref[...]
    sels = [jnp.where(ids[k:k + 1, :] == expert, pick, 0.0) for k in range(top)]
    rows = lax.dot_general(
        jnp.concatenate([sel.astype(BF16) for sel in sels], axis=1), h_rows, TN, preferred_element_type=F32)
    for k, sel in enumerate(sels):
        wide[pl.ds(k, toks, stride=top), :] = rows[k * toks:(k + 1) * toks]
        narrow[k:k + 1, :] = jnp.sum(sel * p_rows, axis=0, keepdims=True)
    grad_h_ref[...] = wide[...].astype(grad_h_ref.dtype)
    grad_p_ref[...] = narrow[...].astype(grad_p_ref.dtype)


def call(kernel, out_shape, operands, scratch=(), flops=0, limit=24):
    shapes = jax.tree.leaves(out_shape)
    moved = sum(a.size * a.dtype.itemsize for a in (*(a for _, a in operands), *shapes))
    return pl.pallas_call(
        kernel,
        out_shape=out_shape,
        in_specs=[pl.BlockSpec(memory_space=space) for space, _ in operands],
        out_specs=jax.tree.map(lambda _: pl.BlockSpec(memory_space=pltpu.VMEM), out_shape),
        scratch_shapes=list(scratch),
        compiler_params=pltpu.CompilerParams(vmem_limit_bytes=limit << 20),
        cost_estimate=pl.CostEstimate(flops=flops, bytes_accessed=moved, transcendentals=0),
    )(*(a for _, a in operands))


def swap(x, bits, count):
    return lax.ppermute(x, "expert", [(i, i ^ bits) for i in range(count)])


def gather_body(cotangent, hidden, probs, expert_ids, send_counts, replica_of, weights):
    toks, d_model = cotangent.shape
    top = expert_ids.shape[1]
    width = hidden.shape[2]
    local_count = weights.shape[0]
    dev_count = lax.axis_size("expert")
    homes = dev_count * local_count * SLOT
    copies = dev_count * CAPR
    slots = homes + copies
    rows = homes + dev_count * copies
    columns = d_model // 2
    sizes = (local_count, dev_count)
    ids = expert_ids.T
    shape = jax.ShapeDtypeStruct
    hbm, vmem, smem = pltpu.HBM, pltpu.VMEM, pltpu.SMEM
    sources = (replica_of, send_counts, ids, probs.T, hidden.reshape(toks * top, width), cotangent)
    per_home = local_count * SLOT
    odd, even = range(1, dev_count, 2), range(2, dev_count, 2)
    packing = [[*odd], [COPIES], [0, COPIES], [*even]]
    sized = [sum(copies if b == COPIES else per_home for b in blocks) for blocks in packing]
    sized[2:] = [padded(n) for n in sized[2:]]
    pick, expert, h_slot, p_slot, to_beside, copy_rows, own_rows, even_rows = call(
        functools.partial(dispatch_kernel, *sizes, packing),
        [shape((slots, toks), F32), shape((slots, toks), jnp.int32), shape((slots, width), F32),
         shape((slots, width), F32)] + [shape((n, d_model + width), BF16) for n in sized],
        [(hbm, a) for a in sources],
        [(smem if n < 2 else vmem)(a.shape, a.dtype) for n, a in enumerate(sources)]
        + [vmem((toks * top, width), F32), pltpu.SemaphoreType.DMA((len(sources),))],
        flops=2 * slots * toks * d_model,
        limit=60,
    )
    near, far, beside = (swap(copy_rows, bits, dev_count) for bits in (2, 4, 1))
    line = swap(to_beside, 1, dev_count)
    flat_w = weights.reshape(local_count * width, d_model)
    own_rows, even_rows, w_held, slot = call(
        functools.partial(hold_kernel, *sizes),
        [shape(a.shape, BF16) for a in (own_rows, even_rows, flat_w)] + [shape((per_home + copies, width), jnp.int32)],
        [(smem, replica_of)] + [(hbm, a) for a in (flat_w, own_rows, even_rows)],
        [pltpu.SemaphoreType.DMA((3,))],
    )
    near, far, line, beside, own_rows, even_rows, w_held, slot = lax.optimization_barrier(
        (near, far, line, beside, own_rows, even_rows, w_held, slot))
    far_near = swap(far, 2, dev_count)
    to_beside, *lines = call(
        functools.partial(turn_kernel, *sizes),
        [shape((2 * copies, d_model + width), BF16)]
        + [shape((4 * per_home, fold_width(d_model + width)), BF16)] * len(even),
        [(vmem, a) for a in (line, far, near, even_rows)],
    )
    onward = swap(to_beside, 1, dev_count)
    lines = [swap(a, m, dev_count) for a, m in zip(lines, even)]
    pieces = {(0, HOME): (0, 0), (0, COPIES): (0, per_home), (1, COPIES): (1, 0), (1, HOME): (5, 0),
              (2, COPIES): (2, 0), (4, COPIES): (3, 0),
              (even[-1], HOME): (4, 0), (even[-1] + 1, HOME): (4, per_home)}
    orders = [list(pieces)]
    height = padded(sum(per_home if kind == HOME else copies for _, kind in pieces))
    early_rows, own = call(
        functools.partial(early_kernel, *sizes, orders[0], pieces),
        (shape((height, d_model + width), BF16), shape((height, width), F32)),
        [(vmem, a) for a in (w_held, slot, own_rows, beside, near, far, lines[-1], line)],
        flops=2 * height * d_model * local_count * width * 30,
    )
    far_across = swap(far_near, 1, dev_count)
    arrays = [far_near, far_across, onward, *lines[-2::-1]]
    pieces = {(6, COPIES): (0, 0), (7, COPIES): (1, 0), (5, COPIES): (2, 0), (3, COPIES): (2, copies)}
    for n, m in enumerate(even[-2::-1]):
        pieces[m, HOME], pieces[m + 1, HOME] = ((3 + n, k * per_home) for k in range(2))
    orders.append(list(pieces))
    height = padded(sum(per_home if kind == HOME else copies for _, kind in pieces))
    block = padded(per_home + copies)
    late_rows, back = call(
        functools.partial(late_kernel, *sizes, *orders, pieces),
        (shape((height, d_model + width), BF16), shape((dev_count * block, width), BF16)),
        [(vmem, a) for a in (own, w_held, slot, *arrays)],
        [vmem((dev_count, block, width), F32)],
        flops=2 * height * d_model * local_count * width,
    )
    back = lax.all_to_all(back, "expert", split_axis=0, concat_axis=0, tiled=True)
    half_flops = 2 * rows * columns * local_count * width
    halves = (slot, early_rows, late_rows)
    other = call(
        functools.partial(other_half_kernel, *sizes, orders),
        shape((local_count * width, columns), BF16),
        [(vmem, a) for a in halves],
        flops=half_flops,
    )
    arrived = lax.ppermute(other, "dp", [(0, 1), (1, 0)])
    grad_w = call(
        functools.partial(own_half_kernel, *sizes, orders),
        shape((local_count * width, columns), BF16),
        [(vmem, a) for a in (*halves, arrived)],
        flops=30 * half_flops,
    )
    grad_w, pick = lax.optimization_barrier((grad_w, pick))
    grad_h, grad_p = call(
        functools.partial(combine_kernel, *sizes),
        (shape((toks * top, width), BF16), shape((top, toks), BF16)),
        [(vmem, a) for a in (back.reshape(dev_count, block, width), pick, expert, h_slot, p_slot, ids)],
        [vmem((toks * top, width), F32), vmem((top, toks), F32)],
        flops=2 * slots * toks * width * top,
    )
    return (
        grad_h.reshape(toks, top, width),
        grad_p.T,
        grad_w.reshape(local_count, width, columns),
    )


def body(cotangent, hidden, probs, expert_ids, send_counts, replica_of, weights):
    dev_count = lax.axis_size("expert")
    local_count, width, _ = weights.shape
    gathered = dev_count * dev_count * CAPR
    if gathered <= (local_count + 3) * width and dev_count == 8 and lax.axis_size("dp") == 2:
        run = gather_body
    else:
        run = replica_body
    return run(cotangent, hidden, probs, expert_ids, send_counts, replica_of, weights)


def solution(mesh):
    in_specs = (
        P(("groups", "expert", "dp"), None),
        P(("groups", "expert", "dp"), None, None),
        P(("groups", "expert", "dp"), None),
        P(("groups", "expert", "dp"), None),
        P(("groups", "expert", "dp"), None),
        P("groups"),
        P("expert", None, None),
    )
    out_specs = (
        P(("groups", "expert", "dp"), None, None),
        P(("groups", "expert", "dp"), None),
        P(("groups", "expert"), None, "dp"),
    )
    return jax.shard_map(body, mesh=mesh, in_specs=in_specs, out_specs=out_specs, check_vma=False)
```

```python
import functools

import jax
import jax.numpy as jnp
from jax import lax
from jax.experimental import pallas as pl
from jax.experimental.pallas import tpu as pltpu
from jax.sharding import PartitionSpec as P

CAPH = 3
CAPR = 3


def ranks_within(keys):
    total_rows = keys.shape[0]
    sort_order = jnp.argsort(keys * total_rows + jnp.arange(total_rows, dtype=jnp.int32))
    sorted_keys = keys[sort_order]
    first_seen = jnp.searchsorted(sorted_keys, sorted_keys, side="left")
    ranked = jnp.arange(total_rows, dtype=jnp.int32) - first_seen
    return jnp.zeros((total_rows,), jnp.int32).at[sort_order].set(ranked)


def route_rows(ids_block, counts_row, replica_of, local_count, cap_home, cap_copy):
    dev_count = replica_of.shape[0]
    experts = ids_block.reshape(-1)
    rank_expert = ranks_within(experts)
    devices = jnp.arange(dev_count, dtype=jnp.int32)
    same_copy = (replica_of[:, None] == replica_of[None, :]) & (devices[None, :] < devices[:, None])
    lower_rank = jnp.sum(jnp.where(same_copy, counts_row[None, :], 0), axis=1)
    upper_rank = lower_rank + counts_row
    hit_table = (
        (replica_of[None, :] == experts[:, None])
        & (lower_rank[None, :] <= rank_expert[:, None])
        & (rank_expert[:, None] < upper_rank[None, :])
    )
    copied = jnp.any(hit_table, axis=1)
    copy_dev = jnp.sum(jnp.where(hit_table, devices[None, :], 0), axis=1)
    dest_dev = jnp.where(copied, copy_dev, experts // local_count)
    index_of_slot = jnp.where(copied, local_count, experts % local_count)
    rank_bucket = ranks_within(dest_dev * (local_count + 1) + index_of_slot)
    keep_row = rank_bucket < jnp.where(copied, cap_copy, cap_home)
    per_dev = local_count * cap_home + cap_copy
    target = dest_dev * per_dev + index_of_slot * cap_home + rank_bucket
    return jnp.where(keep_row, target, dev_count * per_dev)


def replica_body(cotangent, hidden, probs, expert_ids, send_counts, replica_of, weights):
    tok_rows, d_model = cotangent.shape
    top_count = expert_ids.shape[1]
    hidden_width = hidden.shape[2]
    local_count = weights.shape[0]
    dev_count = lax.axis_size("expert")
    data_count = lax.axis_size("dp")
    per_dev = local_count * CAPH + CAPR
    row_count = tok_rows * top_count
    recv_count = dev_count * per_dev
    target = route_rows(expert_ids, send_counts[0], replica_of, local_count, CAPH, CAPR)
    inverse = (
        jnp.full((recv_count,), row_count, jnp.int32)
        .at[target]
        .set(jnp.arange(row_count, dtype=jnp.int32), mode="drop")
    )
    dy_pad = jnp.concatenate([cotangent, jnp.zeros((1, d_model), cotangent.dtype)], axis=0)
    h_pad = jnp.concatenate(
        [hidden.reshape(row_count, hidden_width), jnp.zeros((1, hidden_width), hidden.dtype)],
        axis=0,
    )
    p_pad = jnp.concatenate([probs.reshape(row_count), jnp.zeros((1,), probs.dtype)], axis=0)
    send_dy = dy_pad[inverse // top_count]
    send_h = h_pad[inverse]
    send_p = p_pad[inverse]
    recv_dy, recv_h, recv_p = (
        lax.all_to_all(send_dy, "expert", split_axis=0, concat_axis=0, tiled=True),
        lax.all_to_all(send_h, "expert", split_axis=0, concat_axis=0, tiled=True),
        lax.all_to_all(send_p, "expert", split_axis=0, concat_axis=0, tiled=True),
    )
    flat_size = hidden_width * d_model
    flat_w = weights.reshape(local_count, flat_size)
    pieces = lax.all_to_all(flat_w, "expert", split_axis=1, concat_axis=0, tiled=True)
    chosen = pieces[replica_of]
    copy_weight = lax.all_to_all(chosen, "expert", split_axis=0, concat_axis=0, tiled=True).reshape(
        hidden_width, d_model
    )
    slot_total = local_count + 1
    home_rows = local_count * CAPH
    row_pos = jnp.arange(recv_count, dtype=jnp.int32) % per_dev
    row_slot = jnp.where(row_pos < home_rows, row_pos // CAPH, local_count)
    all_weights = jnp.concatenate(
        [weights.reshape(local_count * hidden_width, d_model), copy_weight], axis=0
    )
    all_in = lax.dot_general(
        recv_dy, all_weights, (((1,), (1,)), ((), ())), preferred_element_type=jnp.float32
    )
    grad_in = jnp.zeros((recv_count, hidden_width), jnp.float32)
    for slot_num in range(slot_total):
        grad_in = grad_in + jnp.where(
            (row_slot == slot_num)[:, None],
            all_in[:, slot_num * hidden_width : (slot_num + 1) * hidden_width],
            0.0,
        )
    p_wide = recv_p.astype(jnp.float32)[:, None]
    h_wide = recv_h.astype(jnp.float32)
    grad_h_buf = (p_wide * grad_in).astype(jnp.bfloat16)
    grad_p_buf = jnp.sum(h_wide * grad_in, axis=1).astype(jnp.bfloat16)
    scaled = (p_wide * h_wide).astype(jnp.bfloat16)
    zero_rows = jnp.zeros_like(scaled)
    scaled_wide = jnp.concatenate(
        [
            jnp.where((row_slot == slot_num)[:, None], scaled, zero_rows)
            for slot_num in range(slot_total)
        ],
        axis=1,
    )
    parts = lax.dot_general(
        scaled_wide, recv_dy, (((0,), (0,)), ((), ())), preferred_element_type=jnp.float32
    ).astype(jnp.bfloat16)
    home_part = parts[: local_count * hidden_width].reshape(local_count, hidden_width, d_model)
    copy_part = parts[local_count * hidden_width :]
    back_h, back_p = (
        lax.all_to_all(grad_h_buf, "expert", split_axis=0, concat_axis=0, tiled=True),
        lax.all_to_all(grad_p_buf, "expert", split_axis=0, concat_axis=0, tiled=True),
    )
    flat_h = jnp.concatenate([back_h, jnp.zeros((1, hidden_width), back_h.dtype)], axis=0)
    flat_p = jnp.concatenate([back_p, jnp.zeros((1,), back_p.dtype)], axis=0)
    hidden_gradient = flat_h[target].reshape(tok_rows, top_count, hidden_width)
    grad_probs = flat_p[target].reshape(tok_rows, top_count)
    expert_total = dev_count * local_count
    cover = replica_of[None, :] == jnp.arange(expert_total, dtype=jnp.int32)[:, None]
    half_width = d_model // data_count
    halves = lax.all_to_all(copy_part, "dp", split_axis=1, concat_axis=0, tiled=True)
    copy_half = jnp.sum(
        halves.reshape(data_count, hidden_width, half_width).astype(jnp.float32), axis=0
    )
    piece_len = hidden_width * half_width // dev_count
    slabs = copy_half.reshape(dev_count, piece_len)
    arrived = lax.all_to_all(slabs, "expert", split_axis=0, concat_axis=0, tiled=True)
    sums = jnp.dot(cover.astype(jnp.float32), arrived, precision=lax.Precision.HIGHEST)
    homed = lax.all_to_all(
        sums.reshape(dev_count, local_count * piece_len),
        "expert",
        split_axis=0,
        concat_axis=0,
        tiled=True,
    )
    homed = (
        homed.reshape(dev_count, local_count, piece_len)
        .transpose(1, 0, 2)
        .reshape(local_count, hidden_width, half_width)
    )
    home_half = lax.psum_scatter(
        home_part.astype(jnp.float32).astype(jnp.bfloat16), "dp", scatter_dimension=2, tiled=True
    ).astype(jnp.float32)
    grad_weights = (home_half + homed).astype(jnp.bfloat16)
    return (hidden_gradient, grad_probs, grad_weights)


SLOT = 3
HOME, COPIES = "home", "copies"
F32 = jnp.float32
BF16 = jnp.bfloat16
NT = (((1,), (1,)), ((), ()))
TN = (((0,), (0,)), ((), ()))


def iota(shape, dim):
    return lax.broadcasted_iota(jnp.int32, shape, dim)


def dispatch_kernel(local_count, dev_count, packing, *refs):
    sources, refs = refs[:6], refs[6:]
    pick_ref, expert_ref, hs_ref, ps_ref = refs[:4]
    packed, (held, wide, sems) = refs[4:4 + len(packing)], (refs[-8:-2], refs[-2], refs[-1])
    moves = [pltpu.make_async_copy(s, h, sems.at[n]) for n, (s, h) in enumerate(zip(sources, held))]
    for move in moves:
        move.start()
    replica_ref, counts_ref, ids_ref, probs_ref, hid_ref, cot_ref = held
    top, toks = ids_ref.shape
    per_home = local_count * SLOT
    homes = dev_count * per_home
    slots = homes + dev_count * CAPR
    me = lax.axis_index("expert")
    row = iota((slots, toks), 0)
    expert = ((row // per_home) ^ me) * local_count + (row % per_home) // SLOT
    within = row % SLOT
    allowed = jnp.where(within < CAPH, 1, 0)
    before = jnp.where(iota((toks, toks), 0) < iota((toks, toks), 1), 1.0, 0.0).astype(BF16)
    for move in moves[:3]:
        move.wait()
    for d in range(dev_count):
        first = homes + d * CAPR
        mine = (row >= first) & (row < first + CAPR)
        expert = jnp.where(mine, replica_ref[d], expert)
        within = jnp.where(mine, row - first, within)
        allowed = jnp.where(mine, jnp.where(row - first < counts_ref[0, d], 1, 0), allowed)
    lower = jnp.zeros((slots, toks), jnp.int32)
    for d in range(dev_count):
        earlier = (row < homes) | (row >= homes + (d + 1) * CAPR)
        lower = lower + jnp.where(earlier & (expert == replica_ref[d]), counts_ref[0, d], 0)
    ids = ids_ref[...]
    named = jnp.zeros((slots, toks), F32)
    for k in range(top):
        named = named + jnp.where(ids[k:k + 1, :] == expert, 1.0, 0.0)
    rank = jnp.dot(named.astype(BF16), before, preferred_element_type=F32)
    wanted = (lower + within).astype(F32)
    pick = jnp.where((rank == wanted) & (allowed > 0), named, 0.0)
    pick_ref[...] = pick
    expert_ref[...] = expert
    for move in moves[3:5]:
        move.wait()
    wide[...] = hid_ref[...].astype(F32)
    p_slot = jnp.zeros((slots, toks), F32)
    probs = probs_ref[...].astype(F32)
    chosen, values = [], []
    for k in range(top):
        sel = jnp.where(ids[k:k + 1, :] == expert, pick, 0.0)
        chosen.append(sel.astype(BF16))
        values.append(wide[pl.ds(k, toks, stride=top), :].astype(BF16))
        p_slot = p_slot + sel * probs[k:k + 1, :]
    h_slot = jnp.dot(
        jnp.concatenate(chosen, axis=1), jnp.concatenate(values, axis=0), preferred_element_type=F32)
    p_slot = jnp.sum(p_slot, axis=1, keepdims=True)
    hs_ref[...] = h_slot
    ps_ref[...] = jnp.broadcast_to(p_slot, ps_ref.shape)
    scaled = p_slot * h_slot
    moves[5].wait()
    rows = jnp.dot(pick.astype(BF16), cot_ref[...], preferred_element_type=F32)
    d_model = cot_ref.shape[1]
    for out_ref, blocks in zip(packed, packing):
        spans = [(homes, slots) if b == COPIES else (b * per_home, (b + 1) * per_home) for b in blocks]
        for columns, value in ((slice(0, d_model), rows), (slice(d_model, None), scaled)):
            chosen = {span: value[span[0]:span[1]] for span in spans}
            out_ref[:, columns] = stack(spans, chosen, out_ref.shape[0]).astype(BF16)


def padded(rows):
    return -(-rows // 16) * 16


def stack(order, blocks, height):
    values = [blocks[key] for key in order]
    missing = height - sum(v.shape[0] for v in values)
    if missing:
        values.append(jnp.zeros((missing, values[0].shape[1]), values[0].dtype))
    return jnp.concatenate(values, axis=0)


def fold_width(columns):
    return -(-columns // 256) * 128


def folded(rows):
    count, columns = rows.shape
    left = fold_width(columns)
    right = [rows[:, left:], jnp.zeros((count, 2 * left - columns), rows.dtype)]
    return jnp.concatenate([rows[:, :left], jnp.concatenate(right, axis=1)], axis=0)


def unfolded(rows, columns):
    count, left = rows.shape
    if left == columns:
        return rows
    return jnp.concatenate([rows[:count // 2], rows[count // 2:, :columns - left]], axis=1)


def slots_of(order, slot_ref, per_home, height):
    kinds = {HOME: slot_ref[:per_home], COPIES: slot_ref[per_home:]}
    return stack(order, {key: kinds[key[1]] for key in order}, height)


def fill_rows(order, pieces, per_home, per_copy, piece_refs, rows_ref):
    values = [unfolded(r[...].astype(F32), rows_ref.shape[1]) for r in piece_refs]
    blocks = {}
    for key in order:
        n, start = pieces[key]
        blocks[key] = values[n][start:start + (per_home if key[1] == HOME else per_copy)]
    rows_ref[...] = stack(order, blocks, rows_ref.shape[0]).astype(BF16)


def own_columns(rows_ref, w_ref, slot, local_count):
    d_model = w_ref.shape[1]
    width = w_ref.shape[0] // local_count
    every = lax.dot_general(rows_ref[:, :d_model], w_ref[...], NT, preferred_element_type=F32)
    own = jnp.zeros((rows_ref.shape[0], width), F32)
    for e in range(local_count):
        own = jnp.where(slot == e, every[:, e * width:(e + 1) * width], own)
    return own


def hold_kernel(local_count, dev_count, replica_ref, w_hbm, own_hbm, even_hbm,
                own_ref, even_ref, w_ref, slot_ref, sems):
    moves = [pltpu.make_async_copy(a, b, sems.at[n]) for n, (a, b) in enumerate(
        ((w_hbm, w_ref), (own_hbm, own_ref), (even_hbm, even_ref)))]
    for move in moves:
        move.start()
    per_home, per_copy = local_count * SLOT, dev_count * CAPR
    first = lax.axis_index("expert") * local_count
    width = slot_ref.shape[1]
    slot_ref[:per_home] = iota((per_home, width), 0) // SLOT
    row = iota((per_copy, width), 0)
    copy = jnp.full((per_copy, width), -1, jnp.int32)
    for d in range(dev_count):
        mine = (row >= d * CAPR) & (row < (d + 1) * CAPR)
        copy = jnp.where(mine, replica_ref[d] - first, copy)
    slot_ref[per_home:] = copy
    for move in moves:
        move.wait()


def turn_kernel(local_count, dev_count, beside_ref, even_ref, *line_refs):
    per_home, per_copy = local_count * SLOT, dev_count * CAPR
    beside = beside_ref[...].astype(F32)[per_home:]
    even = even_ref[...].astype(F32)
    for n, line_ref in enumerate(line_refs):
        span = slice(n * per_home, (n + 1) * per_home)
        line_ref[...] = folded(jnp.concatenate([even[span], beside[span]], axis=0)).astype(BF16)


def place(order, value, per_home, per_copy, placed):
    start = 0
    for m, kind in order:
        lower, size = (0, per_home) if kind == HOME else (per_home, per_copy)
        placed[m, lower:lower + size] = value[start:start + size]
        start += size


def early_kernel(local_count, dev_count, order, pieces, w_ref, slot_ref, *refs):
    piece_refs, (rows_ref, own_ref) = refs[:-2], refs[-2:]
    per_home, per_copy = local_count * SLOT, dev_count * CAPR
    fill_rows(order, pieces, per_home, per_copy, piece_refs, rows_ref)
    slot = slots_of(order, slot_ref, per_home, rows_ref.shape[0])
    own_ref[...] = jnp.zeros_like(own_ref)
    place(order, own_columns(rows_ref, w_ref, slot, local_count), per_home, per_copy, own_ref)


def late_kernel(local_count, dev_count, order, pieces, own_ref, w_ref, slot_ref, *refs):
    piece_refs, (rows_ref, back_ref, placed) = refs[:-3], refs[-3:]
    per_home, per_copy = local_count * SLOT, dev_count * CAPR
    placed[...] = own_ref[...]
    fill_rows(order, pieces, per_home, per_copy, piece_refs, rows_ref)
    slot = slots_of(order, slot_ref, per_home, rows_ref.shape[0])
    place(order, own_columns(rows_ref, w_ref, slot, local_count), per_home, per_copy, placed)
    me = lax.axis_index("expert")
    back = jnp.concatenate([placed[me ^ source] for source in range(dev_count)], axis=0)
    back_ref[...] = back.astype(back_ref.dtype)


def grad_weights_half(local_count, dev_count, orders, half, slot_ref, rows_refs, columns):
    start = pl.multiple_of(half * columns, 128)
    spread = []
    for order, ref in zip(orders, rows_refs):
        slot = slots_of(order, slot_ref, local_count * SLOT, ref.shape[0])
        scaled = ref[:, 2 * columns:].astype(F32)
        spread.append(jnp.concatenate([jnp.where(slot == e, scaled, 0.0) for e in range(local_count)], axis=1))
    rows = jnp.concatenate([ref[:, pl.ds(start, columns)] for ref in rows_refs], axis=0)
    return lax.dot_general(
        jnp.concatenate(spread, axis=0).astype(BF16), rows, TN, preferred_element_type=F32)


def other_half_kernel(local_count, dev_count, orders, slot_ref, early_ref, late_ref, out_ref):
    half = 1 - lax.axis_index("dp")
    out_ref[...] = grad_weights_half(
        local_count, dev_count, orders, half, slot_ref, (early_ref, late_ref), out_ref.shape[1]).astype(out_ref.dtype)


def own_half_kernel(local_count, dev_count, orders, slot_ref, early_ref, late_ref, arrived_ref, out_ref):
    half = lax.axis_index("dp")
    total = grad_weights_half(
        local_count, dev_count, orders, half, slot_ref, (early_ref, late_ref), out_ref.shape[1])
    out_ref[...] = (total + arrived_ref[...].astype(F32)).astype(out_ref.dtype)


def combine_kernel(local_count, dev_count, back_ref, pick_ref, expert_ref, hs_ref, ps_ref, ids_ref,
                   grad_h_ref, grad_p_ref, wide, narrow):
    top, toks = ids_ref.shape
    per_home = local_count * SLOT
    me = lax.axis_index("expert")
    back = [back_ref[me ^ m].astype(F32) for m in range(dev_count)]
    slots = pick_ref.shape[0]
    copies = slots - dev_count * per_home
    copy = functools.reduce(jnp.add, [b[per_home:per_home + copies] for b in back])
    grad_in = jnp.concatenate([b[:per_home] for b in back] + [copy], axis=0)
    h_rows = (ps_ref[...] * grad_in).astype(BF16)
    p_rows = jnp.sum(hs_ref[...] * grad_in, axis=1, keepdims=True)
    ids = ids_ref[...]
    pick = pick_ref[...]
    expert = expert_ref[...]
    sels = [jnp.where(ids[k:k + 1, :] == expert, pick, 0.0) for k in range(top)]
    rows = lax.dot_general(
        jnp.concatenate([sel.astype(BF16) for sel in sels], axis=1), h_rows, TN, preferred_element_type=F32)
    for k, sel in enumerate(sels):
        wide[pl.ds(k, toks, stride=top), :] = rows[k * toks:(k + 1) * toks]
        narrow[k:k + 1, :] = jnp.sum(sel * p_rows, axis=0, keepdims=True)
    grad_h_ref[...] = wide[...].astype(grad_h_ref.dtype)
    grad_p_ref[...] = narrow[...].astype(grad_p_ref.dtype)


def call(kernel, out_shape, operands, scratch=(), flops=0, limit=24):
    shapes = jax.tree.leaves(out_shape)
    moved = sum(a.size * a.dtype.itemsize for a in (*(a for _, a in operands), *shapes))
    return pl.pallas_call(
        kernel,
        out_shape=out_shape,
        in_specs=[pl.BlockSpec(memory_space=space) for space, _ in operands],
        out_specs=jax.tree.map(lambda _: pl.BlockSpec(memory_space=pltpu.VMEM), out_shape),
        scratch_shapes=list(scratch),
        compiler_params=pltpu.CompilerParams(vmem_limit_bytes=limit << 20),
        cost_estimate=pl.CostEstimate(flops=flops, bytes_accessed=moved, transcendentals=0),
    )(*(a for _, a in operands))


def swap(x, bits, count):
    return lax.ppermute(x, "expert", [(i, i ^ bits) for i in range(count)])


def gather_body(cotangent, hidden, probs, expert_ids, send_counts, replica_of, weights):
    toks, d_model = cotangent.shape
    top = expert_ids.shape[1]
    width = hidden.shape[2]
    local_count = weights.shape[0]
    dev_count = lax.axis_size("expert")
    homes = dev_count * local_count * SLOT
    copies = dev_count * CAPR
    slots = homes + copies
    rows = homes + dev_count * copies
    columns = d_model // 2
    sizes = (local_count, dev_count)
    ids = expert_ids.T
    shape = jax.ShapeDtypeStruct
    hbm, vmem, smem = pltpu.HBM, pltpu.VMEM, pltpu.SMEM
    sources = (replica_of, send_counts, ids, probs.T, hidden.reshape(toks * top, width), cotangent)
    per_home = local_count * SLOT
    odd, even = range(1, dev_count, 2), range(2, dev_count, 2)
    packing = [[*odd], [COPIES], [0, COPIES], [*even]]
    sized = [sum(copies if b == COPIES else per_home for b in blocks) for blocks in packing]
    sized[2:] = [padded(n) for n in sized[2:]]
    pick, expert, h_slot, p_slot, to_beside, copy_rows, own_rows, even_rows = call(
        functools.partial(dispatch_kernel, *sizes, packing),
        [shape((slots, toks), F32), shape((slots, toks), jnp.int32), shape((slots, width), F32),
         shape((slots, width), F32)] + [shape((n, d_model + width), BF16) for n in sized],
        [(hbm, a) for a in sources],
        [(smem if n < 2 else vmem)(a.shape, a.dtype) for n, a in enumerate(sources)]
        + [vmem((toks * top, width), F32), pltpu.SemaphoreType.DMA((len(sources),))],
        flops=2 * slots * toks * d_model,
        limit=60,
    )
    near, far, beside = (swap(copy_rows, bits, dev_count) for bits in (2, 4, 1))
    line = swap(to_beside, 1, dev_count)
    flat_w = weights.reshape(local_count * width, d_model)
    own_rows, even_rows, w_held, slot = call(
        functools.partial(hold_kernel, *sizes),
        [shape(a.shape, BF16) for a in (own_rows, even_rows, flat_w)] + [shape((per_home + copies, width), jnp.int32)],
        [(smem, replica_of)] + [(hbm, a) for a in (flat_w, own_rows, even_rows)],
        [pltpu.SemaphoreType.DMA((3,))],
    )
    near, far, line, beside, own_rows, even_rows, w_held, slot = lax.optimization_barrier(
        (near, far, line, beside, own_rows, even_rows, w_held, slot))
    far_near = swap(far, 2, dev_count)
    lines = call(
        functools.partial(turn_kernel, *sizes),
        [shape((4 * per_home, fold_width(d_model + width)), BF16)] * len(even),
        [(vmem, a) for a in (line, even_rows)],
    )
    far_beside, near_beside = swap(far, 1, dev_count), swap(near, 1, dev_count)
    lines = [swap(a, m, dev_count) for a, m in zip(lines, even)]
    pieces = {(0, HOME): (0, 0), (0, COPIES): (0, per_home), (1, COPIES): (1, 0), (1, HOME): (7, 0),
              (2, COPIES): (2, 0), (4, COPIES): (3, 0), (5, COPIES): (4, 0), (3, COPIES): (5, 0),
              (even[-1], HOME): (6, 0), (even[-1] + 1, HOME): (6, per_home)}
    orders, block = [list(pieces)], padded(per_home + copies)
    height = padded(sum(per_home if kind == HOME else copies for _, kind in pieces))
    early_rows, own = call(
        functools.partial(early_kernel, *sizes, orders[0], pieces),
        (shape((height, d_model + width), BF16), shape((dev_count, block, width), F32)),
        [(vmem, a) for a in (w_held, slot, own_rows, beside, near, far, far_beside, near_beside, lines[-1], line)],
        flops=6 * 2 * height * d_model * local_count * width,
    )
    far_across = swap(far_near, 1, dev_count)
    arrays = [far_near, far_across, *lines[:-1]]
    pieces = {(6, COPIES): (0, 0), (7, COPIES): (1, 0)}
    for n, m in enumerate(even[:-1]):
        pieces[m, HOME], pieces[m + 1, HOME] = ((2 + n, k * per_home) for k in range(2))
    orders.append(list(pieces))
    height = padded(sum(per_home if kind == HOME else copies for _, kind in pieces))
    late_rows, back = call(
        functools.partial(late_kernel, *sizes, orders[1], pieces),
        (shape((height, d_model + width), BF16), shape((dev_count * block, width), BF16)),
        [(vmem, a) for a in (own, w_held, slot, *arrays)],
        [vmem((dev_count, block, width), F32)],
        flops=2 * height * d_model * local_count * width,
    )
    back = lax.all_to_all(back, "expert", split_axis=0, concat_axis=0, tiled=True)
    half_flops = 2 * rows * columns * local_count * width
    halves = (slot, early_rows, late_rows)
    other = call(
        functools.partial(other_half_kernel, *sizes, orders),
        shape((local_count * width, columns), BF16),
        [(vmem, a) for a in halves],
        flops=half_flops,
    )
    arrived = lax.ppermute(other, "dp", [(0, 1), (1, 0)])
    grad_w = call(
        functools.partial(own_half_kernel, *sizes, orders),
        shape((local_count * width, columns), BF16),
        [(vmem, a) for a in (*halves, arrived)],
        flops=30 * half_flops,
    )
    grad_w, pick = lax.optimization_barrier((grad_w, pick))
    grad_h, grad_p = call(
        functools.partial(combine_kernel, *sizes),
        (shape((toks * top, width), BF16), shape((top, toks), BF16)),
        [(vmem, a) for a in (back.reshape(dev_count, block, width), pick, expert, h_slot, p_slot, ids)],
        [vmem((toks * top, width), F32), vmem((top, toks), F32)],
        flops=2 * slots * toks * width * top,
    )
    return (
        grad_h.reshape(toks, top, width),
        grad_p.T,
        grad_w.reshape(local_count, width, columns),
    )


def body(cotangent, hidden, probs, expert_ids, send_counts, replica_of, weights):
    dev_count = lax.axis_size("expert")
    local_count, width, _ = weights.shape
    gathered = dev_count * dev_count * CAPR
    if gathered <= (local_count + 3) * width and dev_count == 8 and lax.axis_size("dp") == 2:
        run = gather_body
    else:
        run = replica_body
    return run(cotangent, hidden, probs, expert_ids, send_counts, replica_of, weights)


def solution(mesh):
    in_specs = (
        P(("groups", "expert", "dp"), None),
        P(("groups", "expert", "dp"), None, None),
        P(("groups", "expert", "dp"), None),
        P(("groups", "expert", "dp"), None),
        P(("groups", "expert", "dp"), None),
        P("groups"),
        P("expert", None, None),
    )
    out_specs = (
        P(("groups", "expert", "dp"), None, None),
        P(("groups", "expert", "dp"), None),
        P(("groups", "expert"), None, "dp"),
    )
    return jax.shard_map(body, mesh=mesh, in_specs=in_specs, out_specs=out_specs, check_vma=False)
```
